32 devices in a mesh: gx: 4 (over z), gy: 4 (over y, core), gz: 2 (over x).
Axes of the slice: x: 2, y: 2, z: 4, core: 2. Of those that a mesh axis runs over, the one named last changes fastest.
Arguments:
- basis: bfloat16 [32, 32, 16, 8192], P('gx', 'gy', 'gz'), may hold values from -0.1875 to 0.1875
- classes: int32 [32, 32, 16], P('gx', 'gy', 'gz'), may hold values from 0 to 15
- cond_table: float32 [16], replicated, may hold values from 0.5 to 2
- ground_table: float32 [16], replicated, may hold values from 4 to 40
- port_cells: int32 [2048], replicated, may hold values from 0 to 16383
- port_load: float32 [2048], replicated, may hold values from 20 to 200
Outputs:
- reduced: float32 [8192, 1024], P(('gx', 'gz'), 'gy')
- factor: float32 [8192, 1024], P(('gx', 'gz'), 'gy')
The draws below stay inside these ranges and needn't reach their ends.
Inputs may be any that keep to these rules, and one draw needn't show every extreme that they name: `port_cells`: several ports may name the same cell; their loads add.
All inputs are finite; a program needn't handle non-finite values.
Results may differ from the reference program's by a relative error of at most 0.0024.
Values may be sent and summed in bfloat16 or wider, within the bound.
No kernel may reach another device: no remote copies, remote signals or barrier semaphores. Data moves between devices by JAX's collectives and lax.ppermute only.
A program may use at most 256 MiB of HBM per device.

```python
import math
import jax
import jax.numpy as jnp
from jax import lax

K = 8192
NB = 512
PANELS = 2
NCLS = 16
PORTS = 2048
NX = 32
NY = 32
NZ = 16
CELLS = 16384


def touch_ends(drawn, own_key, least, largest):
    extent = drawn.shape
    spot = [jax.random.randint(jax.random.fold_in(own_key, axis), (), 0, extent[axis]) for axis in range(len(extent))]
    drawn = drawn.at[tuple(spot)].set(least)
    longest = extent.index(max(extent))
    spot[longest] = (spot[longest] + 1) % extent[longest]
    return drawn.at[tuple(spot)].set(largest)


def levels(key, dims, shards, low, largest):
    def one(position, shards_of):
        heights = jax.random.uniform(jax.random.fold_in(jax.random.fold_in(key, 6), position), (shards_of,), jnp.float32, low / len(shards), largest / len(shards))
        return jnp.repeat(jnp.exp(heights), dims[position] // shards_of).reshape((-1,) + (1,) * (len(dims) - position - 1))

    loudness = one(*shards[0])
    for cut in shards[1:]:
        loudness = loudness * one(*cut)
    return loudness


def bell_draw(stream_key, extent, spread, limit, shards=(), kind=jnp.bfloat16):
    values = spread * jax.random.normal(stream_key, extent, jnp.float32)
    if shards:
        values = values * levels(stream_key, extent, shards, -0.22, 0.18)
    return jnp.clip(values, -limit, limit).astype(kind)


def setup_inputs(seed: int = 0) -> dict:
    streams_of = jax.random.split(jax.random.key(seed), 7)
    return {
        "basis": bell_draw(streams_of[0], (NX, NY, NZ, K), (CELLS // 16) ** -0.5, 0.1875, ((0, 4), (1, 4), (2, 2))),
        "classes": touch_ends(jax.random.randint(streams_of[1], (NX, NY, NZ), 0, NCLS), jax.random.fold_in(streams_of[1], 1), 0, NCLS - 1).astype(jnp.int32),
        "cond_table": jnp.clip(jnp.exp(jax.random.uniform(streams_of[2], (NCLS,), jnp.float32, math.log(0.5), math.log(2.0))), 0.5, 2.0),
        "ground_table": jnp.clip(jnp.exp(jax.random.uniform(streams_of[3], (NCLS,), jnp.float32, math.log(4.0), math.log(40.0))), 4.0, 40.0),
        "port_cells": touch_ends(jax.random.randint(streams_of[4], (PORTS,), 0, CELLS), jax.random.fold_in(streams_of[4], 1), 0, CELLS - 1).astype(jnp.int32),
        "port_load": jnp.clip(jnp.exp(jax.random.uniform(streams_of[5], (PORTS,), jnp.float32, math.log(20.0), math.log(200.0))), 20.0, 200.0),
    }


def lead_factor(leading, panel_width, panel_total):
    result = jnp.zeros(leading.shape, jnp.float32)
    row_ids = jnp.arange(leading.shape[0], dtype=jnp.int32)
    diagonals = []
    for panel_index in range(panel_total):
        begin_col = panel_index * panel_width
        block_part = leading[:, begin_col:begin_col + panel_width]
        if panel_index > 0:
            block_part = block_part - jnp.dot(result[:, :begin_col], result[begin_col:begin_col + panel_width, :begin_col].T, precision=lax.Precision.HIGHEST)
        diagonal = jnp.linalg.cholesky(block_part[begin_col:begin_col + panel_width])
        solved = jax.scipy.linalg.solve_triangular(diagonal, block_part.T, lower=True).T
        column_ids = begin_col + jnp.arange(panel_width, dtype=jnp.int32)
        solved = jnp.where(column_ids[None, :] <= row_ids[:, None], solved, jnp.float32(0.0))
        result = result.at[:, begin_col:begin_col + panel_width].set(solved)
        diagonals.append(diagonal)
    return (result, diagonals)

def rows_factor(matrix_rows, offset, lead_l, diagonals, panel_width):
    result = jnp.zeros(matrix_rows.shape, jnp.float32)
    row_ids = offset + jnp.arange(matrix_rows.shape[0], dtype=jnp.int32)
    for panel_index in range(len(diagonals)):
        begin_col = panel_index * panel_width
        block_part = matrix_rows[:, begin_col:begin_col + panel_width]
        if panel_index > 0:
            block_part = block_part - jnp.dot(result[:, :begin_col], lead_l[begin_col:begin_col + panel_width, :begin_col].T, precision=lax.Precision.HIGHEST)
        solved = jax.scipy.linalg.solve_triangular(diagonals[panel_index], block_part.T, lower=True).T
        column_ids = begin_col + jnp.arange(panel_width, dtype=jnp.int32)
        solved = jnp.where(column_ids[None, :] <= row_ids[:, None], solved, jnp.float32(0.0))
        result = result.at[:, begin_col:begin_col + panel_width].set(solved)
    return result

def reference(basis, classes, cond_table, ground_table, port_cells, port_load):
    panel_cols = PANELS * NB
    conduct = cond_table[classes]
    terminal = jax.ops.segment_sum(port_load, port_cells, num_segments=CELLS).reshape(NX, NY, NZ)
    grounds = ground_table[classes] + terminal
    panel_part = basis[:, :, :, :panel_cols].astype(jnp.float32)
    scaled = (conduct[..., None] * panel_part).astype(jnp.bfloat16)
    scaled_wide = scaled.astype(jnp.float32)
    padded = jnp.pad(scaled_wide, ((1, 1), (1, 1), (1, 1), (0, 0)))
    beside = padded[2:, 1:-1, 1:-1] + padded[:-2, 1:-1, 1:-1]
    beside = beside + padded[1:-1, 2:, 1:-1] + padded[1:-1, :-2, 1:-1]
    beside = beside + padded[1:-1, 1:-1, 2:] + padded[1:-1, 1:-1, :-2]
    image_full = (conduct[..., None] * (6.0 * scaled_wide - beside) + grounds[..., None] * panel_part).astype(jnp.bfloat16)
    reduced = lax.dot_general(basis.reshape(CELLS, K).astype(jnp.float32), image_full.reshape(CELLS, panel_cols).astype(jnp.float32), (((0,), (0,)), ((), ())), preferred_element_type=jnp.float32)
    lead_l, diagonals = lead_factor(reduced[:panel_cols], NB, PANELS)
    factor = rows_factor(reduced, 0, lead_l, diagonals, NB)
    return (reduced, factor)
```

```python
import jax
import jax.numpy as jnp
from jax import lax
from jax.experimental import pallas as pl
from jax.experimental.pallas import tpu as pltpu
from jax.sharding import PartitionSpec as P

NB = 512
PANELS = 2
LEAF = 128
SUB = 8


def dot3(a, b, dims):
    a_hi = a.astype(jnp.bfloat16)
    b_hi = b.astype(jnp.bfloat16)
    a_lo = (a - a_hi.astype(jnp.float32)).astype(jnp.bfloat16)
    b_lo = (b - b_hi.astype(jnp.float32)).astype(jnp.bfloat16)

    def dot(x, y):
        return lax.dot_general(x, y, (dims, ((), ())), preferred_element_type=jnp.float32)

    return dot(a_hi, b_hi) + (dot(a_hi, b_lo) + dot(a_lo, b_hi))


def inverse_of(d):
    guess = pl.reciprocal(d, approx=True)
    return guess * (2.0 - d * guess)


def leaf_inverse(block_ref):
    lanes = lax.broadcasted_iota(jnp.int32, (SUB, LEAF), 1)
    subs = lax.broadcasted_iota(jnp.int32, (SUB, LEAF), 0)
    shape = (SUB, LEAF)
    for t in range(LEAF // SUB):
        j0 = t * SUB
        rows = block_ref[j0 : j0 + SUB, :]
        cols = [jnp.broadcast_to(rows[:, j0 + k : j0 + k + 1], shape) for k in range(SUB)]
        p = [[jnp.broadcast_to(cols[k][i : i + 1, :], shape) for k in range(i + 1)] for i in range(SUB)]
        in_block = jnp.logical_and(lanes >= j0, lanes < j0 + SUB)
        start = jnp.where(in_block, (lanes - j0 == subs).astype(jnp.float32), rows)
        u = [jnp.broadcast_to(start[k : k + 1, :], shape) for k in range(SUB)]
        inv = [None] * SUB
        factor = [[None] * SUB for _ in range(SUB)]
        for k in range(SUB):
            inv[k] = inverse_of(p[k][k])
            for i in range(k + 1, SUB):
                factor[i][k] = p[i][k] * inv[k]
                for j in range(k + 1, i + 1):
                    p[i][j] = p[i][j] - factor[i][k] * p[j][k] if j < i else p[i][j] - factor[i][k] * p[i][k]
                u[i] = u[i] - factor[i][k] * u[k]
        out = u[0] * lax.rsqrt(p[0][0])
        for k in range(1, SUB):
            out = jnp.where(subs == k, u[k] * lax.rsqrt(p[k][k]), out)
        block_ref[j0 : j0 + SUB, :] = out
        if t + 1 == LEAF // SUB:
            break
        z = [None] * SUB
        for k in reversed(range(SUB)):
            z[k] = u[k] * inv[k]
            for i in range(k + 1, SUB):
                z[k] = z[k] - factor[i][k] * z[i]
        for v in range(t + 1, LEAF // SUB):
            below = block_ref[v * SUB : (v + 1) * SUB, :]
            upd = jnp.where(in_block, 0.0, below)
            for k in range(SUB):
                upd = upd - jnp.broadcast_to(below[:, j0 + k : j0 + k + 1], shape) * z[k]
            block_ref[v * SUB : (v + 1) * SUB, :] = upd


def factor_inverse(s_ref, d_ref):
    width = s_ref.shape[0]
    row_ids = lax.broadcasted_iota(jnp.int32, (width, width), 0)
    col_ids = lax.broadcasted_iota(jnp.int32, (width, width), 1)
    wide_cols = lax.broadcasted_iota(jnp.int32, (LEAF, width), 1)
    leaf_rows = lax.broadcasted_iota(jnp.int32, (LEAF, LEAF), 0)
    leaf_cols = lax.broadcasted_iota(jnp.int32, (LEAF, LEAF), 1)

    def step(b, carry):
        off = pl.multiple_of(b * LEAF, LEAF)
        span = pl.ds(off, LEAF)
        d_ref[...] = s_ref[span, span]
        leaf_inverse(d_ref)
        inverse = jnp.where(leaf_rows >= leaf_cols, d_ref[...], 0.0)
        s_ref[span, span] = (leaf_rows == leaf_cols).astype(jnp.float32)
        upper = dot3(inverse, s_ref[span, :], ((1,), (0,)))
        s_ref[span, :] = upper
        tail = jnp.where(wide_cols >= off + LEAF, upper, 0.0)
        current = s_ref[...]
        dead = jnp.logical_and(
            row_ids >= off + LEAF, jnp.logical_and(col_ids >= off, col_ids < off + LEAF)
        )
        s_ref[...] = jnp.where(dead, 0.0, current) - dot3(tail, upper, ((0,), (0,)))
        return carry

    lax.fori_loop(0, width // LEAF, step, 0)
    s_ref[...] = jnp.where(row_ids >= col_ids, s_ref[...], 0.0)


def unpack_symmetric(packed_ref, s_ref, first=0):
    at = first
    for i in range(s_ref.shape[0] // LEAF):
        for j in range(i + 1):
            block = packed_ref[at * LEAF : (at + 1) * LEAF, :]
            s_ref[i * LEAF : (i + 1) * LEAF, j * LEAF : (j + 1) * LEAF] = block
            if j < i:
                s_ref[j * LEAF : (j + 1) * LEAF, i * LEAF : (i + 1) * LEAF] = block.T
            at += 1


def first_panel_kernel(packed_ref, w_ref, d_ref):
    unpack_symmetric(packed_ref, w_ref)
    factor_inverse(w_ref, d_ref)


def next_panel_kernel(packed_ref, below_ref, w0_ref, f_ref, w_ref, d_ref):
    unpack_symmetric(packed_ref, w_ref)
    below = dot3(below_ref[...], w0_ref[...], ((1,), (1,)))
    f_ref[...] = below
    w_ref[...] = w_ref[...] - dot3(below, below, ((1,), (1,)))
    factor_inverse(w_ref, d_ref)


def first_panel(packed, nb):
    return pl.pallas_call(
        first_panel_kernel,
        out_shape=jax.ShapeDtypeStruct((nb, nb), jnp.float32),
        in_specs=[pl.BlockSpec(memory_space=pltpu.VMEM)],
        out_specs=pl.BlockSpec(memory_space=pltpu.VMEM),
        scratch_shapes=[pltpu.VMEM((LEAF, LEAF), jnp.float32)],
        compiler_params=pltpu.CompilerParams(vmem_limit_bytes=24 * 2**20),
    )(packed)


def next_panel(packed, below, w0):
    nb = w0.shape[0]
    return pl.pallas_call(
        next_panel_kernel,
        out_shape=[jax.ShapeDtypeStruct((nb, nb), jnp.float32)] * 2,
        in_specs=[pl.BlockSpec(memory_space=pltpu.VMEM)] * 3,
        out_specs=[pl.BlockSpec(memory_space=pltpu.VMEM)] * 2,
        scratch_shapes=[pltpu.VMEM((LEAF, LEAF), jnp.float32)],
        compiler_params=pltpu.CompilerParams(vmem_limit_bytes=24 * 2**20),
    )(packed, below, w0)


def shifted_pairs(count, step):
    return [(i, (i + step) % count) for i in range(count)]


def take(blocks, index):
    return lax.dynamic_index_in_dim(blocks, index, 0, keepdims=False)


def halving(blocks, axis, pairs_of, count, mine):
    total = take(blocks, mine)
    for step in range(1, count):
        sent = take(blocks, (mine + step) % count).astype(jnp.bfloat16)
        total = total + lax.ppermute(sent, axis, pairs_of(step)).astype(jnp.float32)
    return total


def beside_sum(cells, cell_dims):
    total = None
    for axis, dim in cell_dims:
        count = lax.axis_size(axis)
        length = cells.shape[dim]
        head = lax.slice_in_dim(cells, 0, 1, axis=dim)
        tail = lax.slice_in_dim(cells, length - 1, length, axis=dim)
        before = lax.ppermute(tail, axis, [(i, i + 1) for i in range(count - 1)])
        after = lax.ppermute(head, axis, [(i + 1, i) for i in range(count - 1)])
        low = jnp.concatenate([before, lax.slice_in_dim(cells, 0, length - 1, axis=dim)], dim)
        high = jnp.concatenate([lax.slice_in_dim(cells, 1, length, axis=dim), after], dim)
        pair = low.astype(jnp.float32) + high.astype(jnp.float32)
        total = pair if total is None else total + pair
    return total


def lower_blocks(square):
    return [
        square[i * LEAF : (i + 1) * LEAF, j * LEAF : (j + 1) * LEAF]
        for i in range(square.shape[0] // LEAF)
        for j in range(i + 1)
    ]


def sum_everywhere(rows, axes, devices):
    count = rows.shape[0]
    share = -(-count // devices)
    rows = jnp.pad(rows, ((0, share * devices - count), (0, 0))).reshape(devices, share, LEAF)
    terms = lax.all_to_all(rows, axes, split_axis=0, concat_axis=0, tiled=True)
    return lax.all_gather(jnp.sum(terms, axis=0), axes, axis=0, tiled=True)[:count]


def local(basis, classes, cond_table, ground_table, port_cells, port_load):
    cells_x, cells_y, cells_z, width_k = basis.shape
    devices_x = lax.axis_size("gx")
    devices_y = lax.axis_size("gy")
    devices_z = lax.axis_size("gz")
    devices = devices_x * devices_y * devices_z
    chips_y = devices_y // 2
    local_cells = cells_x * cells_y * cells_z
    panel_cols = PANELS * NB
    class_total = cond_table.shape[0]
    at_x, at_y, at_z = (lax.axis_index(axis) for axis in ("gx", "gy", "gz"))
    core = at_y % 2
    chip_y = at_y // 2

    flat_basis = basis.reshape(local_cells, width_k)
    half = width_k // 2
    other_core = [(i, i ^ 1) for i in range(devices_y)]
    kept = lax.dynamic_slice_in_dim(flat_basis, core * half, half, 1)
    given = lax.dynamic_slice_in_dim(flat_basis, (1 - core) * half, half, 1)
    chip_basis = jnp.concatenate([kept, lax.ppermute(given, "gy", other_core)], 0)

    onehot = (classes[..., None] == jnp.arange(class_total, dtype=jnp.int32)).astype(jnp.float32)
    conduct = jnp.dot(onehot, cond_table, precision=lax.Precision.HIGHEST)
    grounds = jnp.dot(onehot, ground_table, precision=lax.Precision.HIGHEST)
    global_x = at_x * cells_x + jnp.arange(cells_x, dtype=jnp.int32)
    global_y = at_y * cells_y + jnp.arange(cells_y, dtype=jnp.int32)
    global_z = at_z * cells_z + jnp.arange(cells_z, dtype=jnp.int32)
    flat_ids = (
        (global_x[:, None, None] * (cells_y * devices_y) + global_y[None, :, None])
        * (cells_z * devices_z)
        + global_z[None, None, :]
    ).reshape(local_cells)
    matches = (port_cells[:, None] == flat_ids[None, :]).astype(jnp.float32)
    terminal = jnp.dot(port_load, matches, precision=lax.Precision.HIGHEST).reshape(
        cells_x, cells_y, cells_z
    )
    grounds = grounds + terminal
    panel_part = basis[:, :, :, :panel_cols].astype(jnp.float32)
    scaled = (conduct[..., None] * panel_part).astype(jnp.bfloat16)
    beside = beside_sum(scaled, (("gx", 0), ("gy", 1), ("gz", 2)))
    image = (
        conduct[..., None] * (6.0 * scaled.astype(jnp.float32) - beside)
        + grounds[..., None] * panel_part
    ).astype(jnp.bfloat16)
    flat_image = image.reshape(local_cells, panel_cols)

    lead = lax.dot_general(
        flat_basis[:, :panel_cols],
        flat_image,
        (((0,), (0,)), ((), ())),
        preferred_element_type=jnp.float32,
    )
    axes = ("gx", "gy", "gz")
    first = lead[:NB, :NB]
    later = lead[NB:, NB:]
    first_rows = sum_everywhere(
        jnp.concatenate(lower_blocks(0.5 * (first + first.T)), 0), axes, devices
    )
    later_blocks = lower_blocks(0.5 * (later + later.T))
    below_blocks = [lead[NB:, i * LEAF : (i + 1) * LEAF] for i in range(NB // LEAF)]
    later_rows = sum_everywhere(jnp.concatenate(later_blocks + below_blocks, 0), axes, devices)
    later_count = len(later_blocks) * LEAF
    below = jnp.concatenate(
        [
            later_rows[later_count + i * NB : later_count + (i + 1) * NB]
            for i in range(NB // LEAF)
        ],
        1,
    )
    inverse_0 = first_panel(first_rows, NB)
    factor_10, inverse_1 = next_panel(later_rows[:later_count], below, inverse_0)

    chip_image = jnp.concatenate([flat_image, lax.ppermute(flat_image, "gy", other_core)], 0)
    products = lax.dot_general(
        chip_basis, chip_image, (((0,), (0,)), ((), ())), preferred_element_type=jnp.float32
    )
    spans = devices_x // 2
    part_rows = width_k // (devices_x * devices_z * devices_y)
    products = products.reshape(spans, devices_z, chips_y, 2 * part_rows, panel_cols)

    def over_z(terms):
        return halving(
            terms, "gz", lambda step: shifted_pairs(devices_z, step), devices_z, at_z
        )

    def over_y(terms):
        def pairs(step):
            return [
                (2 * i + c, 2 * ((i + step) % chips_y) + c) for i in range(chips_y) for c in (0, 1)
            ]

        return halving(terms, "gy", pairs, chips_y, chip_y)

    split = spans // 2
    sums_a = over_z(jnp.moveaxis(products[:split], 1, 0))
    sums_b = over_y(jnp.moveaxis(products[split:], 2, 0))
    sums_a = over_y(jnp.moveaxis(sums_a, 1, 0))
    sums_b = over_z(jnp.moveaxis(sums_b, 1, 0))
    plane = jnp.concatenate([sums_a, sums_b], 0).reshape(devices_x, part_rows, panel_cols)
    rows = jnp.zeros((part_rows, panel_cols), jnp.float32)
    for step in range(devices_x):
        sent = take(plane, (at_x + step) % devices_x)
        pairs = []
        for x in range(devices_x):
            for y in range(devices_y):
                to = (x + step) % devices_x
                dest_x = (y % 2) * spans + to // 2
                dest_y = (y // 2) * 2 + to % 2
                pairs.append((x * devices_y + y, dest_x * devices_y + dest_y))
        rows = rows + lax.ppermute(sent, ("gx", "gy"), pairs)
    reduced = lax.all_to_all(rows, "gy", split_axis=1, concat_axis=0, tiled=True)

    def times(a, b):
        return lax.dot_general(
            a, b, (((1,), (1,)), ((), ())), precision=lax.Precision.HIGHEST
        )

    factor_0 = times(rows[:, :NB], inverse_0)
    factor_1 = times(rows[:, NB:] - times(factor_0, factor_10), inverse_1)
    row_ids = (
        (at_x * devices_z + at_z) * devices_y + at_y
    ) * part_rows + jnp.arange(part_rows, dtype=jnp.int32)
    factor = jnp.concatenate([factor_0, factor_1], 1)
    factor = jnp.where(
        jnp.arange(panel_cols, dtype=jnp.int32)[None, :] <= row_ids[:, None], factor, 0.0
    )
    factor = lax.all_to_all(factor, "gy", split_axis=1, concat_axis=0, tiled=True)
    return (reduced, factor)


def solution(mesh):
    placed = (P("gx", "gy", "gz", None), P("gx", "gy", "gz"), P(), P(), P(), P())
    return jax.shard_map(
        local,
        mesh=mesh,
        in_specs=placed,
        out_specs=(P(("gx", "gz"), "gy"), P(("gx", "gz"), "gy")),
        check_vma=False,
    )
```

```python
import functools

import jax
import jax.numpy as jnp
from jax import lax
from jax.experimental import pallas as pl
from jax.experimental.pallas import tpu as pltpu
from jax.sharding import PartitionSpec as P

NB = 512
PANELS = 2
LEAF = 128
SUB = 8


def dot3(a, b, dims):
    a_hi = a.astype(jnp.bfloat16)
    b_hi = b.astype(jnp.bfloat16)
    a_lo = (a - a_hi.astype(jnp.float32)).astype(jnp.bfloat16)
    b_lo = (b - b_hi.astype(jnp.float32)).astype(jnp.bfloat16)

    def dot(x, y):
        return lax.dot_general(x, y, (dims, ((), ())), preferred_element_type=jnp.float32)

    return dot(a_hi, b_hi) + (dot(a_hi, b_lo) + dot(a_lo, b_hi))


def inverse_of(d):
    guess = pl.reciprocal(d, approx=True)
    return guess * (2.0 - d * guess)


def leaf_inverse(block_ref):
    lanes = lax.broadcasted_iota(jnp.int32, (SUB, LEAF), 1)
    subs = lax.broadcasted_iota(jnp.int32, (SUB, LEAF), 0)
    shape = (SUB, LEAF)
    for t in range(LEAF // SUB):
        j0 = t * SUB
        rows = block_ref[j0 : j0 + SUB, :]
        cols = [jnp.broadcast_to(rows[:, j0 + k : j0 + k + 1], shape) for k in range(SUB)]
        p = [[jnp.broadcast_to(cols[k][i : i + 1, :], shape) for k in range(i + 1)] for i in range(SUB)]
        in_block = jnp.logical_and(lanes >= j0, lanes < j0 + SUB)
        start = jnp.where(in_block, (lanes - j0 == subs).astype(jnp.float32), rows)
        u = [jnp.broadcast_to(start[k : k + 1, :], shape) for k in range(SUB)]
        inv = [None] * SUB
        factor = [[None] * SUB for _ in range(SUB)]
        for k in range(SUB):
            inv[k] = inverse_of(p[k][k])
            for i in range(k + 1, SUB):
                factor[i][k] = p[i][k] * inv[k]
                for j in range(k + 1, i + 1):
                    p[i][j] = p[i][j] - factor[i][k] * p[j][k] if j < i else p[i][j] - factor[i][k] * p[i][k]
                u[i] = u[i] - factor[i][k] * u[k]
        out = u[0] * lax.rsqrt(p[0][0])
        for k in range(1, SUB):
            out = jnp.where(subs == k, u[k] * lax.rsqrt(p[k][k]), out)
        block_ref[j0 : j0 + SUB, :] = out
        if t + 1 == LEAF // SUB:
            break
        z = [None] * SUB
        for k in reversed(range(SUB)):
            z[k] = u[k] * inv[k]
            for i in range(k + 1, SUB):
                z[k] = z[k] - factor[i][k] * z[i]
        for v in range(t + 1, LEAF // SUB):
            below = block_ref[v * SUB : (v + 1) * SUB, :]
            upd = jnp.where(in_block, 0.0, below)
            for k in range(SUB):
                upd = upd - jnp.broadcast_to(below[:, j0 + k : j0 + k + 1], shape) * z[k]
            block_ref[v * SUB : (v + 1) * SUB, :] = upd


def factor_inverse(s_ref, d_ref):
    width = s_ref.shape[0]
    row_ids = lax.broadcasted_iota(jnp.int32, (width, width), 0)
    col_ids = lax.broadcasted_iota(jnp.int32, (width, width), 1)
    wide_cols = lax.broadcasted_iota(jnp.int32, (LEAF, width), 1)
    leaf_rows = lax.broadcasted_iota(jnp.int32, (LEAF, LEAF), 0)
    leaf_cols = lax.broadcasted_iota(jnp.int32, (LEAF, LEAF), 1)

    def step(b, carry):
        off = pl.multiple_of(b * LEAF, LEAF)
        span = pl.ds(off, LEAF)
        d_ref[...] = s_ref[span, span]
        leaf_inverse(d_ref)
        inverse = jnp.where(leaf_rows >= leaf_cols, d_ref[...], 0.0)
        s_ref[span, span] = (leaf_rows == leaf_cols).astype(jnp.float32)
        upper = dot3(inverse, s_ref[span, :], ((1,), (0,)))
        s_ref[span, :] = upper
        tail = jnp.where(wide_cols >= off + LEAF, upper, 0.0)
        current = s_ref[...]
        dead = jnp.logical_and(
            row_ids >= off + LEAF, jnp.logical_and(col_ids >= off, col_ids < off + LEAF)
        )
        s_ref[...] = jnp.where(dead, 0.0, current) - dot3(tail, upper, ((0,), (0,)))
        return carry

    lax.fori_loop(0, width // LEAF, step, 0)
    s_ref[...] = jnp.where(row_ids >= col_ids, s_ref[...], 0.0)


def unpack_symmetric(packed_ref, s_ref, first=0):
    at = first
    for i in range(s_ref.shape[0] // LEAF):
        for j in range(i + 1):
            block = packed_ref[at * LEAF : (at + 1) * LEAF, :]
            s_ref[i * LEAF : (i + 1) * LEAF, j * LEAF : (j + 1) * LEAF] = block
            if j < i:
                s_ref[j * LEAF : (j + 1) * LEAF, i * LEAF : (i + 1) * LEAF] = block.T
            at += 1


def first_panel_kernel(packed_ref, w_ref, d_ref):
    unpack_symmetric(packed_ref, w_ref)
    factor_inverse(w_ref, d_ref)


def next_panel_kernel(packed_ref, w0_ref, f_ref, w_ref, d_ref):
    unpack_symmetric(packed_ref, w_ref)
    nb = w0_ref.shape[0]
    start = packed_ref.shape[0] - nb // LEAF * nb
    below = jnp.concatenate(
        [packed_ref[start + i * nb : start + (i + 1) * nb, :] for i in range(nb // LEAF)], 1
    )
    below = dot3(below, w0_ref[...], ((1,), (1,)))
    f_ref[...] = below
    w_ref[...] = w_ref[...] - dot3(below, below, ((1,), (1,)))
    factor_inverse(w_ref, d_ref)


def factor_kernel(first_ref, rows_ref, w0_ref, f_ref, w1_ref, out_ref):
    nb = w0_ref.shape[0]
    ids = first_ref[0] + lax.broadcasted_iota(jnp.int32, (rows_ref.shape[0], nb), 0)
    cols = lax.broadcasted_iota(jnp.int32, (rows_ref.shape[0], nb), 1)
    part = dot3(rows_ref[:, :nb], w0_ref[...], ((1,), (1,)))
    out_ref[:, :nb] = jnp.where(cols <= ids, part, 0.0)
    rest = rows_ref[:, nb:] - dot3(part, f_ref[...], ((1,), (1,)))
    rest = dot3(rest, w1_ref[...], ((1,), (1,)))
    out_ref[:, nb:] = jnp.where(cols + nb <= ids, rest, 0.0)


def panel_call(kernel, outputs, nb, *operands):
    return pl.pallas_call(
        kernel,
        out_shape=[jax.ShapeDtypeStruct((nb, nb), jnp.float32)] * outputs,
        in_specs=[pl.BlockSpec(memory_space=pltpu.VMEM)] * len(operands),
        out_specs=[pl.BlockSpec(memory_space=pltpu.VMEM)] * outputs,
        scratch_shapes=[pltpu.VMEM((LEAF, LEAF), jnp.float32)],
        compiler_params=pltpu.CompilerParams(vmem_limit_bytes=24 * 2**20),
        cost_estimate=pl.CostEstimate(
            flops=24 * nb**3 * 8, transcendentals=0, bytes_accessed=8 * nb * nb
        ),
    )(*operands)


def first_panel(packed, nb):
    return panel_call(first_panel_kernel, 1, nb, packed)[0]


def next_panel(packed, w0):
    return panel_call(next_panel_kernel, 2, w0.shape[0], packed, w0)


def whole(memory=pltpu.VMEM):
    return pl.BlockSpec(memory_space=memory)


def faces_kernel(cond_ref, ground_ref, info_ref, cells_ref, load_ref, panel_ref, *refs, sides):
    outs, (conduct_ref, grounds_ref, scaled_ref) = refs[:6], refs[6:]
    size_x, size_y, size_z = sides
    count, width = panel_ref.shape
    tile = 64
    classes = cond_ref.shape[0]
    ports = cells_ref.shape[1]

    def by_tile(t, carry):
        rows = pl.ds(pl.multiple_of(t * tile, tile), tile)
        kind = jnp.broadcast_to(info_ref[rows, 0:1], (tile, LEAF))
        ids = jnp.broadcast_to(info_ref[rows, 1:2], (tile, LEAF))
        conduct = jnp.zeros((tile, LEAF), jnp.float32)
        grounds = jnp.zeros((tile, LEAF), jnp.float32)
        for c in range(classes):
            conduct = jnp.where(kind == c, cond_ref[c], conduct)
            grounds = jnp.where(kind == c, ground_ref[c], grounds)
        loads = jnp.zeros((tile, LEAF), jnp.float32)
        for p in range(0, ports, LEAF):
            hit = ids == cells_ref[:, p : p + LEAF]
            loads = loads + jnp.where(hit, load_ref[:, p : p + LEAF], 0.0)
        conduct_ref[rows, :] = conduct
        grounds_ref[rows, :] = grounds + jnp.sum(loads, axis=1, keepdims=True)
        for p in range(0, width, LEAF):
            part = panel_ref[rows, p : p + LEAF].astype(jnp.float32)
            scaled_ref[p // LEAF, rows, :] = (
                (conduct * part).astype(jnp.bfloat16).astype(jnp.float32)
            )
        return carry

    lax.fori_loop(0, count // tile, by_tile, 0)
    plane = size_y * size_z
    for p in range(width // LEAF):
        lanes = slice(p * LEAF, (p + 1) * LEAF)
        outs[0][:, lanes] = scaled_ref[p, 0:plane, :].astype(jnp.bfloat16)
        outs[1][:, lanes] = scaled_ref[p, count - plane : count, :].astype(jnp.bfloat16)
        for out, at in ((outs[2], 0), (outs[3], plane - size_z)):
            face = [
                scaled_ref[p, x * plane + at : x * plane + at + size_z, :] for x in range(size_x)
            ]
            out[:, lanes] = jnp.concatenate(face, 0).astype(jnp.bfloat16)
        for out, at in ((outs[4], 0), (outs[5], size_z - 1)):
            face = scaled_ref[p, pl.ds(at, size_x * size_y, stride=size_z), :]
            out[:, lanes] = face.astype(jnp.bfloat16)


def image_kernel(panel_ref, conduct_ref, grounds_ref, *refs, sides, nb):
    halos, (image_ref, first_ref, later_ref, scaled_ref, square_ref) = refs[:6], refs[6:]
    size_x, size_y, size_z = sides
    width = panel_ref.shape[1]
    plane = size_y * size_z
    subs = lax.broadcasted_iota(jnp.int32, (size_z, LEAF), 0)

    def by_lane(p, carry):
        lanes = pl.ds(pl.multiple_of(p * LEAF, LEAF), LEAF)
        x_low, x_high, y_low, y_high, z_low, z_high = (
            h[:, lanes].astype(jnp.float32) for h in halos
        )
        scaled_ref[...] = (
            (conduct_ref[...] * panel_ref[:, lanes].astype(jnp.float32))
            .astype(jnp.bfloat16)
            .astype(jnp.float32)
        )

        def cell_rows(x, y):
            at = x * plane + y * size_z
            return scaled_ref[at : at + size_z, :]

        for x in range(size_x):
            done = []
            for y in range(size_y):
                at = x * plane + y * size_z
                here = cell_rows(x, y)
                span = slice(y * size_z, (y + 1) * size_z)
                total = cell_rows(x + 1, y) if x + 1 < size_x else x_high[span, :]
                total = total + (cell_rows(x - 1, y) if x > 0 else x_low[span, :])
                span = slice(x * size_z, (x + 1) * size_z)
                total = total + (cell_rows(x, y + 1) if y + 1 < size_y else y_high[span, :])
                total = total + (cell_rows(x, y - 1) if y > 0 else y_low[span, :])
                k = x * size_y + y
                up = jnp.where(
                    subs == size_z - 1, z_high[k : k + 1, :], pltpu.roll(here, size_z - 1, 0)
                )
                down = jnp.where(subs == 0, z_low[k : k + 1, :], pltpu.roll(here, 1, 0))
                total = total + up + down
                own = slice(at, at + size_z)
                done.append(
                    conduct_ref[own, :] * (6.0 * here - total)
                    + grounds_ref[own, :] * panel_ref[at : at + size_z, lanes].astype(jnp.float32)
                )
            image_ref[x * plane : (x + 1) * plane, lanes] = jnp.concatenate(done, 0).astype(
                jnp.bfloat16
            )
        return carry

    lax.fori_loop(0, width // LEAF, by_lane, 0)

    def product(rows, cols):
        return lax.dot_general(
            panel_ref[:, rows],
            image_ref[:, cols],
            (((0,), (0,)), ((), ())),
            preferred_element_type=jnp.float32,
        )

    blocks = nb // LEAF

    def lower(out_ref):
        at = 0
        for i in range(blocks):
            for j in range(i + 1):
                row, col = slice(i * LEAF, (i + 1) * LEAF), slice(j * LEAF, (j + 1) * LEAF)
                out_ref[at : at + LEAF, :] = 0.5 * (square_ref[row, col] + square_ref[col, row].T)
                at += LEAF
        return at

    head, tail = slice(0, nb), slice(nb, 2 * nb)
    square_ref[...] = product(head, head)
    lower(first_ref)
    square_ref[...] = product(tail, tail)
    at = lower(later_ref)
    below = product(tail, head)
    for i in range(blocks):
        later_ref[at + i * nb : at + (i + 1) * nb, :] = below[:, i * LEAF : (i + 1) * LEAF]


def pieces_kernel(index_ref, *refs, groups):
    del index_ref
    total = sum(groups)
    ins, outs = refs[:total], refs[total:]
    at = 0
    for out, count in zip(outs, groups):
        width = out.shape[1] // count
        for i in range(count):
            out[:, i * width : (i + 1) * width] = ins[at][...]
            at += 1


def take_pieces(flat_basis, lists):
    rows = flat_basis.shape[0]
    tile = min(128, rows)
    index = jnp.stack([jnp.asarray(b, jnp.int32) for blocks, _ in lists for b in blocks])
    in_specs, out_specs, out_shape = [], [], []
    for blocks, width in lists:
        for _ in blocks:
            k = len(in_specs)
            in_specs.append(pl.BlockSpec((tile, width), lambda t, idx, k=k: (t, idx[k])))
        out_specs.append(pl.BlockSpec((tile, width * len(blocks)), lambda t, idx: (t, 0)))
        out_shape.append(jax.ShapeDtypeStruct((rows, width * len(blocks)), flat_basis.dtype))
    kernel = functools.partial(pieces_kernel, groups=[len(blocks) for blocks, _ in lists])
    return pl.pallas_call(
        kernel,
        grid_spec=pltpu.PrefetchScalarGridSpec(
            num_scalar_prefetch=1, grid=(rows // tile,), in_specs=in_specs, out_specs=out_specs
        ),
        out_shape=out_shape,
        compiler_params=pltpu.CompilerParams(vmem_limit_bytes=32 * 2**20),
        cost_estimate=pl.CostEstimate(
            flops=0, transcendentals=0, bytes_accessed=4 * rows * flat_basis.shape[1]
        ),
    )(index, *([flat_basis] * len(in_specs)))


def products_kernel(index_ref, *refs):
    del index_ref
    out, count = refs[-1], len(refs) // 2
    total = None
    for b, image in zip(refs[:count], refs[count:-1]):
        term = lax.dot_general(
            b[...], image[...], (((0,), (0,)), ((), ())), preferred_element_type=jnp.float32
        )
        total = term if total is None else total + term
    out[...] = total.astype(out.dtype)


def products(bases, images, blocks, width, dtype):
    rows, cols = images[0].shape
    step = 256 if width % 256 == 0 else width
    parts = width // step
    index = jnp.stack([jnp.asarray(b * parts + i, jnp.int32) for b in blocks for i in range(parts)])
    in_specs = [pl.BlockSpec((rows, step), lambda t, idx: (0, idx[t]))] * len(bases)
    in_specs += [pl.BlockSpec((rows, cols), lambda t, idx: (0, 0))] * len(images)
    total = len(blocks) * width
    return pl.pallas_call(
        products_kernel,
        grid_spec=pltpu.PrefetchScalarGridSpec(
            num_scalar_prefetch=1,
            grid=(len(blocks) * parts,),
            in_specs=in_specs,
            out_specs=pl.BlockSpec((step, cols), lambda t, idx: (t, 0)),
        ),
        out_shape=jax.ShapeDtypeStruct((total, cols), dtype),
        compiler_params=pltpu.CompilerParams(vmem_limit_bytes=48 * 2**20),
        cost_estimate=pl.CostEstimate(
            flops=2 * total * cols * rows * len(bases),
            transcendentals=0,
            bytes_accessed=2 * rows * (total + cols) * len(bases) + 4 * total * cols,
        ),
    )(index, *bases, *images)


def swap_everywhere(rows, axes, devices):
    count = rows.shape[0]
    share = -(-count // devices)
    if share * devices > count:
        rows = jnp.pad(rows, ((0, share * devices - count), (0, 0)))
    rows = rows.reshape(devices, share, LEAF)
    terms = lax.all_to_all(rows, axes, split_axis=0, concat_axis=0, tiled=True)
    own = jnp.broadcast_to(jnp.sum(terms, axis=0), (devices, share, LEAF))
    sums = lax.all_to_all(own, axes, split_axis=0, concat_axis=0, tiled=True)
    return sums.reshape(devices * share, LEAF)[:count]


def local(basis, classes, cond_table, ground_table, port_cells, port_load):
    sides = classes.shape
    cells_x, cells_y, cells_z = sides
    width_k = basis.shape[3]
    devices_x = lax.axis_size("gx")
    devices_y = lax.axis_size("gy")
    devices_z = lax.axis_size("gz")
    devices = devices_x * devices_y * devices_z
    chips_y = devices_y // 2
    spans = devices_x // 2
    split = spans // 2
    count = cells_x * cells_y * cells_z
    cols = PANELS * NB
    at_x, at_y, at_z = (lax.axis_index(axis) for axis in ("gx", "gy", "gz"))
    core = at_y % 2
    chip = at_y // 2
    axes = ("gx", "gy", "gz")
    f32, bf16 = jnp.float32, jnp.bfloat16

    flat_basis = basis.reshape(count, width_k)
    panel = flat_basis[:, :cols]
    global_x = at_x * cells_x + jnp.arange(cells_x, dtype=jnp.int32)
    global_y = at_y * cells_y + jnp.arange(cells_y, dtype=jnp.int32)
    global_z = at_z * cells_z + jnp.arange(cells_z, dtype=jnp.int32)
    flat_ids = (
        (global_x[:, None, None] * (cells_y * devices_y) + global_y[None, :, None])
        * (cells_z * devices_z)
        + global_z[None, None, :]
    )
    info = jnp.stack([classes, flat_ids], -1).reshape(count, 2)

    face_rows = [cells_y * cells_z] * 2 + [cells_x * cells_z] * 2 + [cells_x * cells_y] * 2
    *faces, conduct, grounds = pl.pallas_call(
        functools.partial(faces_kernel, sides=sides),
        out_shape=[jax.ShapeDtypeStruct((n, cols), bf16) for n in face_rows]
        + [jax.ShapeDtypeStruct((count, LEAF), f32)] * 2,
        in_specs=[whole(pltpu.SMEM)] * 2 + [whole()] * 4,
        out_specs=[whole()] * 8,
        scratch_shapes=[pltpu.VMEM((cols // LEAF, count, LEAF), f32)],
        compiler_params=pltpu.CompilerParams(vmem_limit_bytes=24 * 2**20),
    )(cond_table, ground_table, info, port_cells[None, :], port_load[None, :], panel)
    halos = []
    for i, (axis, size) in enumerate((("gx", devices_x), ("gy", devices_y), ("gz", devices_z))):
        low, high = faces[2 * i : 2 * i + 2]
        halos.append(lax.ppermute(high, axis, [(k, k + 1) for k in range(size - 1)]))
        halos.append(lax.ppermute(low, axis, [(k + 1, k) for k in range(size - 1)]))

    wide = width_k // (devices_x * devices_z)
    narrow = wide // chips_y

    def over_z_blocks(s, x):
        return [(s * spans + zz) * devices_z + x for zz in range(split)]

    def over_y_blocks(s, y):
        return [
            ((s * spans + zz) * devices_z + x) * chips_y + y
            for zz in range(split, spans)
            for x in range(devices_z)
        ]

    z_steps = [(ds, d) for d in range(devices_z) for ds in (0, 1)]
    y_steps = [(ds, d) for d in range(chips_y) for ds in (0, 1)]
    lists = [(over_z_blocks(core ^ ds, (at_z + d) % devices_z), wide) for ds, d in z_steps]
    lists += [(over_y_blocks(core ^ ds, (chip + d) % chips_y), narrow) for ds, d in y_steps]
    pieces = take_pieces(flat_basis, lists)

    def z_pairs(ds, d):
        return [
            (y * devices_z + z, (y ^ ds) * devices_z + (z + d) % devices_z)
            for y in range(devices_y)
            for z in range(devices_z)
        ]

    def y_pairs(ds, d):
        return [(2 * y + c, 2 * ((y + d) % chips_y) + (c ^ ds)) for y in range(chips_y) for c in (0, 1)]

    def move_z(array, ds, d):
        return array if (ds, d) == (0, 0) else lax.ppermute(array, ("gy", "gz"), z_pairs(ds, d))

    def move_y(array, ds, d):
        return array if (ds, d) == (0, 0) else lax.ppermute(array, "gy", y_pairs(ds, d))

    z_bases = [move_z(p, ds, d) for p, (ds, d) in zip(pieces, z_steps)]
    y_bases = [move_y(p, ds, d) for p, (ds, d) in zip(pieces[len(z_steps) :], y_steps)]

    blocks = NB // LEAF
    lower_rows = blocks * (blocks + 1) // 2 * LEAF
    image, first_rows, later_rows = pl.pallas_call(
        functools.partial(image_kernel, sides=sides, nb=NB),
        out_shape=[
            jax.ShapeDtypeStruct((count, cols), bf16),
            jax.ShapeDtypeStruct((lower_rows, LEAF), f32),
            jax.ShapeDtypeStruct((lower_rows + blocks * NB, LEAF), f32),
        ],
        in_specs=[whole()] * 9,
        out_specs=[whole()] * 3,
        scratch_shapes=[pltpu.VMEM((count, LEAF), f32), pltpu.VMEM((NB, NB), f32)],
        compiler_params=pltpu.CompilerParams(vmem_limit_bytes=32 * 2**20),
    )(panel, conduct, grounds, *halos)

    by_z = {(0, d): move_z(image, 0, d) for d in range(devices_z)}
    by_y = {(0, d): move_y(image, 0, d) for d in range(1, chips_y)}
    by_z.update({(1, d): move_y(by_z[0, d], 1, 0) for d in range(devices_z)})
    by_y.update({(1, d): move_y(by_y[0, d], 1, 0) for d in range(1, chips_y)})
    by_y.update({(ds, 0): by_z[ds, 0] for ds in (0, 1)})
    z_images = [by_z[key] for key in z_steps]
    y_images = [by_y[key] for key in y_steps]

    first_rows = swap_everywhere(first_rows, axes, devices)
    later_rows = swap_everywhere(later_rows, axes, devices)
    inverse_0 = first_panel(first_rows, NB)
    factor_10, inverse_1 = next_panel(later_rows, inverse_0)

    part = narrow // 2

    def y_block(d):
        return [zz * chips_y + (chip + d) % chips_y for zz in range(split)]

    def z_block(d):
        return [zz * devices_z + (at_z + d) % devices_z for zz in range(spans - split)]

    y_sent = [products(z_bases, z_images, y_block(d), narrow, bf16) for d in range(1, chips_y)]
    y_got = [move_y(a, 0, d) for d, a in zip(range(1, chips_y), y_sent)]
    z_sent = [products(y_bases, y_images, z_block(d), narrow, bf16) for d in range(1, devices_z)]
    z_got = [move_z(a, 0, d) for d, a in zip(range(1, devices_z), z_sent)]
    sums_a = products(z_bases, z_images, y_block(0), narrow, f32)
    sums_b = products(y_bases, y_images, z_block(0), narrow, f32)
    y_got, z_got, inverse_0 = lax.optimization_barrier((y_got, z_got, inverse_0))
    for got in y_got:
        sums_a = sums_a + got.astype(f32)
    for got in z_got:
        sums_b = sums_b + got.astype(f32)
    plane = jnp.concatenate([sums_a.astype(bf16), sums_b.astype(bf16)], 0)
    plane = plane.reshape(devices_x, part, cols)
    rows = jnp.zeros((part, cols), f32)
    for step in range(devices_x):
        sent = lax.dynamic_index_in_dim(plane, (at_x + step) % devices_x, 0, keepdims=False)
        pairs = []
        for x in range(devices_x):
            for y in range(devices_y):
                to = (x + step) % devices_x
                dest_x = (y % 2) * spans + to // 2
                dest_y = (y // 2) * 2 + to % 2
                pairs.append((x * devices_y + y, dest_x * devices_y + dest_y))
        rows = rows + lax.ppermute(sent, ("gx", "gy"), pairs).astype(f32)
    reduced = lax.all_to_all(rows, "gy", split_axis=1, concat_axis=0, tiled=True)

    first_row = ((at_x * devices_z + at_z) * devices_y + at_y) * part
    factor = pl.pallas_call(
        factor_kernel,
        out_shape=jax.ShapeDtypeStruct((part, cols), f32),
        in_specs=[whole(pltpu.SMEM)] + [whole()] * 4,
        out_specs=whole(),
        compiler_params=pltpu.CompilerParams(vmem_limit_bytes=32 * 2**20),
    )(first_row[None], rows, inverse_0, factor_10, inverse_1)
    factor = lax.all_to_all(factor, "gy", split_axis=1, concat_axis=0, tiled=True)
    return (reduced, factor)


def solution(mesh):
    placed = (P("gx", "gy", "gz", None), P("gx", "gy", "gz"), P(), P(), P(), P())
    return jax.shard_map(
        local,
        mesh=mesh,
        in_specs=placed,
        out_specs=(P(("gx", "gz"), "gy"), P(("gx", "gz"), "gy")),
        check_vma=False,
    )
```

```python
import functools

import jax
import jax.numpy as jnp
from jax import lax
from jax.experimental import pallas as pl
from jax.experimental.pallas import tpu as pltpu
from jax.sharding import PartitionSpec as P

NB = 512
PANELS = 2
LEAF = 128
SUB = 8


def dot3(a, b, dims):
    a_hi = a.astype(jnp.bfloat16)
    b_hi = b.astype(jnp.bfloat16)
    a_lo = (a - a_hi.astype(jnp.float32)).astype(jnp.bfloat16)
    b_lo = (b - b_hi.astype(jnp.float32)).astype(jnp.bfloat16)

    def dot(x, y):
        return lax.dot_general(x, y, (dims, ((), ())), preferred_element_type=jnp.float32)

    return dot(a_hi, b_hi) + (dot(a_hi, b_lo) + dot(a_lo, b_hi))


def inverse_of(d):
    guess = pl.reciprocal(d, approx=True)
    return guess * (2.0 - d * guess)


def leaf_inverse(block_ref):
    lanes = lax.broadcasted_iota(jnp.int32, (SUB, LEAF), 1)
    subs = lax.broadcasted_iota(jnp.int32, (SUB, LEAF), 0)
    shape = (SUB, LEAF)
    for t in range(LEAF // SUB):
        j0 = t * SUB
        rows = block_ref[j0 : j0 + SUB, :]
        cols = [jnp.broadcast_to(rows[:, j0 + k : j0 + k + 1], shape) for k in range(SUB)]
        p = [[jnp.broadcast_to(cols[k][i : i + 1, :], shape) for k in range(i + 1)] for i in range(SUB)]
        in_block = jnp.logical_and(lanes >= j0, lanes < j0 + SUB)
        start = jnp.where(in_block, (lanes - j0 == subs).astype(jnp.float32), rows)
        u = [jnp.broadcast_to(start[k : k + 1, :], shape) for k in range(SUB)]
        inv = [None] * SUB
        factor = [[None] * SUB for _ in range(SUB)]
        for k in range(SUB):
            inv[k] = inverse_of(p[k][k])
            for i in range(k + 1, SUB):
                factor[i][k] = p[i][k] * inv[k]
                for j in range(k + 1, i + 1):
                    p[i][j] = p[i][j] - factor[i][k] * p[j][k] if j < i else p[i][j] - factor[i][k] * p[i][k]
                u[i] = u[i] - factor[i][k] * u[k]
        out = u[0] * lax.rsqrt(p[0][0])
        for k in range(1, SUB):
            out = jnp.where(subs == k, u[k] * lax.rsqrt(p[k][k]), out)
        block_ref[j0 : j0 + SUB, :] = out
        if t + 1 == LEAF // SUB:
            break
        z = [None] * SUB
        for k in reversed(range(SUB)):
            z[k] = u[k] * inv[k]
            for i in range(k + 1, SUB):
                z[k] = z[k] - factor[i][k] * z[i]
        for v in range(t + 1, LEAF // SUB):
            below = block_ref[v * SUB : (v + 1) * SUB, :]
            upd = jnp.where(in_block, 0.0, below)
            for k in range(SUB):
                upd = upd - jnp.broadcast_to(below[:, j0 + k : j0 + k + 1], shape) * z[k]
            block_ref[v * SUB : (v + 1) * SUB, :] = upd


def factor_inverse(s_ref, d_ref):
    width = s_ref.shape[0]
    row_ids = lax.broadcasted_iota(jnp.int32, (width, width), 0)
    col_ids = lax.broadcasted_iota(jnp.int32, (width, width), 1)
    wide_cols = lax.broadcasted_iota(jnp.int32, (LEAF, width), 1)
    leaf_rows = lax.broadcasted_iota(jnp.int32, (LEAF, LEAF), 0)
    leaf_cols = lax.broadcasted_iota(jnp.int32, (LEAF, LEAF), 1)

    def step(b, carry):
        off = pl.multiple_of(b * LEAF, LEAF)
        span = pl.ds(off, LEAF)
        d_ref[...] = s_ref[span, span]
        leaf_inverse(d_ref)
        inverse = jnp.where(leaf_rows >= leaf_cols, d_ref[...], 0.0)
        s_ref[span, span] = (leaf_rows == leaf_cols).astype(jnp.float32)
        upper = dot3(inverse, s_ref[span, :], ((1,), (0,)))
        s_ref[span, :] = upper
        tail = jnp.where(wide_cols >= off + LEAF, upper, 0.0)
        current = s_ref[...]
        dead = jnp.logical_and(
            row_ids >= off + LEAF, jnp.logical_and(col_ids >= off, col_ids < off + LEAF)
        )
        s_ref[...] = jnp.where(dead, 0.0, current) - dot3(tail, upper, ((0,), (0,)))
        return carry

    lax.fori_loop(0, width // LEAF, step, 0)
    s_ref[...] = jnp.where(row_ids >= col_ids, s_ref[...], 0.0)


def unpack_symmetric(packed_ref, s_ref, first=0):
    at = first
    for i in range(s_ref.shape[0] // LEAF):
        for j in range(i + 1):
            block = packed_ref[at * LEAF : (at + 1) * LEAF, :]
            s_ref[i * LEAF : (i + 1) * LEAF, j * LEAF : (j + 1) * LEAF] = block
            if j < i:
                s_ref[j * LEAF : (j + 1) * LEAF, i * LEAF : (i + 1) * LEAF] = block.T
            at += 1


def first_panel_kernel(packed_ref, w_ref, d_ref):
    unpack_symmetric(packed_ref, w_ref)
    factor_inverse(w_ref, d_ref)


def next_panel_kernel(packed_ref, w0_ref, f_ref, w_ref, d_ref):
    unpack_symmetric(packed_ref, w_ref)
    nb = w0_ref.shape[0]
    start = packed_ref.shape[0] - nb // LEAF * nb
    below = jnp.concatenate(
        [packed_ref[start + i * nb : start + (i + 1) * nb, :] for i in range(nb // LEAF)], 1
    )
    below = dot3(below, w0_ref[...], ((1,), (1,)))
    f_ref[...] = below
    w_ref[...] = w_ref[...] - dot3(below, below, ((1,), (1,)))
    factor_inverse(w_ref, d_ref)


def factor_kernel(first_ref, rows_ref, w0_ref, f_ref, w1_ref, out_ref):
    nb = w0_ref.shape[0]
    ids = first_ref[0] + lax.broadcasted_iota(jnp.int32, (rows_ref.shape[0], nb), 0)
    cols = lax.broadcasted_iota(jnp.int32, (rows_ref.shape[0], nb), 1)
    part = dot3(rows_ref[:, :nb], w0_ref[...], ((1,), (1,)))
    rest = rows_ref[:, nb:] - dot3(part, f_ref[...], ((1,), (1,)))
    rest = dot3(rest, w1_ref[...], ((1,), (1,)))
    width = out_ref.shape[2]
    for at, value in ((0, part), (nb, rest)):
        value = jnp.where(cols + at <= ids, value, 0.0)
        for i in range(nb // width):
            out_ref[at // width + i] = value[:, i * width : (i + 1) * width]


def panel_call(kernel, outputs, nb, *operands):
    return pl.pallas_call(
        kernel,
        out_shape=[jax.ShapeDtypeStruct((nb, nb), jnp.float32)] * outputs,
        in_specs=[pl.BlockSpec(memory_space=pltpu.VMEM)] * len(operands),
        out_specs=[pl.BlockSpec(memory_space=pltpu.VMEM)] * outputs,
        scratch_shapes=[pltpu.VMEM((LEAF, LEAF), jnp.float32)],
        compiler_params=pltpu.CompilerParams(vmem_limit_bytes=24 * 2**20),
        cost_estimate=pl.CostEstimate(
            flops=24 * nb**3 * 8, transcendentals=0, bytes_accessed=8 * nb * nb
        ),
    )(*operands)


def first_panel(packed, nb):
    return panel_call(first_panel_kernel, 1, nb, packed)[0]


def next_panel(packed, w0):
    return panel_call(next_panel_kernel, 2, w0.shape[0], packed, w0)


def whole(memory=pltpu.VMEM):
    return pl.BlockSpec(memory_space=memory)


def faces_kernel(cond_ref, ground_ref, info_ref, cells_ref, load_ref, panel_ref, *refs, sides):
    outs, (conduct_ref, grounds_ref, scaled_ref) = refs[:6], refs[6:]
    size_x, size_y, size_z = sides
    count, width = panel_ref.shape
    tile = 64
    classes = cond_ref.shape[0]
    ports = cells_ref.shape[1]

    def by_tile(t, carry):
        rows = pl.ds(pl.multiple_of(t * tile, tile), tile)
        kind = jnp.broadcast_to(info_ref[rows, 0:1], (tile, LEAF))
        ids = jnp.broadcast_to(info_ref[rows, 1:2], (tile, LEAF))
        conduct = jnp.zeros((tile, LEAF), jnp.float32)
        grounds = jnp.zeros((tile, LEAF), jnp.float32)
        for c in range(classes):
            conduct = jnp.where(kind == c, cond_ref[c], conduct)
            grounds = jnp.where(kind == c, ground_ref[c], grounds)
        loads = jnp.zeros((tile, LEAF), jnp.float32)
        for p in range(0, ports, LEAF):
            hit = ids == cells_ref[:, p : p + LEAF]
            loads = loads + jnp.where(hit, load_ref[:, p : p + LEAF], 0.0)
        conduct_ref[rows, :] = conduct
        grounds_ref[rows, :] = grounds + jnp.sum(loads, axis=1, keepdims=True)
        for p in range(0, width, LEAF):
            part = panel_ref[rows, p : p + LEAF].astype(jnp.float32)
            scaled_ref[p // LEAF, rows, :] = (
                (conduct * part).astype(jnp.bfloat16).astype(jnp.float32)
            )
        return carry

    lax.fori_loop(0, count // tile, by_tile, 0)
    plane = size_y * size_z
    for p in range(width // LEAF):
        lanes = slice(p * LEAF, (p + 1) * LEAF)
        outs[0][:, lanes] = scaled_ref[p, 0:plane, :].astype(jnp.bfloat16)
        outs[1][:, lanes] = scaled_ref[p, count - plane : count, :].astype(jnp.bfloat16)
        for out, at in ((outs[2], 0), (outs[3], plane - size_z)):
            face = [
                scaled_ref[p, x * plane + at : x * plane + at + size_z, :] for x in range(size_x)
            ]
            out[:, lanes] = jnp.concatenate(face, 0).astype(jnp.bfloat16)
        for out, at in ((outs[4], 0), (outs[5], size_z - 1)):
            face = scaled_ref[p, pl.ds(at, size_x * size_y, stride=size_z), :]
            out[:, lanes] = face.astype(jnp.bfloat16)


def image_kernel(panel_ref, conduct_ref, grounds_ref, *refs, sides, nb):
    halos, (image_ref, first_ref, later_ref, scaled_ref, square_ref) = refs[:6], refs[6:]
    size_x, size_y, size_z = sides
    width = panel_ref.shape[1]
    plane = size_y * size_z
    subs = lax.broadcasted_iota(jnp.int32, (size_z, LEAF), 0)

    def by_lane(p, carry):
        lanes = pl.ds(pl.multiple_of(p * LEAF, LEAF), LEAF)
        x_low, x_high, y_low, y_high, z_low, z_high = (
            h[:, lanes].astype(jnp.float32) for h in halos
        )
        scaled_ref[...] = (
            (conduct_ref[...] * panel_ref[:, lanes].astype(jnp.float32))
            .astype(jnp.bfloat16)
            .astype(jnp.float32)
        )

        def cell_rows(x, y):
            at = x * plane + y * size_z
            return scaled_ref[at : at + size_z, :]

        for x in range(size_x):
            done = []
            for y in range(size_y):
                at = x * plane + y * size_z
                here = cell_rows(x, y)
                span = slice(y * size_z, (y + 1) * size_z)
                total = cell_rows(x + 1, y) if x + 1 < size_x else x_high[span, :]
                total = total + (cell_rows(x - 1, y) if x > 0 else x_low[span, :])
                span = slice(x * size_z, (x + 1) * size_z)
                total = total + (cell_rows(x, y + 1) if y + 1 < size_y else y_high[span, :])
                total = total + (cell_rows(x, y - 1) if y > 0 else y_low[span, :])
                k = x * size_y + y
                up = jnp.where(
                    subs == size_z - 1, z_high[k : k + 1, :], pltpu.roll(here, size_z - 1, 0)
                )
                down = jnp.where(subs == 0, z_low[k : k + 1, :], pltpu.roll(here, 1, 0))
                total = total + up + down
                own = slice(at, at + size_z)
                done.append(
                    conduct_ref[own, :] * (6.0 * here - total)
                    + grounds_ref[own, :] * panel_ref[at : at + size_z, lanes].astype(jnp.float32)
                )
            image_ref[x * plane : (x + 1) * plane, lanes] = jnp.concatenate(done, 0).astype(
                jnp.bfloat16
            )
        return carry

    lax.fori_loop(0, width // LEAF, by_lane, 0)

    def product(rows, cols):
        return lax.dot_general(
            panel_ref[:, rows],
            image_ref[:, cols],
            (((0,), (0,)), ((), ())),
            preferred_element_type=jnp.float32,
        )

    blocks = nb // LEAF

    def lower(out_ref):
        at = 0
        for i in range(blocks):
            for j in range(i + 1):
                row, col = slice(i * LEAF, (i + 1) * LEAF), slice(j * LEAF, (j + 1) * LEAF)
                out_ref[at : at + LEAF, :] = 0.5 * (square_ref[row, col] + square_ref[col, row].T)
                at += LEAF
        return at

    head, tail = slice(0, nb), slice(nb, 2 * nb)
    square_ref[...] = product(head, head)
    lower(first_ref)
    square_ref[...] = product(tail, tail)
    at = lower(later_ref)
    below = product(tail, head)
    for i in range(blocks):
        later_ref[at + i * nb : at + (i + 1) * nb, :] = below[:, i * LEAF : (i + 1) * LEAF]


def pieces_kernel(index_ref, *refs, groups):
    del index_ref
    total = sum(groups)
    ins, outs = refs[:total], refs[total:]
    at = 0
    for out, count in zip(outs, groups):
        width = out.shape[1] // count
        for i in range(count):
            out[:, i * width : (i + 1) * width] = ins[at][...]
            at += 1


def take_pieces(flat_basis, lists):
    rows = flat_basis.shape[0]
    tile = min(128, rows)
    index = jnp.stack([jnp.asarray(b, jnp.int32) for blocks, _ in lists for b in blocks])
    in_specs, out_specs, out_shape = [], [], []
    for blocks, width in lists:
        for _ in blocks:
            k = len(in_specs)
            in_specs.append(pl.BlockSpec((tile, width), lambda t, idx, k=k: (t, idx[k])))
        out_specs.append(pl.BlockSpec((tile, width * len(blocks)), lambda t, idx: (t, 0)))
        out_shape.append(jax.ShapeDtypeStruct((rows, width * len(blocks)), flat_basis.dtype))
    kernel = functools.partial(pieces_kernel, groups=[len(blocks) for blocks, _ in lists])
    return pl.pallas_call(
        kernel,
        grid_spec=pltpu.PrefetchScalarGridSpec(
            num_scalar_prefetch=1, grid=(rows // tile,), in_specs=in_specs, out_specs=out_specs
        ),
        out_shape=out_shape,
        compiler_params=pltpu.CompilerParams(vmem_limit_bytes=32 * 2**20),
        cost_estimate=pl.CostEstimate(
            flops=0, transcendentals=0, bytes_accessed=4 * rows * flat_basis.shape[1]
        ),
    )(index, *([flat_basis] * len(in_specs)))


def products_kernel(index_ref, *refs):
    del index_ref
    out, count = refs[-1], len(refs) // 2
    total = None
    for b, image in zip(refs[:count], refs[count:-1]):
        term = lax.dot_general(
            b[...], image[...], (((0,), (0,)), ((), ())), preferred_element_type=jnp.float32
        )
        total = term if total is None else total + term
    out[...] = total.astype(out.dtype)


def products(bases, images, lists, width, dtype):
    rows, cols = images[0].shape
    step = 512 if width % 512 == 0 else width
    parts = width // step
    steps = len(lists[0]) * parts
    index = jnp.stack(
        [jnp.asarray(b * parts + i, jnp.int32) for blocks in lists for b in blocks for i in range(parts)]
    )
    in_specs = [
        pl.BlockSpec((rows, step), lambda t, idx, k=k: (0, idx[k * steps + t]))
        for k in range(len(bases))
    ]
    in_specs += [pl.BlockSpec((rows, cols), lambda t, idx: (0, 0))] * len(images)
    total = steps * step
    return pl.pallas_call(
        products_kernel,
        grid_spec=pltpu.PrefetchScalarGridSpec(
            num_scalar_prefetch=1,
            grid=(steps,),
            in_specs=in_specs,
            out_specs=pl.BlockSpec((step, cols), lambda t, idx: (t, 0)),
        ),
        out_shape=jax.ShapeDtypeStruct((total, cols), dtype),
        compiler_params=pltpu.CompilerParams(vmem_limit_bytes=48 * 2**20),
        cost_estimate=pl.CostEstimate(
            flops=2 * total * cols * rows * len(bases),
            transcendentals=0,
            bytes_accessed=2 * rows * (total + cols) * len(bases) + 4 * total * cols,
        ),
    )(index, *bases, *images)


def add_kernel(index_ref, *refs):
    del index_ref
    total = refs[0][...].astype(jnp.float32)
    for got in refs[1:-1]:
        total = total + got[...].astype(jnp.float32)
    refs[-1][...] = total.astype(refs[-1].dtype)


def add_blocks(arrays, lists, height, dtype):
    cols = arrays[0].shape[1]
    step = min(128, height)
    parts = height // step
    steps = len(lists[0]) * parts
    index = jnp.stack(
        [jnp.asarray(b * parts + i, jnp.int32) for blocks in lists for b in blocks for i in range(parts)]
    )
    return pl.pallas_call(
        add_kernel,
        grid_spec=pltpu.PrefetchScalarGridSpec(
            num_scalar_prefetch=1,
            grid=(steps,),
            in_specs=[
                pl.BlockSpec((step, cols), lambda t, idx, k=k: (idx[k * steps + t], 0))
                for k in range(len(arrays))
            ],
            out_specs=pl.BlockSpec((step, cols), lambda t, idx: (t, 0)),
        ),
        out_shape=jax.ShapeDtypeStruct((steps * step, cols), dtype),
        compiler_params=pltpu.CompilerParams(vmem_limit_bytes=24 * 2**20),
        cost_estimate=pl.CostEstimate(
            flops=steps * step * cols,
            transcendentals=0,
            bytes_accessed=steps * step * cols * 4 * len(arrays),
        ),
    )(index, *arrays)


def pick_kernel(index_ref, *refs):
    half = (len(refs) - 1) // 2

    def total(group):
        out = group[0][...].astype(jnp.float32)
        for got in group[1:]:
            out = out + got[...].astype(jnp.float32)
        refs[-1][...] = out.astype(refs[-1].dtype)

    @pl.when(index_ref[0] == 0)
    def _():
        total(refs[:half])

    @pl.when(index_ref[0] != 0)
    def _():
        total(refs[half:-1])


def pick_block(second, arrays_a, arrays_b, at_a, at_b, height, dtype):
    cols = arrays_a[0].shape[1]
    step = min(128, height)
    parts = height // step
    arrays = [*arrays_a, *arrays_b]
    index = jnp.stack([jnp.asarray(v, jnp.int32) for v in (second, *at_a, *at_b)])
    return pl.pallas_call(
        pick_kernel,
        grid_spec=pltpu.PrefetchScalarGridSpec(
            num_scalar_prefetch=1,
            grid=(parts,),
            in_specs=[
                pl.BlockSpec((step, cols), lambda t, idx, k=k: (idx[1 + k] * parts + t, 0))
                for k in range(len(arrays))
            ],
            out_specs=pl.BlockSpec((step, cols), lambda t, idx: (t, 0)),
        ),
        out_shape=jax.ShapeDtypeStruct((height, cols), dtype),
        compiler_params=pltpu.CompilerParams(vmem_limit_bytes=24 * 2**20),
        cost_estimate=pl.CostEstimate(
            flops=height * cols, transcendentals=0, bytes_accessed=height * cols * 18
        ),
    )(index, *arrays)


def swap_pairs():
    return [(0, 1), (1, 0)]


def sum_everywhere(rows, core, axes, devices):
    half = rows.shape[0] // 2
    share = half // devices
    both = rows.reshape(2, half, LEAF)
    kept = lax.dynamic_index_in_dim(both, core, 0, keepdims=False)
    sent = lax.dynamic_index_in_dim(both, 1 - core, 0, keepdims=False)
    mine = kept + lax.ppermute(sent, "core", swap_pairs())
    terms = lax.all_to_all(
        mine.reshape(devices, share, LEAF), axes, split_axis=0, concat_axis=0, tiled=True
    )
    own = jnp.broadcast_to(jnp.sum(terms, axis=0), (devices, share, LEAF))
    own = lax.all_to_all(own, axes, split_axis=0, concat_axis=0, tiled=True).reshape(half, LEAF)
    other = lax.ppermute(own, "core", swap_pairs())
    first = core == 0
    return jnp.concatenate([jnp.where(first, own, other), jnp.where(first, other, own)], 0)


def sums_kernel(home_ref, own_ref, swapped_ref, *refs):
    ins, (rows_ref, blocks_ref) = refs[:-2], refs[-2:]
    total = jnp.where(home_ref[0] != 0, own_ref[...], swapped_ref[...])
    for got in ins:
        total = total + got[...].astype(jnp.float32)
    rows_ref[...] = total
    width = blocks_ref.shape[2]
    for i in range(blocks_ref.shape[0]):
        blocks_ref[i] = total[:, i * width : (i + 1) * width]


def local(basis, classes, cond_table, ground_table, port_cells, port_load):
    sides = classes.shape
    cells_x, cells_y, cells_z = sides
    width_k = basis.shape[3]
    devices_x = lax.axis_size("gx")
    chips_y = lax.axis_size("gy")
    devices_z = lax.axis_size("gz")
    devices_y = 2 * chips_y
    spans = devices_x // 2
    split = spans // 2
    count = cells_x * cells_y * cells_z
    cols = PANELS * NB
    at_x, chip, core, at_z = (lax.axis_index(axis) for axis in ("gx", "gy", "core", "gz"))
    at_y = 2 * chip + core
    f32, bf16 = jnp.float32, jnp.bfloat16

    flat_basis = basis.reshape(count, width_k)
    wide = width_k // (devices_x * devices_z)
    narrow = wide // chips_y
    part = narrow // 2
    (given,) = take_pieces(flat_basis, [([1 - core], width_k // 2)])

    def move(array, axis, d):
        size = lax.axis_size(axis)
        return lax.ppermute(array, axis, [(i, (i + d) % size) for i in range(size)])

    panel = flat_basis[:, :cols]
    global_x = at_x * cells_x + jnp.arange(cells_x, dtype=jnp.int32)
    global_y = at_y * cells_y + jnp.arange(cells_y, dtype=jnp.int32)
    global_z = at_z * cells_z + jnp.arange(cells_z, dtype=jnp.int32)
    flat_ids = (
        (global_x[:, None, None] * (cells_y * devices_y) + global_y[None, :, None])
        * (cells_z * devices_z)
        + global_z[None, None, :]
    )
    info = jnp.stack([classes, flat_ids], -1).reshape(count, 2)
    face_rows = [cells_y * cells_z] * 2 + [cells_x * cells_z] * 2 + [cells_x * cells_y] * 2
    *faces, conduct, grounds = pl.pallas_call(
        functools.partial(faces_kernel, sides=sides),
        out_shape=[jax.ShapeDtypeStruct((n, cols), bf16) for n in face_rows]
        + [jax.ShapeDtypeStruct((count, LEAF), f32)] * 2,
        in_specs=[whole(pltpu.SMEM)] * 2 + [whole()] * 4,
        out_specs=[whole()] * 8,
        scratch_shapes=[pltpu.VMEM((cols // LEAF, count, LEAF), f32)],
        compiler_params=pltpu.CompilerParams(vmem_limit_bytes=24 * 2**20),
    )(cond_table, ground_table, info, port_cells[None, :], port_load[None, :], panel)
    halos = []
    for i, (axis, size) in enumerate(
        (("gx", devices_x), (("gy", "core"), devices_y), ("gz", devices_z))
    ):
        low, high = faces[2 * i : 2 * i + 2]
        if size == 2:
            last = lax.axis_index(axis) == 1
            got = lax.ppermute(jnp.where(last, low, high), axis, swap_pairs())
            halos.append(jnp.where(last, got, 0))
            halos.append(jnp.where(last, 0, got))
        else:
            halos.append(lax.ppermute(high, axis, [(k, k + 1) for k in range(size - 1)]))
            halos.append(lax.ppermute(low, axis, [(k + 1, k) for k in range(size - 1)]))
    other_basis = lax.ppermute(given, "core", swap_pairs())

    blocks = NB // LEAF
    lower_rows = blocks * (blocks + 1) // 2 * LEAF
    halos, _ = lax.optimization_barrier((halos, given))
    image, first_rows, later_rows = pl.pallas_call(
        functools.partial(image_kernel, sides=sides, nb=NB),
        out_shape=[
            jax.ShapeDtypeStruct((count, cols), bf16),
            jax.ShapeDtypeStruct((lower_rows, LEAF), f32),
            jax.ShapeDtypeStruct((lower_rows + blocks * NB, LEAF), f32),
        ],
        in_specs=[whole()] * 9,
        out_specs=[whole()] * 3,
        scratch_shapes=[pltpu.VMEM((count, LEAF), f32), pltpu.VMEM((NB, NB), f32)],
        compiler_params=pltpu.CompilerParams(vmem_limit_bytes=32 * 2**20),
    )(panel, conduct, grounds, *halos)

    other_image = lax.ppermute(image, "core", swap_pairs())

    axes = ("gx", "gy", "gz")
    chips = devices_x * chips_y * devices_z
    first_rows = sum_everywhere(first_rows, core, axes, chips)
    inverse_0 = first_panel(first_rows, NB)

    shift = core * spans * devices_z * chips_y

    def chip_products(blocks, dtype):
        lists = [[b + shift for b in blocks], blocks]
        return products([flat_basis, other_basis], [image, other_image], lists, narrow, dtype)

    def products_a(d, dtype):
        x = (at_z + d) % devices_z
        blocks = [(zz * devices_z + x) * chips_y + y for zz in range(split) for y in range(chips_y)]
        return chip_products(blocks, dtype)

    def products_b(d, dtype):
        y = (chip + d) % chips_y
        blocks = [
            (zz * devices_z + x) * chips_y + y for zz in range(split, spans) for x in range(devices_z)
        ]
        return chip_products(blocks, dtype)

    got_a = [move(products_a(d, bf16), "gz", d) for d in range(1, devices_z)]
    got_b = [move(products_b(d, bf16), "gy", d) for d in range(1, chips_y)]
    own_a, own_b = products_a(0, f32), products_b(0, f32)
    (got_a, got_b, own_a, own_b, later_rows), inverse_0 = lax.optimization_barrier(
        ((got_a, got_b, own_a, own_b, later_rows), inverse_0)
    )
    later_rows = sum_everywhere(later_rows, core, axes, chips)
    sums_a, sums_b = [own_a, *got_a], [own_b, *got_b]

    def further(arrays, axis, mine, size, groups):
        got = []
        for d in range(1, size):
            blocks = [zz * size + (mine + d) % size for zz in range(groups)]
            got.append(move(add_blocks(arrays, [blocks] * len(arrays), narrow, bf16), axis, d))
        return got

    further_a = further(sums_a, "gy", chip, chips_y, split)
    further_b = further(sums_b, "gz", at_z, devices_z, spans - split)

    def plane_block(zz, c, dtype):
        in_b = zz >= split
        zz_a, zz_b = jnp.minimum(zz, split - 1), jnp.maximum(zz - split, 0)
        at_a = [(zz_a * chips_y + chip) * 2 + c] * len(sums_a) + [zz_a * 2 + c] * len(further_a)
        at_b = [(zz_b * devices_z + at_z) * 2 + c] * len(sums_b) + [zz_b * 2 + c] * len(further_b)
        return pick_block(
            in_b, sums_a + further_a, sums_b + further_b, at_a, at_b, part, dtype
        )

    x_got, x_sent = [], []
    for step in range(devices_x):
        to = (at_x + step) % devices_x
        x_sent.append(plane_block(to // 2, to % 2, bf16))
        pairs = []
        for x in range(devices_x):
            for y in range(devices_y):
                to = (x + step) % devices_x
                dest_x = (y % 2) * spans + to // 2
                dest_y = (y // 2) * 2 + to % 2
                if dest_x != x:
                    pairs.append((x * devices_y + y, dest_x * devices_y + dest_y))
        x_got.append(lax.ppermute(x_sent[-1], ("gx", "gy", "core"), pairs))
    home = at_x // spans == core
    own = plane_block(at_x % spans, core, f32)
    swapped = lax.ppermute(plane_block(at_x % spans, 1 - core, f32), "core", swap_pairs())
    later_rows, x_sent, own = lax.optimization_barrier((later_rows, x_sent, own))
    factor_10, inverse_1 = next_panel(later_rows, inverse_0)
    (x_got, swapped), inverse_1 = lax.optimization_barrier(((x_got, swapped), inverse_1))
    by_blocks = jax.ShapeDtypeStruct((devices_y, part, cols // devices_y), f32)
    rows, reduced = pl.pallas_call(
        sums_kernel,
        out_shape=[jax.ShapeDtypeStruct((part, cols), f32), by_blocks],
        in_specs=[whole(pltpu.SMEM)] + [whole()] * (devices_x + 2),
        out_specs=[whole()] * 2,
        compiler_params=pltpu.CompilerParams(vmem_limit_bytes=32 * 2**20),
    )(home.astype(jnp.int32)[None], own, swapped, *x_got)

    def to_columns(array):
        array = lax.all_to_all(array, ("gy", "core"), split_axis=0, concat_axis=0, tiled=True)
        return array.reshape(devices_y * part, cols // devices_y)

    reduced = to_columns(reduced)
    first_row = ((at_x * devices_z + at_z) * devices_y + at_y) * part
    factor = pl.pallas_call(
        factor_kernel,
        out_shape=by_blocks,
        in_specs=[whole(pltpu.SMEM)] + [whole()] * 4,
        out_specs=whole(),
        compiler_params=pltpu.CompilerParams(vmem_limit_bytes=32 * 2**20),
    )(first_row[None], rows, inverse_0, factor_10, inverse_1)
    return (reduced, to_columns(factor))


def solution(mesh):
    sizes = mesh.shape
    fine = jax.sharding.Mesh(
        mesh.devices.reshape(sizes["gx"], sizes["gy"] // 2, 2, sizes["gz"]),
        ("gx", "gy", "core", "gz"),
    )
    grid = ("gx", ("gy", "core"), "gz")
    out = P(("gx", "gz"), ("gy", "core"))
    return jax.shard_map(
        local,
        mesh=fine,
        in_specs=(P(*grid, None), P(*grid), P(), P(), P(), P()),
        out_specs=(out, out),
        check_vma=False,
    )
```

```python
import functools

import jax
import jax.numpy as jnp
from jax import lax
from jax.experimental import pallas as pl
from jax.experimental.pallas import tpu as pltpu
from jax.sharding import PartitionSpec as P

NB = 512
PANELS = 2
LEAF = 128
SUB = 8


def dot3(a, b, dims):
    a_hi = a.astype(jnp.bfloat16)
    b_hi = b.astype(jnp.bfloat16)
    a_lo = (a - a_hi.astype(jnp.float32)).astype(jnp.bfloat16)
    b_lo = (b - b_hi.astype(jnp.float32)).astype(jnp.bfloat16)

    def dot(x, y):
        return lax.dot_general(x, y, (dims, ((), ())), preferred_element_type=jnp.float32)

    return dot(a_hi, b_hi) + (dot(a_hi, b_lo) + dot(a_lo, b_hi))


def inverse_of(d):
    guess = pl.reciprocal(d, approx=True)
    return guess * (2.0 - d * guess)


def leaf_inverse(block_ref):
    lanes = lax.broadcasted_iota(jnp.int32, (SUB, LEAF), 1)
    subs = lax.broadcasted_iota(jnp.int32, (SUB, LEAF), 0)
    shape = (SUB, LEAF)
    for t in range(LEAF // SUB):
        j0 = t * SUB
        rows = block_ref[j0 : j0 + SUB, :]
        cols = [jnp.broadcast_to(rows[:, j0 + k : j0 + k + 1], shape) for k in range(SUB)]
        p = [[jnp.broadcast_to(cols[k][i : i + 1, :], shape) for k in range(i + 1)] for i in range(SUB)]
        in_block = jnp.logical_and(lanes >= j0, lanes < j0 + SUB)
        start = jnp.where(in_block, (lanes - j0 == subs).astype(jnp.float32), rows)
        u = [jnp.broadcast_to(start[k : k + 1, :], shape) for k in range(SUB)]
        inv = [None] * SUB
        factor = [[None] * SUB for _ in range(SUB)]
        for k in range(SUB):
            inv[k] = inverse_of(p[k][k])
            for i in range(k + 1, SUB):
                factor[i][k] = p[i][k] * inv[k]
                for j in range(k + 1, i + 1):
                    p[i][j] = p[i][j] - factor[i][k] * p[j][k] if j < i else p[i][j] - factor[i][k] * p[i][k]
                u[i] = u[i] - factor[i][k] * u[k]
        out = u[0] * lax.rsqrt(p[0][0])
        for k in range(1, SUB):
            out = jnp.where(subs == k, u[k] * lax.rsqrt(p[k][k]), out)
        block_ref[j0 : j0 + SUB, :] = out
        if t + 1 == LEAF // SUB:
            break
        z = [None] * SUB
        for k in reversed(range(SUB)):
            z[k] = u[k] * inv[k]
            for i in range(k + 1, SUB):
                z[k] = z[k] - factor[i][k] * z[i]
        for v in range(t + 1, LEAF // SUB):
            below = block_ref[v * SUB : (v + 1) * SUB, :]
            upd = jnp.where(in_block, 0.0, below)
            for k in range(SUB):
                upd = upd - jnp.broadcast_to(below[:, j0 + k : j0 + k + 1], shape) * z[k]
            block_ref[v * SUB : (v + 1) * SUB, :] = upd


def factor_inverse(s_ref, d_ref):
    width = s_ref.shape[0]
    row_ids = lax.broadcasted_iota(jnp.int32, (width, width), 0)
    col_ids = lax.broadcasted_iota(jnp.int32, (width, width), 1)
    wide_cols = lax.broadcasted_iota(jnp.int32, (LEAF, width), 1)
    leaf_rows = lax.broadcasted_iota(jnp.int32, (LEAF, LEAF), 0)
    leaf_cols = lax.broadcasted_iota(jnp.int32, (LEAF, LEAF), 1)

    def step(b, carry):
        off = pl.multiple_of(b * LEAF, LEAF)
        span = pl.ds(off, LEAF)
        d_ref[...] = s_ref[span, span]
        leaf_inverse(d_ref)
        inverse = jnp.where(leaf_rows >= leaf_cols, d_ref[...], 0.0)
        s_ref[span, span] = (leaf_rows == leaf_cols).astype(jnp.float32)
        upper = dot3(inverse, s_ref[span, :], ((1,), (0,)))
        s_ref[span, :] = upper
        tail = jnp.where(wide_cols >= off + LEAF, upper, 0.0)
        current = s_ref[...]
        dead = jnp.logical_and(
            row_ids >= off + LEAF, jnp.logical_and(col_ids >= off, col_ids < off + LEAF)
        )
        s_ref[...] = jnp.where(dead, 0.0, current) - dot3(tail, upper, ((0,), (0,)))
        return carry

    lax.fori_loop(0, width // LEAF, step, 0)
    s_ref[...] = jnp.where(row_ids >= col_ids, s_ref[...], 0.0)


def unpack_symmetric(packed_ref, s_ref, first=0):
    at = first
    for i in range(s_ref.shape[0] // LEAF):
        for j in range(i + 1):
            block = packed_ref[at * LEAF : (at + 1) * LEAF, :]
            s_ref[i * LEAF : (i + 1) * LEAF, j * LEAF : (j + 1) * LEAF] = block
            if j < i:
                s_ref[j * LEAF : (j + 1) * LEAF, i * LEAF : (i + 1) * LEAF] = block.T
            at += 1


def first_panel_kernel(packed_ref, w_ref, d_ref):
    unpack_symmetric(packed_ref, w_ref)
    factor_inverse(w_ref, d_ref)


def next_panel_kernel(packed_ref, w0_ref, f_ref, w_ref, d_ref):
    nb = w0_ref.shape[0]
    blocks = nb // LEAF
    unpack_symmetric(packed_ref, w_ref, blocks * (blocks + 1) // 2)
    start = packed_ref.shape[0] - blocks * nb
    below = jnp.concatenate(
        [packed_ref[start + i * nb : start + (i + 1) * nb, :] for i in range(nb // LEAF)], 1
    )
    below = dot3(below, w0_ref[...], ((1,), (1,)))
    f_ref[...] = below
    w_ref[...] = w_ref[...] - dot3(below, below, ((1,), (1,)))
    factor_inverse(w_ref, d_ref)


def factor_kernel(first_ref, rows_ref, w0_ref, f_ref, w1_ref, *refs):
    blocks, all_ref = refs[:-1], refs[-1]
    nb = w0_ref.shape[0]
    ids = first_ref[0] + lax.broadcasted_iota(jnp.int32, (rows_ref.shape[0], nb), 0)
    cols = lax.broadcasted_iota(jnp.int32, (rows_ref.shape[0], nb), 1)
    part = dot3(rows_ref[:, :nb], w0_ref[...], ((1,), (1,)))
    rest = rows_ref[:, nb:] - dot3(part, f_ref[...], ((1,), (1,)))
    rest = dot3(rest, w1_ref[...], ((1,), (1,)))
    all_ref[:, :nb] = jnp.where(cols <= ids, part, 0.0)
    all_ref[:, nb:] = jnp.where(cols + nb <= ids, rest, 0.0)
    for d, block in enumerate(blocks):
        width = block.shape[1]
        block[...] = all_ref[:, pl.ds(pl.multiple_of(first_ref[1 + d] * width, width), width)]


def panel_call(kernel, outputs, nb, *operands):
    return pl.pallas_call(
        kernel,
        out_shape=[jax.ShapeDtypeStruct((nb, nb), jnp.float32)] * outputs,
        in_specs=[pl.BlockSpec(memory_space=pltpu.VMEM)] * len(operands),
        out_specs=[pl.BlockSpec(memory_space=pltpu.VMEM)] * outputs,
        scratch_shapes=[pltpu.VMEM((LEAF, LEAF), jnp.float32)],
        compiler_params=pltpu.CompilerParams(vmem_limit_bytes=24 * 2**20),
        cost_estimate=pl.CostEstimate(
            flops=24 * nb**3 * 4, transcendentals=0, bytes_accessed=8 * nb * nb
        ),
    )(*operands)


def first_panel(packed, nb):
    return panel_call(first_panel_kernel, 1, nb, packed)[0]


def next_panel(packed, w0):
    return panel_call(next_panel_kernel, 2, w0.shape[0], packed, w0)


def whole(memory=pltpu.VMEM):
    return pl.BlockSpec(memory_space=memory)


def faces_kernel(cond_ref, ground_ref, info_ref, cells_ref, load_ref, panel_ref, *refs, sides):
    outs, (conduct_ref, grounds_ref, scaled_ref) = refs[:6], refs[6:]
    size_x, size_y, size_z = sides
    count, width = panel_ref.shape
    tile = 64
    classes = cond_ref.shape[0]
    ports = cells_ref.shape[1]

    def by_tile(t, carry):
        rows = pl.ds(pl.multiple_of(t * tile, tile), tile)
        kind = jnp.broadcast_to(info_ref[rows, 0:1], (tile, LEAF))
        ids = jnp.broadcast_to(info_ref[rows, 1:2], (tile, LEAF))
        conduct = jnp.zeros((tile, LEAF), jnp.float32)
        grounds = jnp.zeros((tile, LEAF), jnp.float32)
        for c in range(classes):
            conduct = jnp.where(kind == c, cond_ref[c], conduct)
            grounds = jnp.where(kind == c, ground_ref[c], grounds)
        loads = jnp.zeros((tile, LEAF), jnp.float32)
        for p in range(0, ports, LEAF):
            hit = ids == cells_ref[:, p : p + LEAF]
            loads = loads + jnp.where(hit, load_ref[:, p : p + LEAF], 0.0)
        conduct_ref[rows, :] = conduct
        grounds_ref[rows, :] = grounds + jnp.sum(loads, axis=1, keepdims=True)
        for p in range(0, width, LEAF):
            part = panel_ref[rows, p : p + LEAF].astype(jnp.float32)
            scaled_ref[p // LEAF, rows, :] = (
                (conduct * part).astype(jnp.bfloat16).astype(jnp.float32)
            )
        return carry

    lax.fori_loop(0, count // tile, by_tile, 0)
    plane = size_y * size_z
    for p in range(width // LEAF):
        lanes = slice(p * LEAF, (p + 1) * LEAF)
        outs[0][:, lanes] = scaled_ref[p, 0:plane, :].astype(jnp.bfloat16)
        outs[1][:, lanes] = scaled_ref[p, count - plane : count, :].astype(jnp.bfloat16)
        for out, at in ((outs[2], 0), (outs[3], plane - size_z)):
            face = [
                scaled_ref[p, x * plane + at : x * plane + at + size_z, :] for x in range(size_x)
            ]
            out[:, lanes] = jnp.concatenate(face, 0).astype(jnp.bfloat16)
        for out, at in ((outs[4], 0), (outs[5], size_z - 1)):
            face = scaled_ref[p, pl.ds(at, size_x * size_y, stride=size_z), :]
            out[:, lanes] = face.astype(jnp.bfloat16)


def image_kernel(panel_ref, conduct_ref, grounds_ref, *refs, sides, nb):
    halos, (image_ref, first_ref, later_ref, scaled_ref, square_ref) = refs[:6], refs[6:]
    size_x, size_y, size_z = sides
    width = panel_ref.shape[1]
    plane = size_y * size_z
    subs = lax.broadcasted_iota(jnp.int32, (size_z, LEAF), 0)

    def by_lane(p, carry):
        lanes = pl.ds(pl.multiple_of(p * LEAF, LEAF), LEAF)
        x_low, x_high, y_low, y_high, z_low, z_high = (
            h[:, lanes].astype(jnp.float32) for h in halos
        )
        scaled_ref[...] = (
            (conduct_ref[...] * panel_ref[:, lanes].astype(jnp.float32))
            .astype(jnp.bfloat16)
            .astype(jnp.float32)
        )

        def cell_rows(x, y):
            at = x * plane + y * size_z
            return scaled_ref[at : at + size_z, :]

        for x in range(size_x):
            done = []
            for y in range(size_y):
                at = x * plane + y * size_z
                here = cell_rows(x, y)
                span = slice(y * size_z, (y + 1) * size_z)
                total = cell_rows(x + 1, y) if x + 1 < size_x else x_high[span, :]
                total = total + (cell_rows(x - 1, y) if x > 0 else x_low[span, :])
                span = slice(x * size_z, (x + 1) * size_z)
                total = total + (cell_rows(x, y + 1) if y + 1 < size_y else y_high[span, :])
                total = total + (cell_rows(x, y - 1) if y > 0 else y_low[span, :])
                k = x * size_y + y
                up = jnp.where(
                    subs == size_z - 1, z_high[k : k + 1, :], pltpu.roll(here, size_z - 1, 0)
                )
                down = jnp.where(subs == 0, z_low[k : k + 1, :], pltpu.roll(here, 1, 0))
                total = total + up + down
                own = slice(at, at + size_z)
                done.append(
                    conduct_ref[own, :] * (6.0 * here - total)
                    + grounds_ref[own, :] * panel_ref[at : at + size_z, lanes].astype(jnp.float32)
                )
            image_ref[x * plane : (x + 1) * plane, lanes] = jnp.concatenate(done, 0).astype(
                jnp.bfloat16
            )
        return carry

    lax.fori_loop(0, width // LEAF, by_lane, 0)

    def product(rows, cols):
        return lax.dot_general(
            panel_ref[:, rows],
            image_ref[:, cols],
            (((0,), (0,)), ((), ())),
            preferred_element_type=jnp.float32,
        )

    blocks = nb // LEAF

    def lower(out_ref):
        at = 0
        for i in range(blocks):
            for j in range(i + 1):
                row, col = slice(i * LEAF, (i + 1) * LEAF), slice(j * LEAF, (j + 1) * LEAF)
                out_ref[at : at + LEAF, :] = 0.5 * (square_ref[row, col] + square_ref[col, row].T)
                at += LEAF
        return at

    head, tail = slice(0, nb), slice(nb, 2 * nb)
    square_ref[...] = product(head, head)
    lower(first_ref)
    square_ref[...] = product(tail, tail)
    at = lower(later_ref)
    below = product(tail, head)
    for i in range(blocks):
        later_ref[at + i * nb : at + (i + 1) * nb, :] = below[:, i * LEAF : (i + 1) * LEAF]


def pieces_kernel(index_ref, *refs, groups):
    del index_ref
    total = sum(groups)
    ins, outs = refs[:total], refs[total:]
    at = 0
    for out, count in zip(outs, groups):
        width = out.shape[1] // count
        for i in range(count):
            out[:, i * width : (i + 1) * width] = ins[at][...]
            at += 1


def take_pieces(flat_basis, lists):
    rows = flat_basis.shape[0]
    tile = min(128, rows)
    index = jnp.stack([jnp.asarray(b, jnp.int32) for blocks, _ in lists for b in blocks])
    in_specs, out_specs, out_shape = [], [], []
    for blocks, width in lists:
        for _ in blocks:
            k = len(in_specs)
            in_specs.append(pl.BlockSpec((tile, width), lambda t, idx, k=k: (t, idx[k])))
        out_specs.append(pl.BlockSpec((tile, width * len(blocks)), lambda t, idx: (t, 0)))
        out_shape.append(jax.ShapeDtypeStruct((rows, width * len(blocks)), flat_basis.dtype))
    kernel = functools.partial(pieces_kernel, groups=[len(blocks) for blocks, _ in lists])
    return pl.pallas_call(
        kernel,
        grid_spec=pltpu.PrefetchScalarGridSpec(
            num_scalar_prefetch=1, grid=(rows // tile,), in_specs=in_specs, out_specs=out_specs
        ),
        out_shape=out_shape,
        compiler_params=pltpu.CompilerParams(vmem_limit_bytes=32 * 2**20),
        cost_estimate=pl.CostEstimate(
            flops=0, transcendentals=0, bytes_accessed=4 * rows * flat_basis.shape[1]
        ),
    )(index, *([flat_basis] * len(in_specs)))


def products_kernel(index_ref, *refs):
    del index_ref
    out, count = refs[-1], len(refs) // 2
    total = None
    for b, image in zip(refs[:count], refs[count:-1]):
        term = lax.dot_general(
            b[...], image[...], (((0,), (0,)), ((), ())), preferred_element_type=jnp.float32
        )
        total = term if total is None else total + term
    out[...] = total.astype(out.dtype)


def products(bases, images, lists, width, dtype):
    rows, cols = images[0].shape
    step = 512 if width % 512 == 0 else width
    parts = width // step
    steps = len(lists[0]) * parts
    index = jnp.stack(
        [jnp.asarray(b * parts + i, jnp.int32) for blocks in lists for b in blocks for i in range(parts)]
    )
    in_specs = [
        pl.BlockSpec((rows, step), lambda t, idx, k=k: (0, idx[k * steps + t]))
        for k in range(len(bases))
    ]
    in_specs += [pl.BlockSpec((rows, cols), lambda t, idx: (0, 0))] * len(images)
    total = steps * step
    return pl.pallas_call(
        products_kernel,
        grid_spec=pltpu.PrefetchScalarGridSpec(
            num_scalar_prefetch=1,
            grid=(steps,),
            in_specs=in_specs,
            out_specs=pl.BlockSpec((step, cols), lambda t, idx: (t, 0)),
        ),
        out_shape=jax.ShapeDtypeStruct((total, cols), dtype),
        compiler_params=pltpu.CompilerParams(vmem_limit_bytes=56 * 2**20),
        cost_estimate=pl.CostEstimate(
            flops=2 * total * cols * rows * len(bases),
            transcendentals=0,
            bytes_accessed=2 * rows * (total + cols) * len(bases) + 4 * total * cols,
        ),
    )(index, *bases, *images)


def add_kernel(index_ref, *refs):
    del index_ref
    total = refs[0][...].astype(jnp.float32)
    for got in refs[1:-1]:
        total = total + got[...].astype(jnp.float32)
    refs[-1][...] = total.astype(refs[-1].dtype)


def add_blocks(arrays, lists, height, dtype):
    cols = arrays[0].shape[1]
    step = min(128, height)
    parts = height // step
    steps = len(lists[0]) * parts
    index = jnp.stack(
        [jnp.asarray(b * parts + i, jnp.int32) for blocks in lists for b in blocks for i in range(parts)]
    )
    return pl.pallas_call(
        add_kernel,
        grid_spec=pltpu.PrefetchScalarGridSpec(
            num_scalar_prefetch=1,
            grid=(steps,),
            in_specs=[
                pl.BlockSpec((step, cols), lambda t, idx, k=k: (idx[k * steps + t], 0))
                for k in range(len(arrays))
            ],
            out_specs=pl.BlockSpec((step, cols), lambda t, idx: (t, 0)),
        ),
        out_shape=jax.ShapeDtypeStruct((steps * step, cols), dtype),
        compiler_params=pltpu.CompilerParams(vmem_limit_bytes=56 * 2**20),
        cost_estimate=pl.CostEstimate(
            flops=steps * step * cols,
            transcendentals=0,
            bytes_accessed=steps * step * cols * 4 * len(arrays),
        ),
    )(index, *arrays)


def pick_kernel(index_ref, *refs):
    half = (len(refs) - 1) // 2

    def total(group):
        out = group[0][...].astype(jnp.float32)
        for got in group[1:]:
            out = out + got[...].astype(jnp.float32)
        refs[-1][...] = out.astype(refs[-1].dtype)

    @pl.when(index_ref[0] == 0)
    def _():
        total(refs[:half])

    @pl.when(index_ref[0] != 0)
    def _():
        total(refs[half:-1])


def pick_block(second, arrays_a, arrays_b, at_a, at_b, height, dtype):
    cols = arrays_a[0].shape[1]
    step = min(128, height)
    parts = height // step
    arrays = [*arrays_a, *arrays_b]
    index = jnp.stack([jnp.asarray(v, jnp.int32) for v in (second, *at_a, *at_b)])
    return pl.pallas_call(
        pick_kernel,
        grid_spec=pltpu.PrefetchScalarGridSpec(
            num_scalar_prefetch=1,
            grid=(parts,),
            in_specs=[
                pl.BlockSpec((step, cols), lambda t, idx, k=k: (idx[1 + k] * parts + t, 0))
                for k in range(len(arrays))
            ],
            out_specs=pl.BlockSpec((step, cols), lambda t, idx: (t, 0)),
        ),
        out_shape=jax.ShapeDtypeStruct((height, cols), dtype),
        compiler_params=pltpu.CompilerParams(vmem_limit_bytes=56 * 2**20),
        cost_estimate=pl.CostEstimate(
            flops=height * cols, transcendentals=0, bytes_accessed=height * cols * 18
        ),
    )(index, *arrays)


def swap_pairs():
    return [(0, 1), (1, 0)]


def other_half(half, core):
    other = lax.ppermute(half, "core", swap_pairs())
    first = core == 0
    return jnp.concatenate([jnp.where(first, half, other), jnp.where(first, other, half)], 0)


def join_kernel(place_ref, *refs):
    out = refs[-1]
    part = refs[0].shape[0]
    for d, block in enumerate(refs[:-1]):
        out[pl.ds(pl.multiple_of(place_ref[d] * part, part), part), :] = block[...]


def sums_kernel(home_ref, own_ref, swapped_ref, *refs):
    cols, width = own_ref.shape[1], refs[-1].shape[1]
    ins, rows_ref, blocks = refs[: -1 - cols // width], refs[-1 - cols // width], refs[-(cols // width) :]
    total = jnp.where(home_ref[0] != 0, own_ref[...], swapped_ref[...])
    for got in ins:
        total = total + got[...].astype(jnp.float32)
    rows_ref[...] = total
    for d, block in enumerate(blocks):
        at = pl.multiple_of(home_ref[1 + d] * width, width)
        block[...] = rows_ref[:, pl.ds(at, width)]


def local(basis, classes, cond_table, ground_table, port_cells, port_load):
    sides = classes.shape
    cells_x, cells_y, cells_z = sides
    width_k = basis.shape[3]
    devices_x = lax.axis_size("gx")
    chips_y = lax.axis_size("gy")
    devices_z = lax.axis_size("gz")
    devices_y = 2 * chips_y
    spans = devices_x // 2
    split = spans // 2
    count = cells_x * cells_y * cells_z
    cols = PANELS * NB
    at_x, chip, core, at_z = (lax.axis_index(axis) for axis in ("gx", "gy", "core", "gz"))
    at_y = 2 * chip + core
    f32, bf16 = jnp.float32, jnp.bfloat16

    flat_basis = basis.reshape(count, width_k)
    wide = width_k // (devices_x * devices_z)
    narrow = wide // chips_y
    part = narrow // 2

    def move(array, axis, d):
        size = lax.axis_size(axis)
        return lax.ppermute(array, axis, [(i, (i + d) % size) for i in range(size)])

    panel_spec = pl.BlockSpec((count, cols), lambda i: (0, 0))
    global_x = at_x * cells_x + jnp.arange(cells_x, dtype=jnp.int32)
    global_y = at_y * cells_y + jnp.arange(cells_y, dtype=jnp.int32)
    global_z = at_z * cells_z + jnp.arange(cells_z, dtype=jnp.int32)
    flat_ids = (
        (global_x[:, None, None] * (cells_y * devices_y) + global_y[None, :, None])
        * (cells_z * devices_z)
        + global_z[None, None, :]
    )
    info = jnp.stack([classes, flat_ids], -1).reshape(count, 2)
    face_rows = [cells_y * cells_z] * 2 + [cells_x * cells_z] * 2 + [cells_x * cells_y] * 2
    *faces, conduct, grounds = pl.pallas_call(
        functools.partial(faces_kernel, sides=sides),
        out_shape=[jax.ShapeDtypeStruct((n, cols), bf16) for n in face_rows]
        + [jax.ShapeDtypeStruct((count, LEAF), f32)] * 2,
        grid=(1,),
        in_specs=[whole(pltpu.SMEM)] * 2 + [whole()] * 3 + [panel_spec],
        out_specs=[whole()] * 8,
        scratch_shapes=[pltpu.VMEM((cols // LEAF, count, LEAF), f32)],
        compiler_params=pltpu.CompilerParams(vmem_limit_bytes=24 * 2**20),
    )(cond_table, ground_table, info, port_cells[None, :], port_load[None, :], flat_basis)
    faces, other_core = lax.optimization_barrier((faces, 1 - core))
    (given,) = take_pieces(flat_basis, [([other_core], width_k // 2)])
    halos = []
    for i, (axis, size) in enumerate(
        (("gx", devices_x), (("gy", "core"), devices_y), ("gz", devices_z))
    ):
        low, high = faces[2 * i : 2 * i + 2]
        if size == 2:
            last = lax.axis_index(axis) == 1
            got = lax.ppermute(jnp.where(last, low, high), axis, swap_pairs())
            halos.append(jnp.where(last, got, 0))
            halos.append(jnp.where(last, 0, got))
        else:
            halos.append(lax.ppermute(high, axis, [(k, k + 1) for k in range(size - 1)]))
            halos.append(lax.ppermute(low, axis, [(k + 1, k) for k in range(size - 1)]))
    other_basis = lax.ppermute(given, "core", swap_pairs())

    blocks = NB // LEAF
    lower_rows = blocks * (blocks + 1) // 2 * LEAF
    halos, _ = lax.optimization_barrier((halos, given))
    image, first_rows, later_rows = pl.pallas_call(
        functools.partial(image_kernel, sides=sides, nb=NB),
        out_shape=[
            jax.ShapeDtypeStruct((count, cols), bf16),
            jax.ShapeDtypeStruct((lower_rows, LEAF), f32),
            jax.ShapeDtypeStruct((lower_rows + blocks * NB, LEAF), f32),
        ],
        grid=(1,),
        in_specs=[panel_spec] + [whole()] * 8,
        out_specs=[whole()] * 3,
        scratch_shapes=[pltpu.VMEM((count, LEAF), f32), pltpu.VMEM((NB, NB), f32)],
        compiler_params=pltpu.CompilerParams(vmem_limit_bytes=32 * 2**20),
    )(flat_basis, conduct, grounds, *halos)

    other_image = lax.ppermute(image, "core", swap_pairs())

    axes = ("gx", "gy", "gz")
    both = jnp.concatenate([first_rows, later_rows], 0).reshape(2, -1, LEAF)
    kept = lax.dynamic_index_in_dim(both, core, 0, keepdims=False)
    sent = lax.dynamic_index_in_dim(both, 1 - core, 0, keepdims=False)
    lead_half = lax.psum(kept + lax.ppermute(sent, "core", swap_pairs()), axes)

    shift = core * spans * devices_z * chips_y

    def chip_products(blocks, dtype):
        lists = [[b + shift for b in blocks], blocks]
        return products([flat_basis, other_basis], [image, other_image], lists, narrow, dtype)

    def products_a(d, dtype):
        x = (at_z + d) % devices_z
        blocks = [(zz * devices_z + x) * chips_y + y for zz in range(split) for y in range(chips_y)]
        return chip_products(blocks, dtype)

    def products_b(d, dtype):
        y = (chip + d) % chips_y
        blocks = [
            (zz * devices_z + x) * chips_y + y for zz in range(split, spans) for x in range(devices_z)
        ]
        return chip_products(blocks, dtype)

    got_a = [move(products_a(d, bf16), "gz", d) for d in range(1, devices_z)]
    got_b = [move(products_b(d, bf16), "gy", d) for d in range(1, chips_y)]
    own_a, own_b = products_a(0, f32), products_b(0, f32)
    sums_a, sums_b = [own_a, *got_a], [own_b, *got_b]

    def further(arrays, mine, size, groups):
        sent = []
        for d in range(1, size):
            blocks = [zz * size + (mine + d) % size for zz in range(groups)]
            sent.append(add_blocks(arrays, [blocks] * len(arrays), narrow, bf16))
        return sent

    further_a = further(sums_a, chip, chips_y, split)
    further_b = further(sums_b, at_z, devices_z, spans - split)
    lead_half, _ = lax.optimization_barrier((lead_half, (further_a, further_b)))
    further_a = [move(a, "gy", d) for d, a in enumerate(further_a, 1)]
    further_b = [move(a, "gz", d) for d, a in enumerate(further_b, 1)]
    lead_rows = other_half(lead_half, core)
    inverse_0 = first_panel(lead_rows, NB)
    (further_a, further_b), inverse_0 = lax.optimization_barrier(
        ((further_a, further_b), inverse_0)
    )

    def plane_block(zz, c, dtype):
        in_b = zz >= split
        zz_a, zz_b = jnp.minimum(zz, split - 1), jnp.maximum(zz - split, 0)
        at_a = [(zz_a * chips_y + chip) * 2 + c] * len(sums_a) + [zz_a * 2 + c] * len(further_a)
        at_b = [(zz_b * devices_z + at_z) * 2 + c] * len(sums_b) + [zz_b * 2 + c] * len(further_b)
        return pick_block(
            in_b, sums_a + further_a, sums_b + further_b, at_a, at_b, part, dtype
        )

    x_got, x_sent = [], []
    for step in range(devices_x):
        to = (at_x + step) % devices_x
        x_sent.append(plane_block(to // 2, to % 2, bf16))
        pairs = []
        for x in range(devices_x):
            for y in range(devices_y):
                to = (x + step) % devices_x
                dest_x = (y % 2) * spans + to // 2
                dest_y = (y // 2) * 2 + to % 2
                if dest_x != x:
                    pairs.append((x * devices_y + y, dest_x * devices_y + dest_y))
        x_got.append(lax.ppermute(x_sent[-1], ("gx", "gy", "core"), pairs))
    home = at_x // spans == core
    own = plane_block(at_x % spans, core, f32)
    swapped = lax.ppermute(plane_block(at_x % spans, 1 - core, f32), "core", swap_pairs())
    lead_rows, _ = lax.optimization_barrier((lead_rows, (x_sent, own)))
    factor_10, inverse_1 = next_panel(lead_rows, inverse_0)
    (x_got, swapped), inverse_1 = lax.optimization_barrier(((x_got, swapped), inverse_1))
    by_blocks = [jax.ShapeDtypeStruct((part, cols // devices_y), f32)] * devices_y
    order = jnp.stack([(at_y + d) % devices_y for d in range(devices_y)])
    home = jnp.concatenate([home.astype(jnp.int32)[None], order])
    rows, *reduced = pl.pallas_call(
        sums_kernel,
        out_shape=[jax.ShapeDtypeStruct((part, cols), f32), *by_blocks],
        in_specs=[whole(pltpu.SMEM)] + [whole()] * (devices_x + 2),
        out_specs=[whole()] * (1 + devices_y),
        compiler_params=pltpu.CompilerParams(vmem_limit_bytes=32 * 2**20),
    )(home, own, swapped, *x_got)

    block = jax.ShapeDtypeStruct((devices_y * part, cols // devices_y), f32)
    places = jnp.stack([(at_y - d) % devices_y for d in range(devices_y)])

    def to_columns(blocks):
        got = [blocks[0]]
        for d in range(1, devices_y):
            pairs = [(i, (i + d) % devices_y) for i in range(devices_y)]
            got.append(lax.ppermute(blocks[d], ("gy", "core"), pairs))
        return pl.pallas_call(
            join_kernel,
            out_shape=block,
            in_specs=[whole(pltpu.SMEM)] + [whole()] * devices_y,
            out_specs=whole(),
            compiler_params=pltpu.CompilerParams(vmem_limit_bytes=24 * 2**20),
        )(places, *got)

    reduced = to_columns(reduced)
    first_row = ((at_x * devices_z + at_z) * devices_y + at_y) * part
    factor = pl.pallas_call(
        factor_kernel,
        out_shape=by_blocks,
        in_specs=[whole(pltpu.SMEM)] + [whole()] * 4,
        out_specs=[whole()] * devices_y,
        scratch_shapes=[pltpu.VMEM((part, cols), f32)],
        compiler_params=pltpu.CompilerParams(vmem_limit_bytes=32 * 2**20),
    )(jnp.concatenate([first_row[None], order]), rows, inverse_0, factor_10, inverse_1)
    return (reduced, to_columns(factor))


def solution(mesh):
    sizes = mesh.shape
    fine = jax.sharding.Mesh(
        mesh.devices.reshape(sizes["gx"], sizes["gy"] // 2, 2, sizes["gz"]),
        ("gx", "gy", "core", "gz"),
    )
    grid = ("gx", ("gy", "core"), "gz")
    out = P(("gx", "gz"), ("gy", "core"))
    return jax.shard_map(
        local,
        mesh=fine,
        in_specs=(P(*grid, None), P(*grid), P(), P(), P(), P()),
        out_specs=(out, out),
        check_vma=False,
    )
```

```python
import functools

import jax
import jax.numpy as jnp
from jax import lax
from jax.experimental import pallas as pl
from jax.experimental.pallas import tpu as pltpu
from jax.sharding import PartitionSpec as P

NB = 512
PANELS = 2
LEAF = 128
SUB = 8


def dot3(a, b, dims):
    a_hi = a.astype(jnp.bfloat16)
    b_hi = b.astype(jnp.bfloat16)
    a_lo = (a - a_hi.astype(jnp.float32)).astype(jnp.bfloat16)
    b_lo = (b - b_hi.astype(jnp.float32)).astype(jnp.bfloat16)

    def dot(x, y):
        return lax.dot_general(x, y, (dims, ((), ())), preferred_element_type=jnp.float32)

    return dot(a_hi, b_hi) + (dot(a_hi, b_lo) + dot(a_lo, b_hi))


def inverse_of(d):
    guess = pl.reciprocal(d, approx=True)
    return guess * (2.0 - d * guess)


def leaf_inverse(block_ref):
    lanes = lax.broadcasted_iota(jnp.int32, (SUB, LEAF), 1)
    subs = lax.broadcasted_iota(jnp.int32, (SUB, LEAF), 0)
    shape = (SUB, LEAF)
    for t in range(LEAF // SUB):
        j0 = t * SUB
        rows = block_ref[j0 : j0 + SUB, :]
        cols = [jnp.broadcast_to(rows[:, j0 + k : j0 + k + 1], shape) for k in range(SUB)]
        p = [[jnp.broadcast_to(cols[k][i : i + 1, :], shape) for k in range(i + 1)] for i in range(SUB)]
        in_block = jnp.logical_and(lanes >= j0, lanes < j0 + SUB)
        start = jnp.where(in_block, (lanes - j0 == subs).astype(jnp.float32), rows)
        u = [jnp.broadcast_to(start[k : k + 1, :], shape) for k in range(SUB)]
        inv = [None] * SUB
        factor = [[None] * SUB for _ in range(SUB)]
        for k in range(SUB):
            inv[k] = inverse_of(p[k][k])
            for i in range(k + 1, SUB):
                factor[i][k] = p[i][k] * inv[k]
                for j in range(k + 1, i + 1):
                    p[i][j] = p[i][j] - factor[i][k] * p[j][k] if j < i else p[i][j] - factor[i][k] * p[i][k]
                u[i] = u[i] - factor[i][k] * u[k]
        out = u[0] * lax.rsqrt(p[0][0])
        for k in range(1, SUB):
            out = jnp.where(subs == k, u[k] * lax.rsqrt(p[k][k]), out)
        block_ref[j0 : j0 + SUB, :] = out
        if t + 1 == LEAF // SUB:
            break
        z = [None] * SUB
        for k in reversed(range(SUB)):
            z[k] = u[k] * inv[k]
            for i in range(k + 1, SUB):
                z[k] = z[k] - factor[i][k] * z[i]
        for v in range(t + 1, LEAF // SUB):
            below = block_ref[v * SUB : (v + 1) * SUB, :]
            upd = jnp.where(in_block, 0.0, below)
            for k in range(SUB):
                upd = upd - jnp.broadcast_to(below[:, j0 + k : j0 + k + 1], shape) * z[k]
            block_ref[v * SUB : (v + 1) * SUB, :] = upd


def factor_inverse(s_ref, d_ref):
    width = s_ref.shape[0]
    row_ids = lax.broadcasted_iota(jnp.int32, (width, width), 0)
    col_ids = lax.broadcasted_iota(jnp.int32, (width, width), 1)
    wide_cols = lax.broadcasted_iota(jnp.int32, (LEAF, width), 1)
    leaf_rows = lax.broadcasted_iota(jnp.int32, (LEAF, LEAF), 0)
    leaf_cols = lax.broadcasted_iota(jnp.int32, (LEAF, LEAF), 1)

    def step(b, carry):
        off = pl.multiple_of(b * LEAF, LEAF)
        span = pl.ds(off, LEAF)
        d_ref[...] = s_ref[span, span]
        leaf_inverse(d_ref)
        inverse = jnp.where(leaf_rows >= leaf_cols, d_ref[...], 0.0)
        s_ref[span, span] = (leaf_rows == leaf_cols).astype(jnp.float32)
        upper = dot3(inverse, s_ref[span, :], ((1,), (0,)))
        s_ref[span, :] = upper
        tail = jnp.where(wide_cols >= off + LEAF, upper, 0.0)
        current = s_ref[...]
        dead = jnp.logical_and(
            row_ids >= off + LEAF, jnp.logical_and(col_ids >= off, col_ids < off + LEAF)
        )
        s_ref[...] = jnp.where(dead, 0.0, current) - dot3(tail, upper, ((0,), (0,)))
        return carry

    lax.fori_loop(0, width // LEAF, step, 0)
    s_ref[...] = jnp.where(row_ids >= col_ids, s_ref[...], 0.0)


def unpack_symmetric(packed_ref, s_ref):
    at = 0
    for i in range(s_ref.shape[0] // LEAF):
        for j in range(i + 1):
            block = packed_ref[at * LEAF : (at + 1) * LEAF, :]
            s_ref[i * LEAF : (i + 1) * LEAF, j * LEAF : (j + 1) * LEAF] = block
            if j < i:
                s_ref[j * LEAF : (j + 1) * LEAF, i * LEAF : (i + 1) * LEAF] = block.T
            at += 1


def first_panel_kernel(packed_ref, w_ref, d_ref):
    unpack_symmetric(packed_ref, w_ref)
    factor_inverse(w_ref, d_ref)


def next_panel_kernel(packed_ref, w0_ref, f_ref, w_ref, d_ref):
    nb = w0_ref.shape[0]
    blocks = nb // LEAF
    unpack_symmetric(packed_ref, w_ref)
    start = packed_ref.shape[0] - blocks * nb
    below = jnp.concatenate(
        [packed_ref[start + i * nb : start + (i + 1) * nb, :] for i in range(nb // LEAF)], 1
    )
    below = dot3(below, w0_ref[...], ((1,), (1,)))
    f_ref[...] = below
    w_ref[...] = w_ref[...] - dot3(below, below, ((1,), (1,)))
    factor_inverse(w_ref, d_ref)


def factor_kernel(first_ref, rows_ref, w0_ref, f_ref, w1_ref, *refs):
    blocks, all_ref = refs[:-1], refs[-1]
    nb = w0_ref.shape[0]
    ids = first_ref[0] + lax.broadcasted_iota(jnp.int32, (rows_ref.shape[0], nb), 0)
    cols = lax.broadcasted_iota(jnp.int32, (rows_ref.shape[0], nb), 1)
    part = dot3(rows_ref[:, :nb], w0_ref[...], ((1,), (1,)))
    rest = rows_ref[:, nb:] - dot3(part, f_ref[...], ((1,), (1,)))
    rest = dot3(rest, w1_ref[...], ((1,), (1,)))
    all_ref[:, :nb] = jnp.where(cols <= ids, part, 0.0)
    all_ref[:, nb:] = jnp.where(cols + nb <= ids, rest, 0.0)
    for d, block in enumerate(blocks):
        width = block.shape[1]
        block[...] = all_ref[:, pl.ds(pl.multiple_of(first_ref[1 + d] * width, width), width)]


def panel_call(kernel, outputs, nb, *operands):
    return pl.pallas_call(
        kernel,
        out_shape=[jax.ShapeDtypeStruct((nb, nb), jnp.float32)] * outputs,
        in_specs=[pl.BlockSpec(memory_space=pltpu.VMEM)] * len(operands),
        out_specs=[pl.BlockSpec(memory_space=pltpu.VMEM)] * outputs,
        scratch_shapes=[pltpu.VMEM((LEAF, LEAF), jnp.float32)],
        compiler_params=pltpu.CompilerParams(vmem_limit_bytes=24 * 2**20),
        cost_estimate=pl.CostEstimate(
            flops=24 * nb**3 * 4, transcendentals=0, bytes_accessed=8 * nb * nb
        ),
    )(*operands)


def first_panel(packed, nb):
    return panel_call(first_panel_kernel, 1, nb, packed)[0]


def next_panel(packed, w0):
    return panel_call(next_panel_kernel, 2, w0.shape[0], packed, w0)


def whole(memory=pltpu.VMEM):
    return pl.BlockSpec(memory_space=memory)


def faces_kernel(cond_ref, ground_ref, info_ref, cells_ref, load_ref, panel_ref, *refs, sides):
    outs, (conduct_ref, grounds_ref, scaled_ref) = refs[:6], refs[6:]
    size_x, size_y, size_z = sides
    count, width = panel_ref.shape
    tile = 64
    classes = cond_ref.shape[0]
    ports = cells_ref.shape[1]

    def by_tile(t, carry):
        rows = pl.ds(pl.multiple_of(t * tile, tile), tile)
        kind = jnp.broadcast_to(info_ref[rows, 0:1], (tile, LEAF))
        ids = jnp.broadcast_to(info_ref[rows, 1:2], (tile, LEAF))
        conduct = jnp.zeros((tile, LEAF), jnp.float32)
        grounds = jnp.zeros((tile, LEAF), jnp.float32)
        for c in range(classes):
            conduct = jnp.where(kind == c, cond_ref[c], conduct)
            grounds = jnp.where(kind == c, ground_ref[c], grounds)
        loads = jnp.zeros((tile, LEAF), jnp.float32)
        for p in range(0, ports, LEAF):
            hit = ids == cells_ref[:, p : p + LEAF]
            loads = loads + jnp.where(hit, load_ref[:, p : p + LEAF], 0.0)
        conduct_ref[rows, :] = conduct
        grounds_ref[rows, :] = grounds + jnp.sum(loads, axis=1, keepdims=True)
        for p in range(0, width, LEAF):
            part = panel_ref[rows, p : p + LEAF].astype(jnp.float32)
            scaled_ref[p // LEAF, rows, :] = (
                (conduct * part).astype(jnp.bfloat16).astype(jnp.float32)
            )
        return carry

    lax.fori_loop(0, count // tile, by_tile, 0)
    plane = size_y * size_z
    for p in range(width // LEAF):
        lanes = slice(p * LEAF, (p + 1) * LEAF)
        outs[0][:, lanes] = scaled_ref[p, 0:plane, :].astype(jnp.bfloat16)
        outs[1][:, lanes] = scaled_ref[p, count - plane : count, :].astype(jnp.bfloat16)
        for out, at in ((outs[2], 0), (outs[3], plane - size_z)):
            face = [
                scaled_ref[p, x * plane + at : x * plane + at + size_z, :] for x in range(size_x)
            ]
            out[:, lanes] = jnp.concatenate(face, 0).astype(jnp.bfloat16)
        for out, at in ((outs[4], 0), (outs[5], size_z - 1)):
            face = scaled_ref[p, pl.ds(at, size_x * size_y, stride=size_z), :]
            out[:, lanes] = face.astype(jnp.bfloat16)


def image_kernel(panel_ref, conduct_ref, grounds_ref, *refs, sides, nb):
    halos, (image_ref, first_ref, later_ref, scaled_ref, square_ref) = refs[:6], refs[6:]
    size_x, size_y, size_z = sides
    width = panel_ref.shape[1]
    plane = size_y * size_z
    subs = lax.broadcasted_iota(jnp.int32, (size_z, LEAF), 0)

    def by_lane(p, carry):
        lanes = pl.ds(pl.multiple_of(p * LEAF, LEAF), LEAF)
        x_low, x_high, y_low, y_high, z_low, z_high = (
            h[:, lanes].astype(jnp.float32) for h in halos
        )
        scaled_ref[...] = (
            (conduct_ref[...] * panel_ref[:, lanes].astype(jnp.float32))
            .astype(jnp.bfloat16)
            .astype(jnp.float32)
        )

        def cell_rows(x, y):
            at = x * plane + y * size_z
            return scaled_ref[at : at + size_z, :]

        for x in range(size_x):
            done = []
            for y in range(size_y):
                at = x * plane + y * size_z
                here = cell_rows(x, y)
                span = slice(y * size_z, (y + 1) * size_z)
                total = cell_rows(x + 1, y) if x + 1 < size_x else x_high[span, :]
                total = total + (cell_rows(x - 1, y) if x > 0 else x_low[span, :])
                span = slice(x * size_z, (x + 1) * size_z)
                total = total + (cell_rows(x, y + 1) if y + 1 < size_y else y_high[span, :])
                total = total + (cell_rows(x, y - 1) if y > 0 else y_low[span, :])
                k = x * size_y + y
                up = jnp.where(
                    subs == size_z - 1, z_high[k : k + 1, :], pltpu.roll(here, size_z - 1, 0)
                )
                down = jnp.where(subs == 0, z_low[k : k + 1, :], pltpu.roll(here, 1, 0))
                total = total + up + down
                own = slice(at, at + size_z)
                done.append(
                    conduct_ref[own, :] * (6.0 * here - total)
                    + grounds_ref[own, :] * panel_ref[at : at + size_z, lanes].astype(jnp.float32)
                )
            image_ref[x * plane : (x + 1) * plane, lanes] = jnp.concatenate(done, 0).astype(
                jnp.bfloat16
            )
        return carry

    lax.fori_loop(0, width // LEAF, by_lane, 0)

    def product(rows, cols):
        return lax.dot_general(
            panel_ref[:, rows],
            image_ref[:, cols],
            (((0,), (0,)), ((), ())),
            preferred_element_type=jnp.float32,
        )

    blocks = nb // LEAF

    def lower(out_ref):
        at = 0
        for i in range(blocks):
            for j in range(i + 1):
                row, col = slice(i * LEAF, (i + 1) * LEAF), slice(j * LEAF, (j + 1) * LEAF)
                out_ref[at : at + LEAF, :] = 0.5 * (square_ref[row, col] + square_ref[col, row].T)
                at += LEAF
        return at

    head, tail = slice(0, nb), slice(nb, 2 * nb)
    square_ref[...] = product(head, head)
    lower(first_ref)
    square_ref[...] = product(tail, tail)
    at = lower(later_ref)
    below = product(tail, head)
    for i in range(blocks):
        later_ref[at + i * nb : at + (i + 1) * nb, :] = below[:, i * LEAF : (i + 1) * LEAF]


def copy_kernel(table_ref, in_ref, out_ref):
    del table_ref
    out_ref[...] = in_ref[...]


def take_columns(table, at, array, width):
    rows = array.shape[0]
    tile = min(64, rows)
    return pl.pallas_call(
        copy_kernel,
        grid_spec=pltpu.PrefetchScalarGridSpec(
            num_scalar_prefetch=1,
            grid=(rows // tile,),
            in_specs=[pl.BlockSpec((tile, width), lambda t, tab: (t, tab[at]))],
            out_specs=pl.BlockSpec((tile, width), lambda t, tab: (t, 0)),
        ),
        out_shape=jax.ShapeDtypeStruct((rows, width), array.dtype),
        compiler_params=pltpu.CompilerParams(vmem_limit_bytes=32 * 2**20),
        cost_estimate=pl.CostEstimate(
            flops=0, transcendentals=0, bytes_accessed=4 * rows * width
        ),
    )(table, array)


def products_kernel(table_ref, *refs):
    del table_ref
    out, count = refs[-1], len(refs) // 2
    total = None
    for b, image in zip(refs[:count], refs[count:-1]):
        term = lax.dot_general(
            b[...], image[...], (((0,), (0,)), ((), ())), preferred_element_type=jnp.float32
        )
        total = term if total is None else total + term
    out[...] = total.astype(out.dtype)


def products(table, bases, images, lists, width, dtype):
    rows, cols = images[0].shape
    step = 512 if width % 512 == 0 else width
    parts = width // step
    steps = lists[0][1] * parts
    in_specs = [
        pl.BlockSpec(
            (rows, step), lambda t, tab, at=at: (0, tab[at + t // parts] * parts + t % parts)
        )
        for at, _ in lists
    ]
    in_specs += [pl.BlockSpec((rows, cols), lambda t, tab: (0, 0))] * len(images)
    total = steps * step
    return pl.pallas_call(
        products_kernel,
        grid_spec=pltpu.PrefetchScalarGridSpec(
            num_scalar_prefetch=1,
            grid=(steps,),
            in_specs=in_specs,
            out_specs=pl.BlockSpec((step, cols), lambda t, tab: (t, 0)),
        ),
        out_shape=jax.ShapeDtypeStruct((total, cols), dtype),
        compiler_params=pltpu.CompilerParams(vmem_limit_bytes=48 * 2**20),
        cost_estimate=pl.CostEstimate(
            flops=2 * total * cols * rows * len(bases),
            transcendentals=0,
            bytes_accessed=2 * rows * (total + cols) * len(bases) + 4 * total * cols,
        ),
    )(table, *bases, *images)


def add_kernel(table_ref, *refs):
    del table_ref
    total = refs[0][...].astype(jnp.float32)
    for got in refs[1:-1]:
        total = total + got[...].astype(jnp.float32)
    refs[-1][...] = total.astype(refs[-1].dtype)


def add_blocks(table, arrays, at, count, height, dtype):
    cols = arrays[0].shape[1]
    step = min(256, height)
    parts = height // step
    steps = count * parts
    spec = pl.BlockSpec((step, cols), lambda t, tab: (tab[at + t // parts] * parts + t % parts, 0))
    return pl.pallas_call(
        add_kernel,
        grid_spec=pltpu.PrefetchScalarGridSpec(
            num_scalar_prefetch=1,
            grid=(steps,),
            in_specs=[spec] * len(arrays),
            out_specs=pl.BlockSpec((step, cols), lambda t, tab: (t, 0)),
        ),
        out_shape=jax.ShapeDtypeStruct((steps * step, cols), dtype),
        compiler_params=pltpu.CompilerParams(vmem_limit_bytes=24 * 2**20),
        cost_estimate=pl.CostEstimate(
            flops=steps * step * cols,
            transcendentals=0,
            bytes_accessed=steps * step * cols * 4 * len(arrays),
        ),
    )(table, *arrays)


def plane_kernel(table_ref, *refs, groups, at):
    ins, outs, plane_ref = refs[: sum(groups)], refs[sum(groups) : -1], refs[-1]
    height = ins[0].shape[0]
    done = 0
    for i, count in enumerate(groups):
        total = ins[done][...].astype(jnp.float32)
        for got in ins[done + 1 : done + count]:
            total = total + got[...].astype(jnp.float32)
        plane_ref[i * height : (i + 1) * height, :] = total
        done += count
    for i, out in enumerate(outs):
        part = out.shape[0]
        rows = pl.ds(pl.multiple_of(table_ref[at + i] * part, part), part)
        out[...] = plane_ref[rows, :].astype(out.dtype)


def plane_parts(table, sums, height, at, outs):
    cols = sums[0][0][0].shape[1]

    def spec(place, block):
        if place is None:
            return pl.BlockSpec((height, cols), lambda t, tab: (block, 0))
        return pl.BlockSpec((height, cols), lambda t, tab: (tab[place], 0))

    return pl.pallas_call(
        functools.partial(plane_kernel, groups=[len(terms) for terms in sums], at=at),
        grid_spec=pltpu.PrefetchScalarGridSpec(
            num_scalar_prefetch=1,
            grid=(1,),
            in_specs=[spec(place, block) for terms in sums for _, place, block in terms],
            out_specs=[pl.BlockSpec(out.shape, lambda t, tab: (0, 0)) for out in outs],
            scratch_shapes=[pltpu.VMEM((height * len(sums), cols), jnp.float32)],
        ),
        out_shape=outs,
        compiler_params=pltpu.CompilerParams(vmem_limit_bytes=44 * 2**20),
        cost_estimate=pl.CostEstimate(
            flops=0, transcendentals=0, bytes_accessed=height * len(sums) * cols * 14
        ),
    )(table, *(array for terms in sums for array, _, _ in terms))


def swap_pairs():
    return [(0, 1), (1, 0)]


def other_half(half, core):
    other = lax.ppermute(half, "core", swap_pairs())
    first = core == 0
    return jnp.concatenate([jnp.where(first, half, other), jnp.where(first, other, half)], 0)


def join_kernel(place_ref, *refs):
    out = refs[-1]
    part = refs[0].shape[0]
    for d, block in enumerate(refs[:-1]):
        out[pl.ds(pl.multiple_of(place_ref[d] * part, part), part), :] = block[...]


def sums_kernel(home_ref, own_ref, swapped_ref, *refs):
    cols, width = own_ref.shape[1], refs[-1].shape[1]
    ins, rows_ref, blocks = refs[: -1 - cols // width], refs[-1 - cols // width], refs[-(cols // width) :]
    total = jnp.where(home_ref[0] != 0, own_ref[...], swapped_ref[...])
    for got in ins:
        total = total + got[...].astype(jnp.float32)
    rows_ref[...] = total
    for d, block in enumerate(blocks):
        at = pl.multiple_of(home_ref[1 + d] * width, width)
        block[...] = rows_ref[:, pl.ds(at, width)]


def local(basis, classes, cond_table, ground_table, port_cells, port_load):
    sides = classes.shape
    cells_x, cells_y, cells_z = sides
    width_k = basis.shape[3]
    devices_x = lax.axis_size("gx")
    chips_y = lax.axis_size("gy")
    devices_z = lax.axis_size("gz")
    devices_y = 2 * chips_y
    spans = devices_x // 2
    split = spans // 2
    count = cells_x * cells_y * cells_z
    cols = PANELS * NB
    at_x, chip, core, at_z = (lax.axis_index(axis) for axis in ("gx", "gy", "core", "gz"))
    at_y = 2 * chip + core
    f32, bf16 = jnp.float32, jnp.bfloat16

    flat_basis = basis.reshape(count, width_k)
    wide = width_k // (devices_x * devices_z)
    narrow = wide // chips_y
    part = narrow // 2

    entries = []

    def put(values):
        entries.extend(values)
        return len(entries) - len(values), len(values)

    shift = core * spans * devices_z * chips_y

    def put_products(blocks):
        return [put([b + shift for b in blocks]), put(blocks)]

    lists_a, lists_b, next_a, next_b = [], [], [], []
    for d in range(devices_z):
        x = (at_z + d) % devices_z
        lists_a.append(
            put_products(
                [(zz * devices_z + x) * chips_y + y for zz in range(split) for y in range(chips_y)]
            )
        )
        next_b.append(put([zz * devices_z + x for zz in range(spans - split)]))
    for d in range(chips_y):
        y = (chip + d) % chips_y
        lists_b.append(
            put_products(
                [(zz * devices_z + x) * chips_y + y for zz in range(split, spans) for x in range(devices_z)]
            )
        )
        next_a.append(put([zz * chips_y + y for zz in range(split)]))
    leaving = [(at_x + step) % devices_x for step in range(devices_x)]
    leaving_at, _ = put(leaving + [at_x % spans * 2 + core, at_x % spans * 2 + 1 - core])
    given_at, _ = put([1 - core])
    table = jnp.stack([jnp.asarray(e, jnp.int32) for e in entries])

    def move(array, axis, d):
        size = lax.axis_size(axis)
        return lax.ppermute(array, axis, [(i, (i + d) % size) for i in range(size)])

    panel_spec = pl.BlockSpec((count, cols), lambda i: (0, 0))
    global_x = at_x * cells_x + jnp.arange(cells_x, dtype=jnp.int32)
    global_y = at_y * cells_y + jnp.arange(cells_y, dtype=jnp.int32)
    global_z = at_z * cells_z + jnp.arange(cells_z, dtype=jnp.int32)
    flat_ids = (
        (global_x[:, None, None] * (cells_y * devices_y) + global_y[None, :, None])
        * (cells_z * devices_z)
        + global_z[None, None, :]
    )
    info = jnp.stack([classes, flat_ids], -1).reshape(count, 2)
    face_rows = [cells_y * cells_z] * 2 + [cells_x * cells_z] * 2 + [cells_x * cells_y] * 2
    *faces, conduct, grounds = pl.pallas_call(
        functools.partial(faces_kernel, sides=sides),
        out_shape=[jax.ShapeDtypeStruct((n, cols), bf16) for n in face_rows]
        + [jax.ShapeDtypeStruct((count, LEAF), f32)] * 2,
        grid=(1,),
        in_specs=[whole(pltpu.SMEM)] * 2 + [whole()] * 3 + [panel_spec],
        out_specs=[whole()] * 8,
        scratch_shapes=[pltpu.VMEM((cols // LEAF, count, LEAF), f32)],
        compiler_params=pltpu.CompilerParams(vmem_limit_bytes=24 * 2**20),
    )(cond_table, ground_table, info, port_cells[None, :], port_load[None, :], flat_basis)
    later_table, _ = lax.optimization_barrier((table, faces))
    given = take_columns(later_table, given_at, flat_basis, width_k // 2)
    halos = []
    for i, (axis, size) in enumerate(
        (("gx", devices_x), (("gy", "core"), devices_y), ("gz", devices_z))
    ):
        low, high = faces[2 * i : 2 * i + 2]
        if size == 2:
            last = lax.axis_index(axis) == 1
            got = lax.ppermute(jnp.where(last, low, high), axis, swap_pairs())
            halos.append(jnp.where(last, got, 0))
            halos.append(jnp.where(last, 0, got))
        else:
            halos.append(lax.ppermute(high, axis, [(k, k + 1) for k in range(size - 1)]))
            halos.append(lax.ppermute(low, axis, [(k + 1, k) for k in range(size - 1)]))
    other_basis = lax.ppermute(given, "core", swap_pairs())

    blocks = NB // LEAF
    lower_rows = blocks * (blocks + 1) // 2 * LEAF
    halos, _ = lax.optimization_barrier((halos, given))
    image, first_rows, later_rows = pl.pallas_call(
        functools.partial(image_kernel, sides=sides, nb=NB),
        out_shape=[
            jax.ShapeDtypeStruct((count, cols), bf16),
            jax.ShapeDtypeStruct((lower_rows, LEAF), f32),
            jax.ShapeDtypeStruct((lower_rows + blocks * NB, LEAF), f32),
        ],
        grid=(1,),
        in_specs=[panel_spec] + [whole()] * 8,
        out_specs=[whole()] * 3,
        scratch_shapes=[pltpu.VMEM((count, LEAF), f32), pltpu.VMEM((NB, NB), f32)],
        compiler_params=pltpu.CompilerParams(vmem_limit_bytes=32 * 2**20),
    )(flat_basis, conduct, grounds, *halos)

    other_image = lax.ppermute(image, "core", swap_pairs())

    axes = ("gx", "gy", "gz")
    chips = devices_x * chips_y * devices_z

    def halved(rows):
        both = rows.reshape(2, -1, LEAF)
        kept = lax.dynamic_index_in_dim(both, core, 0, keepdims=False)
        sent = lax.dynamic_index_in_dim(both, 1 - core, 0, keepdims=False)
        return kept + lax.ppermute(sent, "core", swap_pairs())

    def exchanged(rows):
        rows = rows.reshape(chips, -1, LEAF)
        return lax.all_to_all(rows, axes, split_axis=0, concat_axis=0, tiled=True)

    def spread(terms):
        own = jnp.sum(terms, axis=0)
        return own, exchanged(jnp.broadcast_to(own, terms.shape)).reshape(-1, LEAF)

    first_half, later_half = halved(first_rows), halved(later_rows)
    first_terms = exchanged(first_half)

    def chip_products(images, lists, dtype):
        return products(table, [flat_basis, other_basis], images, lists, narrow, dtype)

    images, _ = lax.optimization_barrier(([image, other_image], first_half))
    sent_a = [chip_products(images, lists_a[d], bf16) for d in range(1, devices_z)]
    sent_b = [chip_products(images, lists_b[d], bf16) for d in range(1, chips_y)]
    got_a = [move(a, "gz", d) for d, a in enumerate(sent_a, 1)]
    got_b = [move(a, "gy", d) for d, a in enumerate(sent_b, 1)]
    first_terms, _ = lax.optimization_barrier((first_terms, (sent_a, sent_b)))
    own, first_half = spread(first_terms)
    images, _ = lax.optimization_barrier((images, own))
    own_a, own_b = (chip_products(images, lists[0], f32) for lists in (lists_a, lists_b))
    first_half, later_half, _ = lax.optimization_barrier((first_half, later_half, (own_a, own_b)))
    first_rows = other_half(first_half, core)
    later_half, _ = lax.optimization_barrier((later_half, first_half))
    later_terms = exchanged(later_half)
    sums_a, sums_b = [own_a, *got_a], [own_b, *got_b]

    further_a = [add_blocks(table, sums_a, *next_a[d], narrow, bf16) for d in range(1, chips_y)]
    further_b = [add_blocks(table, sums_b, *next_b[d], narrow, bf16) for d in range(1, devices_z)]
    later_terms, _ = lax.optimization_barrier((later_terms, (further_a, further_b)))
    further_a = [move(a, "gy", d) for d, a in enumerate(further_a, 1)]
    further_b = [move(a, "gz", d) for d, a in enumerate(further_b, 1)]
    own, later_half = spread(later_terms)
    first_rows, _ = lax.optimization_barrier((first_rows, own))
    inverse_0 = first_panel(first_rows, NB)
    (further_a, further_b, later_half), inverse_0 = lax.optimization_barrier(
        ((further_a, further_b, later_half), inverse_0)
    )
    later_rows = other_half(later_half, core)

    terms = []
    for zz in range(split):
        at = next_a[0][0] + zz
        terms.append([(a, at, None) for a in sums_a] + [(a, None, zz) for a in further_a])
    for zz in range(spans - split):
        at = next_b[0][0] + zz
        terms.append([(a, at, None) for a in sums_b] + [(a, None, zz) for a in further_b])
    outs = [jax.ShapeDtypeStruct((part, cols), bf16)] * devices_x
    outs += [jax.ShapeDtypeStruct((part, cols), f32)] * 2
    *x_sent, own, swapped = plane_parts(table, terms, narrow, leaving_at, outs)
    x_got = []
    for step in range(devices_x):
        pairs = []
        for x in range(devices_x):
            for y in range(devices_y):
                to = (x + step) % devices_x
                dest_x = (y % 2) * spans + to // 2
                dest_y = (y // 2) * 2 + to % 2
                if dest_x != x:
                    pairs.append((x * devices_y + y, dest_x * devices_y + dest_y))
        x_got.append(lax.ppermute(x_sent[step], ("gx", "gy", "core"), pairs))
    swapped = lax.ppermute(swapped, "core", swap_pairs())
    home = at_x // spans == core
    later_rows, _ = lax.optimization_barrier((later_rows, x_sent))
    factor_10, inverse_1 = next_panel(later_rows, inverse_0)
    (x_got, swapped), inverse_1 = lax.optimization_barrier(((x_got, swapped), inverse_1))
    by_blocks = [jax.ShapeDtypeStruct((part, cols // devices_y), f32)] * devices_y
    order = jnp.stack([(at_y + d) % devices_y for d in range(devices_y)])
    home = jnp.concatenate([home.astype(jnp.int32)[None], order])
    rows, *reduced = pl.pallas_call(
        sums_kernel,
        out_shape=[jax.ShapeDtypeStruct((part, cols), f32), *by_blocks],
        in_specs=[whole(pltpu.SMEM)] + [whole()] * (devices_x + 2),
        out_specs=[whole()] * (1 + devices_y),
        compiler_params=pltpu.CompilerParams(vmem_limit_bytes=32 * 2**20),
    )(home, own, swapped, *x_got)

    block = jax.ShapeDtypeStruct((devices_y * part, cols // devices_y), f32)
    places = jnp.stack([(at_y - d) % devices_y for d in range(devices_y)])

    def to_columns(blocks):
        got = [blocks[0]]
        for d in range(1, devices_y):
            pairs = [(i, (i + d) % devices_y) for i in range(devices_y)]
            got.append(lax.ppermute(blocks[d], ("gy", "core"), pairs))
        return pl.pallas_call(
            join_kernel,
            out_shape=block,
            in_specs=[whole(pltpu.SMEM)] + [whole()] * devices_y,
            out_specs=whole(),
            compiler_params=pltpu.CompilerParams(vmem_limit_bytes=24 * 2**20),
        )(places, *got)

    reduced = to_columns(reduced)
    first_row = ((at_x * devices_z + at_z) * devices_y + at_y) * part
    factor = pl.pallas_call(
        factor_kernel,
        out_shape=by_blocks,
        in_specs=[whole(pltpu.SMEM)] + [whole()] * 4,
        out_specs=[whole()] * devices_y,
        scratch_shapes=[pltpu.VMEM((part, cols), f32)],
        compiler_params=pltpu.CompilerParams(vmem_limit_bytes=32 * 2**20),
    )(jnp.concatenate([first_row[None], order]), rows, inverse_0, factor_10, inverse_1)
    return (reduced, to_columns(factor))


def solution(mesh):
    sizes = mesh.shape
    fine = jax.sharding.Mesh(
        mesh.devices.reshape(sizes["gx"], sizes["gy"] // 2, 2, sizes["gz"]),
        ("gx", "gy", "core", "gz"),
    )
    grid = ("gx", ("gy", "core"), "gz")
    out = P(("gx", "gz"), ("gy", "core"))
    return jax.shard_map(
        local,
        mesh=fine,
        in_specs=(P(*grid, None), P(*grid), P(), P(), P(), P()),
        out_specs=(out, out),
        check_vma=False,
    )
```

```python
import functools

import jax
import jax.numpy as jnp
from jax import lax
from jax.experimental import pallas as pl
from jax.experimental.pallas import tpu as pltpu
from jax.sharding import PartitionSpec as P

NB = 512
PANELS = 2
LEAF = 128
SUB = 8


def dot3(a, b, dims):
    a_hi = a.astype(jnp.bfloat16)
    b_hi = b.astype(jnp.bfloat16)
    a_lo = (a - a_hi.astype(jnp.float32)).astype(jnp.bfloat16)
    b_lo = (b - b_hi.astype(jnp.float32)).astype(jnp.bfloat16)

    def dot(x, y):
        return lax.dot_general(x, y, (dims, ((), ())), preferred_element_type=jnp.float32)

    return dot(a_hi, b_hi) + (dot(a_hi, b_lo) + dot(a_lo, b_hi))


def inverse_of(d):
    guess = pl.reciprocal(d, approx=True)
    return guess * (2.0 - d * guess)


def leaf_inverse(block_ref):
    lanes = lax.broadcasted_iota(jnp.int32, (SUB, LEAF), 1)
    subs = lax.broadcasted_iota(jnp.int32, (SUB, LEAF), 0)
    shape = (SUB, LEAF)
    for t in range(LEAF // SUB):
        j0 = t * SUB
        rows = block_ref[j0 : j0 + SUB, :]
        cols = [jnp.broadcast_to(rows[:, j0 + k : j0 + k + 1], shape) for k in range(SUB)]
        p = [[jnp.broadcast_to(cols[k][i : i + 1, :], shape) for k in range(i + 1)] for i in range(SUB)]
        in_block = jnp.logical_and(lanes >= j0, lanes < j0 + SUB)
        start = jnp.where(in_block, (lanes - j0 == subs).astype(jnp.float32), rows)
        u = [jnp.broadcast_to(start[k : k + 1, :], shape) for k in range(SUB)]
        inv = [None] * SUB
        factor = [[None] * SUB for _ in range(SUB)]
        for k in range(SUB):
            inv[k] = inverse_of(p[k][k])
            for i in range(k + 1, SUB):
                factor[i][k] = p[i][k] * inv[k]
                for j in range(k + 1, i + 1):
                    p[i][j] = p[i][j] - factor[i][k] * p[j][k] if j < i else p[i][j] - factor[i][k] * p[i][k]
                u[i] = u[i] - factor[i][k] * u[k]
        out = u[0] * lax.rsqrt(p[0][0])
        for k in range(1, SUB):
            out = jnp.where(subs == k, u[k] * lax.rsqrt(p[k][k]), out)
        block_ref[j0 : j0 + SUB, :] = out
        if t + 1 == LEAF // SUB:
            break
        z = [None] * SUB
        for k in reversed(range(SUB)):
            z[k] = u[k] * inv[k]
            for i in range(k + 1, SUB):
                z[k] = z[k] - factor[i][k] * z[i]
        for v in range(t + 1, LEAF // SUB):
            below = block_ref[v * SUB : (v + 1) * SUB, :]
            upd = jnp.where(in_block, 0.0, below)
            for k in range(SUB):
                upd = upd - jnp.broadcast_to(below[:, j0 + k : j0 + k + 1], shape) * z[k]
            block_ref[v * SUB : (v + 1) * SUB, :] = upd


def factor_inverse(s_ref, d_ref):
    width = s_ref.shape[0]
    row_ids = lax.broadcasted_iota(jnp.int32, (width, width), 0)
    col_ids = lax.broadcasted_iota(jnp.int32, (width, width), 1)
    wide_cols = lax.broadcasted_iota(jnp.int32, (LEAF, width), 1)
    leaf_rows = lax.broadcasted_iota(jnp.int32, (LEAF, LEAF), 0)
    leaf_cols = lax.broadcasted_iota(jnp.int32, (LEAF, LEAF), 1)

    def step(b, carry):
        off = pl.multiple_of(b * LEAF, LEAF)
        span = pl.ds(off, LEAF)
        d_ref[...] = s_ref[span, span]
        leaf_inverse(d_ref)
        inverse = jnp.where(leaf_rows >= leaf_cols, d_ref[...], 0.0)
        s_ref[span, span] = (leaf_rows == leaf_cols).astype(jnp.float32)
        upper = dot3(inverse, s_ref[span, :], ((1,), (0,)))
        s_ref[span, :] = upper
        tail = jnp.where(wide_cols >= off + LEAF, upper, 0.0)
        current = s_ref[...]
        dead = jnp.logical_and(
            row_ids >= off + LEAF, jnp.logical_and(col_ids >= off, col_ids < off + LEAF)
        )
        s_ref[...] = jnp.where(dead, 0.0, current) - dot3(tail, upper, ((0,), (0,)))
        return carry

    lax.fori_loop(0, width // LEAF, step, 0)
    s_ref[...] = jnp.where(row_ids >= col_ids, s_ref[...], 0.0)


def unpack_symmetric(packed_ref, s_ref):
    at = 0
    for i in range(s_ref.shape[0] // LEAF):
        for j in range(i + 1):
            block = packed_ref[at * LEAF : (at + 1) * LEAF, :]
            s_ref[i * LEAF : (i + 1) * LEAF, j * LEAF : (j + 1) * LEAF] = block
            if j < i:
                s_ref[j * LEAF : (j + 1) * LEAF, i * LEAF : (i + 1) * LEAF] = block.T
            at += 1


def first_panel_kernel(packed_ref, w_ref, d_ref):
    unpack_symmetric(packed_ref, w_ref)
    factor_inverse(w_ref, d_ref)


def next_panel_kernel(packed_ref, w0_ref, f_ref, w_ref, d_ref):
    nb = w0_ref.shape[0]
    blocks = nb // LEAF
    unpack_symmetric(packed_ref, w_ref)
    start = packed_ref.shape[0] - blocks * nb
    below = jnp.concatenate(
        [packed_ref[start + i * nb : start + (i + 1) * nb, :] for i in range(nb // LEAF)], 1
    )
    below = dot3(below, w0_ref[...], ((1,), (1,)))
    f_ref[...] = below
    w_ref[...] = w_ref[...] - dot3(below, below, ((1,), (1,)))
    factor_inverse(w_ref, d_ref)


def factor_kernel(table_ref, own_ref, swapped_ref, *refs, at):
    home_at, order_at, first_at = at
    cols = own_ref.shape[1]
    *ins, rows_ref, all_ref = refs
    count = cols // ins[-1].shape[2]
    ins, blocks = ins[:-count], ins[-count:]
    *ins, w0_ref, f_ref, w1_ref = ins
    total = jnp.where(table_ref[home_at] != 0, own_ref[...], swapped_ref[...])
    for got in ins:
        total = total + got[...].astype(jnp.float32)
    rows_ref[...] = total
    nb = w0_ref.shape[0]
    ids = table_ref[first_at] + lax.broadcasted_iota(jnp.int32, (rows_ref.shape[0], nb), 0)
    columns = lax.broadcasted_iota(jnp.int32, (rows_ref.shape[0], nb), 1)
    part = dot3(rows_ref[:, :nb], w0_ref[...], ((1,), (1,)))
    rest = rows_ref[:, nb:] - dot3(part, f_ref[...], ((1,), (1,)))
    rest = dot3(rest, w1_ref[...], ((1,), (1,)))
    all_ref[:, :nb] = jnp.where(columns <= ids, part, 0.0)
    all_ref[:, nb:] = jnp.where(columns + nb <= ids, rest, 0.0)
    for d, block in enumerate(blocks):
        width = block.shape[2]
        span = pl.ds(pl.multiple_of(table_ref[order_at + d] * width, width), width)
        block[0] = rows_ref[:, span]
        block[1] = all_ref[:, span]


def panel_call(kernel, outputs, nb, *operands):
    return pl.pallas_call(
        kernel,
        out_shape=[jax.ShapeDtypeStruct((nb, nb), jnp.float32)] * outputs,
        in_specs=[pl.BlockSpec(memory_space=pltpu.VMEM)] * len(operands),
        out_specs=[pl.BlockSpec(memory_space=pltpu.VMEM)] * outputs,
        scratch_shapes=[pltpu.VMEM((LEAF, LEAF), jnp.float32)],
        compiler_params=pltpu.CompilerParams(vmem_limit_bytes=24 * 2**20),
        cost_estimate=pl.CostEstimate(
            flops=nb, transcendentals=0, bytes_accessed=nb
        ),
    )(*operands)


def first_panel(packed, nb):
    return panel_call(first_panel_kernel, 1, nb, packed)[0]


def next_panel(packed, w0):
    return panel_call(next_panel_kernel, 2, w0.shape[0], packed, w0)


def whole(memory=pltpu.VMEM):
    return pl.BlockSpec(memory_space=memory)


def block_of(array, memory=pltpu.VMEM):
    return pl.BlockSpec(array.shape, lambda *_: (0,) * array.ndim, memory_space=memory)


def faces_kernel(cond_ref, ground_ref, info_ref, cells_ref, load_ref, panel_ref, *refs, sides):
    outs, (conduct_ref, grounds_ref, scaled_ref) = refs[:6], refs[6:]
    size_x, size_y, size_z = sides
    count, width = panel_ref.shape
    tile = 64
    classes = cond_ref.shape[0]
    ports = cells_ref.shape[1]

    def by_tile(t, carry):
        rows = pl.ds(pl.multiple_of(t * tile, tile), tile)
        kind = jnp.broadcast_to(info_ref[rows, 0:1], (tile, LEAF))
        ids = jnp.broadcast_to(info_ref[rows, 1:2], (tile, LEAF))
        conduct = jnp.zeros((tile, LEAF), jnp.float32)
        grounds = jnp.zeros((tile, LEAF), jnp.float32)
        for c in range(classes):
            conduct = jnp.where(kind == c, cond_ref[c], conduct)
            grounds = jnp.where(kind == c, ground_ref[c], grounds)
        loads = jnp.zeros((tile, LEAF), jnp.float32)
        for p in range(0, ports, LEAF):
            hit = ids == cells_ref[:, p : p + LEAF]
            loads = loads + jnp.where(hit, load_ref[:, p : p + LEAF], 0.0)
        conduct_ref[rows, :] = conduct
        grounds_ref[rows, :] = grounds + jnp.sum(loads, axis=1, keepdims=True)
        for p in range(0, width, LEAF):
            part = panel_ref[rows, p : p + LEAF].astype(jnp.float32)
            scaled_ref[p // LEAF, rows, :] = (
                (conduct * part).astype(jnp.bfloat16).astype(jnp.float32)
            )
        return carry

    lax.fori_loop(0, count // tile, by_tile, 0)
    plane = size_y * size_z
    for p in range(width // LEAF):
        lanes = slice(p * LEAF, (p + 1) * LEAF)
        outs[0][:, lanes] = scaled_ref[p, 0:plane, :].astype(jnp.bfloat16)
        outs[1][:, lanes] = scaled_ref[p, count - plane : count, :].astype(jnp.bfloat16)
        for out, at in ((outs[2], 0), (outs[3], plane - size_z)):
            face = [
                scaled_ref[p, x * plane + at : x * plane + at + size_z, :] for x in range(size_x)
            ]
            out[:, lanes] = jnp.concatenate(face, 0).astype(jnp.bfloat16)
        for out, at in ((outs[4], 0), (outs[5], size_z - 1)):
            face = scaled_ref[p, pl.ds(at, size_x * size_y, stride=size_z), :]
            out[:, lanes] = face.astype(jnp.bfloat16)


def image_kernel(table_ref, panel_ref, conduct_ref, grounds_ref, *refs, sides, nb, at):
    halos, (image_ref, *lead_refs, scaled_ref, square_ref) = refs[:6], refs[6:]
    core = table_ref[at]
    size_x, size_y, size_z = sides
    width = panel_ref.shape[1]
    plane = size_y * size_z
    subs = lax.broadcasted_iota(jnp.int32, (size_z, LEAF), 0)

    def by_lane(p, carry):
        lanes = pl.ds(pl.multiple_of(p * LEAF, LEAF), LEAF)
        x_low, x_high, y_low, y_high, z_low, z_high = (
            h[:, lanes].astype(jnp.float32) for h in halos
        )
        scaled_ref[...] = (
            (conduct_ref[...] * panel_ref[:, lanes].astype(jnp.float32))
            .astype(jnp.bfloat16)
            .astype(jnp.float32)
        )

        def cell_rows(x, y):
            at = x * plane + y * size_z
            return scaled_ref[at : at + size_z, :]

        for x in range(size_x):
            done = []
            for y in range(size_y):
                at = x * plane + y * size_z
                here = cell_rows(x, y)
                span = slice(y * size_z, (y + 1) * size_z)
                total = cell_rows(x + 1, y) if x + 1 < size_x else x_high[span, :]
                total = total + (cell_rows(x - 1, y) if x > 0 else x_low[span, :])
                span = slice(x * size_z, (x + 1) * size_z)
                total = total + (cell_rows(x, y + 1) if y + 1 < size_y else y_high[span, :])
                total = total + (cell_rows(x, y - 1) if y > 0 else y_low[span, :])
                k = x * size_y + y
                up = jnp.where(
                    subs == size_z - 1, z_high[k : k + 1, :], pltpu.roll(here, size_z - 1, 0)
                )
                down = jnp.where(subs == 0, z_low[k : k + 1, :], pltpu.roll(here, 1, 0))
                total = total + up + down
                own = slice(at, at + size_z)
                done.append(
                    conduct_ref[own, :] * (6.0 * here - total)
                    + grounds_ref[own, :] * panel_ref[at : at + size_z, lanes].astype(jnp.float32)
                )
            image_ref[x * plane : (x + 1) * plane, lanes] = jnp.concatenate(done, 0).astype(
                jnp.bfloat16
            )
        return carry

    lax.fori_loop(0, width // LEAF, by_lane, 0)

    def product(rows, cols):
        return lax.dot_general(
            panel_ref[:, rows],
            image_ref[:, cols],
            (((0,), (0,)), ((), ())),
            preferred_element_type=jnp.float32,
        )

    blocks = nb // LEAF

    def put_block(refs, number, value):
        half = refs[0].shape[0] // LEAF
        rows = slice(number % half * LEAF, (number % half + 1) * LEAF)
        kept = core == number // half

        @pl.when(kept)
        def _():
            refs[0][rows, :] = value

        @pl.when(jnp.logical_not(kept))
        def _():
            refs[1][rows, :] = value

    def lower(refs):
        number = 0
        for i in range(blocks):
            for j in range(i + 1):
                row, col = slice(i * LEAF, (i + 1) * LEAF), slice(j * LEAF, (j + 1) * LEAF)
                put_block(refs, number, 0.5 * (square_ref[row, col] + square_ref[col, row].T))
                number += 1
        return number

    head, tail = slice(0, nb), slice(nb, 2 * nb)
    square_ref[...] = product(head, head)
    lower(lead_refs[:2])
    square_ref[...] = product(tail, tail)
    number = lower(lead_refs[2:])
    square_ref[...] = product(tail, head)
    for j in range(blocks):
        for i in range(blocks):
            row, col = slice(i * LEAF, (i + 1) * LEAF), slice(j * LEAF, (j + 1) * LEAF)
            put_block(lead_refs[2:], number + j * blocks + i, square_ref[row, col])


def copy_kernel(table_ref, in_ref, out_ref):
    del table_ref
    out_ref[...] = in_ref[...]


def take_columns(table, at, array, width):
    rows = array.shape[0]
    tile = min(128, rows)
    return pl.pallas_call(
        copy_kernel,
        grid_spec=pltpu.PrefetchScalarGridSpec(
            num_scalar_prefetch=1,
            grid=(rows // tile,),
            in_specs=[pl.BlockSpec((tile, width), lambda t, tab: (t, tab[at]))],
            out_specs=pl.BlockSpec((tile, width), lambda t, tab: (t, 0)),
        ),
        out_shape=jax.ShapeDtypeStruct((rows, width), array.dtype),
        compiler_params=pltpu.CompilerParams(vmem_limit_bytes=58 * 2**20),
        cost_estimate=pl.CostEstimate(
            flops=0, transcendentals=0, bytes_accessed=4 * rows * width
        ),
    )(table, array)


def products_kernel(table_ref, *refs):
    del table_ref
    out, count = refs[-1], len(refs) // 2
    total = None
    for b, image in zip(refs[:count], refs[count:-1]):
        term = lax.dot_general(
            b[...], image[...], (((0,), (0,)), ((), ())), preferred_element_type=jnp.float32
        )
        total = term if total is None else total + term
    out[...] = total.astype(out.dtype)


def products(table, bases, images, lists, width, dtype):
    rows, cols = images[0].shape
    step = 512 if width % 512 == 0 else width
    parts = width // step
    steps = lists[0][1] * parts
    in_specs = [
        pl.BlockSpec(
            (rows, step), lambda t, tab, at=at: (0, tab[at + t // parts] * parts + t % parts)
        )
        for at, _ in lists
    ]
    in_specs += [pl.BlockSpec((rows, cols), lambda t, tab: (0, 0))] * len(images)
    total = steps * step
    return pl.pallas_call(
        products_kernel,
        grid_spec=pltpu.PrefetchScalarGridSpec(
            num_scalar_prefetch=1,
            grid=(steps,),
            in_specs=in_specs,
            out_specs=pl.BlockSpec((step, cols), lambda t, tab: (t, 0)),
        ),
        out_shape=jax.ShapeDtypeStruct((total, cols), dtype),
        compiler_params=pltpu.CompilerParams(vmem_limit_bytes=48 * 2**20),
        cost_estimate=pl.CostEstimate(
            flops=2 * total * cols * rows * len(bases),
            transcendentals=0,
            bytes_accessed=2 * rows * (total + cols) * len(bases) + 4 * total * cols,
        ),
    )(table, *bases, *images)


def add_kernel(table_ref, *refs):
    del table_ref
    total = refs[0][...].astype(jnp.float32)
    for got in refs[1:-1]:
        total = total + got[...].astype(jnp.float32)
    refs[-1][...] = total.astype(refs[-1].dtype)


def add_blocks(table, arrays, at, count, height, dtype):
    cols = arrays[0].shape[1]
    step = min(256, height)
    parts = height // step
    steps = count * parts
    spec = pl.BlockSpec((step, cols), lambda t, tab: (tab[at + t // parts] * parts + t % parts, 0))
    return pl.pallas_call(
        add_kernel,
        grid_spec=pltpu.PrefetchScalarGridSpec(
            num_scalar_prefetch=1,
            grid=(steps,),
            in_specs=[spec] * len(arrays),
            out_specs=pl.BlockSpec((step, cols), lambda t, tab: (t, 0)),
        ),
        out_shape=jax.ShapeDtypeStruct((steps * step, cols), dtype),
        compiler_params=pltpu.CompilerParams(vmem_limit_bytes=24 * 2**20),
        cost_estimate=pl.CostEstimate(
            flops=steps * step * cols,
            transcendentals=0,
            bytes_accessed=steps * step * cols * 4 * len(arrays),
        ),
    )(table, *arrays)


def plane_kernel(table_ref, *refs, groups, at):
    ins, outs, plane_ref = refs[: sum(groups)], refs[sum(groups) : -1], refs[-1]
    height = ins[0].shape[0]
    done = 0
    for i, count in enumerate(groups):
        total = ins[done][...].astype(jnp.float32)
        for got in ins[done + 1 : done + count]:
            total = total + got[...].astype(jnp.float32)
        plane_ref[i * height : (i + 1) * height, :] = total
        done += count
    for i, out in enumerate(outs):
        part = out.shape[0]
        rows = pl.ds(pl.multiple_of(table_ref[at + i] * part, part), part)
        out[...] = plane_ref[rows, :].astype(out.dtype)


def plane_parts(table, sums, height, at, outs):
    cols = sums[0][0][0].shape[1]

    def spec(place, block):
        if place is None:
            return pl.BlockSpec((height, cols), lambda t, tab: (block, 0))
        return pl.BlockSpec((height, cols), lambda t, tab: (tab[place], 0))

    return pl.pallas_call(
        functools.partial(plane_kernel, groups=[len(terms) for terms in sums], at=at),
        grid_spec=pltpu.PrefetchScalarGridSpec(
            num_scalar_prefetch=1,
            grid=(1,),
            in_specs=[spec(place, block) for terms in sums for _, place, block in terms],
            out_specs=[pl.BlockSpec(out.shape, lambda t, tab: (0, 0)) for out in outs],
            scratch_shapes=[pltpu.VMEM((height * len(sums), cols), jnp.float32)],
        ),
        out_shape=outs,
        compiler_params=pltpu.CompilerParams(vmem_limit_bytes=44 * 2**20),
        cost_estimate=pl.CostEstimate(
            flops=0, transcendentals=0, bytes_accessed=height * len(sums) * cols * 14
        ),
    )(table, *(array for terms in sums for array, _, _ in terms))


def swap_pairs():
    return [(0, 1), (1, 0)]


def other_half(half, core):
    other = lax.ppermute(half, "core", swap_pairs())
    first = core == 0
    return jnp.concatenate([jnp.where(first, half, other), jnp.where(first, other, half)], 0)


def join_kernel(table_ref, *refs, at):
    ins, outs = refs[:-2], refs[-2:]
    part = ins[0].shape[1]
    for d, block in enumerate(ins):
        rows = pl.ds(pl.multiple_of(table_ref[at + d] * part, part), part)
        for i, out in enumerate(outs):
            out[rows, :] = block[i]


def local(basis, classes, cond_table, ground_table, port_cells, port_load):
    sides = classes.shape
    cells_x, cells_y, cells_z = sides
    width_k = basis.shape[3]
    devices_x = lax.axis_size("gx")
    chips_y = lax.axis_size("gy")
    devices_z = lax.axis_size("gz")
    devices_y = 2 * chips_y
    spans = devices_x // 2
    split = spans // 2
    count = cells_x * cells_y * cells_z
    cols = PANELS * NB
    at_x, chip, core, at_z = (lax.axis_index(axis) for axis in ("gx", "gy", "core", "gz"))
    at_y = 2 * chip + core
    f32, bf16 = jnp.float32, jnp.bfloat16

    flat_basis = basis.reshape(count, width_k)
    wide = width_k // (devices_x * devices_z)
    narrow = wide // chips_y
    part = narrow // 2

    entries = []

    def put(values):
        entries.extend(values)
        return len(entries) - len(values), len(values)

    shift = core * spans * devices_z * chips_y

    def put_products(blocks):
        return [put([b + shift for b in blocks]), put(blocks)]

    lists_a, lists_b, next_a, next_b = [], [], [], []
    for d in range(devices_z):
        x = (at_z + d) % devices_z
        lists_a.append(
            put_products(
                [(zz * devices_z + x) * chips_y + y for zz in range(split) for y in range(chips_y)]
            )
        )
        next_b.append(put([zz * devices_z + x for zz in range(spans - split)]))
    for d in range(chips_y):
        y = (chip + d) % chips_y
        lists_b.append(
            put_products(
                [(zz * devices_z + x) * chips_y + y for zz in range(split, spans) for x in range(devices_z)]
            )
        )
        next_a.append(put([zz * chips_y + y for zz in range(split)]))
    leaving = [(at_x + step) % devices_x for step in range(devices_x)]
    leaving_at, _ = put(leaving + [at_x % spans * 2 + core, at_x % spans * 2 + 1 - core])
    given_at, _ = put([1 - core])
    core_at, _ = put([core])
    places_at, _ = put([(at_y - d) % devices_y for d in range(devices_y)])
    order_at, _ = put([(at_y + d) % devices_y for d in range(devices_y)])
    home_at, _ = put([at_x // spans == core])
    first_at, _ = put([((at_x * devices_z + at_z) * devices_y + at_y) * part])
    table = jnp.stack([jnp.asarray(e, jnp.int32) for e in entries])

    def move(array, axis, d):
        size = lax.axis_size(axis)
        return lax.ppermute(array, axis, [(i, (i + d) % size) for i in range(size)])

    panel_spec = pl.BlockSpec((count, cols), lambda *_: (0, 0))
    port_rows, load_rows = port_cells[None, :], port_load[None, :]
    global_x = at_x * cells_x + jnp.arange(cells_x, dtype=jnp.int32)
    global_y = at_y * cells_y + jnp.arange(cells_y, dtype=jnp.int32)
    global_z = at_z * cells_z + jnp.arange(cells_z, dtype=jnp.int32)
    flat_ids = (
        (global_x[:, None, None] * (cells_y * devices_y) + global_y[None, :, None])
        * (cells_z * devices_z)
        + global_z[None, None, :]
    )
    info = jnp.stack([classes, flat_ids], -1).reshape(count, 2)
    face_rows = [cells_y * cells_z] * 2 + [cells_x * cells_z] * 2 + [cells_x * cells_y] * 2
    outs = [jax.ShapeDtypeStruct((n, cols), bf16) for n in face_rows]
    outs += [jax.ShapeDtypeStruct((count, LEAF), f32)] * 2
    *faces, conduct, grounds = pl.pallas_call(
        functools.partial(faces_kernel, sides=sides),
        out_shape=outs,
        grid=(1,),
        in_specs=[block_of(cond_table, pltpu.SMEM), block_of(ground_table, pltpu.SMEM)]
        + [block_of(info), block_of(port_rows), block_of(load_rows), panel_spec],
        out_specs=[block_of(a) for a in outs],
        scratch_shapes=[pltpu.VMEM((cols // LEAF, count, LEAF), f32)],
        compiler_params=pltpu.CompilerParams(vmem_limit_bytes=58 * 2**20),
    )(cond_table, ground_table, info, port_rows, load_rows, flat_basis)
    later_table, _ = lax.optimization_barrier((table, faces))
    given = take_columns(later_table, given_at, flat_basis, width_k // 2)
    halos = []
    for i, (axis, size) in enumerate(
        (("gx", devices_x), (("gy", "core"), devices_y), ("gz", devices_z))
    ):
        low, high = faces[2 * i : 2 * i + 2]
        if size == 2:
            last = lax.axis_index(axis) == 1
            got = lax.ppermute(jnp.where(last, low, high), axis, swap_pairs())
            halos.append(jnp.where(last, got, 0))
            halos.append(jnp.where(last, 0, got))
        else:
            halos.append(lax.ppermute(high, axis, [(k, k + 1) for k in range(size - 1)]))
            halos.append(lax.ppermute(low, axis, [(k + 1, k) for k in range(size - 1)]))
    other_basis = lax.ppermute(given, "core", swap_pairs())

    blocks = NB // LEAF
    lower_rows = blocks * (blocks + 1) // 2 * LEAF
    halos, _ = lax.optimization_barrier((halos, given))
    first_part = jax.ShapeDtypeStruct((lower_rows // 2, LEAF), f32)
    later_part = jax.ShapeDtypeStruct(((lower_rows + blocks * NB) // 2, LEAF), f32)
    lead_parts = [first_part] * 2 + [later_part] * 2
    outs = [jax.ShapeDtypeStruct((count, cols), bf16), *lead_parts]
    image, first_kept, first_sent, later_kept, later_sent = pl.pallas_call(
        functools.partial(image_kernel, sides=sides, nb=NB, at=core_at),
        out_shape=outs,
        grid_spec=pltpu.PrefetchScalarGridSpec(
            num_scalar_prefetch=1,
            grid=(1,),
            in_specs=[panel_spec] + [block_of(a) for a in (conduct, grounds, *halos)],
            out_specs=[block_of(a) for a in outs],
            scratch_shapes=[pltpu.VMEM((count, LEAF), f32), pltpu.VMEM((NB, NB), f32)],
        ),
        compiler_params=pltpu.CompilerParams(vmem_limit_bytes=58 * 2**20),
    )(table, flat_basis, conduct, grounds, *halos)

    other_image = lax.ppermute(image, "core", swap_pairs())

    axes = ("gx", "gy", "gz")
    chips = devices_x * chips_y * devices_z

    def halved(kept, sent):
        return kept + lax.ppermute(sent, "core", swap_pairs())

    def exchanged(rows):
        rows = rows.reshape(chips, -1, LEAF)
        return lax.all_to_all(rows, axes, split_axis=0, concat_axis=0, tiled=True)

    def for_all(own):
        return jnp.broadcast_to(own, (chips, *own.shape))

    first_half, later_half = halved(first_kept, first_sent), halved(later_kept, later_sent)
    first_terms = exchanged(first_half)

    def chip_products(images, lists, dtype):
        return products(table, [flat_basis, other_basis], images, lists, narrow, dtype)

    images, _ = lax.optimization_barrier(([image, other_image], first_half))
    sent_a = [chip_products(images, lists_a[d], bf16) for d in range(1, devices_z)]
    sent_b = [chip_products(images, lists_b[d], bf16) for d in range(1, chips_y)]
    got_a = [move(a, "gz", d) for d, a in enumerate(sent_a, 1)]
    got_b = [move(a, "gy", d) for d, a in enumerate(sent_b, 1)]
    first_terms, _ = lax.optimization_barrier((first_terms, (sent_a, sent_b)))
    own = jnp.sum(first_terms, axis=0)
    share = own.shape[0]
    images, _ = lax.optimization_barrier((images, own))
    own_a, own_b = (chip_products(images, lists[0], f32) for lists in (lists_a, lists_b))
    both = jnp.concatenate([for_all(own), later_half.reshape(chips, -1, LEAF)], 1)
    both = lax.all_to_all(both, axes, split_axis=0, concat_axis=0, tiled=True)
    both, _ = lax.optimization_barrier((both, (own_a, own_b)))
    sums_a, sums_b = [own_a, *got_a], [own_b, *got_b]

    further_a = [add_blocks(table, sums_a, *next_a[d], narrow, bf16) for d in range(1, chips_y)]
    further_b = [add_blocks(table, sums_b, *next_b[d], narrow, bf16) for d in range(1, devices_z)]
    both, _ = lax.optimization_barrier((both, (further_a, further_b)))
    further_a = [move(a, "gy", d) for d, a in enumerate(further_a, 1)]
    further_b = [move(a, "gz", d) for d, a in enumerate(further_b, 1)]
    first_rows = other_half(both[:, :share].reshape(-1, LEAF), core)
    later_half = exchanged(for_all(jnp.sum(both[:, share:], axis=0))).reshape(-1, LEAF)
    inverse_0 = first_panel(first_rows, NB)
    (further_a, further_b, later_half), inverse_0 = lax.optimization_barrier(
        ((further_a, further_b, later_half), inverse_0)
    )
    later_rows = other_half(later_half, core)

    terms = []
    for zz in range(split):
        at = next_a[0][0] + zz
        terms.append([(a, at, None) for a in sums_a] + [(a, None, zz) for a in further_a])
    for zz in range(spans - split):
        at = next_b[0][0] + zz
        terms.append([(a, at, None) for a in sums_b] + [(a, None, zz) for a in further_b])
    outs = [jax.ShapeDtypeStruct((part, cols), bf16)] * devices_x
    outs += [jax.ShapeDtypeStruct((part, cols), f32)] * 2
    *x_sent, own, swapped = plane_parts(table, terms, narrow, leaving_at, outs)
    x_got = []
    for step in range(devices_x):
        pairs = []
        for x in range(devices_x):
            for y in range(devices_y):
                to = (x + step) % devices_x
                dest_x = (y % 2) * spans + to // 2
                dest_y = (y // 2) * 2 + to % 2
                if dest_x != x:
                    pairs.append((x * devices_y + y, dest_x * devices_y + dest_y))
        x_got.append(lax.ppermute(x_sent[step], ("gx", "gy", "core"), pairs))
    swapped = lax.ppermute(swapped, "core", swap_pairs())
    later_rows, _ = lax.optimization_barrier((later_rows, x_sent))
    factor_10, inverse_1 = next_panel(later_rows, inverse_0)
    (x_got, swapped), inverse_1 = lax.optimization_barrier(((x_got, swapped), inverse_1))
    pair = jax.ShapeDtypeStruct((2, part, cols // devices_y), f32)
    ins = [own, swapped, *x_got, inverse_0, factor_10, inverse_1]
    pairs = list(pl.pallas_call(
        functools.partial(factor_kernel, at=(home_at, order_at, first_at)),
        out_shape=[pair] * devices_y,
        grid_spec=pltpu.PrefetchScalarGridSpec(
            num_scalar_prefetch=1,
            grid=(1,),
            in_specs=[block_of(a) for a in ins],
            out_specs=[block_of(pair)] * devices_y,
            scratch_shapes=[pltpu.VMEM((part, cols), f32)] * 2,
        ),
        compiler_params=pltpu.CompilerParams(vmem_limit_bytes=44 * 2**20),
    )(table, *ins))
    for d in range(1, devices_y):
        route = [(i, (i + d) % devices_y) for i in range(devices_y)]
        pairs[d] = lax.ppermute(pairs[d], ("gy", "core"), route)
    out = jax.ShapeDtypeStruct((devices_y * part, cols // devices_y), f32)
    return pl.pallas_call(
        functools.partial(join_kernel, at=places_at),
        out_shape=(out, out),
        grid_spec=pltpu.PrefetchScalarGridSpec(
            num_scalar_prefetch=1,
            grid=(1,),
            in_specs=[block_of(a) for a in pairs],
            out_specs=[block_of(out)] * 2,
        ),
        compiler_params=pltpu.CompilerParams(vmem_limit_bytes=44 * 2**20),
    )(table, *pairs)


def solution(mesh):
    sizes = mesh.shape
    fine = jax.sharding.Mesh(
        mesh.devices.reshape(sizes["gx"], sizes["gy"] // 2, 2, sizes["gz"]),
        ("gx", "gy", "core", "gz"),
    )
    grid = ("gx", ("gy", "core"), "gz")
    out = P(("gx", "gz"), ("gy", "core"))
    return jax.shard_map(
        local,
        mesh=fine,
        in_specs=(P(*grid, None), P(*grid), P(), P(), P(), P()),
        out_specs=(out, out),
        check_vma=False,
    )
```

```python
import functools

import jax
import jax.numpy as jnp
from jax import lax
from jax.experimental import pallas as pl
from jax.experimental.pallas import tpu as pltpu
from jax.sharding import PartitionSpec as P

NB = 512
PANELS = 2
LEAF = 128
LIGHT = pl.CostEstimate(flops=1, transcendentals=0, bytes_accessed=1)
SUB = 8


def dot3(a, b, dims):
    a_hi = a.astype(jnp.bfloat16)
    b_hi = b.astype(jnp.bfloat16)
    a_lo = (a - a_hi.astype(jnp.float32)).astype(jnp.bfloat16)
    b_lo = (b - b_hi.astype(jnp.float32)).astype(jnp.bfloat16)

    def dot(x, y):
        return lax.dot_general(x, y, (dims, ((), ())), preferred_element_type=jnp.float32)

    return dot(a_hi, b_hi) + (dot(a_hi, b_lo) + dot(a_lo, b_hi))


def inverse_of(d):
    guess = pl.reciprocal(d, approx=True)
    return guess * (2.0 - d * guess)


def leaf_inverse(block_ref):
    lanes = lax.broadcasted_iota(jnp.int32, (SUB, LEAF), 1)
    subs = lax.broadcasted_iota(jnp.int32, (SUB, LEAF), 0)
    shape = (SUB, LEAF)
    for t in range(LEAF // SUB):
        j0 = t * SUB
        rows = block_ref[j0 : j0 + SUB, :]
        cols = [jnp.broadcast_to(rows[:, j0 + k : j0 + k + 1], shape) for k in range(SUB)]
        p = [[jnp.broadcast_to(cols[k][i : i + 1, :], shape) for k in range(i + 1)] for i in range(SUB)]
        in_block = jnp.logical_and(lanes >= j0, lanes < j0 + SUB)
        start = jnp.where(in_block, (lanes - j0 == subs).astype(jnp.float32), rows)
        u = [jnp.broadcast_to(start[k : k + 1, :], shape) for k in range(SUB)]
        inv = [None] * SUB
        factor = [[None] * SUB for _ in range(SUB)]
        for k in range(SUB):
            inv[k] = inverse_of(p[k][k])
            for i in range(k + 1, SUB):
                factor[i][k] = p[i][k] * inv[k]
                for j in range(k + 1, i + 1):
                    p[i][j] = p[i][j] - factor[i][k] * p[j][k] if j < i else p[i][j] - factor[i][k] * p[i][k]
                u[i] = u[i] - factor[i][k] * u[k]
        out = u[0] * lax.rsqrt(p[0][0])
        for k in range(1, SUB):
            out = jnp.where(subs == k, u[k] * lax.rsqrt(p[k][k]), out)
        block_ref[j0 : j0 + SUB, :] = out
        if t + 1 == LEAF // SUB:
            break
        z = [None] * SUB
        for k in reversed(range(SUB)):
            z[k] = u[k] * inv[k]
            for i in range(k + 1, SUB):
                z[k] = z[k] - factor[i][k] * z[i]
        for v in range(t + 1, LEAF // SUB):
            below = block_ref[v * SUB : (v + 1) * SUB, :]
            upd = jnp.where(in_block, 0.0, below)
            for k in range(SUB):
                upd = upd - jnp.broadcast_to(below[:, j0 + k : j0 + k + 1], shape) * z[k]
            block_ref[v * SUB : (v + 1) * SUB, :] = upd


def factor_inverse(s_ref, d_ref):
    width = s_ref.shape[0]
    row_ids = lax.broadcasted_iota(jnp.int32, (width, width), 0)
    col_ids = lax.broadcasted_iota(jnp.int32, (width, width), 1)
    wide_cols = lax.broadcasted_iota(jnp.int32, (LEAF, width), 1)
    leaf_rows = lax.broadcasted_iota(jnp.int32, (LEAF, LEAF), 0)
    leaf_cols = lax.broadcasted_iota(jnp.int32, (LEAF, LEAF), 1)

    def step(b, carry):
        off = pl.multiple_of(b * LEAF, LEAF)
        span = pl.ds(off, LEAF)
        d_ref[...] = s_ref[span, span]
        leaf_inverse(d_ref)
        inverse = jnp.where(leaf_rows >= leaf_cols, d_ref[...], 0.0)
        s_ref[span, span] = (leaf_rows == leaf_cols).astype(jnp.float32)
        upper = dot3(inverse, s_ref[span, :], ((1,), (0,)))
        s_ref[span, :] = upper
        tail = jnp.where(wide_cols >= off + LEAF, upper, 0.0)
        current = s_ref[...]
        dead = jnp.logical_and(
            row_ids >= off + LEAF, jnp.logical_and(col_ids >= off, col_ids < off + LEAF)
        )
        s_ref[...] = jnp.where(dead, 0.0, current) - dot3(tail, upper, ((0,), (0,)))
        return carry

    lax.fori_loop(0, width // LEAF, step, 0)
    s_ref[...] = jnp.where(row_ids >= col_ids, s_ref[...], 0.0)


def unpack_symmetric(packed_ref, s_ref):
    at = 0
    for i in range(s_ref.shape[0] // LEAF):
        for j in range(i + 1):
            block = packed_ref[at * LEAF : (at + 1) * LEAF, :]
            s_ref[i * LEAF : (i + 1) * LEAF, j * LEAF : (j + 1) * LEAF] = block
            if j < i:
                s_ref[j * LEAF : (j + 1) * LEAF, i * LEAF : (i + 1) * LEAF] = block.T
            at += 1


def first_panel_kernel(packed_ref, w_ref, d_ref):
    unpack_symmetric(packed_ref, w_ref)
    factor_inverse(w_ref, d_ref)


def next_panel_kernel(packed_ref, w0_ref, f_ref, w_ref, d_ref):
    nb = w0_ref.shape[0]
    blocks = nb // LEAF
    unpack_symmetric(packed_ref, w_ref)
    start = packed_ref.shape[0] - blocks * nb
    below = jnp.concatenate(
        [packed_ref[start + i * nb : start + (i + 1) * nb, :] for i in range(nb // LEAF)], 1
    )
    below = dot3(below, w0_ref[...], ((1,), (1,)))
    f_ref[...] = below
    w_ref[...] = w_ref[...] - dot3(below, below, ((1,), (1,)))
    factor_inverse(w_ref, d_ref)


def factor_kernel(table_ref, own_ref, swapped_ref, *refs, at):
    home_at, order_at, first_at = at
    cols = own_ref.shape[1]
    *ins, rows_ref, all_ref = refs
    count = cols // ins[-1].shape[2]
    ins, blocks = ins[:-count], ins[-count:]
    *ins, w0_ref, f_ref, w1_ref = ins
    total = jnp.where(table_ref[home_at] != 0, own_ref[...], swapped_ref[...])
    for got in ins:
        total = total + got[...].astype(jnp.float32)
    rows_ref[...] = total
    nb = w0_ref.shape[0]
    ids = table_ref[first_at] + lax.broadcasted_iota(jnp.int32, (rows_ref.shape[0], nb), 0)
    columns = lax.broadcasted_iota(jnp.int32, (rows_ref.shape[0], nb), 1)
    part = dot3(rows_ref[:, :nb], w0_ref[...], ((1,), (1,)))
    rest = rows_ref[:, nb:] - dot3(part, f_ref[...], ((1,), (1,)))
    rest = dot3(rest, w1_ref[...], ((1,), (1,)))
    all_ref[:, :nb] = jnp.where(columns <= ids, part, 0.0)
    all_ref[:, nb:] = jnp.where(columns + nb <= ids, rest, 0.0)
    for d, block in enumerate(blocks):
        width = block.shape[2]
        span = pl.ds(pl.multiple_of(table_ref[order_at + d] * width, width), width)
        block[0] = rows_ref[:, span]
        block[1] = all_ref[:, span]


def panel_call(kernel, outputs, nb, *operands):
    return pl.pallas_call(
        kernel,
        out_shape=[jax.ShapeDtypeStruct((nb, nb), jnp.float32)] * outputs,
        in_specs=[pl.BlockSpec(memory_space=pltpu.VMEM)] * len(operands),
        out_specs=[pl.BlockSpec(memory_space=pltpu.VMEM)] * outputs,
        scratch_shapes=[pltpu.VMEM((LEAF, LEAF), jnp.float32)],
        compiler_params=pltpu.CompilerParams(vmem_limit_bytes=24 * 2**20),
        cost_estimate=LIGHT,
    )(*operands)


def first_panel(packed, nb):
    return panel_call(first_panel_kernel, 1, nb, packed)[0]


def next_panel(packed, w0):
    return panel_call(next_panel_kernel, 2, w0.shape[0], packed, w0)


def whole(memory=pltpu.VMEM):
    return pl.BlockSpec(memory_space=memory)


def block_of(array, memory=pltpu.VMEM):
    return pl.BlockSpec(array.shape, lambda *_: (0,) * array.ndim, memory_space=memory)


def faces_kernel(cond_ref, ground_ref, info_ref, cells_ref, load_ref, panel_ref, *refs, sides):
    outs, (conduct_ref, grounds_ref, scaled_ref) = refs[:6], refs[6:]
    size_x, size_y, size_z = sides
    count, width = panel_ref.shape
    tile = 64
    classes = cond_ref.shape[0]
    ports = cells_ref.shape[1]

    def by_tile(t, carry):
        rows = pl.ds(pl.multiple_of(t * tile, tile), tile)
        kind = jnp.broadcast_to(info_ref[rows, 0:1], (tile, LEAF))
        ids = jnp.broadcast_to(info_ref[rows, 1:2], (tile, LEAF))
        conduct = jnp.zeros((tile, LEAF), jnp.float32)
        grounds = jnp.zeros((tile, LEAF), jnp.float32)
        for c in range(classes):
            conduct = jnp.where(kind == c, cond_ref[c], conduct)
            grounds = jnp.where(kind == c, ground_ref[c], grounds)
        loads = jnp.zeros((tile, LEAF), jnp.float32)
        for p in range(0, ports, LEAF):
            hit = ids == cells_ref[:, p : p + LEAF]
            loads = loads + jnp.where(hit, load_ref[:, p : p + LEAF], 0.0)
        conduct_ref[rows, :] = conduct
        grounds_ref[rows, :] = grounds + jnp.sum(loads, axis=1, keepdims=True)
        for p in range(0, width, LEAF):
            part = panel_ref[rows, p : p + LEAF].astype(jnp.float32)
            scaled_ref[p // LEAF, rows, :] = (
                (conduct * part).astype(jnp.bfloat16).astype(jnp.float32)
            )
        return carry

    lax.fori_loop(0, count // tile, by_tile, 0)
    plane = size_y * size_z
    for p in range(width // LEAF):
        lanes = slice(p * LEAF, (p + 1) * LEAF)
        outs[0][:, lanes] = scaled_ref[p, 0:plane, :].astype(jnp.bfloat16)
        outs[1][:, lanes] = scaled_ref[p, count - plane : count, :].astype(jnp.bfloat16)
        for out, at in ((outs[2], 0), (outs[3], plane - size_z)):
            face = [
                scaled_ref[p, x * plane + at : x * plane + at + size_z, :] for x in range(size_x)
            ]
            out[:, lanes] = jnp.concatenate(face, 0).astype(jnp.bfloat16)
        for out, at in ((outs[4], 0), (outs[5], size_z - 1)):
            face = scaled_ref[p, pl.ds(at, size_x * size_y, stride=size_z), :]
            out[:, lanes] = face.astype(jnp.bfloat16)


def image_kernel(table_ref, panel_ref, conduct_ref, grounds_ref, *refs, sides, nb, at):
    halos, (image_ref, *lead_refs, scaled_ref, square_ref) = refs[:6], refs[6:]
    core = table_ref[at]
    size_x, size_y, size_z = sides
    width = panel_ref.shape[1]
    plane = size_y * size_z
    subs = lax.broadcasted_iota(jnp.int32, (size_z, LEAF), 0)

    def by_lane(p, carry):
        lanes = pl.ds(pl.multiple_of(p * LEAF, LEAF), LEAF)
        x_low, x_high, y_low, y_high, z_low, z_high = (
            h[:, lanes].astype(jnp.float32) for h in halos
        )
        scaled_ref[...] = (
            (conduct_ref[...] * panel_ref[:, lanes].astype(jnp.float32))
            .astype(jnp.bfloat16)
            .astype(jnp.float32)
        )

        def cell_rows(x, y):
            at = x * plane + y * size_z
            return scaled_ref[at : at + size_z, :]

        for x in range(size_x):
            done = []
            for y in range(size_y):
                at = x * plane + y * size_z
                here = cell_rows(x, y)
                span = slice(y * size_z, (y + 1) * size_z)
                total = cell_rows(x + 1, y) if x + 1 < size_x else x_high[span, :]
                total = total + (cell_rows(x - 1, y) if x > 0 else x_low[span, :])
                span = slice(x * size_z, (x + 1) * size_z)
                total = total + (cell_rows(x, y + 1) if y + 1 < size_y else y_high[span, :])
                total = total + (cell_rows(x, y - 1) if y > 0 else y_low[span, :])
                k = x * size_y + y
                up = jnp.where(
                    subs == size_z - 1, z_high[k : k + 1, :], pltpu.roll(here, size_z - 1, 0)
                )
                down = jnp.where(subs == 0, z_low[k : k + 1, :], pltpu.roll(here, 1, 0))
                total = total + up + down
                own = slice(at, at + size_z)
                done.append(
                    conduct_ref[own, :] * (6.0 * here - total)
                    + grounds_ref[own, :] * panel_ref[at : at + size_z, lanes].astype(jnp.float32)
                )
            image_ref[x * plane : (x + 1) * plane, lanes] = jnp.concatenate(done, 0).astype(
                jnp.bfloat16
            )
        return carry

    lax.fori_loop(0, width // LEAF, by_lane, 0)

    def product(rows, cols):
        return lax.dot_general(
            panel_ref[:, rows],
            image_ref[:, cols],
            (((0,), (0,)), ((), ())),
            preferred_element_type=jnp.float32,
        )

    blocks = nb // LEAF

    def put_block(refs, number, value):
        half = refs[0].shape[0] // LEAF
        rows = slice(number % half * LEAF, (number % half + 1) * LEAF)
        kept = core == number // half

        @pl.when(kept)
        def _():
            refs[0][rows, :] = value

        @pl.when(jnp.logical_not(kept))
        def _():
            refs[1][rows, :] = value

    def lower(refs):
        number = 0
        for i in range(blocks):
            for j in range(i + 1):
                row, col = slice(i * LEAF, (i + 1) * LEAF), slice(j * LEAF, (j + 1) * LEAF)
                put_block(refs, number, 0.5 * (square_ref[row, col] + square_ref[col, row].T))
                number += 1
        return number

    head, tail = slice(0, nb), slice(nb, 2 * nb)
    square_ref[...] = product(head, head)
    lower(lead_refs[:2])
    square_ref[...] = product(tail, tail)
    number = lower(lead_refs[2:])
    square_ref[...] = product(tail, head)
    for j in range(blocks):
        for i in range(blocks):
            row, col = slice(i * LEAF, (i + 1) * LEAF), slice(j * LEAF, (j + 1) * LEAF)
            put_block(lead_refs[2:], number + j * blocks + i, square_ref[row, col])


def copy_kernel(table_ref, in_ref, out_ref):
    del table_ref
    out_ref[...] = in_ref[...]


def take_columns(table, at, array, width):
    rows = array.shape[0]
    tile = min(128, rows)
    return pl.pallas_call(
        copy_kernel,
        grid_spec=pltpu.PrefetchScalarGridSpec(
            num_scalar_prefetch=1,
            grid=(rows // tile,),
            in_specs=[pl.BlockSpec((tile, width), lambda t, tab: (t, tab[at]))],
            out_specs=pl.BlockSpec((tile, width), lambda t, tab: (t, 0)),
        ),
        out_shape=jax.ShapeDtypeStruct((rows, width), array.dtype),
        compiler_params=pltpu.CompilerParams(vmem_limit_bytes=58 * 2**20),
        cost_estimate=LIGHT,
    )(table, array)


def products_kernel(table_ref, *refs):
    del table_ref
    out, count = refs[-1], len(refs) // 2
    total = None
    for b, image in zip(refs[:count], refs[count:-1]):
        term = lax.dot_general(
            b[...], image[...], (((0,), (0,)), ((), ())), preferred_element_type=jnp.float32
        )
        total = term if total is None else total + term
    out[...] = total.astype(out.dtype)


def products(table, bases, images, lists, width, dtype):
    rows, cols = images[0].shape
    step = 512 if width % 512 == 0 else width
    parts = width // step
    steps = lists[0][1] * parts
    in_specs = [
        pl.BlockSpec(
            (rows, step), lambda t, tab, at=at: (0, tab[at + t // parts] * parts + t % parts)
        )
        for at, _ in lists
    ]
    in_specs += [pl.BlockSpec((rows, cols), lambda t, tab: (0, 0))] * len(images)
    total = steps * step
    return pl.pallas_call(
        products_kernel,
        grid_spec=pltpu.PrefetchScalarGridSpec(
            num_scalar_prefetch=1,
            grid=(steps,),
            in_specs=in_specs,
            out_specs=pl.BlockSpec((step, cols), lambda t, tab: (t, 0)),
        ),
        out_shape=jax.ShapeDtypeStruct((total, cols), dtype),
        compiler_params=pltpu.CompilerParams(vmem_limit_bytes=48 * 2**20),
        cost_estimate=LIGHT,
    )(table, *bases, *images)


def add_kernel(table_ref, *refs):
    del table_ref
    total = refs[0][...].astype(jnp.float32)
    for got in refs[1:-1]:
        total = total + got[...].astype(jnp.float32)
    refs[-1][...] = total.astype(refs[-1].dtype)


def add_blocks(table, arrays, at, count, height, dtype):
    cols = arrays[0].shape[1]
    step = min(256, height)
    parts = height // step
    steps = count * parts
    spec = pl.BlockSpec((step, cols), lambda t, tab: (tab[at + t // parts] * parts + t % parts, 0))
    return pl.pallas_call(
        add_kernel,
        grid_spec=pltpu.PrefetchScalarGridSpec(
            num_scalar_prefetch=1,
            grid=(steps,),
            in_specs=[spec] * len(arrays),
            out_specs=pl.BlockSpec((step, cols), lambda t, tab: (t, 0)),
        ),
        out_shape=jax.ShapeDtypeStruct((steps * step, cols), dtype),
        compiler_params=pltpu.CompilerParams(vmem_limit_bytes=24 * 2**20),
        cost_estimate=LIGHT,
    )(table, *arrays)


def plane_kernel(table_ref, *refs, groups, at):
    ins, outs, plane_ref = refs[: sum(groups)], refs[sum(groups) : -1], refs[-1]
    height = ins[0].shape[0]
    done = 0
    for i, count in enumerate(groups):
        total = ins[done][...].astype(jnp.float32)
        for got in ins[done + 1 : done + count]:
            total = total + got[...].astype(jnp.float32)
        plane_ref[i * height : (i + 1) * height, :] = total
        done += count
    for i, out in enumerate(outs):
        part = out.shape[0]
        rows = pl.ds(pl.multiple_of(table_ref[at + i] * part, part), part)
        out[...] = plane_ref[rows, :].astype(out.dtype)


def plane_parts(table, sums, height, at, outs):
    cols = sums[0][0][0].shape[1]

    def spec(place, block):
        if place is None:
            return pl.BlockSpec((height, cols), lambda t, tab: (block, 0))
        return pl.BlockSpec((height, cols), lambda t, tab: (tab[place], 0))

    return pl.pallas_call(
        functools.partial(plane_kernel, groups=[len(terms) for terms in sums], at=at),
        grid_spec=pltpu.PrefetchScalarGridSpec(
            num_scalar_prefetch=1,
            grid=(1,),
            in_specs=[spec(place, block) for terms in sums for _, place, block in terms],
            out_specs=[pl.BlockSpec(out.shape, lambda t, tab: (0, 0)) for out in outs],
            scratch_shapes=[pltpu.VMEM((height * len(sums), cols), jnp.float32)],
        ),
        out_shape=outs,
        compiler_params=pltpu.CompilerParams(vmem_limit_bytes=44 * 2**20),
        cost_estimate=LIGHT,
    )(table, *(array for terms in sums for array, _, _ in terms))


def swap_pairs():
    return [(0, 1), (1, 0)]


def other_half(half, core):
    other = lax.ppermute(half, "core", swap_pairs())
    first = core == 0
    return jnp.concatenate([jnp.where(first, half, other), jnp.where(first, other, half)], 0)


def join_kernel(table_ref, *refs, at):
    ins, outs = refs[:-2], refs[-2:]
    part = ins[0].shape[1]
    for d, block in enumerate(ins):
        rows = pl.ds(pl.multiple_of(table_ref[at + d] * part, part), part)
        for i, out in enumerate(outs):
            out[rows, :] = block[i]


def local(basis, classes, cond_table, ground_table, port_cells, port_load):
    sides = classes.shape
    cells_x, cells_y, cells_z = sides
    width_k = basis.shape[3]
    devices_x = lax.axis_size("gx")
    chips_y = lax.axis_size("gy")
    devices_z = lax.axis_size("gz")
    devices_y = 2 * chips_y
    spans = devices_x // 2
    split = spans // 2
    count = cells_x * cells_y * cells_z
    cols = PANELS * NB
    at_x, chip, core, at_z = (lax.axis_index(axis) for axis in ("gx", "gy", "core", "gz"))
    at_y = 2 * chip + core
    f32, bf16 = jnp.float32, jnp.bfloat16

    flat_basis = basis.reshape(count, width_k)
    wide = width_k // (devices_x * devices_z)
    narrow = wide // chips_y
    part = narrow // 2

    entries = []

    def put(values):
        entries.extend(values)
        return len(entries) - len(values), len(values)

    shift = core * spans * devices_z * chips_y

    def put_products(blocks):
        return [put([b + shift for b in blocks]), put(blocks)]

    lists_a, lists_b, next_a, next_b = [], [], [], []
    for d in range(devices_z):
        x = (at_z + d) % devices_z
        lists_a.append(
            put_products(
                [(zz * devices_z + x) * chips_y + y for zz in range(split) for y in range(chips_y)]
            )
        )
        next_b.append(put([zz * devices_z + x for zz in range(spans - split)]))
    for d in range(chips_y):
        y = (chip + d) % chips_y
        lists_b.append(
            put_products(
                [(zz * devices_z + x) * chips_y + y for zz in range(split, spans) for x in range(devices_z)]
            )
        )
        next_a.append(put([zz * chips_y + y for zz in range(split)]))
    leaving = [(at_x + step) % devices_x for step in range(devices_x)]
    leaving_at, _ = put(leaving + [at_x % spans * 2 + core, at_x % spans * 2 + 1 - core])
    given_at, _ = put([1 - core])
    core_at, _ = put([core])
    places_at, _ = put([(at_y - d) % devices_y for d in range(devices_y)])
    order_at, _ = put([(at_y + d) % devices_y for d in range(devices_y)])
    home_at, _ = put([at_x // spans == core])
    first_at, _ = put([((at_x * devices_z + at_z) * devices_y + at_y) * part])
    table = jnp.stack([jnp.asarray(e, jnp.int32) for e in entries])

    def move(array, axis, d):
        size = lax.axis_size(axis)
        return lax.ppermute(array, axis, [(i, (i + d) % size) for i in range(size)])

    panel_spec = pl.BlockSpec((count, cols), lambda *_: (0, 0))
    port_rows, load_rows = port_cells[None, :], port_load[None, :]
    global_x = at_x * cells_x + jnp.arange(cells_x, dtype=jnp.int32)
    global_y = at_y * cells_y + jnp.arange(cells_y, dtype=jnp.int32)
    global_z = at_z * cells_z + jnp.arange(cells_z, dtype=jnp.int32)
    flat_ids = (
        (global_x[:, None, None] * (cells_y * devices_y) + global_y[None, :, None])
        * (cells_z * devices_z)
        + global_z[None, None, :]
    )
    info = jnp.stack([classes, flat_ids], -1).reshape(count, 2)
    face_rows = [cells_y * cells_z] * 2 + [cells_x * cells_z] * 2 + [cells_x * cells_y] * 2
    outs = [jax.ShapeDtypeStruct((n, cols), bf16) for n in face_rows]
    outs += [jax.ShapeDtypeStruct((count, LEAF), f32)] * 2
    *faces, conduct, grounds = pl.pallas_call(
        functools.partial(faces_kernel, sides=sides),
        out_shape=outs,
        grid=(1,),
        in_specs=[block_of(cond_table, pltpu.SMEM), block_of(ground_table, pltpu.SMEM)]
        + [block_of(info), block_of(port_rows), block_of(load_rows), panel_spec],
        out_specs=[block_of(a) for a in outs],
        scratch_shapes=[pltpu.VMEM((cols // LEAF, count, LEAF), f32)],
        compiler_params=pltpu.CompilerParams(vmem_limit_bytes=58 * 2**20),
        cost_estimate=LIGHT,
    )(cond_table, ground_table, info, port_rows, load_rows, flat_basis)
    halos = []
    for i, (axis, size) in enumerate(
        (("gx", devices_x), (("gy", "core"), devices_y), ("gz", devices_z))
    ):
        low, high = faces[2 * i : 2 * i + 2]
        if size == 2:
            last = lax.axis_index(axis) == 1
            got = lax.ppermute(jnp.where(last, low, high), axis, swap_pairs())
            halos.append(jnp.where(last, got, 0))
            halos.append(jnp.where(last, 0, got))
        else:
            halos.append(lax.ppermute(high, axis, [(k, k + 1) for k in range(size - 1)]))
            halos.append(lax.ppermute(low, axis, [(k + 1, k) for k in range(size - 1)]))
    blocks = NB // LEAF
    lower_rows = blocks * (blocks + 1) // 2 * LEAF
    first_part = jax.ShapeDtypeStruct((lower_rows // 2, LEAF), f32)
    later_part = jax.ShapeDtypeStruct(((lower_rows + blocks * NB) // 2, LEAF), f32)
    lead_parts = [first_part] * 2 + [later_part] * 2
    outs = [jax.ShapeDtypeStruct((count, cols), bf16), *lead_parts]
    image, first_kept, first_sent, later_kept, later_sent = pl.pallas_call(
        functools.partial(image_kernel, sides=sides, nb=NB, at=core_at),
        out_shape=outs,
        grid_spec=pltpu.PrefetchScalarGridSpec(
            num_scalar_prefetch=1,
            grid=(1,),
            in_specs=[panel_spec] + [whole()] * 8,
            out_specs=[whole()] * 5,
            scratch_shapes=[pltpu.VMEM((count, LEAF), f32), pltpu.VMEM((NB, NB), f32)],
        ),
        compiler_params=pltpu.CompilerParams(vmem_limit_bytes=54 * 2**20),
        cost_estimate=LIGHT,
    )(table, flat_basis, conduct, grounds, *halos)

    other_image = lax.ppermute(image, "core", swap_pairs())
    later_table, _ = lax.optimization_barrier((table, image))
    given = take_columns(later_table, given_at, flat_basis, width_k // 2)
    other_basis = lax.ppermute(given, "core", swap_pairs())

    axes = ("gx", "gy", "gz")
    chips = devices_x * chips_y * devices_z

    def halved(kept, sent):
        return kept + lax.ppermute(sent, "core", swap_pairs())

    def exchanged(rows):
        rows = rows.reshape(chips, -1, LEAF)
        return lax.all_to_all(rows, axes, split_axis=0, concat_axis=0, tiled=True)

    def for_all(own):
        return jnp.broadcast_to(own, (chips, *own.shape))

    first_half, later_half = halved(first_kept, first_sent), halved(later_kept, later_sent)
    first_terms = exchanged(first_half)

    def chip_products(images, lists, dtype):
        return products(table, [flat_basis, other_basis], images, lists, narrow, dtype)

    images, _ = lax.optimization_barrier(([image, other_image], first_half))
    sent_a = [chip_products(images, lists_a[d], bf16) for d in range(1, devices_z)]
    sent_b = [chip_products(images, lists_b[d], bf16) for d in range(1, chips_y)]
    got_a = [move(a, "gz", d) for d, a in enumerate(sent_a, 1)]
    got_b = [move(a, "gy", d) for d, a in enumerate(sent_b, 1)]
    first_terms, _ = lax.optimization_barrier((first_terms, (sent_a, sent_b)))
    own = jnp.sum(first_terms, axis=0)
    share = own.shape[0]
    images, _ = lax.optimization_barrier((images, own))
    own_a, own_b = (chip_products(images, lists[0], f32) for lists in (lists_a, lists_b))
    both = jnp.concatenate([for_all(own), later_half.reshape(chips, -1, LEAF)], 1)
    both = lax.all_to_all(both, axes, split_axis=0, concat_axis=0, tiled=True)
    both, _ = lax.optimization_barrier((both, (own_a, own_b)))
    sums_a, sums_b = [own_a, *got_a], [own_b, *got_b]

    further_a = [add_blocks(table, sums_a, *next_a[d], narrow, bf16) for d in range(1, chips_y)]
    further_b = [add_blocks(table, sums_b, *next_b[d], narrow, bf16) for d in range(1, devices_z)]
    both, _ = lax.optimization_barrier((both, (further_a, further_b)))
    further_a = [move(a, "gy", d) for d, a in enumerate(further_a, 1)]
    further_b = [move(a, "gz", d) for d, a in enumerate(further_b, 1)]
    first_rows = other_half(both[:, :share].reshape(-1, LEAF), core)
    later_terms, _ = lax.optimization_barrier((both[:, share:], first_rows))
    later_sums = for_all(jnp.sum(later_terms, axis=0))
    later_half = exchanged(later_sums).reshape(-1, LEAF)
    first_rows, _ = lax.optimization_barrier((first_rows, later_sums))
    inverse_0 = first_panel(first_rows, NB)
    (further_a, further_b, later_half), inverse_0 = lax.optimization_barrier(
        ((further_a, further_b, later_half), inverse_0)
    )
    later_rows = other_half(later_half, core)

    terms = []
    for zz in range(split):
        at = next_a[0][0] + zz
        terms.append([(a, at, None) for a in sums_a] + [(a, None, zz) for a in further_a])
    for zz in range(spans - split):
        at = next_b[0][0] + zz
        terms.append([(a, at, None) for a in sums_b] + [(a, None, zz) for a in further_b])
    outs = [jax.ShapeDtypeStruct((part, cols), bf16)] * devices_x
    outs += [jax.ShapeDtypeStruct((part, cols), f32)] * 2
    *x_sent, own, swapped = plane_parts(table, terms, narrow, leaving_at, outs)
    x_got = []
    for step in range(devices_x):
        pairs = []
        for x in range(devices_x):
            for y in range(devices_y):
                to = (x + step) % devices_x
                dest_x = (y % 2) * spans + to // 2
                dest_y = (y // 2) * 2 + to % 2
                if dest_x != x:
                    pairs.append((x * devices_y + y, dest_x * devices_y + dest_y))
        x_got.append(lax.ppermute(x_sent[step], ("gx", "gy", "core"), pairs))
    swapped = lax.ppermute(swapped, "core", swap_pairs())
    later_rows, _ = lax.optimization_barrier((later_rows, x_sent))
    factor_10, inverse_1 = next_panel(later_rows, inverse_0)
    (x_got, swapped), inverse_1 = lax.optimization_barrier(((x_got, swapped), inverse_1))
    pair = jax.ShapeDtypeStruct((2, part, cols // devices_y), f32)
    ins = [own, swapped, *x_got, inverse_0, factor_10, inverse_1]
    pairs = list(pl.pallas_call(
        functools.partial(factor_kernel, at=(home_at, order_at, first_at)),
        out_shape=[pair] * devices_y,
        grid_spec=pltpu.PrefetchScalarGridSpec(
            num_scalar_prefetch=1,
            grid=(1,),
            in_specs=[block_of(a) for a in ins],
            out_specs=[block_of(pair)] * devices_y,
            scratch_shapes=[pltpu.VMEM((part, cols), f32)] * 2,
        ),
        compiler_params=pltpu.CompilerParams(vmem_limit_bytes=44 * 2**20),
        cost_estimate=LIGHT,
    )(table, *ins))
    for d in range(1, devices_y):
        route = [(i, (i + d) % devices_y) for i in range(devices_y)]
        pairs[d] = lax.ppermute(pairs[d], ("gy", "core"), route)
    out = jax.ShapeDtypeStruct((devices_y * part, cols // devices_y), f32)
    return pl.pallas_call(
        functools.partial(join_kernel, at=places_at),
        out_shape=(out, out),
        grid_spec=pltpu.PrefetchScalarGridSpec(
            num_scalar_prefetch=1,
            grid=(1,),
            in_specs=[block_of(a) for a in pairs],
            out_specs=[block_of(out)] * 2,
        ),
        compiler_params=pltpu.CompilerParams(vmem_limit_bytes=44 * 2**20),
        cost_estimate=LIGHT,
    )(table, *pairs)


def solution(mesh):
    sizes = mesh.shape
    fine = jax.sharding.Mesh(
        mesh.devices.reshape(sizes["gx"], sizes["gy"] // 2, 2, sizes["gz"]),
        ("gx", "gy", "core", "gz"),
    )
    grid = ("gx", ("gy", "core"), "gz")
    out = P(("gx", "gz"), ("gy", "core"))
    return jax.shard_map(
        local,
        mesh=fine,
        in_specs=(P(*grid, None), P(*grid), P(), P(), P(), P()),
        out_specs=(out, out),
        check_vma=False,
    )
```

```python
import functools

import jax
import jax.numpy as jnp
from jax import lax
from jax.experimental import pallas as pl
from jax.experimental.pallas import tpu as pltpu
from jax.sharding import PartitionSpec as P

NB = 512
PANELS = 2
LEAF = 128
SUB = 8


def dot3(a, b, dims):
    a_hi = a.astype(jnp.bfloat16)
    b_hi = b.astype(jnp.bfloat16)
    a_lo = (a - a_hi.astype(jnp.float32)).astype(jnp.bfloat16)
    b_lo = (b - b_hi.astype(jnp.float32)).astype(jnp.bfloat16)

    def dot(x, y):
        return lax.dot_general(x, y, (dims, ((), ())), preferred_element_type=jnp.float32)

    return dot(a_hi, b_hi) + (dot(a_hi, b_lo) + dot(a_lo, b_hi))


def inverse_of(d):
    guess = pl.reciprocal(d, approx=True)
    return guess * (2.0 - d * guess)


def leaf_inverse(block_ref):
    lanes = lax.broadcasted_iota(jnp.int32, (SUB, LEAF), 1)
    subs = lax.broadcasted_iota(jnp.int32, (SUB, LEAF), 0)
    shape = (SUB, LEAF)
    for t in range(LEAF // SUB):
        j0 = t * SUB
        rows = block_ref[j0 : j0 + SUB, :]
        cols = [jnp.broadcast_to(rows[:, j0 + k : j0 + k + 1], shape) for k in range(SUB)]
        p = [[jnp.broadcast_to(cols[k][i : i + 1, :], shape) for k in range(i + 1)] for i in range(SUB)]
        in_block = jnp.logical_and(lanes >= j0, lanes < j0 + SUB)
        start = jnp.where(in_block, (lanes - j0 == subs).astype(jnp.float32), rows)
        u = [jnp.broadcast_to(start[k : k + 1, :], shape) for k in range(SUB)]
        inv = [None] * SUB
        factor = [[None] * SUB for _ in range(SUB)]
        for k in range(SUB):
            inv[k] = inverse_of(p[k][k])
            for i in range(k + 1, SUB):
                factor[i][k] = p[i][k] * inv[k]
                for j in range(k + 1, i + 1):
                    p[i][j] = p[i][j] - factor[i][k] * p[j][k] if j < i else p[i][j] - factor[i][k] * p[i][k]
                u[i] = u[i] - factor[i][k] * u[k]
        out = u[0] * lax.rsqrt(p[0][0])
        for k in range(1, SUB):
            out = jnp.where(subs == k, u[k] * lax.rsqrt(p[k][k]), out)
        block_ref[j0 : j0 + SUB, :] = out
        if t + 1 == LEAF // SUB:
            break
        z = [None] * SUB
        for k in reversed(range(SUB)):
            z[k] = u[k] * inv[k]
            for i in range(k + 1, SUB):
                z[k] = z[k] - factor[i][k] * z[i]
        for v in range(t + 1, LEAF // SUB):
            below = block_ref[v * SUB : (v + 1) * SUB, :]
            upd = jnp.where(in_block, 0.0, below)
            for k in range(SUB):
                upd = upd - jnp.broadcast_to(below[:, j0 + k : j0 + k + 1], shape) * z[k]
            block_ref[v * SUB : (v + 1) * SUB, :] = upd


def factor_inverse(s_ref, d_ref):
    width = s_ref.shape[0]
    row_ids = lax.broadcasted_iota(jnp.int32, (width, width), 0)
    col_ids = lax.broadcasted_iota(jnp.int32, (width, width), 1)
    wide_cols = lax.broadcasted_iota(jnp.int32, (LEAF, width), 1)
    leaf_rows = lax.broadcasted_iota(jnp.int32, (LEAF, LEAF), 0)
    leaf_cols = lax.broadcasted_iota(jnp.int32, (LEAF, LEAF), 1)

    def step(b, carry):
        off = pl.multiple_of(b * LEAF, LEAF)
        span = pl.ds(off, LEAF)
        d_ref[...] = s_ref[span, span]
        leaf_inverse(d_ref)
        inverse = jnp.where(leaf_rows >= leaf_cols, d_ref[...], 0.0)
        s_ref[span, span] = (leaf_rows == leaf_cols).astype(jnp.float32)
        upper = dot3(inverse, s_ref[span, :], ((1,), (0,)))
        s_ref[span, :] = upper
        tail = jnp.where(wide_cols >= off + LEAF, upper, 0.0)
        current = s_ref[...]
        dead = jnp.logical_and(
            row_ids >= off + LEAF, jnp.logical_and(col_ids >= off, col_ids < off + LEAF)
        )
        s_ref[...] = jnp.where(dead, 0.0, current) - dot3(tail, upper, ((0,), (0,)))
        return carry

    lax.fori_loop(0, width // LEAF, step, 0)
    s_ref[...] = jnp.where(row_ids >= col_ids, s_ref[...], 0.0)


def unpack_symmetric(packed_ref, s_ref):
    at = 0
    for i in range(s_ref.shape[0] // LEAF):
        for j in range(i + 1):
            block = packed_ref[at * LEAF : (at + 1) * LEAF, :]
            s_ref[i * LEAF : (i + 1) * LEAF, j * LEAF : (j + 1) * LEAF] = block
            if j < i:
                s_ref[j * LEAF : (j + 1) * LEAF, i * LEAF : (i + 1) * LEAF] = block.T
            at += 1


def first_panel_kernel(packed_ref, w_ref, d_ref):
    unpack_symmetric(packed_ref, w_ref)
    factor_inverse(w_ref, d_ref)


def next_panel_kernel(packed_ref, w0_ref, f_ref, w_ref, d_ref):
    nb = w0_ref.shape[0]
    blocks = nb // LEAF
    unpack_symmetric(packed_ref, w_ref)
    start = packed_ref.shape[0] - blocks * nb
    below = jnp.concatenate(
        [packed_ref[start + i * nb : start + (i + 1) * nb, :] for i in range(nb // LEAF)], 1
    )
    below = dot3(below, w0_ref[...], ((1,), (1,)))
    f_ref[...] = below
    w_ref[...] = w_ref[...] - dot3(below, below, ((1,), (1,)))
    factor_inverse(w_ref, d_ref)


def factor_kernel(table_ref, own_ref, swapped_ref, *refs, at):
    home_at, order_at, first_at = at
    cols = own_ref.shape[1]
    *ins, rows_ref, all_ref = refs
    count = cols // ins[-1].shape[2]
    ins, blocks = ins[:-count], ins[-count:]
    *ins, w0_ref, f_ref, w1_ref = ins
    total = jnp.where(table_ref[home_at] != 0, own_ref[...], swapped_ref[...])
    for got in ins:
        total = total + got[...].astype(jnp.float32)
    rows_ref[...] = total
    nb = w0_ref.shape[0]
    ids = table_ref[first_at] + lax.broadcasted_iota(jnp.int32, (rows_ref.shape[0], nb), 0)
    columns = lax.broadcasted_iota(jnp.int32, (rows_ref.shape[0], nb), 1)
    part = dot3(rows_ref[:, :nb], w0_ref[...], ((1,), (1,)))
    rest = rows_ref[:, nb:] - dot3(part, f_ref[...], ((1,), (1,)))
    rest = dot3(rest, w1_ref[...], ((1,), (1,)))
    all_ref[:, :nb] = jnp.where(columns <= ids, part, 0.0)
    all_ref[:, nb:] = jnp.where(columns + nb <= ids, rest, 0.0)
    for d, block in enumerate(blocks):
        width = block.shape[2]
        span = pl.ds(pl.multiple_of(table_ref[order_at + d] * width, width), width)
        block[0] = rows_ref[:, span]
        block[1] = all_ref[:, span]


def panel_call(kernel, outputs, nb, *operands):
    return pl.pallas_call(
        kernel,
        out_shape=[jax.ShapeDtypeStruct((nb, nb), jnp.float32)] * outputs,
        in_specs=[pl.BlockSpec(memory_space=pltpu.VMEM)] * len(operands),
        out_specs=[pl.BlockSpec(memory_space=pltpu.VMEM)] * outputs,
        scratch_shapes=[pltpu.VMEM((LEAF, LEAF), jnp.float32)],
        compiler_params=pltpu.CompilerParams(vmem_limit_bytes=24 * 2**20),
        cost_estimate=pl.CostEstimate(
            flops=nb, transcendentals=0, bytes_accessed=nb
        ),
    )(*operands)


def first_panel(packed, nb):
    return panel_call(first_panel_kernel, 1, nb, packed)[0]


def next_panel(packed, w0):
    return panel_call(next_panel_kernel, 2, w0.shape[0], packed, w0)


def whole(memory=pltpu.VMEM):
    return pl.BlockSpec(memory_space=memory)


def block_of(array, memory=pltpu.VMEM):
    return pl.BlockSpec(array.shape, lambda *_: (0,) * array.ndim, memory_space=memory)


def faces_kernel(
    table_ref, cond_ref, ground_ref, info_ref, cells_ref, load_ref, panel_ref, basis_ref, *refs, sides, at
):
    outs, (conduct_ref, grounds_ref, given_ref, scaled_ref, copy_sem) = refs[:6], refs[6:]
    half = given_ref.shape[1]
    start = pl.multiple_of(table_ref[at] * half, half)
    copy = pltpu.make_async_copy(basis_ref.at[:, pl.ds(start, half)], given_ref, copy_sem)
    copy.start()
    size_x, size_y, size_z = sides
    count, width = panel_ref.shape
    tile = 64
    classes = cond_ref.shape[0]
    ports = cells_ref.shape[1]

    def by_tile(t, carry):
        rows = pl.ds(pl.multiple_of(t * tile, tile), tile)
        kind = jnp.broadcast_to(info_ref[rows, 0:1], (tile, LEAF))
        ids = jnp.broadcast_to(info_ref[rows, 1:2], (tile, LEAF))
        conduct = jnp.zeros((tile, LEAF), jnp.float32)
        grounds = jnp.zeros((tile, LEAF), jnp.float32)
        for c in range(classes):
            conduct = jnp.where(kind == c, cond_ref[c], conduct)
            grounds = jnp.where(kind == c, ground_ref[c], grounds)
        loads = jnp.zeros((tile, LEAF), jnp.float32)
        for p in range(0, ports, LEAF):
            hit = ids == cells_ref[:, p : p + LEAF]
            loads = loads + jnp.where(hit, load_ref[:, p : p + LEAF], 0.0)
        conduct_ref[rows, :] = conduct
        grounds_ref[rows, :] = grounds + jnp.sum(loads, axis=1, keepdims=True)
        for p in range(0, width, LEAF):
            part = panel_ref[rows, p : p + LEAF].astype(jnp.float32)
            scaled_ref[p // LEAF, rows, :] = (
                (conduct * part).astype(jnp.bfloat16).astype(jnp.float32)
            )
        return carry

    lax.fori_loop(0, count // tile, by_tile, 0)
    plane = size_y * size_z
    for p in range(width // LEAF):
        lanes = slice(p * LEAF, (p + 1) * LEAF)
        outs[0][:, lanes] = scaled_ref[p, 0:plane, :].astype(jnp.bfloat16)
        outs[1][:, lanes] = scaled_ref[p, count - plane : count, :].astype(jnp.bfloat16)
        for out, at in ((outs[2], 0), (outs[3], plane - size_z)):
            face = [
                scaled_ref[p, x * plane + at : x * plane + at + size_z, :] for x in range(size_x)
            ]
            out[:, lanes] = jnp.concatenate(face, 0).astype(jnp.bfloat16)
        for out, at in ((outs[4], 0), (outs[5], size_z - 1)):
            face = scaled_ref[p, pl.ds(at, size_x * size_y, stride=size_z), :]
            out[:, lanes] = face.astype(jnp.bfloat16)
    copy.wait()


def image_kernel(table_ref, panel_ref, conduct_ref, grounds_ref, *refs, sides, nb, at):
    halos, (image_ref, kept_ref, sent_ref, scaled_ref, square_ref) = refs[:6], refs[6:]
    core = table_ref[at]
    size_x, size_y, size_z = sides
    width = panel_ref.shape[1]
    plane = size_y * size_z
    subs = lax.broadcasted_iota(jnp.int32, (size_z, LEAF), 0)

    def by_lane(p, carry):
        lanes = pl.ds(pl.multiple_of(p * LEAF, LEAF), LEAF)
        x_low, x_high, y_low, y_high, z_low, z_high = (
            h[:, lanes].astype(jnp.float32) for h in halos
        )
        scaled_ref[...] = (
            (conduct_ref[...] * panel_ref[:, lanes].astype(jnp.float32))
            .astype(jnp.bfloat16)
            .astype(jnp.float32)
        )

        def cell_rows(x, y):
            at = x * plane + y * size_z
            return scaled_ref[at : at + size_z, :]

        for x in range(size_x):
            done = []
            for y in range(size_y):
                at = x * plane + y * size_z
                here = cell_rows(x, y)
                span = slice(y * size_z, (y + 1) * size_z)
                total = cell_rows(x + 1, y) if x + 1 < size_x else x_high[span, :]
                total = total + (cell_rows(x - 1, y) if x > 0 else x_low[span, :])
                span = slice(x * size_z, (x + 1) * size_z)
                total = total + (cell_rows(x, y + 1) if y + 1 < size_y else y_high[span, :])
                total = total + (cell_rows(x, y - 1) if y > 0 else y_low[span, :])
                k = x * size_y + y
                up = jnp.where(
                    subs == size_z - 1, z_high[k : k + 1, :], pltpu.roll(here, size_z - 1, 0)
                )
                down = jnp.where(subs == 0, z_low[k : k + 1, :], pltpu.roll(here, 1, 0))
                total = total + up + down
                own = slice(at, at + size_z)
                done.append(
                    conduct_ref[own, :] * (6.0 * here - total)
                    + grounds_ref[own, :] * panel_ref[at : at + size_z, lanes].astype(jnp.float32)
                )
            image_ref[x * plane : (x + 1) * plane, lanes] = jnp.concatenate(done, 0).astype(
                jnp.bfloat16
            )
        return carry

    lax.fori_loop(0, width // LEAF, by_lane, 0)

    def product(rows, cols):
        return lax.dot_general(
            panel_ref[:, rows],
            image_ref[:, cols],
            (((0,), (0,)), ((), ())),
            preferred_element_type=jnp.float32,
        )

    blocks = nb // LEAF

    first_blocks = blocks * (blocks + 1) // 2
    half = kept_ref.shape[0] // LEAF - 1

    def put_block(number, value):
        if number < first_blocks:
            owner, place = divmod(number, first_blocks // 2)
        else:
            owner, place = divmod(number - first_blocks, half - first_blocks // 2)
            place += first_blocks // 2
        kept = core == owner
        for ref, here in ((kept_ref, kept), (sent_ref, jnp.logical_not(kept))):
            at_row = pl.multiple_of(jnp.where(here, place, half) * LEAF, LEAF)
            ref[pl.ds(at_row, LEAF), :] = value

    def lower(number):
        for i in range(blocks):
            for j in range(i + 1):
                row, col = slice(i * LEAF, (i + 1) * LEAF), slice(j * LEAF, (j + 1) * LEAF)
                put_block(number, 0.5 * (square_ref[row, col] + square_ref[col, row].T))
                number += 1
        return number

    head, tail = slice(0, nb), slice(nb, 2 * nb)
    square_ref[...] = product(head, head)
    number = lower(0)
    square_ref[...] = product(tail, tail)
    number = lower(number)
    square_ref[...] = product(tail, head)
    for j in range(blocks):
        for i in range(blocks):
            row, col = slice(i * LEAF, (i + 1) * LEAF), slice(j * LEAF, (j + 1) * LEAF)
            put_block(number + j * blocks + i, square_ref[row, col])


def products_kernel(table_ref, *refs):
    del table_ref
    out, count = refs[-1], len(refs) // 2
    total = None
    for b, image in zip(refs[:count], refs[count:-1]):
        term = lax.dot_general(
            b[...], image[...], (((0,), (0,)), ((), ())), preferred_element_type=jnp.float32
        )
        total = term if total is None else total + term
    out[...] = total.astype(out.dtype)


def products(table, bases, images, lists, width, dtype):
    rows, cols = images[0].shape
    step = 512 if width % 512 == 0 else width
    parts = width // step
    steps = lists[0][1] * parts
    in_specs = [
        pl.BlockSpec(
            (rows, step), lambda t, tab, at=at: (0, tab[at + t // parts] * parts + t % parts)
        )
        for at, _ in lists
    ]
    in_specs += [pl.BlockSpec((rows, cols), lambda t, tab: (0, 0))] * len(images)
    total = steps * step
    return pl.pallas_call(
        products_kernel,
        grid_spec=pltpu.PrefetchScalarGridSpec(
            num_scalar_prefetch=1,
            grid=(steps,),
            in_specs=in_specs,
            out_specs=pl.BlockSpec((step, cols), lambda t, tab: (t, 0)),
        ),
        out_shape=jax.ShapeDtypeStruct((total, cols), dtype),
        compiler_params=pltpu.CompilerParams(vmem_limit_bytes=48 * 2**20),
        cost_estimate=pl.CostEstimate(
            flops=2 * total * cols * rows * len(bases),
            transcendentals=0,
            bytes_accessed=2 * rows * (total + cols) * len(bases) + 4 * total * cols,
        ),
    )(table, *bases, *images)


def add_kernel(table_ref, *refs):
    del table_ref
    total = refs[0][...].astype(jnp.float32)
    for got in refs[1:-1]:
        total = total + got[...].astype(jnp.float32)
    refs[-1][...] = total.astype(refs[-1].dtype)


def add_blocks(table, arrays, at, count, height, dtype):
    cols = arrays[0].shape[1]
    step = min(256, height)
    parts = height // step
    steps = count * parts
    spec = pl.BlockSpec((step, cols), lambda t, tab: (tab[at + t // parts] * parts + t % parts, 0))
    return pl.pallas_call(
        add_kernel,
        grid_spec=pltpu.PrefetchScalarGridSpec(
            num_scalar_prefetch=1,
            grid=(steps,),
            in_specs=[spec] * len(arrays),
            out_specs=pl.BlockSpec((step, cols), lambda t, tab: (t, 0)),
        ),
        out_shape=jax.ShapeDtypeStruct((steps * step, cols), dtype),
        compiler_params=pltpu.CompilerParams(vmem_limit_bytes=24 * 2**20),
        cost_estimate=pl.CostEstimate(
            flops=steps * step * cols,
            transcendentals=0,
            bytes_accessed=steps * step * cols * 4 * len(arrays),
        ),
    )(table, *arrays)


def plane_kernel(table_ref, *refs, groups, at):
    ins, outs, plane_ref = refs[: sum(groups)], refs[sum(groups) : -1], refs[-1]
    height = ins[0].shape[0]
    done = 0
    for i, count in enumerate(groups):
        total = ins[done][...].astype(jnp.float32)
        for got in ins[done + 1 : done + count]:
            total = total + got[...].astype(jnp.float32)
        plane_ref[i * height : (i + 1) * height, :] = total
        done += count
    for i, out in enumerate(outs):
        part = out.shape[0]
        rows = pl.ds(pl.multiple_of(table_ref[at + i] * part, part), part)
        out[...] = plane_ref[rows, :].astype(out.dtype)


def plane_parts(table, sums, height, at, outs):
    cols = sums[0][0][0].shape[1]

    def spec(place, block):
        if place is None:
            return pl.BlockSpec((height, cols), lambda t, tab: (block, 0))
        return pl.BlockSpec((height, cols), lambda t, tab: (tab[place], 0))

    return pl.pallas_call(
        functools.partial(plane_kernel, groups=[len(terms) for terms in sums], at=at),
        grid_spec=pltpu.PrefetchScalarGridSpec(
            num_scalar_prefetch=1,
            grid=(1,),
            in_specs=[spec(place, block) for terms in sums for _, place, block in terms],
            out_specs=[pl.BlockSpec(out.shape, lambda t, tab: (0, 0)) for out in outs],
            scratch_shapes=[pltpu.VMEM((height * len(sums), cols), jnp.float32)],
        ),
        out_shape=outs,
        compiler_params=pltpu.CompilerParams(vmem_limit_bytes=44 * 2**20),
        cost_estimate=pl.CostEstimate(
            flops=0, transcendentals=0, bytes_accessed=height * len(sums) * cols * 14
        ),
    )(table, *(array for terms in sums for array, _, _ in terms))


def swap_pairs():
    return [(0, 1), (1, 0)]


def join_kernel(table_ref, *refs, at):
    ins, outs = refs[:-2], refs[-2:]
    part = ins[0].shape[1]
    for d, block in enumerate(ins):
        rows = pl.ds(pl.multiple_of(table_ref[at + d] * part, part), part)
        for i, out in enumerate(outs):
            out[rows, :] = block[i]


def local(basis, classes, cond_table, ground_table, port_cells, port_load):
    sides = classes.shape
    cells_x, cells_y, cells_z = sides
    width_k = basis.shape[3]
    devices_x = lax.axis_size("gx")
    chips_y = lax.axis_size("gy")
    devices_z = lax.axis_size("gz")
    devices_y = 2 * chips_y
    spans = devices_x // 2
    split = spans // 2
    count = cells_x * cells_y * cells_z
    cols = PANELS * NB
    at_x, chip, core, at_z = (lax.axis_index(axis) for axis in ("gx", "gy", "core", "gz"))
    at_y = 2 * chip + core
    f32, bf16 = jnp.float32, jnp.bfloat16

    flat_basis = basis.reshape(count, width_k)
    wide = width_k // (devices_x * devices_z)
    narrow = wide // chips_y
    part = narrow // 2

    entries = []

    def put(values):
        entries.extend(values)
        return len(entries) - len(values), len(values)

    shift = core * spans * devices_z * chips_y

    def put_products(blocks):
        return [put([b + shift for b in blocks]), put(blocks)]

    lists_a, lists_b, next_a, next_b = [], [], [], []
    for d in range(devices_z):
        x = (at_z + d) % devices_z
        lists_a.append(
            put_products(
                [(zz * devices_z + x) * chips_y + y for zz in range(split) for y in range(chips_y)]
            )
        )
        next_b.append(put([zz * devices_z + x for zz in range(spans - split)]))
    for d in range(chips_y):
        y = (chip + d) % chips_y
        lists_b.append(
            put_products(
                [(zz * devices_z + x) * chips_y + y for zz in range(split, spans) for x in range(devices_z)]
            )
        )
        next_a.append(put([zz * chips_y + y for zz in range(split)]))
    leaving = [(at_x + step) % devices_x for step in range(devices_x)]
    leaving_at, _ = put(leaving + [at_x % spans * 2 + core, at_x % spans * 2 + 1 - core])
    given_at, _ = put([1 - core])
    core_at, _ = put([core])
    places_at, _ = put([(at_y - d) % devices_y for d in range(devices_y)])
    order_at, _ = put([(at_y + d) % devices_y for d in range(devices_y)])
    home_at, _ = put([at_x // spans == core])
    first_at, _ = put([((at_x * devices_z + at_z) * devices_y + at_y) * part])
    table = jnp.stack([jnp.asarray(e, jnp.int32) for e in entries])

    def move(array, axis, d):
        size = lax.axis_size(axis)
        return lax.ppermute(array, axis, [(i, (i + d) % size) for i in range(size)])

    panel_spec = pl.BlockSpec((count, cols), lambda *_: (0, 0))
    port_rows, load_rows = port_cells[None, :], port_load[None, :]
    global_x = at_x * cells_x + jnp.arange(cells_x, dtype=jnp.int32)
    global_y = at_y * cells_y + jnp.arange(cells_y, dtype=jnp.int32)
    global_z = at_z * cells_z + jnp.arange(cells_z, dtype=jnp.int32)
    flat_ids = (
        (global_x[:, None, None] * (cells_y * devices_y) + global_y[None, :, None])
        * (cells_z * devices_z)
        + global_z[None, None, :]
    )
    info = jnp.stack([classes, flat_ids], -1).reshape(count, 2)
    face_rows = [cells_y * cells_z] * 2 + [cells_x * cells_z] * 2 + [cells_x * cells_y] * 2
    outs = [jax.ShapeDtypeStruct((n, cols), bf16) for n in face_rows]
    outs += [jax.ShapeDtypeStruct((count, LEAF), f32)] * 2
    given = jax.ShapeDtypeStruct((count, width_k // 2), basis.dtype)
    *faces, conduct, grounds, given = pl.pallas_call(
        functools.partial(faces_kernel, sides=sides, at=given_at),
        out_shape=[*outs, given],
        grid_spec=pltpu.PrefetchScalarGridSpec(
            num_scalar_prefetch=1,
            grid=(1,),
            in_specs=[block_of(cond_table, pltpu.SMEM), block_of(ground_table, pltpu.SMEM)]
            + [block_of(info), block_of(port_rows), block_of(load_rows), panel_spec]
            + [pl.BlockSpec(memory_space=pl.ANY)],
            out_specs=[block_of(a) for a in outs] + [pl.BlockSpec(memory_space=pl.ANY)],
            scratch_shapes=[
                pltpu.VMEM((cols // LEAF, count, LEAF), f32),
                pltpu.SemaphoreType.DMA,
            ],
        ),
        compiler_params=pltpu.CompilerParams(vmem_limit_bytes=58 * 2**20),
    )(table, cond_table, ground_table, info, port_rows, load_rows, flat_basis, flat_basis)
    halos = []
    for i, (axis, size) in enumerate(
        (("gx", devices_x), (("gy", "core"), devices_y), ("gz", devices_z))
    ):
        low, high = faces[2 * i : 2 * i + 2]
        if size == 2:
            last = lax.axis_index(axis) == 1
            got = lax.ppermute(jnp.where(last, low, high), axis, swap_pairs())
            halos.append(jnp.where(last, got, 0))
            halos.append(jnp.where(last, 0, got))
        else:
            halos.append(lax.ppermute(high, axis, [(k, k + 1) for k in range(size - 1)]))
            halos.append(lax.ppermute(low, axis, [(k + 1, k) for k in range(size - 1)]))
    other_basis = lax.ppermute(given, "core", swap_pairs())

    blocks = NB // LEAF
    lower_rows = blocks * (blocks + 1) // 2 * LEAF
    half_rows = lower_rows + blocks * NB // 2
    lead_parts = [jax.ShapeDtypeStruct((half_rows + LEAF, LEAF), f32)] * 2
    outs = [jax.ShapeDtypeStruct((count, cols), bf16), *lead_parts]
    image, lead_kept, lead_sent = pl.pallas_call(
        functools.partial(image_kernel, sides=sides, nb=NB, at=core_at),
        out_shape=outs,
        grid_spec=pltpu.PrefetchScalarGridSpec(
            num_scalar_prefetch=1,
            grid=(1,),
            in_specs=[panel_spec] + [whole()] * 8,
            out_specs=[whole()] * 3,
            scratch_shapes=[pltpu.VMEM((count, LEAF), f32), pltpu.VMEM((NB, NB), f32)],
        ),
        compiler_params=pltpu.CompilerParams(vmem_limit_bytes=54 * 2**20),
    )(table, flat_basis, conduct, grounds, *halos)

    other_image = lax.ppermute(image, "core", swap_pairs())
    other_basis = lax.ppermute(given, "core", swap_pairs())

    plane_axes = ("gy", "gz")
    chips = chips_y * devices_z

    def exchanged(rows, axes):
        return lax.all_to_all(rows, axes, split_axis=0, concat_axis=0, tiled=True)

    def for_all(own, size):
        return jnp.broadcast_to(own, (size, *own.shape))

    lead_got = lax.ppermute(lead_sent, "core", swap_pairs())
    lead_half = lead_kept[:half_rows] + lead_got[:half_rows]
    lead_terms = exchanged(lead_half.reshape(chips, -1, LEAF), plane_axes)

    def chip_products(images, lists, dtype):
        return products(table, [flat_basis, other_basis], images, lists, narrow, dtype)

    images, _ = lax.optimization_barrier(([image, other_image], lead_half))
    sent_a = [chip_products(images, lists_a[d], bf16) for d in range(1, devices_z)]
    sent_b = [chip_products(images, lists_b[d], bf16) for d in range(1, chips_y)]
    got_a = [move(a, "gz", d) for d, a in enumerate(sent_a, 1)]
    got_b = [move(a, "gy", d) for d, a in enumerate(sent_b, 1)]
    own_a, own_b = (chip_products(images, lists[0], f32) for lists in (lists_a, lists_b))
    lead_terms, _ = lax.optimization_barrier((lead_terms, (own_a, own_b)))
    own = jnp.sum(lead_terms, axis=0).reshape(devices_x, -1, LEAF)
    own = jnp.sum(exchanged(own, "gx"), axis=0)
    own = exchanged(for_all(own, devices_x), "gx").reshape(-1, LEAF)
    own = for_all(own, chips)
    (got_a, got_b), _ = lax.optimization_barrier(((got_a, got_b), own))
    lead_half = exchanged(own, plane_axes).reshape(-1, LEAF)
    sums_a, sums_b = [own_a, *got_a], [own_b, *got_b]

    further_a = [add_blocks(table, sums_a, *next_a[d], narrow, bf16) for d in range(1, chips_y)]
    further_b = [add_blocks(table, sums_b, *next_b[d], narrow, bf16) for d in range(1, devices_z)]
    lead_half, _ = lax.optimization_barrier((lead_half, (further_a, further_b)))
    further_a = [move(a, "gy", d) for d, a in enumerate(further_a, 1)]
    further_b = [move(a, "gz", d) for d, a in enumerate(further_b, 1)]
    other = lax.ppermute(lead_half, "core", swap_pairs())
    lower_half, upper_half = jnp.where(core == 0, lead_half, other), jnp.where(core == 0, other, lead_half)
    first = lower_rows // 2
    first_rows = jnp.concatenate([lower_half[:first], upper_half[:first]], 0)
    later_rows = jnp.concatenate([lower_half[first:], upper_half[first:]], 0)
    inverse_0 = first_panel(first_rows, NB)
    (further_a, further_b), inverse_0 = lax.optimization_barrier(
        ((further_a, further_b), inverse_0)
    )

    terms = []
    for zz in range(split):
        at = next_a[0][0] + zz
        terms.append([(a, at, None) for a in sums_a] + [(a, None, zz) for a in further_a])
    for zz in range(spans - split):
        at = next_b[0][0] + zz
        terms.append([(a, at, None) for a in sums_b] + [(a, None, zz) for a in further_b])
    outs = [jax.ShapeDtypeStruct((part, cols), bf16)] * devices_x
    outs += [jax.ShapeDtypeStruct((part, cols), f32)] * 2
    *x_sent, own, swapped = plane_parts(table, terms, narrow, leaving_at, outs)
    x_got = []
    for step in range(devices_x):
        pairs = []
        for x in range(devices_x):
            for y in range(devices_y):
                to = (x + step) % devices_x
                dest_x = (y % 2) * spans + to // 2
                dest_y = (y // 2) * 2 + to % 2
                if dest_x != x:
                    pairs.append((x * devices_y + y, dest_x * devices_y + dest_y))
        x_got.append(lax.ppermute(x_sent[step], ("gx", "gy", "core"), pairs))
    swapped = lax.ppermute(swapped, "core", swap_pairs())
    later_rows, _ = lax.optimization_barrier((later_rows, x_sent))
    factor_10, inverse_1 = next_panel(later_rows, inverse_0)
    (x_got, swapped), inverse_1 = lax.optimization_barrier(((x_got, swapped), inverse_1))
    pair = jax.ShapeDtypeStruct((2, part, cols // devices_y), f32)
    ins = [own, swapped, *x_got, inverse_0, factor_10, inverse_1]
    pairs = list(pl.pallas_call(
        functools.partial(factor_kernel, at=(home_at, order_at, first_at)),
        out_shape=[pair] * devices_y,
        grid_spec=pltpu.PrefetchScalarGridSpec(
            num_scalar_prefetch=1,
            grid=(1,),
            in_specs=[block_of(a) for a in ins],
            out_specs=[block_of(pair)] * devices_y,
            scratch_shapes=[pltpu.VMEM((part, cols), f32)] * 2,
        ),
        compiler_params=pltpu.CompilerParams(vmem_limit_bytes=44 * 2**20),
    )(table, *ins))
    for d in range(1, devices_y):
        route = [(i, (i + d) % devices_y) for i in range(devices_y)]
        pairs[d] = lax.ppermute(pairs[d], ("gy", "core"), route)
    out = jax.ShapeDtypeStruct((devices_y * part, cols // devices_y), f32)
    return pl.pallas_call(
        functools.partial(join_kernel, at=places_at),
        out_shape=(out, out),
        grid_spec=pltpu.PrefetchScalarGridSpec(
            num_scalar_prefetch=1,
            grid=(1,),
            in_specs=[block_of(a) for a in pairs],
            out_specs=[block_of(out)] * 2,
        ),
        compiler_params=pltpu.CompilerParams(vmem_limit_bytes=44 * 2**20),
    )(table, *pairs)


def solution(mesh):
    sizes = mesh.shape
    fine = jax.sharding.Mesh(
        mesh.devices.reshape(sizes["gx"], sizes["gy"] // 2, 2, sizes["gz"]),
        ("gx", "gy", "core", "gz"),
    )
    grid = ("gx", ("gy", "core"), "gz")
    out = P(("gx", "gz"), ("gy", "core"))
    return jax.shard_map(
        local,
        mesh=fine,
        in_specs=(P(*grid, None), P(*grid), P(), P(), P(), P()),
        out_specs=(out, out),
        check_vma=False,
    )
```

```python
import functools

import jax
import jax.numpy as jnp
from jax import lax
from jax.experimental import pallas as pl
from jax.experimental.pallas import tpu as pltpu
from jax.sharding import PartitionSpec as P

NB = 512
PANELS = 2
LEAF = 128
SUB = 8


def dot3(a, b, dims):
    a_hi = a.astype(jnp.bfloat16)
    b_hi = b.astype(jnp.bfloat16)
    a_lo = (a - a_hi.astype(jnp.float32)).astype(jnp.bfloat16)
    b_lo = (b - b_hi.astype(jnp.float32)).astype(jnp.bfloat16)

    def dot(x, y):
        return lax.dot_general(x, y, (dims, ((), ())), preferred_element_type=jnp.float32)

    return dot(a_hi, b_hi) + (dot(a_hi, b_lo) + dot(a_lo, b_hi))


def inverse_of(d):
    guess = pl.reciprocal(d, approx=True)
    return guess * (2.0 - d * guess)


def leaf_inverse(block_ref):
    lanes = lax.broadcasted_iota(jnp.int32, (SUB, LEAF), 1)
    subs = lax.broadcasted_iota(jnp.int32, (SUB, LEAF), 0)
    shape = (SUB, LEAF)
    for t in range(LEAF // SUB):
        j0 = t * SUB
        rows = block_ref[j0 : j0 + SUB, :]
        cols = [jnp.broadcast_to(rows[:, j0 + k : j0 + k + 1], shape) for k in range(SUB)]
        p = [[jnp.broadcast_to(cols[k][i : i + 1, :], shape) for k in range(i + 1)] for i in range(SUB)]
        in_block = jnp.logical_and(lanes >= j0, lanes < j0 + SUB)
        start = jnp.where(in_block, (lanes - j0 == subs).astype(jnp.float32), rows)
        u = [jnp.broadcast_to(start[k : k + 1, :], shape) for k in range(SUB)]
        inv = [None] * SUB
        factor = [[None] * SUB for _ in range(SUB)]
        for k in range(SUB):
            inv[k] = inverse_of(p[k][k])
            for i in range(k + 1, SUB):
                factor[i][k] = p[i][k] * inv[k]
                for j in range(k + 1, i + 1):
                    p[i][j] = p[i][j] - factor[i][k] * p[j][k] if j < i else p[i][j] - factor[i][k] * p[i][k]
                u[i] = u[i] - factor[i][k] * u[k]
        out = u[0] * lax.rsqrt(p[0][0])
        for k in range(1, SUB):
            out = jnp.where(subs == k, u[k] * lax.rsqrt(p[k][k]), out)
        block_ref[j0 : j0 + SUB, :] = out
        if t + 1 == LEAF // SUB:
            break
        z = [None] * SUB
        for k in reversed(range(SUB)):
            z[k] = u[k] * inv[k]
            for i in range(k + 1, SUB):
                z[k] = z[k] - factor[i][k] * z[i]
        for v in range(t + 1, LEAF // SUB):
            below = block_ref[v * SUB : (v + 1) * SUB, :]
            upd = jnp.where(in_block, 0.0, below)
            for k in range(SUB):
                upd = upd - jnp.broadcast_to(below[:, j0 + k : j0 + k + 1], shape) * z[k]
            block_ref[v * SUB : (v + 1) * SUB, :] = upd


def factor_inverse(s_ref, d_ref):
    width = s_ref.shape[0]
    row_ids = lax.broadcasted_iota(jnp.int32, (width, width), 0)
    col_ids = lax.broadcasted_iota(jnp.int32, (width, width), 1)
    wide_cols = lax.broadcasted_iota(jnp.int32, (LEAF, width), 1)
    leaf_rows = lax.broadcasted_iota(jnp.int32, (LEAF, LEAF), 0)
    leaf_cols = lax.broadcasted_iota(jnp.int32, (LEAF, LEAF), 1)

    def step(b, carry):
        off = pl.multiple_of(b * LEAF, LEAF)
        span = pl.ds(off, LEAF)
        d_ref[...] = s_ref[span, span]
        leaf_inverse(d_ref)
        inverse = jnp.where(leaf_rows >= leaf_cols, d_ref[...], 0.0)
        s_ref[span, span] = (leaf_rows == leaf_cols).astype(jnp.float32)
        upper = dot3(inverse, s_ref[span, :], ((1,), (0,)))
        s_ref[span, :] = upper
        tail = jnp.where(wide_cols >= off + LEAF, upper, 0.0)
        current = s_ref[...]
        dead = jnp.logical_and(
            row_ids >= off + LEAF, jnp.logical_and(col_ids >= off, col_ids < off + LEAF)
        )
        s_ref[...] = jnp.where(dead, 0.0, current) - dot3(tail, upper, ((0,), (0,)))
        return carry

    lax.fori_loop(0, width // LEAF, step, 0)
    s_ref[...] = jnp.where(row_ids >= col_ids, s_ref[...], 0.0)


def unpack_symmetric(packed_ref, s_ref):
    at = 0
    for i in range(s_ref.shape[0] // LEAF):
        for j in range(i + 1):
            block = packed_ref[at * LEAF : (at + 1) * LEAF, :]
            s_ref[i * LEAF : (i + 1) * LEAF, j * LEAF : (j + 1) * LEAF] = block
            if j < i:
                s_ref[j * LEAF : (j + 1) * LEAF, i * LEAF : (i + 1) * LEAF] = block.T
            at += 1


def first_panel_kernel(packed_ref, w_ref, d_ref):
    unpack_symmetric(packed_ref, w_ref)
    factor_inverse(w_ref, d_ref)


def next_panel_kernel(packed_ref, w0_ref, f_ref, w_ref, d_ref):
    nb = w0_ref.shape[0]
    blocks = nb // LEAF
    unpack_symmetric(packed_ref, w_ref)
    start = packed_ref.shape[0] - blocks * nb
    below = jnp.concatenate(
        [packed_ref[start + i * nb : start + (i + 1) * nb, :] for i in range(nb // LEAF)], 1
    )
    below = dot3(below, w0_ref[...], ((1,), (1,)))
    f_ref[...] = below
    w_ref[...] = w_ref[...] - dot3(below, below, ((1,), (1,)))
    factor_inverse(w_ref, d_ref)


def factor_kernel(table_ref, own_ref, swapped_ref, *refs, at):
    home_at, order_at, first_at = at
    cols = own_ref.shape[1]
    *ins, rows_ref, all_ref = refs
    count = cols // ins[-1].shape[2]
    ins, blocks = ins[:-count], ins[-count:]
    *ins, w0_ref, f_ref, w1_ref = ins
    total = jnp.where(table_ref[home_at] != 0, own_ref[...], swapped_ref[...])
    for got in ins:
        total = total + got[...].astype(jnp.float32)
    rows_ref[...] = total
    nb = w0_ref.shape[0]
    ids = table_ref[first_at] + lax.broadcasted_iota(jnp.int32, (rows_ref.shape[0], nb), 0)
    columns = lax.broadcasted_iota(jnp.int32, (rows_ref.shape[0], nb), 1)
    part = dot3(rows_ref[:, :nb], w0_ref[...], ((1,), (1,)))
    rest = rows_ref[:, nb:] - dot3(part, f_ref[...], ((1,), (1,)))
    rest = dot3(rest, w1_ref[...], ((1,), (1,)))
    all_ref[:, :nb] = jnp.where(columns <= ids, part, 0.0)
    all_ref[:, nb:] = jnp.where(columns + nb <= ids, rest, 0.0)
    for d, block in enumerate(blocks):
        width = block.shape[2]
        span = pl.ds(pl.multiple_of(table_ref[order_at + d] * width, width), width)
        block[0] = rows_ref[:, span]
        block[1] = all_ref[:, span]


def panel_call(kernel, outputs, nb, *operands):
    return pl.pallas_call(
        kernel,
        out_shape=[jax.ShapeDtypeStruct((nb, nb), jnp.float32)] * outputs,
        in_specs=[pl.BlockSpec(memory_space=pltpu.VMEM)] * len(operands),
        out_specs=[pl.BlockSpec(memory_space=pltpu.VMEM)] * outputs,
        scratch_shapes=[pltpu.VMEM((LEAF, LEAF), jnp.float32)],
        compiler_params=pltpu.CompilerParams(vmem_limit_bytes=24 * 2**20),
        cost_estimate=pl.CostEstimate(
            flops=nb, transcendentals=0, bytes_accessed=nb
        ),
    )(*operands)


def first_panel(packed, nb):
    return panel_call(first_panel_kernel, 1, nb, packed)[0]


def next_panel(packed, w0):
    return panel_call(next_panel_kernel, 2, w0.shape[0], packed, w0)


def whole(memory=pltpu.VMEM):
    return pl.BlockSpec(memory_space=memory)


def block_of(array, memory=pltpu.VMEM):
    return pl.BlockSpec(array.shape, lambda *_: (0,) * array.ndim, memory_space=memory)


def faces_kernel(
    table_ref, cond_ref, ground_ref, info_ref, cells_ref, load_ref, panel_ref, basis_ref, *refs, sides, at
):
    outs, (conduct_ref, grounds_ref, given_ref, scaled_ref, held_ref, in_sems, out_sems) = refs[:6], refs[6:]
    half = given_ref.shape[1]
    lanes = pl.ds(pl.multiple_of(table_ref[at] * half, half), half)
    pieces = in_sems.shape[0]
    height = given_ref.shape[0] // pieces
    copies_in, copies_out = [], []
    for i in range(pieces):
        rows = pl.ds(i * height, height)
        copies_in.append(
            pltpu.make_async_copy(basis_ref.at[rows, lanes], held_ref.at[rows], in_sems.at[i])
        )
        copies_out.append(
            pltpu.make_async_copy(held_ref.at[rows], given_ref.at[rows], out_sems.at[i])
        )
        copies_in[i].start()
    size_x, size_y, size_z = sides
    count, width = panel_ref.shape
    tile = 64
    classes = cond_ref.shape[0]
    ports = cells_ref.shape[1]

    def by_tile(t, carry):
        rows = pl.ds(pl.multiple_of(t * tile, tile), tile)
        kind = jnp.broadcast_to(info_ref[rows, 0:1], (tile, LEAF))
        ids = jnp.broadcast_to(info_ref[rows, 1:2], (tile, LEAF))
        conduct = jnp.zeros((tile, LEAF), jnp.float32)
        grounds = jnp.zeros((tile, LEAF), jnp.float32)
        for c in range(classes):
            conduct = jnp.where(kind == c, cond_ref[c], conduct)
            grounds = jnp.where(kind == c, ground_ref[c], grounds)
        loads = jnp.zeros((tile, LEAF), jnp.float32)
        for p in range(0, ports, LEAF):
            hit = ids == cells_ref[:, p : p + LEAF]
            loads = loads + jnp.where(hit, load_ref[:, p : p + LEAF], 0.0)
        conduct_ref[rows, :] = conduct
        grounds_ref[rows, :] = grounds + jnp.sum(loads, axis=1, keepdims=True)
        for p in range(0, width, LEAF):
            part = panel_ref[rows, p : p + LEAF].astype(jnp.float32)
            scaled_ref[p // LEAF, rows, :] = (
                (conduct * part).astype(jnp.bfloat16).astype(jnp.float32)
            )
        return carry

    lax.fori_loop(0, count // tile, by_tile, 0)
    for copy_in, copy_out in zip(copies_in, copies_out):
        copy_in.wait()
        copy_out.start()
    plane = size_y * size_z
    for p in range(width // LEAF):
        lanes = slice(p * LEAF, (p + 1) * LEAF)
        outs[0][:, lanes] = scaled_ref[p, 0:plane, :].astype(jnp.bfloat16)
        outs[1][:, lanes] = scaled_ref[p, count - plane : count, :].astype(jnp.bfloat16)
        for out, at in ((outs[2], 0), (outs[3], plane - size_z)):
            face = [
                scaled_ref[p, x * plane + at : x * plane + at + size_z, :] for x in range(size_x)
            ]
            out[:, lanes] = jnp.concatenate(face, 0).astype(jnp.bfloat16)
        for out, at in ((outs[4], 0), (outs[5], size_z - 1)):
            face = scaled_ref[p, pl.ds(at, size_x * size_y, stride=size_z), :]
            out[:, lanes] = face.astype(jnp.bfloat16)
    for copy_out in copies_out:
        copy_out.wait()


def image_kernel(table_ref, panel_ref, conduct_ref, grounds_ref, *refs, sides, nb, at):
    halos, (image_ref, kept_ref, sent_ref, scaled_ref, square_ref) = refs[:6], refs[6:]
    core = table_ref[at]
    size_x, size_y, size_z = sides
    width = panel_ref.shape[1]
    plane = size_y * size_z
    subs = lax.broadcasted_iota(jnp.int32, (size_z, LEAF), 0)

    def by_lane(p, carry):
        lanes = pl.ds(pl.multiple_of(p * LEAF, LEAF), LEAF)
        x_low, x_high, y_low, y_high, z_low, z_high = (
            h[:, lanes].astype(jnp.float32) for h in halos
        )
        scaled_ref[...] = (
            (conduct_ref[...] * panel_ref[:, lanes].astype(jnp.float32))
            .astype(jnp.bfloat16)
            .astype(jnp.float32)
        )

        def cell_rows(x, y):
            at = x * plane + y * size_z
            return scaled_ref[at : at + size_z, :]

        for x in range(size_x):
            done = []
            for y in range(size_y):
                at = x * plane + y * size_z
                here = cell_rows(x, y)
                span = slice(y * size_z, (y + 1) * size_z)
                total = cell_rows(x + 1, y) if x + 1 < size_x else x_high[span, :]
                total = total + (cell_rows(x - 1, y) if x > 0 else x_low[span, :])
                span = slice(x * size_z, (x + 1) * size_z)
                total = total + (cell_rows(x, y + 1) if y + 1 < size_y else y_high[span, :])
                total = total + (cell_rows(x, y - 1) if y > 0 else y_low[span, :])
                k = x * size_y + y
                up = jnp.where(
                    subs == size_z - 1, z_high[k : k + 1, :], pltpu.roll(here, size_z - 1, 0)
                )
                down = jnp.where(subs == 0, z_low[k : k + 1, :], pltpu.roll(here, 1, 0))
                total = total + up + down
                own = slice(at, at + size_z)
                done.append(
                    conduct_ref[own, :] * (6.0 * here - total)
                    + grounds_ref[own, :] * panel_ref[at : at + size_z, lanes].astype(jnp.float32)
                )
            image_ref[x * plane : (x + 1) * plane, lanes] = jnp.concatenate(done, 0).astype(
                jnp.bfloat16
            )
        return carry

    lax.fori_loop(0, width // LEAF, by_lane, 0)

    def product(rows, cols):
        return lax.dot_general(
            panel_ref[:, rows],
            image_ref[:, cols],
            (((0,), (0,)), ((), ())),
            preferred_element_type=jnp.float32,
        )

    blocks = nb // LEAF

    first_blocks = blocks * (blocks + 1) // 2
    half = kept_ref.shape[0] // LEAF - 1

    def put_block(number, value):
        if number < first_blocks:
            owner, place = divmod(number, first_blocks // 2)
        else:
            owner, place = divmod(number - first_blocks, half - first_blocks // 2)
            place += first_blocks // 2
        kept = core == owner
        for ref, here in ((kept_ref, kept), (sent_ref, jnp.logical_not(kept))):
            at_row = pl.multiple_of(jnp.where(here, place, half) * LEAF, LEAF)
            ref[pl.ds(at_row, LEAF), :] = value

    def lower(number):
        for i in range(blocks):
            for j in range(i + 1):
                row, col = slice(i * LEAF, (i + 1) * LEAF), slice(j * LEAF, (j + 1) * LEAF)
                put_block(number, 0.5 * (square_ref[row, col] + square_ref[col, row].T))
                number += 1
        return number

    head, tail = slice(0, nb), slice(nb, 2 * nb)
    square_ref[...] = product(head, head)
    number = lower(0)
    square_ref[...] = product(tail, tail)
    number = lower(number)
    square_ref[...] = product(tail, head)
    for j in range(blocks):
        for i in range(blocks):
            row, col = slice(i * LEAF, (i + 1) * LEAF), slice(j * LEAF, (j + 1) * LEAF)
            put_block(number + j * blocks + i, square_ref[row, col])


def products_kernel(table_ref, *refs):
    del table_ref
    out, count = refs[-1], len(refs) // 2
    total = None
    for b, image in zip(refs[:count], refs[count:-1]):
        term = lax.dot_general(
            b[...], image[...], (((0,), (0,)), ((), ())), preferred_element_type=jnp.float32
        )
        total = term if total is None else total + term
    out[...] = total.astype(out.dtype)


def products(table, bases, images, lists, width, dtype):
    rows, cols = images[0].shape
    step = 512 if width % 512 == 0 else width
    parts = width // step
    steps = lists[0][1] * parts
    in_specs = [
        pl.BlockSpec(
            (rows, step), lambda t, tab, at=at: (0, tab[at + t // parts] * parts + t % parts)
        )
        for at, _ in lists
    ]
    in_specs += [pl.BlockSpec((rows, cols), lambda t, tab: (0, 0))] * len(images)
    total = steps * step
    return pl.pallas_call(
        products_kernel,
        grid_spec=pltpu.PrefetchScalarGridSpec(
            num_scalar_prefetch=1,
            grid=(steps,),
            in_specs=in_specs,
            out_specs=pl.BlockSpec((step, cols), lambda t, tab: (t, 0)),
        ),
        out_shape=jax.ShapeDtypeStruct((total, cols), dtype),
        compiler_params=pltpu.CompilerParams(vmem_limit_bytes=48 * 2**20),
        cost_estimate=pl.CostEstimate(
            flops=2 * total * cols * rows * len(bases),
            transcendentals=0,
            bytes_accessed=2 * rows * (total + cols) * len(bases) + 4 * total * cols,
        ),
    )(table, *bases, *images)


def add_kernel(table_ref, *refs):
    del table_ref
    total = refs[0][...].astype(jnp.float32)
    for got in refs[1:-1]:
        total = total + got[...].astype(jnp.float32)
    refs[-1][...] = total.astype(refs[-1].dtype)


def add_blocks(table, arrays, at, count, height, dtype):
    cols = arrays[0].shape[1]
    step = min(256, height)
    parts = height // step
    steps = count * parts
    spec = pl.BlockSpec((step, cols), lambda t, tab: (tab[at + t // parts] * parts + t % parts, 0))
    return pl.pallas_call(
        add_kernel,
        grid_spec=pltpu.PrefetchScalarGridSpec(
            num_scalar_prefetch=1,
            grid=(steps,),
            in_specs=[spec] * len(arrays),
            out_specs=pl.BlockSpec((step, cols), lambda t, tab: (t, 0)),
        ),
        out_shape=jax.ShapeDtypeStruct((steps * step, cols), dtype),
        compiler_params=pltpu.CompilerParams(vmem_limit_bytes=24 * 2**20),
        cost_estimate=pl.CostEstimate(
            flops=steps * step * cols,
            transcendentals=0,
            bytes_accessed=steps * step * cols * 4 * len(arrays),
        ),
    )(table, *arrays)


def plane_kernel(table_ref, *refs, groups, at):
    ins, outs, plane_ref = refs[: sum(groups)], refs[sum(groups) : -1], refs[-1]
    height = ins[0].shape[0]
    done = 0
    for i, count in enumerate(groups):
        total = ins[done][...].astype(jnp.float32)
        for got in ins[done + 1 : done + count]:
            total = total + got[...].astype(jnp.float32)
        plane_ref[i * height : (i + 1) * height, :] = total
        done += count
    for i, out in enumerate(outs):
        part = out.shape[0]
        rows = pl.ds(pl.multiple_of(table_ref[at + i] * part, part), part)
        out[...] = plane_ref[rows, :].astype(out.dtype)


def plane_parts(table, sums, height, at, outs):
    cols = sums[0][0][0].shape[1]

    def spec(place, block):
        if place is None:
            return pl.BlockSpec((height, cols), lambda t, tab: (block, 0))
        return pl.BlockSpec((height, cols), lambda t, tab: (tab[place], 0))

    return pl.pallas_call(
        functools.partial(plane_kernel, groups=[len(terms) for terms in sums], at=at),
        grid_spec=pltpu.PrefetchScalarGridSpec(
            num_scalar_prefetch=1,
            grid=(1,),
            in_specs=[spec(place, block) for terms in sums for _, place, block in terms],
            out_specs=[pl.BlockSpec(out.shape, lambda t, tab: (0, 0)) for out in outs],
            scratch_shapes=[pltpu.VMEM((height * len(sums), cols), jnp.float32)],
        ),
        out_shape=outs,
        compiler_params=pltpu.CompilerParams(vmem_limit_bytes=44 * 2**20),
        cost_estimate=pl.CostEstimate(
            flops=0, transcendentals=0, bytes_accessed=height * len(sums) * cols * 14
        ),
    )(table, *(array for terms in sums for array, _, _ in terms))


def swap_pairs():
    return [(0, 1), (1, 0)]


def join_kernel(table_ref, *refs, at):
    ins, outs = refs[:-2], refs[-2:]
    part = ins[0].shape[1]
    for d, block in enumerate(ins):
        rows = pl.ds(pl.multiple_of(table_ref[at + d] * part, part), part)
        for i, out in enumerate(outs):
            out[rows, :] = block[i]


def local(basis, classes, cond_table, ground_table, port_cells, port_load):
    sides = classes.shape
    cells_x, cells_y, cells_z = sides
    width_k = basis.shape[3]
    devices_x = lax.axis_size("gx")
    chips_y = lax.axis_size("gy")
    devices_z = lax.axis_size("gz")
    devices_y = 2 * chips_y
    spans = devices_x // 2
    split = spans // 2
    count = cells_x * cells_y * cells_z
    cols = PANELS * NB
    at_x, chip, core, at_z = (lax.axis_index(axis) for axis in ("gx", "gy", "core", "gz"))
    at_y = 2 * chip + core
    f32, bf16 = jnp.float32, jnp.bfloat16

    flat_basis = basis.reshape(count, width_k)
    wide = width_k // (devices_x * devices_z)
    narrow = wide // chips_y
    part = narrow // 2

    entries = []

    def put(values):
        entries.extend(values)
        return len(entries) - len(values), len(values)

    shift = core * spans * devices_z * chips_y

    def put_products(blocks):
        return [put([b + shift for b in blocks]), put(blocks)]

    lists_a, lists_b, next_a, next_b = [], [], [], []
    for d in range(devices_z):
        x = (at_z + d) % devices_z
        lists_a.append(
            put_products(
                [(zz * devices_z + x) * chips_y + y for zz in range(split) for y in range(chips_y)]
            )
        )
        next_b.append(put([zz * devices_z + x for zz in range(spans - split)]))
    for d in range(chips_y):
        y = (chip + d) % chips_y
        lists_b.append(
            put_products(
                [(zz * devices_z + x) * chips_y + y for zz in range(split, spans) for x in range(devices_z)]
            )
        )
        next_a.append(put([zz * chips_y + y for zz in range(split)]))
    leaving = [(at_x + step) % devices_x for step in range(devices_x)]
    leaving_at, _ = put(leaving + [at_x % spans * 2 + core, at_x % spans * 2 + 1 - core])
    given_at, _ = put([1 - core])
    core_at, _ = put([core])
    places_at, _ = put([(at_y - d) % devices_y for d in range(devices_y)])
    order_at, _ = put([(at_y + d) % devices_y for d in range(devices_y)])
    home_at, _ = put([at_x // spans == core])
    first_at, _ = put([((at_x * devices_z + at_z) * devices_y + at_y) * part])
    table = jnp.stack([jnp.asarray(e, jnp.int32) for e in entries])

    def move(array, axis, d):
        size = lax.axis_size(axis)
        return lax.ppermute(array, axis, [(i, (i + d) % size) for i in range(size)])

    panel_spec = pl.BlockSpec((count, cols), lambda *_: (0, 0))
    port_rows, load_rows = port_cells[None, :], port_load[None, :]
    global_x = at_x * cells_x + jnp.arange(cells_x, dtype=jnp.int32)
    global_y = at_y * cells_y + jnp.arange(cells_y, dtype=jnp.int32)
    global_z = at_z * cells_z + jnp.arange(cells_z, dtype=jnp.int32)
    flat_ids = (
        (global_x[:, None, None] * (cells_y * devices_y) + global_y[None, :, None])
        * (cells_z * devices_z)
        + global_z[None, None, :]
    )
    info = jnp.stack([classes, flat_ids], -1).reshape(count, 2)
    face_rows = [cells_y * cells_z] * 2 + [cells_x * cells_z] * 2 + [cells_x * cells_y] * 2
    outs = [jax.ShapeDtypeStruct((n, cols), bf16) for n in face_rows]
    outs += [jax.ShapeDtypeStruct((count, LEAF), f32)] * 2
    given = jax.ShapeDtypeStruct((count, width_k // 2), basis.dtype)
    *faces, conduct, grounds, given = pl.pallas_call(
        functools.partial(faces_kernel, sides=sides, at=given_at),
        out_shape=[*outs, given],
        grid_spec=pltpu.PrefetchScalarGridSpec(
            num_scalar_prefetch=1,
            grid=(1,),
            in_specs=[block_of(cond_table, pltpu.SMEM), block_of(ground_table, pltpu.SMEM)]
            + [block_of(info), block_of(port_rows), block_of(load_rows), panel_spec]
            + [pl.BlockSpec(memory_space=pl.ANY)],
            out_specs=[block_of(a) for a in outs] + [pl.BlockSpec(memory_space=pl.ANY)],
            scratch_shapes=[
                pltpu.VMEM((cols // LEAF, count, LEAF), f32),
                pltpu.VMEM((count, width_k // 2), basis.dtype),
                pltpu.SemaphoreType.DMA((4,)),
                pltpu.SemaphoreType.DMA((4,)),
            ],
        ),
        compiler_params=pltpu.CompilerParams(vmem_limit_bytes=58 * 2**20),
    )(table, cond_table, ground_table, info, port_rows, load_rows, flat_basis, flat_basis)
    halos = []
    for i, (axis, size) in enumerate(
        (("gx", devices_x), (("gy", "core"), devices_y), ("gz", devices_z))
    ):
        low, high = faces[2 * i : 2 * i + 2]
        if size == 2:
            last = lax.axis_index(axis) == 1
            got = lax.ppermute(jnp.where(last, low, high), axis, swap_pairs())
            halos.append(jnp.where(last, got, 0))
            halos.append(jnp.where(last, 0, got))
        else:
            halos.append(lax.ppermute(high, axis, [(k, k + 1) for k in range(size - 1)]))
            halos.append(lax.ppermute(low, axis, [(k + 1, k) for k in range(size - 1)]))
    other_basis = lax.ppermute(given, "core", swap_pairs())

    blocks = NB // LEAF
    lower_rows = blocks * (blocks + 1) // 2 * LEAF
    half_rows = lower_rows + blocks * NB // 2
    lead_parts = [jax.ShapeDtypeStruct((half_rows + LEAF, LEAF), f32)] * 2
    outs = [jax.ShapeDtypeStruct((count, cols), bf16), *lead_parts]
    image, lead_kept, lead_sent = pl.pallas_call(
        functools.partial(image_kernel, sides=sides, nb=NB, at=core_at),
        out_shape=outs,
        grid_spec=pltpu.PrefetchScalarGridSpec(
            num_scalar_prefetch=1,
            grid=(1,),
            in_specs=[panel_spec] + [whole()] * 8,
            out_specs=[whole()] * 3,
            scratch_shapes=[pltpu.VMEM((count, LEAF), f32), pltpu.VMEM((NB, NB), f32)],
        ),
        compiler_params=pltpu.CompilerParams(vmem_limit_bytes=54 * 2**20),
    )(table, flat_basis, conduct, grounds, *halos)

    other_image = lax.ppermute(image, "core", swap_pairs())
    other_basis = lax.ppermute(given, "core", swap_pairs())

    plane_axes = ("gy", "gz")
    chips = chips_y * devices_z

    def exchanged(rows, axes):
        return lax.all_to_all(rows, axes, split_axis=0, concat_axis=0, tiled=True)

    def for_all(own, size):
        return jnp.broadcast_to(own, (size, *own.shape))

    lead_got = lax.ppermute(lead_sent, "core", swap_pairs())
    lead_half = lead_kept[:half_rows] + lead_got[:half_rows]
    lead_terms = exchanged(lead_half.reshape(chips, -1, LEAF), plane_axes)

    def chip_products(images, lists, dtype):
        return products(table, [flat_basis, other_basis], images, lists, narrow, dtype)

    images, _ = lax.optimization_barrier(([image, other_image], lead_half))
    sent_a = [chip_products(images, lists_a[d], bf16) for d in range(1, devices_z)]
    sent_b = [chip_products(images, lists_b[d], bf16) for d in range(1, chips_y)]
    got_a = [move(a, "gz", d) for d, a in enumerate(sent_a, 1)]
    got_b = [move(a, "gy", d) for d, a in enumerate(sent_b, 1)]
    own_a, own_b = (chip_products(images, lists[0], f32) for lists in (lists_a, lists_b))
    lead_terms, _ = lax.optimization_barrier((lead_terms, (own_a, own_b)))
    own = jnp.sum(lead_terms, axis=0).reshape(devices_x, -1, LEAF)
    own = jnp.sum(exchanged(own, "gx"), axis=0)
    own = exchanged(for_all(own, devices_x), "gx").reshape(-1, LEAF)
    own = for_all(own, chips)
    (got_a, got_b), _ = lax.optimization_barrier(((got_a, got_b), own))
    lead_half = exchanged(own, plane_axes).reshape(-1, LEAF)
    sums_a, sums_b = [own_a, *got_a], [own_b, *got_b]

    further_a = [add_blocks(table, sums_a, *next_a[d], narrow, bf16) for d in range(1, chips_y)]
    further_b = [add_blocks(table, sums_b, *next_b[d], narrow, bf16) for d in range(1, devices_z)]
    lead_half, _ = lax.optimization_barrier((lead_half, (further_a, further_b)))
    further_a = [move(a, "gy", d) for d, a in enumerate(further_a, 1)]
    further_b = [move(a, "gz", d) for d, a in enumerate(further_b, 1)]
    other = lax.ppermute(lead_half, "core", swap_pairs())
    lower_half, upper_half = jnp.where(core == 0, lead_half, other), jnp.where(core == 0, other, lead_half)
    first = lower_rows // 2
    first_rows = jnp.concatenate([lower_half[:first], upper_half[:first]], 0)
    later_rows = jnp.concatenate([lower_half[first:], upper_half[first:]], 0)
    inverse_0 = first_panel(first_rows, NB)
    (further_a, further_b), inverse_0 = lax.optimization_barrier(
        ((further_a, further_b), inverse_0)
    )

    terms = []
    for zz in range(split):
        at = next_a[0][0] + zz
        terms.append([(a, at, None) for a in sums_a] + [(a, None, zz) for a in further_a])
    for zz in range(spans - split):
        at = next_b[0][0] + zz
        terms.append([(a, at, None) for a in sums_b] + [(a, None, zz) for a in further_b])
    outs = [jax.ShapeDtypeStruct((part, cols), bf16)] * devices_x
    outs += [jax.ShapeDtypeStruct((part, cols), f32)] * 2
    *x_sent, own, swapped = plane_parts(table, terms, narrow, leaving_at, outs)
    x_got = []
    for step in range(devices_x):
        pairs = []
        for x in range(devices_x):
            for y in range(devices_y):
                to = (x + step) % devices_x
                dest_x = (y % 2) * spans + to // 2
                dest_y = (y // 2) * 2 + to % 2
                if dest_x != x:
                    pairs.append((x * devices_y + y, dest_x * devices_y + dest_y))
        x_got.append(lax.ppermute(x_sent[step], ("gx", "gy", "core"), pairs))
    swapped = lax.ppermute(swapped, "core", swap_pairs())
    later_rows, _ = lax.optimization_barrier((later_rows, x_sent))
    factor_10, inverse_1 = next_panel(later_rows, inverse_0)
    (x_got, swapped), inverse_1 = lax.optimization_barrier(((x_got, swapped), inverse_1))
    pair = jax.ShapeDtypeStruct((2, part, cols // devices_y), f32)
    ins = [own, swapped, *x_got, inverse_0, factor_10, inverse_1]
    pairs = list(pl.pallas_call(
        functools.partial(factor_kernel, at=(home_at, order_at, first_at)),
        out_shape=[pair] * devices_y,
        grid_spec=pltpu.PrefetchScalarGridSpec(
            num_scalar_prefetch=1,
            grid=(1,),
            in_specs=[block_of(a) for a in ins],
            out_specs=[block_of(pair)] * devices_y,
            scratch_shapes=[pltpu.VMEM((part, cols), f32)] * 2,
        ),
        compiler_params=pltpu.CompilerParams(vmem_limit_bytes=44 * 2**20),
    )(table, *ins))
    for d in range(1, devices_y):
        route = [(i, (i + d) % devices_y) for i in range(devices_y)]
        pairs[d] = lax.ppermute(pairs[d], ("gy", "core"), route)
    out = jax.ShapeDtypeStruct((devices_y * part, cols // devices_y), f32)
    return pl.pallas_call(
        functools.partial(join_kernel, at=places_at),
        out_shape=(out, out),
        grid_spec=pltpu.PrefetchScalarGridSpec(
            num_scalar_prefetch=1,
            grid=(1,),
            in_specs=[block_of(a) for a in pairs],
            out_specs=[block_of(out)] * 2,
        ),
        compiler_params=pltpu.CompilerParams(vmem_limit_bytes=44 * 2**20),
    )(table, *pairs)


def solution(mesh):
    sizes = mesh.shape
    fine = jax.sharding.Mesh(
        mesh.devices.reshape(sizes["gx"], sizes["gy"] // 2, 2, sizes["gz"]),
        ("gx", "gy", "core", "gz"),
    )
    grid = ("gx", ("gy", "core"), "gz")
    out = P(("gx", "gz"), ("gy", "core"))
    return jax.shard_map(
        local,
        mesh=fine,
        in_specs=(P(*grid, None), P(*grid), P(), P(), P(), P()),
        out_specs=(out, out),
        check_vma=False,
    )
```

```python
import functools

import jax
import jax.numpy as jnp
from jax import lax
from jax.experimental import pallas as pl
from jax.experimental.pallas import tpu as pltpu
from jax.sharding import PartitionSpec as P

NB = 512
PANELS = 2
LEAF = 128
SUB = 8


def dot3(a, b, dims):
    a_hi = a.astype(jnp.bfloat16)
    b_hi = b.astype(jnp.bfloat16)
    a_lo = (a - a_hi.astype(jnp.float32)).astype(jnp.bfloat16)
    b_lo = (b - b_hi.astype(jnp.float32)).astype(jnp.bfloat16)

    def dot(x, y):
        return lax.dot_general(x, y, (dims, ((), ())), preferred_element_type=jnp.float32)

    return dot(a_hi, b_hi) + (dot(a_hi, b_lo) + dot(a_lo, b_hi))


def inverse_of(d):
    guess = pl.reciprocal(d, approx=True)
    return guess * (2.0 - d * guess)


def leaf_inverse(block_ref):
    lanes = lax.broadcasted_iota(jnp.int32, (SUB, LEAF), 1)
    subs = lax.broadcasted_iota(jnp.int32, (SUB, LEAF), 0)
    shape = (SUB, LEAF)
    panels = LEAF // SUB
    rows = block_ref[0:SUB, :]
    for t in range(panels):
        j0 = t * SUB
        after = t + 1 < panels

        def columns(array):
            return [jnp.broadcast_to(array[:, j0 + k : j0 + k + 1], shape) for k in range(SUB)]

        cols = columns(rows)
        p = [[jnp.broadcast_to(cols[k][i : i + 1, :], shape) for k in range(i + 1)] for i in range(SUB)]
        in_block = jnp.logical_and(lanes >= j0, lanes < j0 + SUB)
        start = jnp.where(in_block, (lanes - j0 == subs).astype(jnp.float32), rows)
        u = [jnp.broadcast_to(start[k : k + 1, :], shape) for k in range(SUB)]
        if after:
            below = block_ref[j0 + SUB : j0 + 2 * SUB, :]
            c = columns(below)
            rows = jnp.where(in_block, 0.0, below)
        inv = [None] * SUB
        factor = [[None] * SUB for _ in range(SUB)]
        for k in range(SUB):
            products = {(i, j): p[i][k] * p[j][k] for i in range(k + 1, SUB) for j in range(k + 1, i + 1)}
            inv[k] = inverse_of(p[k][k])
            for (i, j), product in products.items():
                p[i][j] = p[i][j] - product * inv[k]
            if after:
                step = c[k] * inv[k]
                rows = rows - step * u[k]
            for i in range(k + 1, SUB):
                factor[i][k] = p[i][k] * inv[k]
                u[i] = u[i] - factor[i][k] * u[k]
                if after:
                    c[i] = c[i] - step * p[i][k]
        out = u[0] * lax.rsqrt(p[0][0])
        for k in range(1, SUB):
            out = jnp.where(subs == k, u[k] * lax.rsqrt(p[k][k]), out)
        block_ref[j0 : j0 + SUB, :] = out
        if t + 2 >= panels:
            continue
        z = [None] * SUB
        for k in reversed(range(SUB)):
            z[k] = u[k] * inv[k]
            for i in range(k + 1, SUB):
                z[k] = z[k] - factor[i][k] * z[i]
        for v in range(t + 2, panels):
            below = block_ref[v * SUB : (v + 1) * SUB, :]
            upd = jnp.where(in_block, 0.0, below)
            for k in reversed(range(SUB)):
                upd = upd - jnp.broadcast_to(below[:, j0 + k : j0 + k + 1], shape) * z[k]
            block_ref[v * SUB : (v + 1) * SUB, :] = upd


def factor_inverse(s_ref, d_ref):
    width = s_ref.shape[0]
    row_ids = lax.broadcasted_iota(jnp.int32, (width, width), 0)
    col_ids = lax.broadcasted_iota(jnp.int32, (width, width), 1)
    wide_cols = lax.broadcasted_iota(jnp.int32, (LEAF, width), 1)
    leaf_rows = lax.broadcasted_iota(jnp.int32, (LEAF, LEAF), 0)
    leaf_cols = lax.broadcasted_iota(jnp.int32, (LEAF, LEAF), 1)

    def step(b, carry):
        off = pl.multiple_of(b * LEAF, LEAF)
        span = pl.ds(off, LEAF)
        d_ref[...] = s_ref[span, span]
        leaf_inverse(d_ref)
        inverse = jnp.where(leaf_rows >= leaf_cols, d_ref[...], 0.0)
        s_ref[span, span] = (leaf_rows == leaf_cols).astype(jnp.float32)
        upper = dot3(inverse, s_ref[span, :], ((1,), (0,)))
        s_ref[span, :] = upper

        @pl.when(b < width // LEAF - 1)
        def _():
            tail = jnp.where(wide_cols >= off + LEAF, upper, 0.0)
            current = s_ref[...]
            dead = jnp.logical_and(
                row_ids >= off + LEAF, jnp.logical_and(col_ids >= off, col_ids < off + LEAF)
            )
            s_ref[...] = jnp.where(dead, 0.0, current) - dot3(tail, upper, ((0,), (0,)))

        return carry

    lax.fori_loop(0, width // LEAF, step, 0)
    s_ref[...] = jnp.where(row_ids >= col_ids, s_ref[...], 0.0)


def unpack_symmetric(packed_ref, s_ref):
    at = 0
    for i in range(s_ref.shape[0] // LEAF):
        for j in range(i + 1):
            block = packed_ref[at * LEAF : (at + 1) * LEAF, :]
            s_ref[i * LEAF : (i + 1) * LEAF, j * LEAF : (j + 1) * LEAF] = block
            if j < i:
                s_ref[j * LEAF : (j + 1) * LEAF, i * LEAF : (i + 1) * LEAF] = block.T
            at += 1


def first_panel_kernel(packed_ref, w_ref, d_ref):
    unpack_symmetric(packed_ref, w_ref)
    factor_inverse(w_ref, d_ref)


def next_panel_kernel(packed_ref, w0_ref, f_ref, w_ref, d_ref):
    nb = w0_ref.shape[0]
    blocks = nb // LEAF
    unpack_symmetric(packed_ref, w_ref)
    start = packed_ref.shape[0] - blocks * nb
    below = jnp.concatenate(
        [packed_ref[start + i * nb : start + (i + 1) * nb, :] for i in range(nb // LEAF)], 1
    )
    below = dot3(below, w0_ref[...], ((1,), (1,)))
    f_ref[...] = below
    w_ref[...] = w_ref[...] - dot3(below, below, ((1,), (1,)))
    factor_inverse(w_ref, d_ref)


def factor_kernel(table_ref, own_ref, swapped_ref, *refs, at):
    home_at, order_at, first_at = at
    cols = own_ref.shape[1]
    *ins, rows_ref, all_ref = refs
    count = cols // ins[-1].shape[2]
    ins, blocks = ins[:-count], ins[-count:]
    *ins, w0_ref, f_ref, w1_ref = ins
    total = jnp.where(table_ref[home_at] != 0, own_ref[...], swapped_ref[...])
    for got in ins:
        total = total + got[...].astype(jnp.float32)
    rows_ref[...] = total
    nb = w0_ref.shape[0]
    ids = table_ref[first_at] + lax.broadcasted_iota(jnp.int32, (rows_ref.shape[0], nb), 0)
    columns = lax.broadcasted_iota(jnp.int32, (rows_ref.shape[0], nb), 1)
    part = dot3(rows_ref[:, :nb], w0_ref[...], ((1,), (1,)))
    rest = rows_ref[:, nb:] - dot3(part, f_ref[...], ((1,), (1,)))
    rest = dot3(rest, w1_ref[...], ((1,), (1,)))
    all_ref[:, :nb] = jnp.where(columns <= ids, part, 0.0)
    all_ref[:, nb:] = jnp.where(columns + nb <= ids, rest, 0.0)
    for d, block in enumerate(blocks):
        width = block.shape[2]
        span = pl.ds(pl.multiple_of(table_ref[order_at + d] * width, width), width)
        block[0] = rows_ref[:, span]
        block[1] = all_ref[:, span]


def panel_call(kernel, outputs, nb, *operands):
    return pl.pallas_call(
        kernel,
        out_shape=[jax.ShapeDtypeStruct((nb, nb), jnp.float32)] * outputs,
        in_specs=[pl.BlockSpec(memory_space=pltpu.VMEM)] * len(operands),
        out_specs=[pl.BlockSpec(memory_space=pltpu.VMEM)] * outputs,
        scratch_shapes=[pltpu.VMEM((LEAF, LEAF), jnp.float32)],
        compiler_params=pltpu.CompilerParams(vmem_limit_bytes=24 * 2**20),
        cost_estimate=pl.CostEstimate(
            flops=nb, transcendentals=0, bytes_accessed=nb
        ),
    )(*operands)


def first_panel(packed, nb):
    return panel_call(first_panel_kernel, 1, nb, packed)[0]


def next_panel(packed, w0):
    return panel_call(next_panel_kernel, 2, w0.shape[0], packed, w0)


def whole(memory=pltpu.VMEM):
    return pl.BlockSpec(memory_space=memory)


def block_of(array, memory=pltpu.VMEM):
    return pl.BlockSpec(array.shape, lambda *_: (0,) * array.ndim, memory_space=memory)


def faces_kernel(
    table_ref, cond_ref, ground_ref, info_ref, cells_ref, load_ref, panel_ref, basis_ref, *refs, sides, at, last_at
):
    *outs, conduct_ref, grounds_ref, given_ref, scaled_ref, held_ref, in_sems, out_sems = refs
    last = table_ref[last_at] != 0
    half = given_ref.shape[1]
    lanes = pl.ds(pl.multiple_of(table_ref[at] * half, half), half)
    pieces = in_sems.shape[0]
    height = given_ref.shape[0] // pieces
    copies_in, copies_out = [], []
    for i in range(pieces):
        rows = pl.ds(i * height, height)
        copies_in.append(
            pltpu.make_async_copy(basis_ref.at[rows, lanes], held_ref.at[rows], in_sems.at[i])
        )
        copies_out.append(
            pltpu.make_async_copy(held_ref.at[rows], given_ref.at[rows], out_sems.at[i])
        )
        copies_in[i].start()
    size_x, size_y, size_z = sides
    count, width = panel_ref.shape
    tile = 64
    classes = cond_ref.shape[0]
    ports = cells_ref.shape[1]

    def by_tile(t, carry):
        rows = pl.ds(pl.multiple_of(t * tile, tile), tile)
        kind = jnp.broadcast_to(info_ref[rows, 0:1], (tile, LEAF))
        ids = jnp.broadcast_to(info_ref[rows, 1:2], (tile, LEAF))
        conduct = jnp.zeros((tile, LEAF), jnp.float32)
        grounds = jnp.zeros((tile, LEAF), jnp.float32)
        for c in range(classes):
            conduct = jnp.where(kind == c, cond_ref[c], conduct)
            grounds = jnp.where(kind == c, ground_ref[c], grounds)
        loads = jnp.zeros((tile, LEAF), jnp.float32)
        for p in range(0, ports, LEAF):
            hit = ids == cells_ref[:, p : p + LEAF]
            loads = loads + jnp.where(hit, load_ref[:, p : p + LEAF], 0.0)
        conduct_ref[rows, :] = conduct
        grounds_ref[rows, :] = grounds + jnp.sum(loads, axis=1, keepdims=True)
        for p in range(0, width, LEAF):
            part = panel_ref[rows, p : p + LEAF].astype(jnp.float32)
            scaled_ref[p // LEAF, rows, :] = (
                (conduct * part).astype(jnp.bfloat16).astype(jnp.float32)
            )
        return carry

    lax.fori_loop(0, count // tile, by_tile, 0)
    for copy_in, copy_out in zip(copies_in, copies_out):
        copy_in.wait()
        copy_out.start()
    plane = size_y * size_z
    for p in range(width // LEAF):
        lanes = slice(p * LEAF, (p + 1) * LEAF)
        outs[0][:, lanes] = scaled_ref[p, 0:plane, :].astype(jnp.bfloat16)
        outs[1][:, lanes] = scaled_ref[p, count - plane : count, :].astype(jnp.bfloat16)
        for out, at in ((outs[2], 0), (outs[3], plane - size_z)):
            face = [
                scaled_ref[p, x * plane + at : x * plane + at + size_z, :] for x in range(size_x)
            ]
            out[:, lanes] = jnp.concatenate(face, 0).astype(jnp.bfloat16)
        low, high = (
            scaled_ref[p, pl.ds(at, size_x * size_y, stride=size_z), :] for at in (0, size_z - 1)
        )
        if len(outs) == 5:
            outs[4][:, lanes] = jnp.where(last, low, high).astype(jnp.bfloat16)
        else:
            outs[4][:, lanes] = low.astype(jnp.bfloat16)
            outs[5][:, lanes] = high.astype(jnp.bfloat16)
    for copy_out in copies_out:
        copy_out.wait()


def image_kernel(table_ref, panel_ref, conduct_ref, grounds_ref, *refs, sides, nb, at, last_at):
    *halos, image_ref, kept_ref, sent_ref, scaled_ref, square_ref = refs
    core = table_ref[at]
    last = table_ref[last_at] != 0
    size_x, size_y, size_z = sides
    width = panel_ref.shape[1]
    plane = size_y * size_z
    subs = lax.broadcasted_iota(jnp.int32, (size_z, LEAF), 0)

    def by_lane(p, carry):
        lanes = pl.ds(pl.multiple_of(p * LEAF, LEAF), LEAF)
        x_low, x_high, y_low, y_high, *z_halos = (h[:, lanes].astype(jnp.float32) for h in halos)
        if len(z_halos) == 1:
            z_halos = [jnp.where(last, z_halos[0], 0.0), jnp.where(last, 0.0, z_halos[0])]
        z_low, z_high = z_halos
        scaled_ref[...] = (
            (conduct_ref[...] * panel_ref[:, lanes].astype(jnp.float32))
            .astype(jnp.bfloat16)
            .astype(jnp.float32)
        )

        def cell_rows(x, y):
            at = x * plane + y * size_z
            return scaled_ref[at : at + size_z, :]

        for x in range(size_x):
            done = []
            for y in range(size_y):
                at = x * plane + y * size_z
                here = cell_rows(x, y)
                span = slice(y * size_z, (y + 1) * size_z)
                total = cell_rows(x + 1, y) if x + 1 < size_x else x_high[span, :]
                total = total + (cell_rows(x - 1, y) if x > 0 else x_low[span, :])
                span = slice(x * size_z, (x + 1) * size_z)
                total = total + (cell_rows(x, y + 1) if y + 1 < size_y else y_high[span, :])
                total = total + (cell_rows(x, y - 1) if y > 0 else y_low[span, :])
                k = x * size_y + y
                up = jnp.where(
                    subs == size_z - 1, z_high[k : k + 1, :], pltpu.roll(here, size_z - 1, 0)
                )
                down = jnp.where(subs == 0, z_low[k : k + 1, :], pltpu.roll(here, 1, 0))
                total = total + up + down
                own = slice(at, at + size_z)
                done.append(
                    conduct_ref[own, :] * (6.0 * here - total)
                    + grounds_ref[own, :] * panel_ref[at : at + size_z, lanes].astype(jnp.float32)
                )
            image_ref[x * plane : (x + 1) * plane, lanes] = jnp.concatenate(done, 0).astype(
                jnp.bfloat16
            )
        return carry

    lax.fori_loop(0, width // LEAF, by_lane, 0)

    def product(rows, cols):
        return lax.dot_general(
            panel_ref[:, rows],
            image_ref[:, cols],
            (((0,), (0,)), ((), ())),
            preferred_element_type=jnp.float32,
        )

    blocks = nb // LEAF

    first_blocks = blocks * (blocks + 1) // 2
    half = kept_ref.shape[0] // LEAF - 1

    def put_block(number, value):
        if number < first_blocks:
            owner, place = divmod(number, first_blocks // 2)
        else:
            owner, place = divmod(number - first_blocks, half - first_blocks // 2)
            place += first_blocks // 2
        kept = core == owner
        for ref, here in ((kept_ref, kept), (sent_ref, jnp.logical_not(kept))):
            at_row = pl.multiple_of(jnp.where(here, place, half) * LEAF, LEAF)
            ref[pl.ds(at_row, LEAF), :] = value

    def lower(number):
        for i in range(blocks):
            for j in range(i + 1):
                row, col = slice(i * LEAF, (i + 1) * LEAF), slice(j * LEAF, (j + 1) * LEAF)
                put_block(number, 0.5 * (square_ref[row, col] + square_ref[col, row].T))
                number += 1
        return number

    head, tail = slice(0, nb), slice(nb, 2 * nb)
    square_ref[...] = product(head, head)
    number = lower(0)
    square_ref[...] = product(tail, tail)
    number = lower(number)
    square_ref[...] = product(tail, head)
    for j in range(blocks):
        for i in range(blocks):
            row, col = slice(i * LEAF, (i + 1) * LEAF), slice(j * LEAF, (j + 1) * LEAF)
            put_block(number + j * blocks + i, square_ref[row, col])


def products_kernel(table_ref, *refs):
    del table_ref
    out, count = refs[-1], len(refs) // 2
    total = None
    for b, image in zip(refs[:count], refs[count:-1]):
        term = lax.dot_general(
            b[...], image[...], (((0,), (0,)), ((), ())), preferred_element_type=jnp.float32
        )
        total = term if total is None else total + term
    out[...] = total.astype(out.dtype)


def products(table, bases, images, lists, width, dtype):
    rows, cols = images[0].shape
    step = 512 if width % 512 == 0 else width
    parts = width // step
    steps = lists[0][1] * parts
    in_specs = [
        pl.BlockSpec(
            (rows, step), lambda t, tab, at=at: (0, tab[at + t // parts] * parts + t % parts)
        )
        for at, _ in lists
    ]
    in_specs += [pl.BlockSpec((rows, cols), lambda t, tab: (0, 0))] * len(images)
    total = steps * step
    return pl.pallas_call(
        products_kernel,
        grid_spec=pltpu.PrefetchScalarGridSpec(
            num_scalar_prefetch=1,
            grid=(steps,),
            in_specs=in_specs,
            out_specs=pl.BlockSpec((step, cols), lambda t, tab: (t, 0)),
        ),
        out_shape=jax.ShapeDtypeStruct((total, cols), dtype),
        compiler_params=pltpu.CompilerParams(vmem_limit_bytes=32 * 2**20),
        cost_estimate=pl.CostEstimate(
            flops=2 * total * cols * rows * len(bases),
            transcendentals=0,
            bytes_accessed=2 * rows * (total + cols) * len(bases) + 4 * total * cols,
        ),
    )(table, *bases, *images)


def add_kernel(table_ref, *refs):
    del table_ref
    total = refs[0][...].astype(jnp.float32)
    for got in refs[1:-1]:
        total = total + got[...].astype(jnp.float32)
    refs[-1][...] = total.astype(refs[-1].dtype)


def add_blocks(table, arrays, at, count, height, dtype):
    cols = arrays[0].shape[1]
    step = min(256, height)
    parts = height // step
    steps = count * parts
    spec = pl.BlockSpec((step, cols), lambda t, tab: (tab[at + t // parts] * parts + t % parts, 0))
    return pl.pallas_call(
        add_kernel,
        grid_spec=pltpu.PrefetchScalarGridSpec(
            num_scalar_prefetch=1,
            grid=(steps,),
            in_specs=[spec] * len(arrays),
            out_specs=pl.BlockSpec((step, cols), lambda t, tab: (t, 0)),
        ),
        out_shape=jax.ShapeDtypeStruct((steps * step, cols), dtype),
        compiler_params=pltpu.CompilerParams(vmem_limit_bytes=24 * 2**20),
        cost_estimate=pl.CostEstimate(
            flops=steps * step * cols,
            transcendentals=0,
            bytes_accessed=steps * step * cols * 4 * len(arrays),
        ),
    )(table, *arrays)


def plane_kernel(table_ref, *refs, groups, at):
    ins, outs, plane_ref = refs[: sum(groups)], refs[sum(groups) : -1], refs[-1]
    height = ins[0].shape[0]
    done = 0
    for i, count in enumerate(groups):
        total = ins[done][...].astype(jnp.float32)
        for got in ins[done + 1 : done + count]:
            total = total + got[...].astype(jnp.float32)
        plane_ref[i * height : (i + 1) * height, :] = total
        done += count
    for i, out in enumerate(outs):
        part = out.shape[0]
        rows = pl.ds(pl.multiple_of(table_ref[at + i] * part, part), part)
        out[...] = plane_ref[rows, :].astype(out.dtype)


def plane_parts(table, sums, height, at, outs):
    cols = sums[0][0][0].shape[1]

    def spec(place, block):
        if place is None:
            return pl.BlockSpec((height, cols), lambda t, tab: (block, 0))
        return pl.BlockSpec((height, cols), lambda t, tab: (tab[place], 0))

    return pl.pallas_call(
        functools.partial(plane_kernel, groups=[len(terms) for terms in sums], at=at),
        grid_spec=pltpu.PrefetchScalarGridSpec(
            num_scalar_prefetch=1,
            grid=(1,),
            in_specs=[spec(place, block) for terms in sums for _, place, block in terms],
            out_specs=[pl.BlockSpec(out.shape, lambda t, tab: (0, 0)) for out in outs],
            scratch_shapes=[pltpu.VMEM((height * len(sums), cols), jnp.float32)],
        ),
        out_shape=outs,
        compiler_params=pltpu.CompilerParams(vmem_limit_bytes=34 * 2**20),
        cost_estimate=pl.CostEstimate(
            flops=0, transcendentals=0, bytes_accessed=height * len(sums) * cols * 14
        ),
    )(table, *(array for terms in sums for array, _, _ in terms))


def swap_pairs():
    return [(0, 1), (1, 0)]


def join_kernel(table_ref, *refs, at):
    ins, outs = refs[:-2], refs[-2:]
    part = ins[0].shape[1]
    for d, block in enumerate(ins):
        rows = pl.ds(pl.multiple_of(table_ref[at + d] * part, part), part)
        for i, out in enumerate(outs):
            out[rows, :] = block[i]


def local(basis, classes, cond_table, ground_table, port_cells, port_load):
    sides = classes.shape
    cells_x, cells_y, cells_z = sides
    width_k = basis.shape[3]
    devices_x = lax.axis_size("gx")
    chips_y = lax.axis_size("gy")
    devices_z = lax.axis_size("gz")
    devices_y = 2 * chips_y
    spans = devices_x // 2
    split = spans // 2
    count = cells_x * cells_y * cells_z
    cols = PANELS * NB
    at_x, chip, core, at_z = (lax.axis_index(axis) for axis in ("gx", "gy", "core", "gz"))
    at_y = 2 * chip + core
    f32, bf16 = jnp.float32, jnp.bfloat16

    flat_basis = basis.reshape(count, width_k)
    wide = width_k // (devices_x * devices_z)
    narrow = wide // chips_y
    part = narrow // 2

    entries = []

    def put(values):
        entries.extend(values)
        return len(entries) - len(values), len(values)

    shift = core * spans * devices_z * chips_y

    def put_products(blocks):
        return [put([b + shift for b in blocks]), put(blocks)]

    lists_a, lists_b, next_a, next_b = [], [], [], []
    for d in range(devices_z):
        x = (at_z + d) % devices_z
        lists_a.append(
            put_products(
                [(zz * devices_z + x) * chips_y + y for zz in range(split) for y in range(chips_y)]
            )
        )
        next_b.append(put([zz * devices_z + x for zz in range(spans - split)]))
    for d in range(chips_y):
        y = (chip + d) % chips_y
        lists_b.append(
            put_products(
                [(zz * devices_z + x) * chips_y + y for zz in range(split, spans) for x in range(devices_z)]
            )
        )
        next_a.append(put([zz * chips_y + y for zz in range(split)]))
    leaving = [(at_x + step) % devices_x for step in range(devices_x)]
    leaving_at, _ = put(leaving + [at_x % spans * 2 + core, at_x % spans * 2 + 1 - core])
    given_at, _ = put([1 - core])
    core_at, _ = put([core])
    last_at, _ = put([at_z == 1])
    places_at, _ = put([(at_y - d) % devices_y for d in range(devices_y)])
    order_at, _ = put([(at_y + d) % devices_y for d in range(devices_y)])
    home_at, _ = put([at_x // spans == core])
    first_at, _ = put([((at_x * devices_z + at_z) * devices_y + at_y) * part])
    table = jnp.stack([jnp.asarray(e, jnp.int32) for e in entries])

    def move(array, axis, d):
        size = lax.axis_size(axis)
        return lax.ppermute(array, axis, [(i, (i + d) % size) for i in range(size)])

    panel_spec = pl.BlockSpec((count, cols), lambda *_: (0, 0))
    port_rows, load_rows = port_cells[None, :], port_load[None, :]
    global_x = at_x * cells_x + jnp.arange(cells_x, dtype=jnp.int32)
    global_y = at_y * cells_y + jnp.arange(cells_y, dtype=jnp.int32)
    global_z = at_z * cells_z + jnp.arange(cells_z, dtype=jnp.int32)
    flat_ids = (
        (global_x[:, None, None] * (cells_y * devices_y) + global_y[None, :, None])
        * (cells_z * devices_z)
        + global_z[None, None, :]
    )
    info = jnp.stack([classes, flat_ids], -1).reshape(count, 2)
    face_rows = [cells_y * cells_z] * 2 + [cells_x * cells_z] * 2
    face_rows += [cells_x * cells_y] * (1 if devices_z == 2 else 2)
    outs = [jax.ShapeDtypeStruct((n, cols), bf16) for n in face_rows]
    outs += [jax.ShapeDtypeStruct((count, LEAF), f32)] * 2
    given = jax.ShapeDtypeStruct((count, width_k // 2), basis.dtype)
    *faces, conduct, grounds, given = pl.pallas_call(
        functools.partial(faces_kernel, sides=sides, at=given_at, last_at=last_at),
        out_shape=[*outs, given],
        grid_spec=pltpu.PrefetchScalarGridSpec(
            num_scalar_prefetch=1,
            grid=(1,),
            in_specs=[block_of(cond_table, pltpu.SMEM), block_of(ground_table, pltpu.SMEM)]
            + [block_of(info), block_of(port_rows), block_of(load_rows), panel_spec]
            + [pl.BlockSpec(memory_space=pl.ANY)],
            out_specs=[block_of(a) for a in outs] + [pl.BlockSpec(memory_space=pl.ANY)],
            scratch_shapes=[
                pltpu.VMEM((cols // LEAF, count, LEAF), f32),
                pltpu.VMEM((count, width_k // 2), basis.dtype),
                pltpu.SemaphoreType.DMA((4,)),
                pltpu.SemaphoreType.DMA((4,)),
            ],
        ),
        compiler_params=pltpu.CompilerParams(vmem_limit_bytes=58 * 2**20),
    )(table, cond_table, ground_table, info, port_rows, load_rows, flat_basis, flat_basis)
    halos = []
    for i, (axis, size) in enumerate(
        (("gx", devices_x), (("gy", "core"), devices_y), ("gz", devices_z))
    ):
        if i == 2 and size == 2:
            halos.append(lax.ppermute(faces[4], axis, swap_pairs()))
            continue
        low, high = faces[2 * i : 2 * i + 2]
        halos.append(lax.ppermute(high, axis, [(k, k + 1) for k in range(size - 1)]))
        halos.append(lax.ppermute(low, axis, [(k + 1, k) for k in range(size - 1)]))

    blocks = NB // LEAF
    lower_rows = blocks * (blocks + 1) // 2 * LEAF
    half_rows = lower_rows + blocks * NB // 2
    lead_parts = [jax.ShapeDtypeStruct((half_rows + LEAF, LEAF), f32)] * 2
    outs = [jax.ShapeDtypeStruct((count, cols), bf16), *lead_parts]
    image, lead_kept, lead_sent = pl.pallas_call(
        functools.partial(image_kernel, sides=sides, nb=NB, at=core_at, last_at=last_at),
        out_shape=outs,
        grid_spec=pltpu.PrefetchScalarGridSpec(
            num_scalar_prefetch=1,
            grid=(1,),
            in_specs=[panel_spec] + [whole()] * (2 + len(halos)),
            out_specs=[whole()] * 3,
            scratch_shapes=[pltpu.VMEM((count, LEAF), f32), pltpu.VMEM((NB, NB), f32)],
        ),
        compiler_params=pltpu.CompilerParams(vmem_limit_bytes=54 * 2**20),
    )(table, flat_basis, conduct, grounds, *halos)

    other_image = lax.ppermute(image, "core", swap_pairs())
    other_basis = lax.ppermute(given, "core", swap_pairs())

    plane_axes = ("gy", "gz")
    chips = chips_y * devices_z

    def exchanged(rows, axes):
        return lax.all_to_all(rows, axes, split_axis=0, concat_axis=0, tiled=True)

    def for_all(own, size):
        return jnp.broadcast_to(own, (size, *own.shape))

    lead_got = lax.ppermute(lead_sent, "core", swap_pairs())
    lead_half = lead_kept[:half_rows] + lead_got[:half_rows]
    lead_terms = exchanged(lead_half.reshape(chips, -1, LEAF), plane_axes)

    def chip_products(images, lists, dtype):
        return products(table, [flat_basis, other_basis], images, lists, narrow, dtype)

    images, _ = lax.optimization_barrier(([image, other_image], lead_half))
    sent_a = [chip_products(images, lists_a[d], bf16) for d in range(1, devices_z)]
    sent_b = [chip_products(images, lists_b[d], bf16) for d in range(1, chips_y)]
    got_a = [move(a, "gz", d) for d, a in enumerate(sent_a, 1)]
    got_b = [move(a, "gy", d) for d, a in enumerate(sent_b, 1)]
    own_a, own_b = (chip_products(images, lists[0], f32) for lists in (lists_a, lists_b))
    lead_terms, _ = lax.optimization_barrier((lead_terms, (own_a, own_b)))
    own = jnp.sum(lead_terms, axis=0).reshape(devices_x, -1, LEAF)
    own = jnp.sum(exchanged(own, "gx"), axis=0)
    own = exchanged(for_all(own, devices_x), "gx").reshape(-1, LEAF)
    own = for_all(own, chips)
    (got_a, got_b), _ = lax.optimization_barrier(((got_a, got_b), own))
    lead_half = exchanged(own, plane_axes).reshape(-1, LEAF)
    sums_a, sums_b = [own_a, *got_a], [own_b, *got_b]

    further_a = [add_blocks(table, sums_a, *next_a[d], narrow, bf16) for d in range(1, chips_y)]
    further_b = [add_blocks(table, sums_b, *next_b[d], narrow, bf16) for d in range(1, devices_z)]
    lead_half, _ = lax.optimization_barrier((lead_half, (further_a, further_b)))
    further_a = [move(a, "gy", d) for d, a in enumerate(further_a, 1)]
    further_b = [move(a, "gz", d) for d, a in enumerate(further_b, 1)]
    other = lax.ppermute(lead_half, "core", swap_pairs())
    lower_half, upper_half = jnp.where(core == 0, lead_half, other), jnp.where(core == 0, other, lead_half)
    first = lower_rows // 2
    first_rows = jnp.concatenate([lower_half[:first], upper_half[:first]], 0)
    later_rows = jnp.concatenate([lower_half[first:], upper_half[first:]], 0)
    inverse_0 = first_panel(first_rows, NB)
    (further_a, further_b), inverse_0 = lax.optimization_barrier(
        ((further_a, further_b), inverse_0)
    )

    terms = []
    for zz in range(split):
        at = next_a[0][0] + zz
        terms.append([(a, at, None) for a in sums_a] + [(a, None, zz) for a in further_a])
    for zz in range(spans - split):
        at = next_b[0][0] + zz
        terms.append([(a, at, None) for a in sums_b] + [(a, None, zz) for a in further_b])
    outs = [jax.ShapeDtypeStruct((part, cols), bf16)] * devices_x
    outs += [jax.ShapeDtypeStruct((part, cols), f32)] * 2
    *x_sent, own, swapped = plane_parts(table, terms, narrow, leaving_at, outs)
    x_got = []
    for step in range(devices_x):
        pairs = []
        for x in range(devices_x):
            for y in range(devices_y):
                to = (x + step) % devices_x
                dest_x = (y % 2) * spans + to // 2
                dest_y = (y // 2) * 2 + to % 2
                if dest_x != x:
                    pairs.append((x * devices_y + y, dest_x * devices_y + dest_y))
        x_got.append(lax.ppermute(x_sent[step], ("gx", "gy", "core"), pairs))
    swapped = lax.ppermute(swapped, "core", swap_pairs())
    later_rows, _ = lax.optimization_barrier((later_rows, x_sent))
    factor_10, inverse_1 = next_panel(later_rows, inverse_0)
    (x_got, swapped), inverse_1 = lax.optimization_barrier(((x_got, swapped), inverse_1))
    pair = jax.ShapeDtypeStruct((2, part, cols // devices_y), f32)
    ins = [own, swapped, *x_got, inverse_0, factor_10, inverse_1]
    pairs = list(pl.pallas_call(
        functools.partial(factor_kernel, at=(home_at, order_at, first_at)),
        out_shape=[pair] * devices_y,
        grid_spec=pltpu.PrefetchScalarGridSpec(
            num_scalar_prefetch=1,
            grid=(1,),
            in_specs=[block_of(a) for a in ins],
            out_specs=[block_of(pair)] * devices_y,
            scratch_shapes=[pltpu.VMEM((part, cols), f32)] * 2,
        ),
        compiler_params=pltpu.CompilerParams(vmem_limit_bytes=44 * 2**20),
    )(table, *ins))
    for d in range(1, devices_y):
        route = [(i, (i + d) % devices_y) for i in range(devices_y)]
        pairs[d] = lax.ppermute(pairs[d], ("gy", "core"), route)
    out = jax.ShapeDtypeStruct((devices_y * part, cols // devices_y), f32)
    return pl.pallas_call(
        functools.partial(join_kernel, at=places_at),
        out_shape=(out, out),
        grid_spec=pltpu.PrefetchScalarGridSpec(
            num_scalar_prefetch=1,
            grid=(1,),
            in_specs=[block_of(a) for a in pairs],
            out_specs=[block_of(out)] * 2,
        ),
        compiler_params=pltpu.CompilerParams(vmem_limit_bytes=44 * 2**20),
    )(table, *pairs)


def solution(mesh):
    sizes = mesh.shape
    fine = jax.sharding.Mesh(
        mesh.devices.reshape(sizes["gx"], sizes["gy"] // 2, 2, sizes["gz"]),
        ("gx", "gy", "core", "gz"),
    )
    grid = ("gx", ("gy", "core"), "gz")
    out = P(("gx", "gz"), ("gy", "core"))
    return jax.shard_map(
        local,
        mesh=fine,
        in_specs=(P(*grid, None), P(*grid), P(), P(), P(), P()),
        out_specs=(out, out),
        check_vma=False,
    )
```

```python
import functools

import jax
import jax.numpy as jnp
from jax import lax
from jax.experimental import pallas as pl
from jax.experimental.pallas import tpu as pltpu
from jax.sharding import PartitionSpec as P

NB = 512
PANELS = 2
LEAF = 128
SUB = 8


def dot3(a, b, dims):
    a_hi = a.astype(jnp.bfloat16)
    b_hi = b.astype(jnp.bfloat16)
    a_lo = (a - a_hi.astype(jnp.float32)).astype(jnp.bfloat16)
    b_lo = (b - b_hi.astype(jnp.float32)).astype(jnp.bfloat16)

    def dot(x, y):
        return lax.dot_general(x, y, (dims, ((), ())), preferred_element_type=jnp.float32)

    return dot(a_hi, b_hi) + (dot(a_hi, b_lo) + dot(a_lo, b_hi))


def inverse_of(d):
    guess = pl.reciprocal(d, approx=True)
    return guess * (2.0 - d * guess)


def leaf_inverse(block_ref):
    lanes = lax.broadcasted_iota(jnp.int32, (SUB, LEAF), 1)
    subs = lax.broadcasted_iota(jnp.int32, (SUB, LEAF), 0)
    shape = (SUB, LEAF)
    panels = LEAF // SUB
    rows = block_ref[0:SUB, :]
    for t in range(panels):
        j0 = t * SUB
        after = t + 1 < panels

        def columns(array):
            return [jnp.broadcast_to(array[:, j0 + k : j0 + k + 1], shape) for k in range(SUB)]

        cols = columns(rows)
        p = [[jnp.broadcast_to(cols[k][i : i + 1, :], shape) for k in range(i + 1)] for i in range(SUB)]
        in_block = jnp.logical_and(lanes >= j0, lanes < j0 + SUB)
        start = jnp.where(in_block, (lanes - j0 == subs).astype(jnp.float32), rows)
        u = [jnp.broadcast_to(start[k : k + 1, :], shape) for k in range(SUB)]
        if after:
            below = block_ref[j0 + SUB : j0 + 2 * SUB, :]
            c = columns(below)
            rows = jnp.where(in_block, 0.0, below)
        inv = [None] * SUB
        factor = [[None] * SUB for _ in range(SUB)]
        for k in range(SUB):
            products = {(i, j): p[i][k] * p[j][k] for i in range(k + 1, SUB) for j in range(k + 1, i + 1)}
            inv[k] = inverse_of(p[k][k])
            for (i, j), product in products.items():
                p[i][j] = p[i][j] - product * inv[k]
            if after:
                step = c[k] * inv[k]
                rows = rows - step * u[k]
            for i in range(k + 1, SUB):
                factor[i][k] = p[i][k] * inv[k]
                u[i] = u[i] - factor[i][k] * u[k]
                if after:
                    c[i] = c[i] - step * p[i][k]
        out = u[0] * lax.rsqrt(p[0][0])
        for k in range(1, SUB):
            out = jnp.where(subs == k, u[k] * lax.rsqrt(p[k][k]), out)
        block_ref[j0 : j0 + SUB, :] = out
        if t + 2 >= panels:
            continue
        z = [None] * SUB
        for k in reversed(range(SUB)):
            z[k] = u[k] * inv[k]
            for i in range(k + 1, SUB):
                z[k] = z[k] - factor[i][k] * z[i]
        for v in range(t + 2, panels):
            below = block_ref[v * SUB : (v + 1) * SUB, :]
            upd = jnp.where(in_block, 0.0, below)
            for k in reversed(range(SUB)):
                upd = upd - jnp.broadcast_to(below[:, j0 + k : j0 + k + 1], shape) * z[k]
            block_ref[v * SUB : (v + 1) * SUB, :] = upd


def factor_inverse(s_ref, d_ref):
    width = s_ref.shape[0]
    row_ids = lax.broadcasted_iota(jnp.int32, (width, width), 0)
    col_ids = lax.broadcasted_iota(jnp.int32, (width, width), 1)
    wide_cols = lax.broadcasted_iota(jnp.int32, (LEAF, width), 1)
    leaf_rows = lax.broadcasted_iota(jnp.int32, (LEAF, LEAF), 0)
    leaf_cols = lax.broadcasted_iota(jnp.int32, (LEAF, LEAF), 1)

    def step(b, carry):
        off = pl.multiple_of(b * LEAF, LEAF)
        span = pl.ds(off, LEAF)
        d_ref[...] = s_ref[span, span]
        leaf_inverse(d_ref)
        inverse = jnp.where(leaf_rows >= leaf_cols, d_ref[...], 0.0)
        s_ref[span, span] = (leaf_rows == leaf_cols).astype(jnp.float32)
        upper = dot3(inverse, s_ref[span, :], ((1,), (0,)))
        s_ref[span, :] = upper

        @pl.when(b < width // LEAF - 1)
        def _():
            tail = jnp.where(wide_cols >= off + LEAF, upper, 0.0)
            current = s_ref[...]
            dead = jnp.logical_and(
                row_ids >= off + LEAF, jnp.logical_and(col_ids >= off, col_ids < off + LEAF)
            )
            s_ref[...] = jnp.where(dead, 0.0, current) - dot3(tail, upper, ((0,), (0,)))

        return carry

    lax.fori_loop(0, width // LEAF, step, 0)
    s_ref[...] = jnp.where(row_ids >= col_ids, s_ref[...], 0.0)


def unpack_symmetric(packed_ref, s_ref):
    at = 0
    for i in range(s_ref.shape[0] // LEAF):
        for j in range(i + 1):
            block = packed_ref[at * LEAF : (at + 1) * LEAF, :]
            s_ref[i * LEAF : (i + 1) * LEAF, j * LEAF : (j + 1) * LEAF] = block
            if j < i:
                s_ref[j * LEAF : (j + 1) * LEAF, i * LEAF : (i + 1) * LEAF] = block.T
            at += 1


def first_panel_kernel(packed_ref, w_ref, d_ref):
    unpack_symmetric(packed_ref, w_ref)
    factor_inverse(w_ref, d_ref)


def next_panel_kernel(packed_ref, w0_ref, f_ref, w_ref, d_ref):
    nb = w0_ref.shape[0]
    blocks = nb // LEAF
    unpack_symmetric(packed_ref, w_ref)
    start = packed_ref.shape[0] - blocks * nb
    below = jnp.concatenate(
        [packed_ref[start + i * nb : start + (i + 1) * nb, :] for i in range(nb // LEAF)], 1
    )
    below = dot3(below, w0_ref[...], ((1,), (1,)))
    f_ref[...] = below
    w_ref[...] = w_ref[...] - dot3(below, below, ((1,), (1,)))
    factor_inverse(w_ref, d_ref)


def factor_kernel(table_ref, own_ref, swapped_ref, *refs, at):
    home_at, order_at, first_at = at
    cols = own_ref.shape[1]
    *ins, rows_ref, all_ref = refs
    count = cols // ins[-1].shape[2]
    ins, blocks = ins[:-count], ins[-count:]
    *ins, w0_ref, f_ref, w1_ref = ins
    total = jnp.where(table_ref[home_at] != 0, own_ref[...], swapped_ref[...])
    for got in ins:
        total = total + got[...].astype(jnp.float32)
    rows_ref[...] = total
    nb = w0_ref.shape[0]
    ids = table_ref[first_at] + lax.broadcasted_iota(jnp.int32, (rows_ref.shape[0], nb), 0)
    columns = lax.broadcasted_iota(jnp.int32, (rows_ref.shape[0], nb), 1)
    part = dot3(rows_ref[:, :nb], w0_ref[...], ((1,), (1,)))
    rest = rows_ref[:, nb:] - dot3(part, f_ref[...], ((1,), (1,)))
    rest = dot3(rest, w1_ref[...], ((1,), (1,)))
    all_ref[:, :nb] = jnp.where(columns <= ids, part, 0.0)
    all_ref[:, nb:] = jnp.where(columns + nb <= ids, rest, 0.0)
    for d, block in enumerate(blocks):
        width = block.shape[2]
        span = pl.ds(pl.multiple_of(table_ref[order_at + d] * width, width), width)
        block[0] = rows_ref[:, span]
        block[1] = all_ref[:, span]


def panel_call(kernel, outputs, nb, *operands):
    return pl.pallas_call(
        kernel,
        out_shape=[jax.ShapeDtypeStruct((nb, nb), jnp.float32)] * outputs,
        in_specs=[pl.BlockSpec(memory_space=pltpu.VMEM)] * len(operands),
        out_specs=[pl.BlockSpec(memory_space=pltpu.VMEM)] * outputs,
        scratch_shapes=[pltpu.VMEM((LEAF, LEAF), jnp.float32)],
        compiler_params=pltpu.CompilerParams(vmem_limit_bytes=24 * 2**20),
        cost_estimate=pl.CostEstimate(
            flops=nb, transcendentals=0, bytes_accessed=nb
        ),
    )(*operands)


def first_panel(packed, nb):
    return panel_call(first_panel_kernel, 1, nb, packed)[0]


def next_panel(packed, w0):
    return panel_call(next_panel_kernel, 2, w0.shape[0], packed, w0)


def whole(memory=pltpu.VMEM):
    return pl.BlockSpec(memory_space=memory)


def block_of(array, memory=pltpu.VMEM):
    return pl.BlockSpec(array.shape, lambda *_: (0,) * array.ndim, memory_space=memory)


def faces_kernel(
    table_ref, cond_ref, ground_ref, info_ref, cells_ref, load_ref, panel_ref, basis_ref, *refs, sides, at, last_at
):
    *outs, conduct_ref, grounds_ref, given_ref, scaled_ref, held_ref, in_sems, out_sems = refs
    last = table_ref[last_at] != 0
    half = given_ref.shape[1]
    lanes = pl.ds(pl.multiple_of(table_ref[at] * half, half), half)
    pieces = in_sems.shape[0]
    height = given_ref.shape[0] // pieces
    copies_in, copies_out = [], []
    for i in range(pieces):
        rows = pl.ds(i * height, height)
        copies_in.append(
            pltpu.make_async_copy(basis_ref.at[rows, lanes], held_ref.at[rows], in_sems.at[i])
        )
        copies_out.append(
            pltpu.make_async_copy(held_ref.at[rows], given_ref.at[rows], out_sems.at[i])
        )
        copies_in[i].start()
    size_x, size_y, size_z = sides
    count, width = panel_ref.shape
    tile = 64
    classes = cond_ref.shape[0]
    ports = cells_ref.shape[1]

    def by_tile(t, carry):
        rows = pl.ds(pl.multiple_of(t * tile, tile), tile)
        kind = jnp.broadcast_to(info_ref[rows, 0:1], (tile, LEAF))
        ids = jnp.broadcast_to(info_ref[rows, 1:2], (tile, LEAF))
        conduct = jnp.zeros((tile, LEAF), jnp.float32)
        grounds = jnp.zeros((tile, LEAF), jnp.float32)
        for c in range(classes):
            conduct = jnp.where(kind == c, cond_ref[c], conduct)
            grounds = jnp.where(kind == c, ground_ref[c], grounds)
        loads = jnp.zeros((tile, LEAF), jnp.float32)
        for p in range(0, ports, LEAF):
            hit = ids == cells_ref[:, p : p + LEAF]
            loads = loads + jnp.where(hit, load_ref[:, p : p + LEAF], 0.0)
        conduct_ref[rows, :] = conduct
        grounds_ref[rows, :] = grounds + jnp.sum(loads, axis=1, keepdims=True)
        for p in range(0, width, LEAF):
            part = panel_ref[rows, p : p + LEAF].astype(jnp.float32)
            scaled_ref[p // LEAF, rows, :] = (
                (conduct * part).astype(jnp.bfloat16).astype(jnp.float32)
            )
        return carry

    lax.fori_loop(0, count // tile, by_tile, 0)
    for copy_in, copy_out in zip(copies_in, copies_out):
        copy_in.wait()
        copy_out.start()
    plane = size_y * size_z
    for p in range(width // LEAF):
        lanes = slice(p * LEAF, (p + 1) * LEAF)
        outs[0][:, lanes] = scaled_ref[p, 0:plane, :].astype(jnp.bfloat16)
        outs[1][:, lanes] = scaled_ref[p, count - plane : count, :].astype(jnp.bfloat16)
        for out, at in ((outs[2], 0), (outs[3], plane - size_z)):
            face = [
                scaled_ref[p, x * plane + at : x * plane + at + size_z, :] for x in range(size_x)
            ]
            out[:, lanes] = jnp.concatenate(face, 0).astype(jnp.bfloat16)
        low, high = (
            scaled_ref[p, pl.ds(at, size_x * size_y, stride=size_z), :] for at in (0, size_z - 1)
        )
        if len(outs) == 5:
            outs[4][:, lanes] = jnp.where(last, low, high).astype(jnp.bfloat16)
        else:
            outs[4][:, lanes] = low.astype(jnp.bfloat16)
            outs[5][:, lanes] = high.astype(jnp.bfloat16)
    for copy_out in copies_out:
        copy_out.wait()


def image_kernel(table_ref, panel_ref, conduct_ref, grounds_ref, *refs, sides, nb, at, last_at):
    *halos, image_ref, kept_ref, sent_ref, scaled_ref, square_ref = refs
    core = table_ref[at]
    last = table_ref[last_at] != 0
    size_x, size_y, size_z = sides
    width = panel_ref.shape[1]
    plane = size_y * size_z
    subs = lax.broadcasted_iota(jnp.int32, (size_z, LEAF), 0)

    def by_lane(p, carry):
        lanes = pl.ds(pl.multiple_of(p * LEAF, LEAF), LEAF)
        x_low, x_high, y_low, y_high, *z_halos = (h[:, lanes].astype(jnp.float32) for h in halos)
        if len(z_halos) == 1:
            z_halos = [jnp.where(last, z_halos[0], 0.0), jnp.where(last, 0.0, z_halos[0])]
        z_low, z_high = z_halos
        scaled_ref[...] = (
            (conduct_ref[...] * panel_ref[:, lanes].astype(jnp.float32))
            .astype(jnp.bfloat16)
            .astype(jnp.float32)
        )

        def cell_rows(x, y):
            at = x * plane + y * size_z
            return scaled_ref[at : at + size_z, :]

        for x in range(size_x):
            done = []
            for y in range(size_y):
                at = x * plane + y * size_z
                here = cell_rows(x, y)
                span = slice(y * size_z, (y + 1) * size_z)
                total = cell_rows(x + 1, y) if x + 1 < size_x else x_high[span, :]
                total = total + (cell_rows(x - 1, y) if x > 0 else x_low[span, :])
                span = slice(x * size_z, (x + 1) * size_z)
                total = total + (cell_rows(x, y + 1) if y + 1 < size_y else y_high[span, :])
                total = total + (cell_rows(x, y - 1) if y > 0 else y_low[span, :])
                k = x * size_y + y
                up = jnp.where(
                    subs == size_z - 1, z_high[k : k + 1, :], pltpu.roll(here, size_z - 1, 0)
                )
                down = jnp.where(subs == 0, z_low[k : k + 1, :], pltpu.roll(here, 1, 0))
                total = total + up + down
                own = slice(at, at + size_z)
                done.append(
                    conduct_ref[own, :] * (6.0 * here - total)
                    + grounds_ref[own, :] * panel_ref[at : at + size_z, lanes].astype(jnp.float32)
                )
            image_ref[x * plane : (x + 1) * plane, lanes] = jnp.concatenate(done, 0).astype(
                jnp.bfloat16
            )
        return carry

    lax.fori_loop(0, width // LEAF, by_lane, 0)

    def product(rows, cols):
        return lax.dot_general(
            panel_ref[:, rows],
            image_ref[:, cols],
            (((0,), (0,)), ((), ())),
            preferred_element_type=jnp.float32,
        )

    blocks = nb // LEAF

    first_blocks = blocks * (blocks + 1) // 2
    half = kept_ref.shape[0] // LEAF - 1

    def put_block(number, value):
        if number < first_blocks:
            owner, place = divmod(number, first_blocks // 2)
        else:
            owner, place = divmod(number - first_blocks, half - first_blocks // 2)
            place += first_blocks // 2
        kept = core == owner
        for ref, here in ((kept_ref, kept), (sent_ref, jnp.logical_not(kept))):
            at_row = pl.multiple_of(jnp.where(here, place, half) * LEAF, LEAF)
            ref[pl.ds(at_row, LEAF), :] = value

    def lower(number):
        for i in range(blocks):
            for j in range(i + 1):
                row, col = slice(i * LEAF, (i + 1) * LEAF), slice(j * LEAF, (j + 1) * LEAF)
                put_block(number, 0.5 * (square_ref[row, col] + square_ref[col, row].T))
                number += 1
        return number

    head, tail = slice(0, nb), slice(nb, 2 * nb)
    square_ref[...] = product(head, head)
    number = lower(0)
    square_ref[...] = product(tail, tail)
    number = lower(number)
    square_ref[...] = product(tail, head)
    for j in range(blocks):
        for i in range(blocks):
            row, col = slice(i * LEAF, (i + 1) * LEAF), slice(j * LEAF, (j + 1) * LEAF)
            put_block(number + j * blocks + i, square_ref[row, col])


def products_kernel(table_ref, *refs):
    del table_ref
    out, count = refs[-1], len(refs) // 2
    bases = jnp.concatenate([ref[...] for ref in refs[:count]], 0)
    images = jnp.concatenate([ref[...] for ref in refs[count:-1]], 0)
    total = lax.dot_general(
        bases, images, (((0,), (0,)), ((), ())), preferred_element_type=jnp.float32
    )
    out[...] = total.astype(out.dtype)


def products(table, bases, images, lists, width, dtype):
    rows, cols = images[0].shape
    step = 512 if width % 512 == 0 else width
    parts = width // step
    steps = lists[0][1] * parts
    in_specs = [
        pl.BlockSpec(
            (rows, step), lambda t, tab, at=at: (0, tab[at + t // parts] * parts + t % parts)
        )
        for at, _ in lists
    ]
    in_specs += [pl.BlockSpec((rows, cols), lambda t, tab: (0, 0))] * len(images)
    total = steps * step
    return pl.pallas_call(
        products_kernel,
        grid_spec=pltpu.PrefetchScalarGridSpec(
            num_scalar_prefetch=1,
            grid=(steps,),
            in_specs=in_specs,
            out_specs=pl.BlockSpec((step, cols), lambda t, tab: (t, 0)),
        ),
        out_shape=jax.ShapeDtypeStruct((total, cols), dtype),
        compiler_params=pltpu.CompilerParams(vmem_limit_bytes=48 * 2**20),
        cost_estimate=pl.CostEstimate(
            flops=2 * total * cols * rows * len(bases),
            transcendentals=0,
            bytes_accessed=2 * rows * (total + cols) * len(bases) + 4 * total * cols,
        ),
    )(table, *bases, *images)


def add_kernel(table_ref, *refs):
    del table_ref
    total = refs[0][...].astype(jnp.float32)
    for got in refs[1:-1]:
        total = total + got[...].astype(jnp.float32)
    refs[-1][...] = total.astype(refs[-1].dtype)


def add_blocks(table, arrays, at, count, height, dtype):
    cols = arrays[0].shape[1]
    step = min(256, height)
    parts = height // step
    steps = count * parts
    spec = pl.BlockSpec((step, cols), lambda t, tab: (tab[at + t // parts] * parts + t % parts, 0))
    return pl.pallas_call(
        add_kernel,
        grid_spec=pltpu.PrefetchScalarGridSpec(
            num_scalar_prefetch=1,
            grid=(steps,),
            in_specs=[spec] * len(arrays),
            out_specs=pl.BlockSpec((step, cols), lambda t, tab: (t, 0)),
        ),
        out_shape=jax.ShapeDtypeStruct((steps * step, cols), dtype),
        compiler_params=pltpu.CompilerParams(vmem_limit_bytes=24 * 2**20),
        cost_estimate=pl.CostEstimate(
            flops=steps * step * cols,
            transcendentals=0,
            bytes_accessed=steps * step * cols * 4 * len(arrays),
        ),
    )(table, *arrays)


def plane_kernel(table_ref, *refs, groups, at):
    ins, outs, plane_ref = refs[: sum(groups)], refs[sum(groups) : -1], refs[-1]
    height = ins[0].shape[0]
    done = 0
    for i, count in enumerate(groups):
        total = ins[done][...].astype(jnp.float32)
        for got in ins[done + 1 : done + count]:
            total = total + got[...].astype(jnp.float32)
        plane_ref[i * height : (i + 1) * height, :] = total
        done += count
    for i, out in enumerate(outs):
        part = out.shape[0]
        rows = pl.ds(pl.multiple_of(table_ref[at + i] * part, part), part)
        out[...] = plane_ref[rows, :].astype(out.dtype)


def plane_parts(table, sums, height, at, outs):
    cols = sums[0][0][0].shape[1]

    def spec(place, block):
        if place is None:
            return pl.BlockSpec((height, cols), lambda t, tab: (block, 0))
        return pl.BlockSpec((height, cols), lambda t, tab: (tab[place], 0))

    return pl.pallas_call(
        functools.partial(plane_kernel, groups=[len(terms) for terms in sums], at=at),
        grid_spec=pltpu.PrefetchScalarGridSpec(
            num_scalar_prefetch=1,
            grid=(1,),
            in_specs=[spec(place, block) for terms in sums for _, place, block in terms],
            out_specs=[pl.BlockSpec(out.shape, lambda t, tab: (0, 0)) for out in outs],
            scratch_shapes=[pltpu.VMEM((height * len(sums), cols), jnp.float32)],
        ),
        out_shape=outs,
        compiler_params=pltpu.CompilerParams(vmem_limit_bytes=34 * 2**20),
        cost_estimate=pl.CostEstimate(
            flops=0, transcendentals=0, bytes_accessed=height * len(sums) * cols * 14
        ),
    )(table, *(array for terms in sums for array, _, _ in terms))


def swap_pairs():
    return [(0, 1), (1, 0)]


def join_kernel(table_ref, *refs, at):
    ins, outs = refs[:-2], refs[-2:]
    part = ins[0].shape[1]
    for d, block in enumerate(ins):
        rows = pl.ds(pl.multiple_of(table_ref[at + d] * part, part), part)
        for i, out in enumerate(outs):
            out[rows, :] = block[i]


def local(basis, classes, cond_table, ground_table, port_cells, port_load):
    sides = classes.shape
    cells_x, cells_y, cells_z = sides
    width_k = basis.shape[3]
    devices_x = lax.axis_size("gx")
    chips_y = lax.axis_size("gy")
    devices_z = lax.axis_size("gz")
    devices_y = 2 * chips_y
    spans = devices_x // 2
    split = spans // 2
    count = cells_x * cells_y * cells_z
    cols = PANELS * NB
    at_x, chip, core, at_z = (lax.axis_index(axis) for axis in ("gx", "gy", "core", "gz"))
    at_y = 2 * chip + core
    f32, bf16 = jnp.float32, jnp.bfloat16

    flat_basis = basis.reshape(count, width_k)
    wide = width_k // (devices_x * devices_z)
    narrow = wide // chips_y
    part = narrow // 2

    entries = []

    def put(values):
        entries.extend(values)
        return len(entries) - len(values), len(values)

    shift = core * spans * devices_z * chips_y

    def put_products(blocks):
        return [put([b + shift for b in blocks]), put(blocks)]

    lists_a, lists_b, next_a, next_b = [], [], [], []
    for d in range(devices_z):
        x = (at_z + d) % devices_z
        lists_a.append(
            put_products(
                [(zz * devices_z + x) * chips_y + y for zz in range(split) for y in range(chips_y)]
            )
        )
        next_b.append(put([zz * devices_z + x for zz in range(spans - split)]))
    for d in range(chips_y):
        y = (chip + d) % chips_y
        lists_b.append(
            put_products(
                [(zz * devices_z + x) * chips_y + y for zz in range(split, spans) for x in range(devices_z)]
            )
        )
        next_a.append(put([zz * chips_y + y for zz in range(split)]))
    leaving = [(at_x + step) % devices_x for step in range(devices_x)]
    leaving_at, _ = put(leaving + [at_x % spans * 2 + core, at_x % spans * 2 + 1 - core])
    given_at, _ = put([1 - core])
    core_at, _ = put([core])
    last_at, _ = put([at_z == 1])
    places_at, _ = put([(at_y - d) % devices_y for d in range(devices_y)])
    order_at, _ = put([(at_y + d) % devices_y for d in range(devices_y)])
    home_at, _ = put([at_x // spans == core])
    first_at, _ = put([((at_x * devices_z + at_z) * devices_y + at_y) * part])
    table = jnp.stack([jnp.asarray(e, jnp.int32) for e in entries])

    def move(array, axis, d):
        size = lax.axis_size(axis)
        return lax.ppermute(array, axis, [(i, (i + d) % size) for i in range(size)])

    panel_spec = pl.BlockSpec((count, cols), lambda *_: (0, 0))
    port_rows, load_rows = port_cells[None, :], port_load[None, :]
    global_x = at_x * cells_x + jnp.arange(cells_x, dtype=jnp.int32)
    global_y = at_y * cells_y + jnp.arange(cells_y, dtype=jnp.int32)
    global_z = at_z * cells_z + jnp.arange(cells_z, dtype=jnp.int32)
    flat_ids = (
        (global_x[:, None, None] * (cells_y * devices_y) + global_y[None, :, None])
        * (cells_z * devices_z)
        + global_z[None, None, :]
    )
    info = jnp.stack([classes, flat_ids], -1).reshape(count, 2)
    face_rows = [cells_y * cells_z] * 2 + [cells_x * cells_z] * 2
    face_rows += [cells_x * cells_y] * (1 if devices_z == 2 else 2)
    outs = [jax.ShapeDtypeStruct((n, cols), bf16) for n in face_rows]
    outs += [jax.ShapeDtypeStruct((count, LEAF), f32)] * 2
    given = jax.ShapeDtypeStruct((count, width_k // 2), basis.dtype)
    *faces, conduct, grounds, given = pl.pallas_call(
        functools.partial(faces_kernel, sides=sides, at=given_at, last_at=last_at),
        out_shape=[*outs, given],
        grid_spec=pltpu.PrefetchScalarGridSpec(
            num_scalar_prefetch=1,
            grid=(1,),
            in_specs=[block_of(cond_table, pltpu.SMEM), block_of(ground_table, pltpu.SMEM)]
            + [block_of(info), block_of(port_rows), block_of(load_rows), panel_spec]
            + [pl.BlockSpec(memory_space=pl.ANY)],
            out_specs=[whole()] * len(outs) + [pl.BlockSpec(memory_space=pl.ANY)],
            scratch_shapes=[
                pltpu.VMEM((cols // LEAF, count, LEAF), f32),
                pltpu.VMEM((count, width_k // 2), basis.dtype),
                pltpu.SemaphoreType.DMA((4,)),
                pltpu.SemaphoreType.DMA((4,)),
            ],
        ),
        compiler_params=pltpu.CompilerParams(vmem_limit_bytes=56 * 2**20),
    )(table, cond_table, ground_table, info, port_rows, load_rows, flat_basis, flat_basis)
    halos = []
    for i, (axis, size) in enumerate(
        (("gx", devices_x), (("gy", "core"), devices_y), ("gz", devices_z))
    ):
        if i == 2 and size == 2:
            halos.append(lax.ppermute(faces[4], axis, swap_pairs()))
            continue
        low, high = faces[2 * i : 2 * i + 2]
        halos.append(lax.ppermute(high, axis, [(k, k + 1) for k in range(size - 1)]))
        halos.append(lax.ppermute(low, axis, [(k + 1, k) for k in range(size - 1)]))

    blocks = NB // LEAF
    lower_rows = blocks * (blocks + 1) // 2 * LEAF
    half_rows = lower_rows + blocks * NB // 2
    lead_parts = [jax.ShapeDtypeStruct((half_rows + LEAF, LEAF), f32)] * 2
    outs = [jax.ShapeDtypeStruct((count, cols), bf16), *lead_parts]
    image, lead_kept, lead_sent = pl.pallas_call(
        functools.partial(image_kernel, sides=sides, nb=NB, at=core_at, last_at=last_at),
        out_shape=outs,
        grid_spec=pltpu.PrefetchScalarGridSpec(
            num_scalar_prefetch=1,
            grid=(1,),
            in_specs=[panel_spec] + [whole()] * (2 + len(halos)),
            out_specs=[whole()] * 3,
            scratch_shapes=[pltpu.VMEM((count, LEAF), f32), pltpu.VMEM((NB, NB), f32)],
        ),
        compiler_params=pltpu.CompilerParams(vmem_limit_bytes=56 * 2**20),
    )(table, flat_basis, conduct, grounds, *halos)

    other_image = lax.ppermute(image, "core", swap_pairs())
    other_basis = lax.ppermute(given, "core", swap_pairs())

    plane_axes = ("gy", "gz")
    chips = chips_y * devices_z

    def exchanged(rows, axes):
        return lax.all_to_all(rows, axes, split_axis=0, concat_axis=0, tiled=True)

    def for_all(own, size):
        return jnp.broadcast_to(own, (size, *own.shape))

    lead_got = lax.ppermute(lead_sent, "core", swap_pairs())
    lead_half = lead_kept[:half_rows] + lead_got[:half_rows]
    lead_terms = exchanged(lead_half.astype(bf16).reshape(chips, -1, LEAF), plane_axes)

    def chip_products(images, lists, dtype):
        return products(table, [flat_basis, other_basis], images, lists, narrow, dtype)

    images, _ = lax.optimization_barrier(([image, other_image], lead_half))
    sent_a = [chip_products(images, lists_a[d], bf16) for d in range(1, devices_z)]
    sent_b = [chip_products(images, lists_b[d], bf16) for d in range(1, chips_y)]
    got_a = [move(a, "gz", d) for d, a in enumerate(sent_a, 1)]
    got_b = [move(a, "gy", d) for d, a in enumerate(sent_b, 1)]
    own_a, own_b = (chip_products(images, lists[0], f32) for lists in (lists_a, lists_b))
    lead_terms, _ = lax.optimization_barrier((lead_terms, (own_a, own_b)))
    own = jnp.sum(lead_terms.astype(f32), axis=0).reshape(devices_x, -1, LEAF)
    own = jnp.sum(exchanged(own, "gx"), axis=0)
    own = exchanged(for_all(own, devices_x), "gx").reshape(-1, LEAF)
    own = for_all(own, chips)
    (got_a, got_b), _ = lax.optimization_barrier(((got_a, got_b), own))
    lead_half = exchanged(own, plane_axes).reshape(-1, LEAF)
    sums_a, sums_b = [own_a, *got_a], [own_b, *got_b]

    further_a = [add_blocks(table, sums_a, *next_a[d], narrow, bf16) for d in range(1, chips_y)]
    further_b = [add_blocks(table, sums_b, *next_b[d], narrow, bf16) for d in range(1, devices_z)]
    lead_half, _ = lax.optimization_barrier((lead_half, (further_a, further_b)))
    further_a = [move(a, "gy", d) for d, a in enumerate(further_a, 1)]
    further_b = [move(a, "gz", d) for d, a in enumerate(further_b, 1)]
    other = lax.ppermute(lead_half, "core", swap_pairs())
    lower_half, upper_half = jnp.where(core == 0, lead_half, other), jnp.where(core == 0, other, lead_half)
    first = lower_rows // 2
    first_rows = jnp.concatenate([lower_half[:first], upper_half[:first]], 0)
    later_rows = jnp.concatenate([lower_half[first:], upper_half[first:]], 0)
    inverse_0 = first_panel(first_rows, NB)
    (further_a, further_b), inverse_0 = lax.optimization_barrier(
        ((further_a, further_b), inverse_0)
    )

    terms = []
    for zz in range(split):
        at = next_a[0][0] + zz
        terms.append([(a, at, None) for a in sums_a] + [(a, None, zz) for a in further_a])
    for zz in range(spans - split):
        at = next_b[0][0] + zz
        terms.append([(a, at, None) for a in sums_b] + [(a, None, zz) for a in further_b])
    outs = [jax.ShapeDtypeStruct((part, cols), bf16)] * devices_x
    outs += [jax.ShapeDtypeStruct((part, cols), f32)] * 2
    *x_sent, own, swapped = plane_parts(table, terms, narrow, leaving_at, outs)
    x_got = []
    for step in range(devices_x):
        pairs = []
        for x in range(devices_x):
            for y in range(devices_y):
                to = (x + step) % devices_x
                dest_x = (y % 2) * spans + to // 2
                dest_y = (y // 2) * 2 + to % 2
                if dest_x != x:
                    pairs.append((x * devices_y + y, dest_x * devices_y + dest_y))
        x_got.append(lax.ppermute(x_sent[step], ("gx", "gy", "core"), pairs))
    swapped = lax.ppermute(swapped, "core", swap_pairs())
    later_rows, _ = lax.optimization_barrier((later_rows, x_sent))
    factor_10, inverse_1 = next_panel(later_rows, inverse_0)
    (x_got, swapped), inverse_1 = lax.optimization_barrier(((x_got, swapped), inverse_1))
    pair = jax.ShapeDtypeStruct((2, part, cols // devices_y), f32)
    ins = [own, swapped, *x_got, inverse_0, factor_10, inverse_1]
    pairs = list(pl.pallas_call(
        functools.partial(factor_kernel, at=(home_at, order_at, first_at)),
        out_shape=[pair] * devices_y,
        grid_spec=pltpu.PrefetchScalarGridSpec(
            num_scalar_prefetch=1,
            grid=(1,),
            in_specs=[block_of(a) for a in ins],
            out_specs=[block_of(pair)] * devices_y,
            scratch_shapes=[pltpu.VMEM((part, cols), f32)] * 2,
        ),
        compiler_params=pltpu.CompilerParams(vmem_limit_bytes=44 * 2**20),
    )(table, *ins))
    for d in range(1, devices_y):
        route = [(i, (i + d) % devices_y) for i in range(devices_y)]
        pairs[d] = lax.ppermute(pairs[d], ("gy", "core"), route)
    out = jax.ShapeDtypeStruct((devices_y * part, cols // devices_y), f32)
    return pl.pallas_call(
        functools.partial(join_kernel, at=places_at),
        out_shape=(out, out),
        grid_spec=pltpu.PrefetchScalarGridSpec(
            num_scalar_prefetch=1,
            grid=(1,),
            in_specs=[block_of(a) for a in pairs],
            out_specs=[block_of(out)] * 2,
        ),
        compiler_params=pltpu.CompilerParams(vmem_limit_bytes=44 * 2**20),
    )(table, *pairs)


def solution(mesh):
    sizes = mesh.shape
    fine = jax.sharding.Mesh(
        mesh.devices.reshape(sizes["gx"], sizes["gy"] // 2, 2, sizes["gz"]),
        ("gx", "gy", "core", "gz"),
    )
    grid = ("gx", ("gy", "core"), "gz")
    out = P(("gx", "gz"), ("gy", "core"))
    return jax.shard_map(
        local,
        mesh=fine,
        in_specs=(P(*grid, None), P(*grid), P(), P(), P(), P()),
        out_specs=(out, out),
        check_vma=False,
    )
```

```python
import functools

import jax
import jax.numpy as jnp
from jax import lax
from jax.experimental import pallas as pl
from jax.experimental.pallas import tpu as pltpu
from jax.sharding import PartitionSpec as P

NB = 512
PANELS = 2
LEAF = 128
SUB = 8


def dot3(a, b, dims):
    a_hi = a.astype(jnp.bfloat16)
    b_hi = b.astype(jnp.bfloat16)
    a_lo = (a - a_hi.astype(jnp.float32)).astype(jnp.bfloat16)
    b_lo = (b - b_hi.astype(jnp.float32)).astype(jnp.bfloat16)

    def dot(x, y):
        return lax.dot_general(x, y, (dims, ((), ())), preferred_element_type=jnp.float32)

    return dot(a_hi, b_hi) + (dot(a_hi, b_lo) + dot(a_lo, b_hi))


def inverse_of(d):
    guess = pl.reciprocal(d, approx=True)
    return guess * (2.0 - d * guess)


def leaf_inverse(block_ref):
    lanes = lax.broadcasted_iota(jnp.int32, (SUB, LEAF), 1)
    subs = lax.broadcasted_iota(jnp.int32, (SUB, LEAF), 0)
    shape = (SUB, LEAF)
    panels = LEAF // SUB
    rows = block_ref[0:SUB, :]
    for t in range(panels):
        j0 = t * SUB
        after = t + 1 < panels

        def columns(array):
            return [jnp.broadcast_to(array[:, j0 + k : j0 + k + 1], shape) for k in range(SUB)]

        cols = columns(rows)
        p = [[jnp.broadcast_to(cols[k][i : i + 1, :], shape) for k in range(i + 1)] for i in range(SUB)]
        in_block = jnp.logical_and(lanes >= j0, lanes < j0 + SUB)
        start = jnp.where(in_block, (lanes - j0 == subs).astype(jnp.float32), rows)
        u = [jnp.broadcast_to(start[k : k + 1, :], shape) for k in range(SUB)]
        if after:
            below = block_ref[j0 + SUB : j0 + 2 * SUB, :]
            c = columns(below)
            rows = jnp.where(in_block, 0.0, below)
        inv = [None] * SUB
        factor = [[None] * SUB for _ in range(SUB)]
        for k in range(SUB):
            products = {(i, j): p[i][k] * p[j][k] for i in range(k + 1, SUB) for j in range(k + 1, i + 1)}
            inv[k] = inverse_of(p[k][k])
            for (i, j), product in products.items():
                p[i][j] = p[i][j] - product * inv[k]
            if after:
                step = c[k] * inv[k]
                rows = rows - step * u[k]
            for i in range(k + 1, SUB):
                factor[i][k] = p[i][k] * inv[k]
                u[i] = u[i] - factor[i][k] * u[k]
                if after:
                    c[i] = c[i] - step * p[i][k]
        out = u[0] * lax.rsqrt(p[0][0])
        for k in range(1, SUB):
            out = jnp.where(subs == k, u[k] * lax.rsqrt(p[k][k]), out)
        block_ref[j0 : j0 + SUB, :] = out
        if t + 2 >= panels:
            continue
        z = [None] * SUB
        for k in reversed(range(SUB)):
            z[k] = u[k] * inv[k]
            for i in range(k + 1, SUB):
                z[k] = z[k] - factor[i][k] * z[i]
        for v in range(t + 2, panels):
            below = block_ref[v * SUB : (v + 1) * SUB, :]
            upd = jnp.where(in_block, 0.0, below)
            for k in reversed(range(SUB)):
                upd = upd - jnp.broadcast_to(below[:, j0 + k : j0 + k + 1], shape) * z[k]
            block_ref[v * SUB : (v + 1) * SUB, :] = upd


def factor_inverse(s_ref, d_ref):
    width = s_ref.shape[0]
    row_ids = lax.broadcasted_iota(jnp.int32, (width, width), 0)
    col_ids = lax.broadcasted_iota(jnp.int32, (width, width), 1)
    wide_cols = lax.broadcasted_iota(jnp.int32, (LEAF, width), 1)
    leaf_rows = lax.broadcasted_iota(jnp.int32, (LEAF, LEAF), 0)
    leaf_cols = lax.broadcasted_iota(jnp.int32, (LEAF, LEAF), 1)

    def step(b, carry):
        off = pl.multiple_of(b * LEAF, LEAF)
        span = pl.ds(off, LEAF)
        d_ref[...] = s_ref[span, span]
        leaf_inverse(d_ref)
        inverse = jnp.where(leaf_rows >= leaf_cols, d_ref[...], 0.0)
        s_ref[span, span] = (leaf_rows == leaf_cols).astype(jnp.float32)
        upper = dot3(inverse, s_ref[span, :], ((1,), (0,)))
        s_ref[span, :] = upper

        @pl.when(b < width // LEAF - 1)
        def _():
            tail = jnp.where(wide_cols >= off + LEAF, upper, 0.0)
            current = s_ref[...]
            dead = jnp.logical_and(
                row_ids >= off + LEAF, jnp.logical_and(col_ids >= off, col_ids < off + LEAF)
            )
            s_ref[...] = jnp.where(dead, 0.0, current) - dot3(tail, upper, ((0,), (0,)))

        return carry

    lax.fori_loop(0, width // LEAF, step, 0)
    s_ref[...] = jnp.where(row_ids >= col_ids, s_ref[...], 0.0)


def unpack_symmetric(packed_ref, s_ref):
    at = 0
    for i in range(s_ref.shape[0] // LEAF):
        for j in range(i + 1):
            block = packed_ref[at * LEAF : (at + 1) * LEAF, :]
            s_ref[i * LEAF : (i + 1) * LEAF, j * LEAF : (j + 1) * LEAF] = block
            if j < i:
                s_ref[j * LEAF : (j + 1) * LEAF, i * LEAF : (i + 1) * LEAF] = block.T
            at += 1


def first_panel_kernel(packed_ref, w_ref, d_ref):
    unpack_symmetric(packed_ref, w_ref)
    factor_inverse(w_ref, d_ref)


def next_panel_kernel(packed_ref, w0_ref, f_ref, w_ref, d_ref):
    nb = w0_ref.shape[0]
    blocks = nb // LEAF
    unpack_symmetric(packed_ref, w_ref)
    start = packed_ref.shape[0] - blocks * nb
    below = jnp.concatenate(
        [packed_ref[start + i * nb : start + (i + 1) * nb, :] for i in range(nb // LEAF)], 1
    )
    below = dot3(below, w0_ref[...], ((1,), (1,)))
    f_ref[...] = below
    w_ref[...] = w_ref[...] - dot3(below, below, ((1,), (1,)))
    factor_inverse(w_ref, d_ref)


def factor_kernel(table_ref, own_ref, swapped_ref, *refs, at):
    home_at, order_at, first_at = at
    cols = own_ref.shape[1]
    *ins, rows_ref, all_ref = refs
    count = cols // ins[-1].shape[2]
    ins, blocks = ins[:-count], ins[-count:]
    *ins, w0_ref, f_ref, w1_ref = ins
    total = jnp.where(table_ref[home_at] != 0, own_ref[...], swapped_ref[...])
    for got in ins:
        total = total + got[...].astype(jnp.float32)
    rows_ref[...] = total
    nb = w0_ref.shape[0]
    ids = table_ref[first_at] + lax.broadcasted_iota(jnp.int32, (rows_ref.shape[0], nb), 0)
    columns = lax.broadcasted_iota(jnp.int32, (rows_ref.shape[0], nb), 1)
    part = dot3(rows_ref[:, :nb], w0_ref[...], ((1,), (1,)))
    rest = rows_ref[:, nb:] - dot3(part, f_ref[...], ((1,), (1,)))
    rest = dot3(rest, w1_ref[...], ((1,), (1,)))
    all_ref[:, :nb] = jnp.where(columns <= ids, part, 0.0)
    all_ref[:, nb:] = jnp.where(columns + nb <= ids, rest, 0.0)
    for d, block in enumerate(blocks):
        width = block.shape[2]
        span = pl.ds(pl.multiple_of(table_ref[order_at + d] * width, width), width)
        block[0] = rows_ref[:, span]
        block[1] = all_ref[:, span]


def panel_call(kernel, outputs, nb, *operands):
    return pl.pallas_call(
        kernel,
        out_shape=[jax.ShapeDtypeStruct((nb, nb), jnp.float32)] * outputs,
        in_specs=[pl.BlockSpec(memory_space=pltpu.VMEM)] * len(operands),
        out_specs=[pl.BlockSpec(memory_space=pltpu.VMEM)] * outputs,
        scratch_shapes=[pltpu.VMEM((LEAF, LEAF), jnp.float32)],
        compiler_params=pltpu.CompilerParams(vmem_limit_bytes=24 * 2**20),
        cost_estimate=pl.CostEstimate(
            flops=nb, transcendentals=0, bytes_accessed=nb
        ),
    )(*operands)


def first_panel(packed, nb):
    return panel_call(first_panel_kernel, 1, nb, packed)[0]


def next_panel(packed, w0):
    return panel_call(next_panel_kernel, 2, w0.shape[0], packed, w0)


def whole(memory=pltpu.VMEM):
    return pl.BlockSpec(memory_space=memory)


def block_of(array, memory=pltpu.VMEM):
    return pl.BlockSpec(array.shape, lambda *_: (0,) * array.ndim, memory_space=memory)


def faces_kernel(
    table_ref, cond_ref, ground_ref, info_ref, cells_ref, load_ref, panel_ref, basis_ref, *refs, sides, at, last_at
):
    *outs, conduct_ref, grounds_ref, given_ref, scaled_ref, held_ref, in_sems, out_sems = refs
    last = table_ref[last_at] != 0
    half = given_ref.shape[1]
    lanes = pl.ds(pl.multiple_of(table_ref[at] * half, half), half)
    pieces = in_sems.shape[0]
    height = given_ref.shape[0] // pieces
    copies_in, copies_out = [], []
    for i in range(pieces):
        rows = pl.ds(i * height, height)
        copies_in.append(
            pltpu.make_async_copy(basis_ref.at[rows, lanes], held_ref.at[rows], in_sems.at[i])
        )
        copies_out.append(
            pltpu.make_async_copy(held_ref.at[rows], given_ref.at[rows], out_sems.at[i])
        )
        copies_in[i].start()
    size_x, size_y, size_z = sides
    count, width = panel_ref.shape
    tile = 64
    classes = cond_ref.shape[0]
    ports = cells_ref.shape[1]

    def by_tile(t, carry):
        rows = pl.ds(pl.multiple_of(t * tile, tile), tile)
        kind = jnp.broadcast_to(info_ref[rows, 0:1], (tile, LEAF))
        ids = jnp.broadcast_to(info_ref[rows, 1:2], (tile, LEAF))
        conduct = jnp.zeros((tile, LEAF), jnp.float32)
        grounds = jnp.zeros((tile, LEAF), jnp.float32)
        for c in range(classes):
            conduct = jnp.where(kind == c, cond_ref[c], conduct)
            grounds = jnp.where(kind == c, ground_ref[c], grounds)
        loads = jnp.zeros((tile, LEAF), jnp.float32)
        for p in range(0, ports, LEAF):
            hit = ids == cells_ref[:, p : p + LEAF]
            loads = loads + jnp.where(hit, load_ref[:, p : p + LEAF], 0.0)
        conduct_ref[rows, :] = conduct
        grounds_ref[rows, :] = grounds + jnp.sum(loads, axis=1, keepdims=True)
        for p in range(0, width, LEAF):
            part = panel_ref[rows, p : p + LEAF].astype(jnp.float32)
            scaled_ref[p // LEAF, rows, :] = (
                (conduct * part).astype(jnp.bfloat16).astype(jnp.float32)
            )
        return carry

    lax.fori_loop(0, count // tile, by_tile, 0)
    for copy_in, copy_out in zip(copies_in, copies_out):
        copy_in.wait()
        copy_out.start()
    plane = size_y * size_z
    for p in range(width // LEAF):
        lanes = slice(p * LEAF, (p + 1) * LEAF)
        outs[0][:, lanes] = scaled_ref[p, 0:plane, :].astype(jnp.bfloat16)
        outs[1][:, lanes] = scaled_ref[p, count - plane : count, :].astype(jnp.bfloat16)
        for out, at in ((outs[2], 0), (outs[3], plane - size_z)):
            face = [
                scaled_ref[p, x * plane + at : x * plane + at + size_z, :] for x in range(size_x)
            ]
            out[:, lanes] = jnp.concatenate(face, 0).astype(jnp.bfloat16)
        low, high = (
            scaled_ref[p, pl.ds(at, size_x * size_y, stride=size_z), :] for at in (0, size_z - 1)
        )
        if len(outs) == 5:
            outs[4][:, lanes] = jnp.where(last, low, high).astype(jnp.bfloat16)
        else:
            outs[4][:, lanes] = low.astype(jnp.bfloat16)
            outs[5][:, lanes] = high.astype(jnp.bfloat16)
    for copy_out in copies_out:
        copy_out.wait()


def image_kernel(table_ref, panel_ref, conduct_ref, grounds_ref, *refs, sides, nb, last_at):
    *halos, image_ref, lead_ref, scaled_ref, square_ref = refs
    last = table_ref[last_at] != 0
    size_x, size_y, size_z = sides
    width = panel_ref.shape[1]
    plane = size_y * size_z
    subs = lax.broadcasted_iota(jnp.int32, (size_z, LEAF), 0)

    def by_lane(p, carry):
        lanes = pl.ds(pl.multiple_of(p * LEAF, LEAF), LEAF)
        x_low, x_high, y_low, y_high, *z_halos = (h[:, lanes].astype(jnp.float32) for h in halos)
        if len(z_halos) == 1:
            z_halos = [jnp.where(last, z_halos[0], 0.0), jnp.where(last, 0.0, z_halos[0])]
        z_low, z_high = z_halos
        scaled_ref[...] = (
            (conduct_ref[...] * panel_ref[:, lanes].astype(jnp.float32))
            .astype(jnp.bfloat16)
            .astype(jnp.float32)
        )

        def cell_rows(x, y):
            at = x * plane + y * size_z
            return scaled_ref[at : at + size_z, :]

        for x in range(size_x):
            done = []
            for y in range(size_y):
                at = x * plane + y * size_z
                here = cell_rows(x, y)
                span = slice(y * size_z, (y + 1) * size_z)
                total = cell_rows(x + 1, y) if x + 1 < size_x else x_high[span, :]
                total = total + (cell_rows(x - 1, y) if x > 0 else x_low[span, :])
                span = slice(x * size_z, (x + 1) * size_z)
                total = total + (cell_rows(x, y + 1) if y + 1 < size_y else y_high[span, :])
                total = total + (cell_rows(x, y - 1) if y > 0 else y_low[span, :])
                k = x * size_y + y
                up = jnp.where(
                    subs == size_z - 1, z_high[k : k + 1, :], pltpu.roll(here, size_z - 1, 0)
                )
                down = jnp.where(subs == 0, z_low[k : k + 1, :], pltpu.roll(here, 1, 0))
                total = total + up + down
                own = slice(at, at + size_z)
                done.append(
                    conduct_ref[own, :] * (6.0 * here - total)
                    + grounds_ref[own, :] * panel_ref[at : at + size_z, lanes].astype(jnp.float32)
                )
            image_ref[x * plane : (x + 1) * plane, lanes] = jnp.concatenate(done, 0).astype(
                jnp.bfloat16
            )
        return carry

    lax.fori_loop(0, width // LEAF, by_lane, 0)

    def product(rows, cols):
        return lax.dot_general(
            panel_ref[:, rows],
            image_ref[:, cols],
            (((0,), (0,)), ((), ())),
            preferred_element_type=jnp.float32,
        )

    blocks = nb // LEAF

    def put_block(number, value):
        lead_ref[number * LEAF : (number + 1) * LEAF, :] = value.astype(lead_ref.dtype)

    def lower(number):
        for i in range(blocks):
            for j in range(i + 1):
                row, col = slice(i * LEAF, (i + 1) * LEAF), slice(j * LEAF, (j + 1) * LEAF)
                put_block(number, 0.5 * (square_ref[row, col] + square_ref[col, row].T))
                number += 1
        return number

    head, tail = slice(0, nb), slice(nb, 2 * nb)
    square_ref[...] = product(head, head)
    number = lower(0)
    square_ref[...] = product(tail, tail)
    number = lower(number)
    below = product(tail, head)
    for j in range(blocks):
        for i in range(blocks):
            put_block(
                number + j * blocks + i,
                below[i * LEAF : (i + 1) * LEAF, j * LEAF : (j + 1) * LEAF],
            )


def products_kernel(table_ref, *refs):
    del table_ref
    out, count = refs[-1], len(refs) // 2
    bases = jnp.concatenate([ref[...] for ref in refs[:count]], 0)
    images = jnp.concatenate([ref[...] for ref in refs[count:-1]], 0)
    total = lax.dot_general(
        bases, images, (((0,), (0,)), ((), ())), preferred_element_type=jnp.float32
    )
    out[...] = total.astype(out.dtype)


def products(table, bases, images, lists, width, dtype):
    rows, cols = images[0].shape
    step = 512 if width % 512 == 0 else width
    parts = width // step
    steps = lists[0][1] * parts
    in_specs = [
        pl.BlockSpec(
            (rows, step), lambda t, tab, at=at: (0, tab[at + t // parts] * parts + t % parts)
        )
        for at, _ in lists
    ]
    in_specs += [pl.BlockSpec((rows, cols), lambda t, tab: (0, 0))] * len(images)
    total = steps * step
    return pl.pallas_call(
        products_kernel,
        grid_spec=pltpu.PrefetchScalarGridSpec(
            num_scalar_prefetch=1,
            grid=(steps,),
            in_specs=in_specs,
            out_specs=pl.BlockSpec((step, cols), lambda t, tab: (t, 0)),
        ),
        out_shape=jax.ShapeDtypeStruct((total, cols), dtype),
        compiler_params=pltpu.CompilerParams(vmem_limit_bytes=48 * 2**20),
        cost_estimate=pl.CostEstimate(
            flops=2 * total * cols * rows * len(bases),
            transcendentals=0,
            bytes_accessed=2 * rows * (total + cols) * len(bases) + 4 * total * cols,
        ),
    )(table, *bases, *images)


def add_kernel(table_ref, *refs):
    del table_ref
    total = refs[0][...].astype(jnp.float32)
    for got in refs[1:-1]:
        total = total + got[...].astype(jnp.float32)
    refs[-1][...] = total.astype(refs[-1].dtype)


def add_blocks(table, arrays, at, count, height, dtype):
    cols = arrays[0].shape[1]
    step = min(256, height)
    parts = height // step
    steps = count * parts
    spec = pl.BlockSpec((step, cols), lambda t, tab: (tab[at + t // parts] * parts + t % parts, 0))
    return pl.pallas_call(
        add_kernel,
        grid_spec=pltpu.PrefetchScalarGridSpec(
            num_scalar_prefetch=1,
            grid=(steps,),
            in_specs=[spec] * len(arrays),
            out_specs=pl.BlockSpec((step, cols), lambda t, tab: (t, 0)),
        ),
        out_shape=jax.ShapeDtypeStruct((steps * step, cols), dtype),
        compiler_params=pltpu.CompilerParams(vmem_limit_bytes=24 * 2**20),
        cost_estimate=pl.CostEstimate(
            flops=steps * step * cols,
            transcendentals=0,
            bytes_accessed=steps * step * cols * 4 * len(arrays),
        ),
    )(table, *arrays)


def plane_kernel(table_ref, *refs, groups, at):
    ins, outs, plane_ref = refs[: sum(groups)], refs[sum(groups) : -1], refs[-1]
    height = ins[0].shape[0]
    done = 0
    for i, count in enumerate(groups):
        total = ins[done][...].astype(jnp.float32)
        for got in ins[done + 1 : done + count]:
            total = total + got[...].astype(jnp.float32)
        plane_ref[i * height : (i + 1) * height, :] = total
        done += count
    for i, out in enumerate(outs):
        part = out.shape[0]
        rows = pl.ds(pl.multiple_of(table_ref[at + i] * part, part), part)
        out[...] = plane_ref[rows, :].astype(out.dtype)


def plane_parts(table, sums, height, at, outs):
    cols = sums[0][0][0].shape[1]

    def spec(place, block):
        if place is None:
            return pl.BlockSpec((height, cols), lambda t, tab: (block, 0))
        return pl.BlockSpec((height, cols), lambda t, tab: (tab[place], 0))

    return pl.pallas_call(
        functools.partial(plane_kernel, groups=[len(terms) for terms in sums], at=at),
        grid_spec=pltpu.PrefetchScalarGridSpec(
            num_scalar_prefetch=1,
            grid=(1,),
            in_specs=[spec(place, block) for terms in sums for _, place, block in terms],
            out_specs=[pl.BlockSpec(out.shape, lambda t, tab: (0, 0)) for out in outs],
            scratch_shapes=[pltpu.VMEM((height * len(sums), cols), jnp.float32)],
        ),
        out_shape=outs,
        compiler_params=pltpu.CompilerParams(vmem_limit_bytes=34 * 2**20),
        cost_estimate=pl.CostEstimate(
            flops=0, transcendentals=0, bytes_accessed=height * len(sums) * cols * 14
        ),
    )(table, *(array for terms in sums for array, _, _ in terms))


def swap_pairs():
    return [(0, 1), (1, 0)]


def join_kernel(table_ref, *refs, at):
    ins, outs = refs[:-2], refs[-2:]
    part = ins[0].shape[1]
    for d, block in enumerate(ins):
        rows = pl.ds(pl.multiple_of(table_ref[at + d] * part, part), part)
        for i, out in enumerate(outs):
            out[rows, :] = block[i]


def local(basis, classes, cond_table, ground_table, port_cells, port_load):
    sides = classes.shape
    cells_x, cells_y, cells_z = sides
    width_k = basis.shape[3]
    devices_x = lax.axis_size("gx")
    chips_y = lax.axis_size("gy")
    devices_z = lax.axis_size("gz")
    devices_y = 2 * chips_y
    spans = devices_x // 2
    split = spans // 2
    count = cells_x * cells_y * cells_z
    cols = PANELS * NB
    at_x, chip, core, at_z = (lax.axis_index(axis) for axis in ("gx", "gy", "core", "gz"))
    at_y = 2 * chip + core
    f32, bf16 = jnp.float32, jnp.bfloat16

    flat_basis = basis.reshape(count, width_k)
    wide = width_k // (devices_x * devices_z)
    narrow = wide // chips_y
    part = narrow // 2

    entries = []

    def put(values):
        entries.extend(values)
        return len(entries) - len(values), len(values)

    shift = core * spans * devices_z * chips_y

    def put_products(blocks):
        return [put([b + shift for b in blocks]), put(blocks)]

    lists_a, lists_b, next_a, next_b = [], [], [], []
    for d in range(devices_z):
        x = (at_z + d) % devices_z
        lists_a.append(
            put_products(
                [(zz * devices_z + x) * chips_y + y for zz in range(split) for y in range(chips_y)]
            )
        )
        next_b.append(put([zz * devices_z + x for zz in range(spans - split)]))
    for d in range(chips_y):
        y = (chip + d) % chips_y
        lists_b.append(
            put_products(
                [(zz * devices_z + x) * chips_y + y for zz in range(split, spans) for x in range(devices_z)]
            )
        )
        next_a.append(put([zz * chips_y + y for zz in range(split)]))
    leaving = [(at_x + step) % devices_x for step in range(devices_x)]
    leaving_at, _ = put(leaving + [at_x % spans * 2 + core, at_x % spans * 2 + 1 - core])
    given_at, _ = put([1 - core])
    last_at, _ = put([at_z == 1])
    places_at, _ = put([(at_y - d) % devices_y for d in range(devices_y)])
    order_at, _ = put([(at_y + d) % devices_y for d in range(devices_y)])
    home_at, _ = put([at_x // spans == core])
    first_at, _ = put([((at_x * devices_z + at_z) * devices_y + at_y) * part])
    table = jnp.stack([jnp.asarray(e, jnp.int32) for e in entries])

    def move(array, axis, d):
        size = lax.axis_size(axis)
        return lax.ppermute(array, axis, [(i, (i + d) % size) for i in range(size)])

    panel_spec = pl.BlockSpec((count, cols), lambda *_: (0, 0))
    port_rows, load_rows = port_cells[None, :], port_load[None, :]
    global_x = at_x * cells_x + jnp.arange(cells_x, dtype=jnp.int32)
    global_y = at_y * cells_y + jnp.arange(cells_y, dtype=jnp.int32)
    global_z = at_z * cells_z + jnp.arange(cells_z, dtype=jnp.int32)
    flat_ids = (
        (global_x[:, None, None] * (cells_y * devices_y) + global_y[None, :, None])
        * (cells_z * devices_z)
        + global_z[None, None, :]
    )
    info = jnp.stack([classes, flat_ids], -1).reshape(count, 2)
    face_rows = [cells_y * cells_z] * 2 + [cells_x * cells_z] * 2
    face_rows += [cells_x * cells_y] * (1 if devices_z == 2 else 2)
    outs = [jax.ShapeDtypeStruct((n, cols), bf16) for n in face_rows]
    outs += [jax.ShapeDtypeStruct((count, LEAF), f32)] * 2
    given = jax.ShapeDtypeStruct((count, width_k // 2), basis.dtype)
    *faces, conduct, grounds, given = pl.pallas_call(
        functools.partial(faces_kernel, sides=sides, at=given_at, last_at=last_at),
        out_shape=[*outs, given],
        grid_spec=pltpu.PrefetchScalarGridSpec(
            num_scalar_prefetch=1,
            grid=(1,),
            in_specs=[block_of(cond_table, pltpu.SMEM), block_of(ground_table, pltpu.SMEM)]
            + [block_of(info), block_of(port_rows), block_of(load_rows), panel_spec]
            + [pl.BlockSpec(memory_space=pl.ANY)],
            out_specs=[whole()] * len(outs) + [pl.BlockSpec(memory_space=pl.ANY)],
            scratch_shapes=[
                pltpu.VMEM((cols // LEAF, count, LEAF), f32),
                pltpu.VMEM((count, width_k // 2), basis.dtype),
                pltpu.SemaphoreType.DMA((4,)),
                pltpu.SemaphoreType.DMA((4,)),
            ],
        ),
        compiler_params=pltpu.CompilerParams(vmem_limit_bytes=56 * 2**20),
    )(table, cond_table, ground_table, info, port_rows, load_rows, flat_basis, flat_basis)
    halos = []
    for i, (axis, size) in enumerate(
        (("gx", devices_x), (("gy", "core"), devices_y), ("gz", devices_z))
    ):
        if i == 2 and size == 2:
            halos.append(lax.ppermute(faces[4], axis, swap_pairs()))
            continue
        low, high = faces[2 * i : 2 * i + 2]
        halos.append(lax.ppermute(high, axis, [(k, k + 1) for k in range(size - 1)]))
        halos.append(lax.ppermute(low, axis, [(k + 1, k) for k in range(size - 1)]))

    blocks = NB // LEAF
    lower_rows = blocks * (blocks + 1) // 2 * LEAF
    lead_rows = 2 * lower_rows + blocks * NB
    outs = [jax.ShapeDtypeStruct((n, width), bf16) for n, width in ((count, cols), (lead_rows, LEAF))]
    image, lead = pl.pallas_call(
        functools.partial(image_kernel, sides=sides, nb=NB, last_at=last_at),
        out_shape=outs,
        grid_spec=pltpu.PrefetchScalarGridSpec(
            num_scalar_prefetch=1,
            grid=(1,),
            in_specs=[panel_spec] + [whole()] * (2 + len(halos)),
            out_specs=[whole()] * 2,
            scratch_shapes=[pltpu.VMEM((count, LEAF), f32), pltpu.VMEM((NB, NB), f32)],
        ),
        compiler_params=pltpu.CompilerParams(vmem_limit_bytes=56 * 2**20),
    )(table, flat_basis, conduct, grounds, *halos)

    other_image = lax.ppermute(image, "core", swap_pairs())
    other_basis = lax.ppermute(given, "core", swap_pairs())

    plane_axes = ("gy", "gz")
    chips = chips_y * devices_z

    def exchanged(rows, axes):
        return lax.all_to_all(rows, axes, split_axis=0, concat_axis=0, tiled=True)

    def for_all(own, size):
        return jnp.broadcast_to(own, (size, *own.shape))

    lead_terms = exchanged(lead.reshape(chips, -1, LEAF), plane_axes)

    def chip_products(images, lists, dtype):
        return products(table, [flat_basis, other_basis], images, lists, narrow, dtype)

    images, _ = lax.optimization_barrier(([image, other_image], lead))
    sent_a = [chip_products(images, lists_a[d], bf16) for d in range(1, devices_z)]
    sent_b = [chip_products(images, lists_b[d], bf16) for d in range(1, chips_y)]
    got_a = [move(a, "gz", d) for d, a in enumerate(sent_a, 1)]
    got_b = [move(a, "gy", d) for d, a in enumerate(sent_b, 1)]
    images, _ = lax.optimization_barrier((images, (sent_a, sent_b)))
    own_a, own_b = (chip_products(images, lists[0], f32) for lists in (lists_a, lists_b))
    lead_terms, _ = lax.optimization_barrier((lead_terms, (own_a, own_b)))
    own = jnp.sum(lead_terms.astype(f32), axis=0).reshape(2, -1, LEAF)
    kept = lax.dynamic_index_in_dim(own, core, 0, keepdims=False)
    sent = lax.dynamic_index_in_dim(own, 1 - core, 0, keepdims=False)
    own = (kept + lax.ppermute(sent, "core", swap_pairs())).reshape(devices_x, -1, LEAF)
    own = jnp.sum(exchanged(own, "gx"), axis=0)
    own = exchanged(for_all(own, devices_x), "gx").reshape(-1, LEAF)
    own = for_all(own, chips)
    (got_a, got_b), _ = lax.optimization_barrier(((got_a, got_b), own))
    lead_half = exchanged(own, plane_axes)
    sums_a, sums_b = [own_a, *got_a], [own_b, *got_b]

    further_a = [add_blocks(table, sums_a, *next_a[d], narrow, bf16) for d in range(1, chips_y)]
    further_b = [add_blocks(table, sums_b, *next_b[d], narrow, bf16) for d in range(1, devices_z)]
    lead_half, _ = lax.optimization_barrier((lead_half, (further_a, further_b)))
    further_a = [move(a, "gy", d) for d, a in enumerate(further_a, 1)]
    further_b = [move(a, "gz", d) for d, a in enumerate(further_b, 1)]
    other = lax.ppermute(lead_half, "core", swap_pairs())
    halves = jnp.where(core == 0, lead_half, other), jnp.where(core == 0, other, lead_half)
    lead = jnp.stack(halves, 1).reshape(lead_rows, LEAF)
    first_rows, later_rows = lead[:lower_rows], lead[lower_rows:]
    inverse_0 = first_panel(first_rows, NB)
    (further_a, further_b), inverse_0 = lax.optimization_barrier(
        ((further_a, further_b), inverse_0)
    )

    terms = []
    for zz in range(split):
        at = next_a[0][0] + zz
        terms.append([(a, at, None) for a in sums_a] + [(a, None, zz) for a in further_a])
    for zz in range(spans - split):
        at = next_b[0][0] + zz
        terms.append([(a, at, None) for a in sums_b] + [(a, None, zz) for a in further_b])
    outs = [jax.ShapeDtypeStruct((part, cols), bf16)] * devices_x
    outs += [jax.ShapeDtypeStruct((part, cols), f32)] * 2
    *x_sent, own, swapped = plane_parts(table, terms, narrow, leaving_at, outs)
    x_got = []
    for step in range(devices_x):
        pairs = []
        for x in range(devices_x):
            for y in range(devices_y):
                to = (x + step) % devices_x
                dest_x = (y % 2) * spans + to // 2
                dest_y = (y // 2) * 2 + to % 2
                if dest_x != x:
                    pairs.append((x * devices_y + y, dest_x * devices_y + dest_y))
        x_got.append(lax.ppermute(x_sent[step], ("gx", "gy", "core"), pairs))
    swapped = lax.ppermute(swapped, "core", swap_pairs())
    later_rows, _ = lax.optimization_barrier((later_rows, x_sent))
    factor_10, inverse_1 = next_panel(later_rows, inverse_0)
    (x_got, swapped), inverse_1 = lax.optimization_barrier(((x_got, swapped), inverse_1))
    pair = jax.ShapeDtypeStruct((2, part, cols // devices_y), f32)
    ins = [own, swapped, *x_got, inverse_0, factor_10, inverse_1]
    pairs = list(pl.pallas_call(
        functools.partial(factor_kernel, at=(home_at, order_at, first_at)),
        out_shape=[pair] * devices_y,
        grid_spec=pltpu.PrefetchScalarGridSpec(
            num_scalar_prefetch=1,
            grid=(1,),
            in_specs=[block_of(a) for a in ins],
            out_specs=[block_of(pair)] * devices_y,
            scratch_shapes=[pltpu.VMEM((part, cols), f32)] * 2,
        ),
        compiler_params=pltpu.CompilerParams(vmem_limit_bytes=44 * 2**20),
    )(table, *ins))
    for d in range(1, devices_y):
        route = [(i, (i + d) % devices_y) for i in range(devices_y)]
        pairs[d] = lax.ppermute(pairs[d], ("gy", "core"), route)
    out = jax.ShapeDtypeStruct((devices_y * part, cols // devices_y), f32)
    return pl.pallas_call(
        functools.partial(join_kernel, at=places_at),
        out_shape=(out, out),
        grid_spec=pltpu.PrefetchScalarGridSpec(
            num_scalar_prefetch=1,
            grid=(1,),
            in_specs=[block_of(a) for a in pairs],
            out_specs=[block_of(out)] * 2,
        ),
        compiler_params=pltpu.CompilerParams(vmem_limit_bytes=44 * 2**20),
    )(table, *pairs)


def solution(mesh):
    sizes = mesh.shape
    fine = jax.sharding.Mesh(
        mesh.devices.reshape(sizes["gx"], sizes["gy"] // 2, 2, sizes["gz"]),
        ("gx", "gy", "core", "gz"),
    )
    grid = ("gx", ("gy", "core"), "gz")
    out = P(("gx", "gz"), ("gy", "core"))
    return jax.shard_map(
        local,
        mesh=fine,
        in_specs=(P(*grid, None), P(*grid), P(), P(), P(), P()),
        out_specs=(out, out),
        check_vma=False,
    )
```

```python
import functools

import jax
import jax.numpy as jnp
from jax import lax
from jax.experimental import pallas as pl
from jax.experimental.pallas import tpu as pltpu
from jax.sharding import PartitionSpec as P

NB = 512
PANELS = 2
LEAF = 128
SUB = 8


def dot3(a, b, dims):
    a_hi = a.astype(jnp.bfloat16)
    b_hi = b.astype(jnp.bfloat16)
    a_lo = (a - a_hi.astype(jnp.float32)).astype(jnp.bfloat16)
    b_lo = (b - b_hi.astype(jnp.float32)).astype(jnp.bfloat16)

    def dot(x, y):
        return lax.dot_general(x, y, (dims, ((), ())), preferred_element_type=jnp.float32)

    return dot(a_hi, b_hi) + (dot(a_hi, b_lo) + dot(a_lo, b_hi))


def inverse_of(d):
    guess = pl.reciprocal(d, approx=True)
    return guess * (2.0 - d * guess)


def leaf_inverse(block_ref):
    lanes = lax.broadcasted_iota(jnp.int32, (SUB, LEAF), 1)
    subs = lax.broadcasted_iota(jnp.int32, (SUB, LEAF), 0)
    shape = (SUB, LEAF)
    panels = LEAF // SUB
    rows = block_ref[0:SUB, :]
    for t in range(panels):
        j0 = t * SUB
        after = t + 1 < panels

        def columns(array):
            return [jnp.broadcast_to(array[:, j0 + k : j0 + k + 1], shape) for k in range(SUB)]

        cols = columns(rows)
        p = [[jnp.broadcast_to(cols[k][i : i + 1, :], shape) for k in range(i + 1)] for i in range(SUB)]
        in_block = jnp.logical_and(lanes >= j0, lanes < j0 + SUB)
        start = jnp.where(in_block, (lanes - j0 == subs).astype(jnp.float32), rows)
        u = [jnp.broadcast_to(start[k : k + 1, :], shape) for k in range(SUB)]
        if after:
            below = block_ref[j0 + SUB : j0 + 2 * SUB, :]
            c = columns(below)
            rows = jnp.where(in_block, 0.0, below)
        inv = [None] * SUB
        factor = [[None] * SUB for _ in range(SUB)]
        for k in range(SUB):
            products = {(i, j): p[i][k] * p[j][k] for i in range(k + 1, SUB) for j in range(k + 1, i + 1)}
            inv[k] = inverse_of(p[k][k])
            for (i, j), product in products.items():
                p[i][j] = p[i][j] - product * inv[k]
            if after:
                step = c[k] * inv[k]
                rows = rows - step * u[k]
            for i in range(k + 1, SUB):
                factor[i][k] = p[i][k] * inv[k]
                u[i] = u[i] - factor[i][k] * u[k]
                if after:
                    c[i] = c[i] - step * p[i][k]
        out = u[0] * lax.rsqrt(p[0][0])
        for k in range(1, SUB):
            out = jnp.where(subs == k, u[k] * lax.rsqrt(p[k][k]), out)
        block_ref[j0 : j0 + SUB, :] = out
        if t + 2 >= panels:
            continue
        z = [None] * SUB
        for k in reversed(range(SUB)):
            z[k] = u[k] * inv[k]
            for i in range(k + 1, SUB):
                z[k] = z[k] - factor[i][k] * z[i]
        for v in range(t + 2, panels):
            below = block_ref[v * SUB : (v + 1) * SUB, :]
            upd = jnp.where(in_block, 0.0, below)
            for k in reversed(range(SUB)):
                upd = upd - jnp.broadcast_to(below[:, j0 + k : j0 + k + 1], shape) * z[k]
            block_ref[v * SUB : (v + 1) * SUB, :] = upd


def factor_inverse(s_ref, d_ref):
    width = s_ref.shape[0]
    row_ids = lax.broadcasted_iota(jnp.int32, (width, width), 0)
    col_ids = lax.broadcasted_iota(jnp.int32, (width, width), 1)
    wide_cols = lax.broadcasted_iota(jnp.int32, (LEAF, width), 1)
    leaf_rows = lax.broadcasted_iota(jnp.int32, (LEAF, LEAF), 0)
    leaf_cols = lax.broadcasted_iota(jnp.int32, (LEAF, LEAF), 1)

    def step(b, carry):
        off = pl.multiple_of(b * LEAF, LEAF)
        span = pl.ds(off, LEAF)
        d_ref[...] = s_ref[span, span]
        leaf_inverse(d_ref)
        inverse = jnp.where(leaf_rows >= leaf_cols, d_ref[...], 0.0)
        s_ref[span, span] = (leaf_rows == leaf_cols).astype(jnp.float32)
        upper = dot3(inverse, s_ref[span, :], ((1,), (0,)))
        s_ref[span, :] = upper

        @pl.when(b < width // LEAF - 1)
        def _():
            tail = jnp.where(wide_cols >= off + LEAF, upper, 0.0)
            current = s_ref[...]
            dead = jnp.logical_and(
                row_ids >= off + LEAF, jnp.logical_and(col_ids >= off, col_ids < off + LEAF)
            )
            s_ref[...] = jnp.where(dead, 0.0, current) - dot3(tail, upper, ((0,), (0,)))

        return carry

    lax.fori_loop(0, width // LEAF, step, 0)
    s_ref[...] = jnp.where(row_ids >= col_ids, s_ref[...], 0.0)


def unpack_symmetric(packed_ref, s_ref):
    at = 0
    for i in range(s_ref.shape[0] // LEAF):
        for j in range(i + 1):
            block = packed_ref[at * LEAF : (at + 1) * LEAF, :]
            s_ref[i * LEAF : (i + 1) * LEAF, j * LEAF : (j + 1) * LEAF] = block
            if j < i:
                s_ref[j * LEAF : (j + 1) * LEAF, i * LEAF : (i + 1) * LEAF] = block.T
            at += 1


def first_panel_kernel(packed_ref, w_ref, d_ref):
    unpack_symmetric(packed_ref, w_ref)
    factor_inverse(w_ref, d_ref)


def next_panel_kernel(packed_ref, w0_ref, f_ref, w_ref, d_ref):
    nb = w0_ref.shape[0]
    blocks = nb // LEAF
    unpack_symmetric(packed_ref, w_ref)
    start = packed_ref.shape[0] - blocks * nb
    below = jnp.concatenate(
        [packed_ref[start + i * nb : start + (i + 1) * nb, :] for i in range(nb // LEAF)], 1
    )
    below = dot3(below, w0_ref[...], ((1,), (1,)))
    f_ref[...] = below
    w_ref[...] = w_ref[...] - dot3(below, below, ((1,), (1,)))
    factor_inverse(w_ref, d_ref)


def factor_kernel(table_ref, own_ref, swapped_ref, *refs, at):
    home_at, order_at, first_at = at
    cols = own_ref.shape[1]
    *ins, rows_ref, all_ref = refs
    count = cols // ins[-1].shape[2]
    ins, blocks = ins[:-count], ins[-count:]
    *ins, w0_ref, f_ref, w1_ref = ins
    total = jnp.where(table_ref[home_at] != 0, own_ref[...], swapped_ref[...])
    for got in ins:
        total = total + got[...].astype(jnp.float32)
    rows_ref[...] = total
    nb = w0_ref.shape[0]
    ids = table_ref[first_at] + lax.broadcasted_iota(jnp.int32, (rows_ref.shape[0], nb), 0)
    columns = lax.broadcasted_iota(jnp.int32, (rows_ref.shape[0], nb), 1)
    part = dot3(rows_ref[:, :nb], w0_ref[...], ((1,), (1,)))
    rest = rows_ref[:, nb:] - dot3(part, f_ref[...], ((1,), (1,)))
    rest = dot3(rest, w1_ref[...], ((1,), (1,)))
    all_ref[:, :nb] = jnp.where(columns <= ids, part, 0.0)
    all_ref[:, nb:] = jnp.where(columns + nb <= ids, rest, 0.0)
    for d, block in enumerate(blocks):
        width = block.shape[2]
        span = pl.ds(pl.multiple_of(table_ref[order_at + d] * width, width), width)
        block[0] = rows_ref[:, span]
        block[1] = all_ref[:, span]


def panel_call(kernel, outputs, nb, *operands):
    return pl.pallas_call(
        kernel,
        out_shape=[jax.ShapeDtypeStruct((nb, nb), jnp.float32)] * outputs,
        in_specs=[pl.BlockSpec(memory_space=pltpu.VMEM)] * len(operands),
        out_specs=[pl.BlockSpec(memory_space=pltpu.VMEM)] * outputs,
        scratch_shapes=[pltpu.VMEM((LEAF, LEAF), jnp.float32)],
        compiler_params=pltpu.CompilerParams(vmem_limit_bytes=24 * 2**20),
        cost_estimate=pl.CostEstimate(
            flops=nb, transcendentals=0, bytes_accessed=nb
        ),
    )(*operands)


def first_panel(packed, nb):
    return panel_call(first_panel_kernel, 1, nb, packed)[0]


def next_panel(packed, w0):
    return panel_call(next_panel_kernel, 2, w0.shape[0], packed, w0)


def whole(memory=pltpu.VMEM):
    return pl.BlockSpec(memory_space=memory)


def block_of(array, memory=pltpu.VMEM):
    return pl.BlockSpec(array.shape, lambda *_: (0,) * array.ndim, memory_space=memory)


def faces_kernel(
    table_ref, cond_ref, ground_ref, info_ref, cells_ref, load_ref, panel_ref, basis_ref, *refs, sides, at, last_at
):
    *outs, conduct_ref, grounds_ref, given_ref, scaled_ref, held_ref, in_sems, out_sems = refs
    last = table_ref[last_at] != 0
    half = given_ref.shape[1]
    lanes = pl.ds(pl.multiple_of(table_ref[at] * half, half), half)
    pieces = in_sems.shape[0]
    height = given_ref.shape[0] // pieces
    copies_in, copies_out = [], []
    for i in range(pieces):
        rows = pl.ds(i * height, height)
        copies_in.append(
            pltpu.make_async_copy(basis_ref.at[rows, lanes], held_ref.at[rows], in_sems.at[i])
        )
        copies_out.append(
            pltpu.make_async_copy(held_ref.at[rows], given_ref.at[rows], out_sems.at[i])
        )
        copies_in[i].start()
    size_x, size_y, size_z = sides
    count, width = panel_ref.shape
    tile = 64
    classes = cond_ref.shape[0]
    ports = cells_ref.shape[1]

    def by_tile(t, carry):
        rows = pl.ds(pl.multiple_of(t * tile, tile), tile)
        kind = jnp.broadcast_to(info_ref[rows, 0:1], (tile, LEAF))
        ids = jnp.broadcast_to(info_ref[rows, 1:2], (tile, LEAF))
        conduct = jnp.zeros((tile, LEAF), jnp.float32)
        grounds = jnp.zeros((tile, LEAF), jnp.float32)
        for c in range(classes):
            conduct = jnp.where(kind == c, cond_ref[c], conduct)
            grounds = jnp.where(kind == c, ground_ref[c], grounds)
        loads = jnp.zeros((tile, LEAF), jnp.float32)
        for p in range(0, ports, LEAF):
            hit = ids == cells_ref[:, p : p + LEAF]
            loads = loads + jnp.where(hit, load_ref[:, p : p + LEAF], 0.0)
        conduct_ref[rows, :] = conduct
        grounds_ref[rows, :] = grounds + jnp.sum(loads, axis=1, keepdims=True)
        for p in range(0, width, LEAF):
            part = panel_ref[rows, p : p + LEAF].astype(jnp.float32)
            scaled_ref[p // LEAF, rows, :] = (
                (conduct * part).astype(jnp.bfloat16).astype(jnp.float32)
            )
        return carry

    lax.fori_loop(0, count // tile, by_tile, 0)
    for copy_in, copy_out in zip(copies_in, copies_out):
        copy_in.wait()
        copy_out.start()
    plane = size_y * size_z
    for p in range(width // LEAF):
        lanes = slice(p * LEAF, (p + 1) * LEAF)
        outs[0][:, lanes] = scaled_ref[p, 0:plane, :].astype(jnp.bfloat16)
        outs[1][:, lanes] = scaled_ref[p, count - plane : count, :].astype(jnp.bfloat16)
        for out, at in ((outs[2], 0), (outs[3], plane - size_z)):
            face = [
                scaled_ref[p, x * plane + at : x * plane + at + size_z, :] for x in range(size_x)
            ]
            out[:, lanes] = jnp.concatenate(face, 0).astype(jnp.bfloat16)
        low, high = (
            scaled_ref[p, pl.ds(at, size_x * size_y, stride=size_z), :] for at in (0, size_z - 1)
        )
        if len(outs) == 5:
            outs[4][:, lanes] = jnp.where(last, low, high).astype(jnp.bfloat16)
        else:
            outs[4][:, lanes] = low.astype(jnp.bfloat16)
            outs[5][:, lanes] = high.astype(jnp.bfloat16)
    for copy_out in copies_out:
        copy_out.wait()


def image_kernel(table_ref, panel_ref, conduct_ref, grounds_ref, *refs, sides, nb, last_at):
    *halos, image_ref, lead_ref, scaled_ref, square_ref = refs
    last = table_ref[last_at] != 0
    size_x, size_y, size_z = sides
    width = panel_ref.shape[1]
    plane = size_y * size_z
    subs = lax.broadcasted_iota(jnp.int32, (size_z, LEAF), 0)

    def by_lane(p, carry):
        lanes = pl.ds(pl.multiple_of(p * LEAF, LEAF), LEAF)
        x_low, x_high, y_low, y_high, *z_halos = (h[:, lanes].astype(jnp.float32) for h in halos)
        if len(z_halos) == 1:
            z_halos = [jnp.where(last, z_halos[0], 0.0), jnp.where(last, 0.0, z_halos[0])]
        z_low, z_high = z_halos
        scaled_ref[...] = (
            (conduct_ref[...] * panel_ref[:, lanes].astype(jnp.float32))
            .astype(jnp.bfloat16)
            .astype(jnp.float32)
        )

        def cell_rows(x, y):
            at = x * plane + y * size_z
            return scaled_ref[at : at + size_z, :]

        for x in range(size_x):
            done = []
            for y in range(size_y):
                at = x * plane + y * size_z
                here = cell_rows(x, y)
                span = slice(y * size_z, (y + 1) * size_z)
                total = cell_rows(x + 1, y) if x + 1 < size_x else x_high[span, :]
                total = total + (cell_rows(x - 1, y) if x > 0 else x_low[span, :])
                span = slice(x * size_z, (x + 1) * size_z)
                total = total + (cell_rows(x, y + 1) if y + 1 < size_y else y_high[span, :])
                total = total + (cell_rows(x, y - 1) if y > 0 else y_low[span, :])
                k = x * size_y + y
                up = jnp.where(
                    subs == size_z - 1, z_high[k : k + 1, :], pltpu.roll(here, size_z - 1, 0)
                )
                down = jnp.where(subs == 0, z_low[k : k + 1, :], pltpu.roll(here, 1, 0))
                total = total + up + down
                own = slice(at, at + size_z)
                done.append(
                    conduct_ref[own, :] * (6.0 * here - total)
                    + grounds_ref[own, :] * panel_ref[at : at + size_z, lanes].astype(jnp.float32)
                )
            image_ref[x * plane : (x + 1) * plane, lanes] = jnp.concatenate(done, 0).astype(
                jnp.bfloat16
            )
        return carry

    lax.fori_loop(0, width // LEAF, by_lane, 0)

    def product(rows, cols):
        return lax.dot_general(
            panel_ref[:, rows],
            image_ref[:, cols],
            (((0,), (0,)), ((), ())),
            preferred_element_type=jnp.float32,
        )

    blocks = nb // LEAF

    def put_block(number, value):
        lead_ref[number * LEAF : (number + 1) * LEAF, :] = value.astype(lead_ref.dtype)

    def lower(number):
        for i in range(blocks):
            for j in range(i + 1):
                row, col = slice(i * LEAF, (i + 1) * LEAF), slice(j * LEAF, (j + 1) * LEAF)
                put_block(number, 0.5 * (square_ref[row, col] + square_ref[col, row].T))
                number += 1
        return number

    head, tail = slice(0, nb), slice(nb, 2 * nb)
    square_ref[...] = product(head, head)
    number = lower(0)
    square_ref[...] = product(tail, tail)
    number = lower(number)
    below = product(tail, head)
    for j in range(blocks):
        for i in range(blocks):
            put_block(
                number + j * blocks + i,
                below[i * LEAF : (i + 1) * LEAF, j * LEAF : (j + 1) * LEAF],
            )


def products_kernel(table_ref, *refs):
    del table_ref
    out, count = refs[-1], len(refs) // 2
    bases = jnp.concatenate([ref[...] for ref in refs[:count]], 0)
    images = jnp.concatenate([ref[...] for ref in refs[count:-1]], 0)
    total = lax.dot_general(
        bases, images, (((0,), (0,)), ((), ())), preferred_element_type=jnp.float32
    )
    out[...] = total.astype(out.dtype)


def products(table, bases, images, lists, width, dtype):
    rows, cols = images[0].shape
    step = 512 if width % 512 == 0 else width
    parts = width // step
    steps = lists[0][1] * parts
    in_specs = [
        pl.BlockSpec(
            (rows, step), lambda t, tab, at=at: (0, tab[at + t // parts] * parts + t % parts)
        )
        for at, _ in lists
    ]
    in_specs += [pl.BlockSpec((rows, cols), lambda t, tab: (0, 0))] * len(images)
    total = steps * step
    return pl.pallas_call(
        products_kernel,
        grid_spec=pltpu.PrefetchScalarGridSpec(
            num_scalar_prefetch=1,
            grid=(steps,),
            in_specs=in_specs,
            out_specs=pl.BlockSpec((step, cols), lambda t, tab: (t, 0)),
        ),
        out_shape=jax.ShapeDtypeStruct((total, cols), dtype),
        compiler_params=pltpu.CompilerParams(vmem_limit_bytes=48 * 2**20),
        cost_estimate=pl.CostEstimate(
            flops=2 * total * cols * rows * len(bases),
            transcendentals=0,
            bytes_accessed=2 * rows * (total + cols) * len(bases) + 4 * total * cols,
        ),
    )(table, *bases, *images)


def add_kernel(table_ref, *refs):
    del table_ref
    total = refs[0][...].astype(jnp.float32)
    for got in refs[1:-1]:
        total = total + got[...].astype(jnp.float32)
    refs[-1][...] = total.astype(refs[-1].dtype)


def add_blocks(table, arrays, at, count, height, dtype):
    cols = arrays[0].shape[1]
    step = min(256, height)
    parts = height // step
    steps = count * parts
    spec = pl.BlockSpec((step, cols), lambda t, tab: (tab[at + t // parts] * parts + t % parts, 0))
    return pl.pallas_call(
        add_kernel,
        grid_spec=pltpu.PrefetchScalarGridSpec(
            num_scalar_prefetch=1,
            grid=(steps,),
            in_specs=[spec] * len(arrays),
            out_specs=pl.BlockSpec((step, cols), lambda t, tab: (t, 0)),
        ),
        out_shape=jax.ShapeDtypeStruct((steps * step, cols), dtype),
        compiler_params=pltpu.CompilerParams(vmem_limit_bytes=24 * 2**20),
        cost_estimate=pl.CostEstimate(
            flops=steps * step * cols,
            transcendentals=0,
            bytes_accessed=steps * step * cols * 4 * len(arrays),
        ),
    )(table, *arrays)


def plane_kernel(table_ref, *refs, groups, at):
    ins, outs, plane_ref = refs[: sum(groups)], refs[sum(groups) : -1], refs[-1]
    height = ins[0].shape[0]
    done = 0
    for i, count in enumerate(groups):
        total = ins[done][...].astype(jnp.float32)
        for got in ins[done + 1 : done + count]:
            total = total + got[...].astype(jnp.float32)
        plane_ref[i * height : (i + 1) * height, :] = total
        done += count
    for i, out in enumerate(outs):
        part = out.shape[0]
        rows = pl.ds(pl.multiple_of(table_ref[at + i] * part, part), part)
        out[...] = plane_ref[rows, :].astype(out.dtype)


def plane_parts(table, sums, height, at, outs):
    cols = sums[0][0][0].shape[1]

    def spec(place, block):
        if place is None:
            return pl.BlockSpec((height, cols), lambda t, tab: (block, 0))
        return pl.BlockSpec((height, cols), lambda t, tab: (tab[place], 0))

    return pl.pallas_call(
        functools.partial(plane_kernel, groups=[len(terms) for terms in sums], at=at),
        grid_spec=pltpu.PrefetchScalarGridSpec(
            num_scalar_prefetch=1,
            grid=(1,),
            in_specs=[spec(place, block) for terms in sums for _, place, block in terms],
            out_specs=[pl.BlockSpec(out.shape, lambda t, tab: (0, 0)) for out in outs],
            scratch_shapes=[pltpu.VMEM((height * len(sums), cols), jnp.float32)],
        ),
        out_shape=outs,
        compiler_params=pltpu.CompilerParams(vmem_limit_bytes=34 * 2**20),
        cost_estimate=pl.CostEstimate(
            flops=0, transcendentals=0, bytes_accessed=height * len(sums) * cols * 14
        ),
    )(table, *(array for terms in sums for array, _, _ in terms))


def swap_pairs():
    return [(0, 1), (1, 0)]


def join_kernel(table_ref, *refs, at):
    ins, outs = refs[:-2], refs[-2:]
    part = ins[0].shape[1]
    for d, block in enumerate(ins):
        rows = pl.ds(pl.multiple_of(table_ref[at + d] * part, part), part)
        for i, out in enumerate(outs):
            out[rows, :] = block[i]


def local(basis, classes, cond_table, ground_table, port_cells, port_load):
    sides = classes.shape
    cells_x, cells_y, cells_z = sides
    width_k = basis.shape[3]
    devices_x = lax.axis_size("gx")
    chips_y = lax.axis_size("gy")
    devices_z = lax.axis_size("gz")
    devices_y = 2 * chips_y
    spans = devices_x // 2
    split = spans // 2
    count = cells_x * cells_y * cells_z
    cols = PANELS * NB
    at_x, chip, core, at_z = (lax.axis_index(axis) for axis in ("gx", "gy", "core", "gz"))
    at_y = 2 * chip + core
    f32, bf16 = jnp.float32, jnp.bfloat16

    flat_basis = basis.reshape(count, width_k)
    wide = width_k // (devices_x * devices_z)
    narrow = wide // chips_y
    part = narrow // 2

    entries = []

    def put(values):
        entries.extend(values)
        return len(entries) - len(values), len(values)

    shift = core * spans * devices_z * chips_y

    def put_products(blocks):
        return [put([b + shift for b in blocks]), put(blocks)]

    lists_a, lists_b, next_a, next_b = [], [], [], []
    for d in range(devices_z):
        x = (at_z + d) % devices_z
        lists_a.append(
            put_products(
                [(zz * devices_z + x) * chips_y + y for zz in range(split) for y in range(chips_y)]
            )
        )
        next_b.append(put([zz * devices_z + x for zz in range(spans - split)]))
    for d in range(chips_y):
        y = (chip + d) % chips_y
        lists_b.append(
            put_products(
                [(zz * devices_z + x) * chips_y + y for zz in range(split, spans) for x in range(devices_z)]
            )
        )
        next_a.append(put([zz * chips_y + y for zz in range(split)]))
    leaving = [(at_x + step) % devices_x for step in range(devices_x)]
    leaving_at, _ = put(leaving + [at_x % spans * 2 + core, at_x % spans * 2 + 1 - core])
    given_at, _ = put([1 - core])
    last_at, _ = put([at_z == 1])
    places_at, _ = put([(at_y - d) % devices_y for d in range(devices_y)])
    order_at, _ = put([(at_y + d) % devices_y for d in range(devices_y)])
    home_at, _ = put([at_x // spans == core])
    first_at, _ = put([((at_x * devices_z + at_z) * devices_y + at_y) * part])
    table = jnp.stack([jnp.asarray(e, jnp.int32) for e in entries])

    def move(array, axis, d):
        size = lax.axis_size(axis)
        return lax.ppermute(array, axis, [(i, (i + d) % size) for i in range(size)])

    panel_spec = pl.BlockSpec((count, cols), lambda *_: (0, 0))
    port_rows, load_rows = port_cells[None, :], port_load[None, :]
    global_x = at_x * cells_x + jnp.arange(cells_x, dtype=jnp.int32)
    global_y = at_y * cells_y + jnp.arange(cells_y, dtype=jnp.int32)
    global_z = at_z * cells_z + jnp.arange(cells_z, dtype=jnp.int32)
    flat_ids = (
        (global_x[:, None, None] * (cells_y * devices_y) + global_y[None, :, None])
        * (cells_z * devices_z)
        + global_z[None, None, :]
    )
    info = jnp.stack([classes, flat_ids], -1).reshape(count, 2)
    face_rows = [cells_y * cells_z] * 2 + [cells_x * cells_z] * 2
    face_rows += [cells_x * cells_y] * (1 if devices_z == 2 else 2)
    outs = [jax.ShapeDtypeStruct((n, cols), bf16) for n in face_rows]
    outs += [jax.ShapeDtypeStruct((count, LEAF), f32)] * 2
    given = jax.ShapeDtypeStruct((count, width_k // 2), basis.dtype)
    *faces, conduct, grounds, given = pl.pallas_call(
        functools.partial(faces_kernel, sides=sides, at=given_at, last_at=last_at),
        out_shape=[*outs, given],
        grid_spec=pltpu.PrefetchScalarGridSpec(
            num_scalar_prefetch=1,
            grid=(1,),
            in_specs=[block_of(cond_table, pltpu.SMEM), block_of(ground_table, pltpu.SMEM)]
            + [block_of(info), block_of(port_rows), block_of(load_rows), panel_spec]
            + [pl.BlockSpec(memory_space=pl.ANY)],
            out_specs=[whole()] * len(outs) + [pl.BlockSpec(memory_space=pl.ANY)],
            scratch_shapes=[
                pltpu.VMEM((cols // LEAF, count, LEAF), f32),
                pltpu.VMEM((count, width_k // 2), basis.dtype),
                pltpu.SemaphoreType.DMA((4,)),
                pltpu.SemaphoreType.DMA((4,)),
            ],
        ),
        compiler_params=pltpu.CompilerParams(vmem_limit_bytes=56 * 2**20),
    )(table, cond_table, ground_table, info, port_rows, load_rows, flat_basis, flat_basis)
    halos = []
    for i, (axis, size) in enumerate(
        (("gx", devices_x), (("gy", "core"), devices_y), ("gz", devices_z))
    ):
        if i == 2 and size == 2:
            halos.append(lax.ppermute(faces[4], axis, swap_pairs()))
            continue
        low, high = faces[2 * i : 2 * i + 2]
        halos.append(lax.ppermute(high, axis, [(k, k + 1) for k in range(size - 1)]))
        halos.append(lax.ppermute(low, axis, [(k + 1, k) for k in range(size - 1)]))

    blocks = NB // LEAF
    lower_rows = blocks * (blocks + 1) // 2 * LEAF
    lead_rows = 2 * lower_rows + blocks * NB
    outs = [jax.ShapeDtypeStruct((n, width), bf16) for n, width in ((count, cols), (lead_rows, LEAF))]
    image, lead = pl.pallas_call(
        functools.partial(image_kernel, sides=sides, nb=NB, last_at=last_at),
        out_shape=outs,
        grid_spec=pltpu.PrefetchScalarGridSpec(
            num_scalar_prefetch=1,
            grid=(1,),
            in_specs=[panel_spec] + [whole()] * (2 + len(halos)),
            out_specs=[whole()] * 2,
            scratch_shapes=[pltpu.VMEM((count, LEAF), f32), pltpu.VMEM((NB, NB), f32)],
        ),
        compiler_params=pltpu.CompilerParams(vmem_limit_bytes=56 * 2**20),
    )(table, flat_basis, conduct, grounds, *halos)

    other_image = lax.ppermute(image, "core", swap_pairs())
    other_basis = lax.ppermute(given, "core", swap_pairs())

    plane_axes = ("gy", "gz")
    chips = chips_y * devices_z

    def exchanged(rows, axes):
        return lax.all_to_all(rows, axes, split_axis=0, concat_axis=0, tiled=True)

    def for_all(own, size):
        return jnp.broadcast_to(own, (size, *own.shape))

    lead_terms = exchanged(lead.reshape(chips, -1, LEAF), plane_axes)

    def chip_products(images, lists, dtype):
        return products(table, [flat_basis, other_basis], images, lists, narrow, dtype)

    images, _ = lax.optimization_barrier(([image, other_image], lead))
    sent_a = [chip_products(images, lists_a[d], bf16) for d in range(1, devices_z)]
    sent_b = [chip_products(images, lists_b[d], bf16) for d in range(1, chips_y)]
    got_a = [move(a, "gz", d) for d, a in enumerate(sent_a, 1)]
    got_b = [move(a, "gy", d) for d, a in enumerate(sent_b, 1)]
    images, _ = lax.optimization_barrier((images, (sent_a, sent_b)))
    own_a, own_b = (chip_products(images, lists[0], f32) for lists in (lists_a, lists_b))
    lead_terms, _ = lax.optimization_barrier((lead_terms, (sent_a, sent_b)))
    own = jnp.sum(lead_terms.astype(f32), axis=0).reshape(2, -1, LEAF)
    kept = lax.dynamic_index_in_dim(own, core, 0, keepdims=False)
    sent = lax.dynamic_index_in_dim(own, 1 - core, 0, keepdims=False)
    own = kept + lax.ppermute(sent, "core", swap_pairs())
    own, _ = lax.optimization_barrier((own, (own_a, own_b)))
    own = own.reshape(devices_x, -1, LEAF)
    own = jnp.sum(exchanged(own, "gx"), axis=0)
    own = exchanged(for_all(own, devices_x), "gx").reshape(-1, LEAF)
    own = for_all(own, chips)
    (got_a, got_b), _ = lax.optimization_barrier(((got_a, got_b), own))
    lead_half = exchanged(own, plane_axes)
    sums_a, sums_b = [own_a, *got_a], [own_b, *got_b]

    further_a = [add_blocks(table, sums_a, *next_a[d], narrow, bf16) for d in range(1, chips_y)]
    further_b = [add_blocks(table, sums_b, *next_b[d], narrow, bf16) for d in range(1, devices_z)]
    lead_half, _ = lax.optimization_barrier((lead_half, (further_a, further_b)))
    further_a = [move(a, "gy", d) for d, a in enumerate(further_a, 1)]
    further_b = [move(a, "gz", d) for d, a in enumerate(further_b, 1)]
    other = lax.ppermute(lead_half, "core", swap_pairs())
    halves = jnp.where(core == 0, lead_half, other), jnp.where(core == 0, other, lead_half)
    lead = jnp.stack(halves, 1).reshape(lead_rows, LEAF)
    first_rows, later_rows = lead[:lower_rows], lead[lower_rows:]
    inverse_0 = first_panel(first_rows, NB)
    (further_a, further_b), inverse_0 = lax.optimization_barrier(
        ((further_a, further_b), inverse_0)
    )

    terms = []
    for zz in range(split):
        at = next_a[0][0] + zz
        terms.append([(a, at, None) for a in sums_a] + [(a, None, zz) for a in further_a])
    for zz in range(spans - split):
        at = next_b[0][0] + zz
        terms.append([(a, at, None) for a in sums_b] + [(a, None, zz) for a in further_b])
    outs = [jax.ShapeDtypeStruct((part, cols), bf16)] * devices_x
    outs += [jax.ShapeDtypeStruct((part, cols), f32)] * 2
    *x_sent, own, swapped = plane_parts(table, terms, narrow, leaving_at, outs)
    x_got = []
    for step in range(devices_x):
        pairs = []
        for x in range(devices_x):
            for y in range(devices_y):
                to = (x + step) % devices_x
                dest_x = (y % 2) * spans + to // 2
                dest_y = (y // 2) * 2 + to % 2
                if dest_x != x:
                    pairs.append((x * devices_y + y, dest_x * devices_y + dest_y))
        x_got.append(lax.ppermute(x_sent[step], ("gx", "gy", "core"), pairs))
    swapped = lax.ppermute(swapped, "core", swap_pairs())
    later_rows, _ = lax.optimization_barrier((later_rows, x_sent))
    factor_10, inverse_1 = next_panel(later_rows, inverse_0)
    (x_got, swapped), inverse_1 = lax.optimization_barrier(((x_got, swapped), inverse_1))
    pair = jax.ShapeDtypeStruct((2, part, cols // devices_y), f32)
    ins = [own, swapped, *x_got, inverse_0, factor_10, inverse_1]
    pairs = list(pl.pallas_call(
        functools.partial(factor_kernel, at=(home_at, order_at, first_at)),
        out_shape=[pair] * devices_y,
        grid_spec=pltpu.PrefetchScalarGridSpec(
            num_scalar_prefetch=1,
            grid=(1,),
            in_specs=[block_of(a) for a in ins],
            out_specs=[block_of(pair)] * devices_y,
            scratch_shapes=[pltpu.VMEM((part, cols), f32)] * 2,
        ),
        compiler_params=pltpu.CompilerParams(vmem_limit_bytes=44 * 2**20),
    )(table, *ins))
    for d in range(1, devices_y):
        route = [(i, (i + d) % devices_y) for i in range(devices_y)]
        pairs[d] = lax.ppermute(pairs[d], ("gy", "core"), route)
    out = jax.ShapeDtypeStruct((devices_y * part, cols // devices_y), f32)
    return pl.pallas_call(
        functools.partial(join_kernel, at=places_at),
        out_shape=(out, out),
        grid_spec=pltpu.PrefetchScalarGridSpec(
            num_scalar_prefetch=1,
            grid=(1,),
            in_specs=[block_of(a) for a in pairs],
            out_specs=[block_of(out)] * 2,
        ),
        compiler_params=pltpu.CompilerParams(vmem_limit_bytes=44 * 2**20),
    )(table, *pairs)


def solution(mesh):
    sizes = mesh.shape
    fine = jax.sharding.Mesh(
        mesh.devices.reshape(sizes["gx"], sizes["gy"] // 2, 2, sizes["gz"]),
        ("gx", "gy", "core", "gz"),
    )
    grid = ("gx", ("gy", "core"), "gz")
    out = P(("gx", "gz"), ("gy", "core"))
    return jax.shard_map(
        local,
        mesh=fine,
        in_specs=(P(*grid, None), P(*grid), P(), P(), P(), P()),
        out_specs=(out, out),
        check_vma=False,
    )
```

```python
import functools

import jax
import jax.numpy as jnp
from jax import lax
from jax.experimental import pallas as pl
from jax.experimental.pallas import tpu as pltpu
from jax.sharding import PartitionSpec as P

NB = 512
PANELS = 2
LEAF = 128
SUB = 8


def dot3(a, b, dims):
    a_hi = a.astype(jnp.bfloat16)
    b_hi = b.astype(jnp.bfloat16)
    a_lo = (a - a_hi.astype(jnp.float32)).astype(jnp.bfloat16)
    b_lo = (b - b_hi.astype(jnp.float32)).astype(jnp.bfloat16)

    def dot(x, y):
        return lax.dot_general(x, y, (dims, ((), ())), preferred_element_type=jnp.float32)

    return dot(a_hi, b_hi) + (dot(a_hi, b_lo) + dot(a_lo, b_hi))


def inverse_of(d):
    guess = pl.reciprocal(d, approx=True)
    return guess * (2.0 - d * guess)


def leaf_inverse(block_ref):
    lanes = lax.broadcasted_iota(jnp.int32, (SUB, LEAF), 1)
    subs = lax.broadcasted_iota(jnp.int32, (SUB, LEAF), 0)
    shape = (SUB, LEAF)
    panels = LEAF // SUB
    rows = block_ref[0:SUB, :]
    for t in range(panels):
        j0 = t * SUB
        after = t + 1 < panels

        def columns(array):
            return [jnp.broadcast_to(array[:, j0 + k : j0 + k + 1], shape) for k in range(SUB)]

        cols = columns(rows)
        p = [[jnp.broadcast_to(cols[k][i : i + 1, :], shape) for k in range(i + 1)] for i in range(SUB)]
        in_block = jnp.logical_and(lanes >= j0, lanes < j0 + SUB)
        start = jnp.where(in_block, (lanes - j0 == subs).astype(jnp.float32), rows)
        u = [jnp.broadcast_to(start[k : k + 1, :], shape) for k in range(SUB)]
        if after:
            below = block_ref[j0 + SUB : j0 + 2 * SUB, :]
            c = columns(below)
            rows = jnp.where(in_block, 0.0, below)
        inv = [None] * SUB
        factor = [[None] * SUB for _ in range(SUB)]
        for k in range(SUB):
            products = {(i, j): p[i][k] * p[j][k] for i in range(k + 1, SUB) for j in range(k + 1, i + 1)}
            inv[k] = inverse_of(p[k][k])
            for (i, j), product in products.items():
                p[i][j] = p[i][j] - product * inv[k]
            if after:
                step = c[k] * inv[k]
                rows = rows - step * u[k]
            for i in range(k + 1, SUB):
                factor[i][k] = p[i][k] * inv[k]
                u[i] = u[i] - factor[i][k] * u[k]
                if after:
                    c[i] = c[i] - step * p[i][k]
        out = u[0] * lax.rsqrt(p[0][0])
        for k in range(1, SUB):
            out = jnp.where(subs == k, u[k] * lax.rsqrt(p[k][k]), out)
        block_ref[j0 : j0 + SUB, :] = out
        if t + 2 >= panels:
            continue
        z = [None] * SUB
        for k in reversed(range(SUB)):
            z[k] = u[k] * inv[k]
            for i in range(k + 1, SUB):
                z[k] = z[k] - factor[i][k] * z[i]
        for v in range(t + 2, panels):
            below = block_ref[v * SUB : (v + 1) * SUB, :]
            upd = jnp.where(in_block, 0.0, below)
            for k in reversed(range(SUB)):
                upd = upd - jnp.broadcast_to(below[:, j0 + k : j0 + k + 1], shape) * z[k]
            block_ref[v * SUB : (v + 1) * SUB, :] = upd


def factor_inverse(s_ref, d_ref):
    width = s_ref.shape[0]
    row_ids = lax.broadcasted_iota(jnp.int32, (width, width), 0)
    col_ids = lax.broadcasted_iota(jnp.int32, (width, width), 1)
    wide_cols = lax.broadcasted_iota(jnp.int32, (LEAF, width), 1)
    leaf_rows = lax.broadcasted_iota(jnp.int32, (LEAF, LEAF), 0)
    leaf_cols = lax.broadcasted_iota(jnp.int32, (LEAF, LEAF), 1)

    def step(b, carry):
        off = pl.multiple_of(b * LEAF, LEAF)
        span = pl.ds(off, LEAF)
        d_ref[...] = s_ref[span, span]
        leaf_inverse(d_ref)
        inverse = jnp.where(leaf_rows >= leaf_cols, d_ref[...], 0.0)
        s_ref[span, span] = (leaf_rows == leaf_cols).astype(jnp.float32)
        upper = dot3(inverse, s_ref[span, :], ((1,), (0,)))
        s_ref[span, :] = upper

        @pl.when(b < width // LEAF - 1)
        def _():
            tail = jnp.where(wide_cols >= off + LEAF, upper, 0.0)
            current = s_ref[...]
            dead = jnp.logical_and(
                row_ids >= off + LEAF, jnp.logical_and(col_ids >= off, col_ids < off + LEAF)
            )
            s_ref[...] = jnp.where(dead, 0.0, current) - dot3(tail, upper, ((0,), (0,)))

        return carry

    lax.fori_loop(0, width // LEAF, step, 0)
    s_ref[...] = jnp.where(row_ids >= col_ids, s_ref[...], 0.0)


def unpack_symmetric(packed_ref, s_ref):
    at = 0
    for i in range(s_ref.shape[0] // LEAF):
        for j in range(i + 1):
            block = packed_ref[at * LEAF : (at + 1) * LEAF, :]
            s_ref[i * LEAF : (i + 1) * LEAF, j * LEAF : (j + 1) * LEAF] = block
            if j < i:
                s_ref[j * LEAF : (j + 1) * LEAF, i * LEAF : (i + 1) * LEAF] = block.T
            at += 1


def first_panel_kernel(packed_ref, w_ref, d_ref):
    unpack_symmetric(packed_ref, w_ref)
    factor_inverse(w_ref, d_ref)


def next_panel_kernel(packed_ref, w0_ref, f_ref, w_ref, d_ref):
    nb = w0_ref.shape[0]
    blocks = nb // LEAF
    unpack_symmetric(packed_ref, w_ref)
    start = packed_ref.shape[0] - blocks * nb
    below = jnp.concatenate(
        [packed_ref[start + i * nb : start + (i + 1) * nb, :] for i in range(nb // LEAF)], 1
    )
    below = dot3(below, w0_ref[...], ((1,), (1,)))
    f_ref[...] = below
    w_ref[...] = w_ref[...] - dot3(below, below, ((1,), (1,)))
    factor_inverse(w_ref, d_ref)


def factor_kernel(table_ref, own_ref, swapped_ref, *refs, at):
    home_at, order_at, first_at = at
    cols = own_ref.shape[1]
    *ins, rows_ref, all_ref = refs
    count = cols // ins[-1].shape[2]
    ins, blocks = ins[:-count], ins[-count:]
    *ins, w0_ref, f_ref, w1_ref = ins
    total = jnp.where(table_ref[home_at] != 0, own_ref[...], swapped_ref[...])
    for got in ins:
        total = total + got[...].astype(jnp.float32)
    rows_ref[...] = total
    nb = w0_ref.shape[0]
    ids = table_ref[first_at] + lax.broadcasted_iota(jnp.int32, (rows_ref.shape[0], nb), 0)
    columns = lax.broadcasted_iota(jnp.int32, (rows_ref.shape[0], nb), 1)
    part = dot3(rows_ref[:, :nb], w0_ref[...], ((1,), (1,)))
    rest = rows_ref[:, nb:] - dot3(part, f_ref[...], ((1,), (1,)))
    rest = dot3(rest, w1_ref[...], ((1,), (1,)))
    all_ref[:, :nb] = jnp.where(columns <= ids, part, 0.0)
    all_ref[:, nb:] = jnp.where(columns + nb <= ids, rest, 0.0)
    for d, block in enumerate(blocks):
        width = block.shape[2]
        span = pl.ds(pl.multiple_of(table_ref[order_at + d] * width, width), width)
        block[0] = rows_ref[:, span]
        block[1] = all_ref[:, span]


def panel_call(kernel, outputs, nb, *operands):
    return pl.pallas_call(
        kernel,
        out_shape=[jax.ShapeDtypeStruct((nb, nb), jnp.float32)] * outputs,
        in_specs=[pl.BlockSpec(memory_space=pltpu.VMEM)] * len(operands),
        out_specs=[pl.BlockSpec(memory_space=pltpu.VMEM)] * outputs,
        scratch_shapes=[pltpu.VMEM((LEAF, LEAF), jnp.float32)],
        compiler_params=pltpu.CompilerParams(vmem_limit_bytes=24 * 2**20),
        cost_estimate=pl.CostEstimate(
            flops=nb, transcendentals=0, bytes_accessed=nb
        ),
    )(*operands)


def first_panel(packed, nb):
    return panel_call(first_panel_kernel, 1, nb, packed)[0]


def next_panel(packed, w0):
    return panel_call(next_panel_kernel, 2, w0.shape[0], packed, w0)


def whole(memory=pltpu.VMEM):
    return pl.BlockSpec(memory_space=memory)


def block_of(array, memory=pltpu.VMEM):
    return pl.BlockSpec(array.shape, lambda *_: (0,) * array.ndim, memory_space=memory)


def faces_kernel(
    table_ref, cond_ref, ground_ref, info_ref, cells_ref, load_ref, panel_ref, basis_ref, *refs, sides, at, last_at
):
    *outs, conduct_ref, grounds_ref, given_ref, scaled_ref, held_ref, in_sems, out_sems = refs
    last = table_ref[last_at] != 0
    half = given_ref.shape[1]
    lanes = pl.ds(pl.multiple_of(table_ref[at] * half, half), half)
    pieces = in_sems.shape[0]
    height = given_ref.shape[0] // pieces
    copies_in, copies_out = [], []
    for i in range(pieces):
        rows = pl.ds(i * height, height)
        copies_in.append(
            pltpu.make_async_copy(basis_ref.at[rows, lanes], held_ref.at[rows], in_sems.at[i])
        )
        copies_out.append(
            pltpu.make_async_copy(held_ref.at[rows], given_ref.at[rows], out_sems.at[i])
        )
        copies_in[i].start()
    size_x, size_y, size_z = sides
    count, width = panel_ref.shape
    tile = 64
    classes = cond_ref.shape[0]
    ports = cells_ref.shape[1]

    def by_tile(t, carry):
        rows = pl.ds(pl.multiple_of(t * tile, tile), tile)
        kind = jnp.broadcast_to(info_ref[rows, 0:1], (tile, LEAF))
        ids = jnp.broadcast_to(info_ref[rows, 1:2], (tile, LEAF))
        conduct = jnp.zeros((tile, LEAF), jnp.float32)
        grounds = jnp.zeros((tile, LEAF), jnp.float32)
        for c in range(classes):
            conduct = jnp.where(kind == c, cond_ref[c], conduct)
            grounds = jnp.where(kind == c, ground_ref[c], grounds)
        loads = jnp.zeros((tile, LEAF), jnp.float32)
        for p in range(0, ports, LEAF):
            hit = ids == cells_ref[:, p : p + LEAF]
            loads = loads + jnp.where(hit, load_ref[:, p : p + LEAF], 0.0)
        conduct_ref[rows, :] = conduct
        grounds_ref[rows, :] = grounds + jnp.sum(loads, axis=1, keepdims=True)
        for p in range(0, width, LEAF):
            part = panel_ref[rows, p : p + LEAF].astype(jnp.float32)
            scaled_ref[p // LEAF, rows, :] = (
                (conduct * part).astype(jnp.bfloat16).astype(jnp.float32)
            )
        return carry

    lax.fori_loop(0, count // tile, by_tile, 0)
    for copy_in, copy_out in zip(copies_in, copies_out):
        copy_in.wait()
        copy_out.start()
    plane = size_y * size_z
    for p in range(width // LEAF):
        lanes = slice(p * LEAF, (p + 1) * LEAF)
        outs[0][:, lanes] = scaled_ref[p, 0:plane, :].astype(jnp.bfloat16)
        outs[1][:, lanes] = scaled_ref[p, count - plane : count, :].astype(jnp.bfloat16)
        for out, at in ((outs[2], 0), (outs[3], plane - size_z)):
            face = [
                scaled_ref[p, x * plane + at : x * plane + at + size_z, :] for x in range(size_x)
            ]
            out[:, lanes] = jnp.concatenate(face, 0).astype(jnp.bfloat16)
        low, high = (
            scaled_ref[p, pl.ds(at, size_x * size_y, stride=size_z), :] for at in (0, size_z - 1)
        )
        if len(outs) == 5:
            outs[4][:, lanes] = jnp.where(last, low, high).astype(jnp.bfloat16)
        else:
            outs[4][:, lanes] = low.astype(jnp.bfloat16)
            outs[5][:, lanes] = high.astype(jnp.bfloat16)
    for copy_out in copies_out:
        copy_out.wait()


def image_kernel(table_ref, panel_ref, conduct_ref, grounds_ref, *refs, sides, nb, last_at):
    *halos, image_ref, lead_ref, scaled_ref, square_ref = refs
    last = table_ref[last_at] != 0
    size_x, size_y, size_z = sides
    width = panel_ref.shape[1]
    plane = size_y * size_z
    subs = lax.broadcasted_iota(jnp.int32, (size_z, LEAF), 0)

    def by_lane(p, carry):
        lanes = pl.ds(pl.multiple_of(p * LEAF, LEAF), LEAF)
        x_low, x_high, y_low, y_high, *z_halos = (h[:, lanes].astype(jnp.float32) for h in halos)
        if len(z_halos) == 1:
            z_halos = [jnp.where(last, z_halos[0], 0.0), jnp.where(last, 0.0, z_halos[0])]
        z_low, z_high = z_halos
        scaled_ref[...] = (
            (conduct_ref[...] * panel_ref[:, lanes].astype(jnp.float32))
            .astype(jnp.bfloat16)
            .astype(jnp.float32)
        )

        def cell_rows(x, y):
            at = x * plane + y * size_z
            return scaled_ref[at : at + size_z, :]

        for x in range(size_x):
            done = []
            for y in range(size_y):
                at = x * plane + y * size_z
                here = cell_rows(x, y)
                span = slice(y * size_z, (y + 1) * size_z)
                total = cell_rows(x + 1, y) if x + 1 < size_x else x_high[span, :]
                total = total + (cell_rows(x - 1, y) if x > 0 else x_low[span, :])
                span = slice(x * size_z, (x + 1) * size_z)
                total = total + (cell_rows(x, y + 1) if y + 1 < size_y else y_high[span, :])
                total = total + (cell_rows(x, y - 1) if y > 0 else y_low[span, :])
                k = x * size_y + y
                up = jnp.where(
                    subs == size_z - 1, z_high[k : k + 1, :], pltpu.roll(here, size_z - 1, 0)
                )
                down = jnp.where(subs == 0, z_low[k : k + 1, :], pltpu.roll(here, 1, 0))
                total = total + up + down
                own = slice(at, at + size_z)
                done.append(
                    conduct_ref[own, :] * (6.0 * here - total)
                    + grounds_ref[own, :] * panel_ref[at : at + size_z, lanes].astype(jnp.float32)
                )
            image_ref[x * plane : (x + 1) * plane, lanes] = jnp.concatenate(done, 0).astype(
                jnp.bfloat16
            )
        return carry

    lax.fori_loop(0, width // LEAF, by_lane, 0)

    def product(rows, cols):
        return lax.dot_general(
            panel_ref[:, rows],
            image_ref[:, cols],
            (((0,), (0,)), ((), ())),
            preferred_element_type=jnp.float32,
        )

    blocks = nb // LEAF

    def put_block(number, value):
        lead_ref[number * LEAF : (number + 1) * LEAF, :] = value.astype(lead_ref.dtype)

    def lower(number):
        for i in range(blocks):
            for j in range(i + 1):
                row, col = slice(i * LEAF, (i + 1) * LEAF), slice(j * LEAF, (j + 1) * LEAF)
                put_block(number, 0.5 * (square_ref[row, col] + square_ref[col, row].T))
                number += 1
        return number

    head, tail = slice(0, nb), slice(nb, 2 * nb)
    square_ref[...] = product(head, head)
    number = lower(0)
    square_ref[...] = product(tail, tail)
    number = lower(number)
    below = product(tail, head)
    for j in range(blocks):
        for i in range(blocks):
            put_block(
                number + j * blocks + i,
                below[i * LEAF : (i + 1) * LEAF, j * LEAF : (j + 1) * LEAF],
            )


def products_kernel(table_ref, *refs):
    del table_ref
    out, count = refs[-1], len(refs) // 2
    bases = jnp.concatenate([ref[...] for ref in refs[:count]], 0)
    images = jnp.concatenate([ref[...] for ref in refs[count:-1]], 0)
    total = lax.dot_general(
        bases, images, (((0,), (0,)), ((), ())), preferred_element_type=jnp.float32
    )
    out[...] = total.astype(out.dtype)


def products(table, bases, images, lists, width, dtype, weight=1):
    rows, cols = images[0].shape
    step = 512 if width % 512 == 0 else width
    parts = width // step
    steps = lists[0][1] * parts
    in_specs = [
        pl.BlockSpec(
            (rows, step), lambda t, tab, at=at: (0, tab[at + t // parts] * parts + t % parts)
        )
        for at, _ in lists
    ]
    in_specs += [pl.BlockSpec((rows, cols), lambda t, tab: (0, 0))] * len(images)
    total = steps * step
    return pl.pallas_call(
        products_kernel,
        grid_spec=pltpu.PrefetchScalarGridSpec(
            num_scalar_prefetch=1,
            grid=(steps,),
            in_specs=in_specs,
            out_specs=pl.BlockSpec((step, cols), lambda t, tab: (t, 0)),
        ),
        out_shape=jax.ShapeDtypeStruct((total, cols), dtype),
        compiler_params=pltpu.CompilerParams(vmem_limit_bytes=48 * 2**20),
        cost_estimate=pl.CostEstimate(
            flops=2 * total * cols * rows * len(bases) * weight,
            transcendentals=0,
            bytes_accessed=2 * rows * (total + cols) * len(bases) + 4 * total * cols,
        ),
    )(table, *bases, *images)


def add_kernel(table_ref, *refs):
    del table_ref
    total = refs[0][...].astype(jnp.float32)
    for got in refs[1:-1]:
        total = total + got[...].astype(jnp.float32)
    refs[-1][...] = total.astype(refs[-1].dtype)


def add_blocks(table, arrays, at, count, height, dtype):
    cols = arrays[0].shape[1]
    step = min(256, height)
    parts = height // step
    steps = count * parts
    spec = pl.BlockSpec((step, cols), lambda t, tab: (tab[at + t // parts] * parts + t % parts, 0))
    return pl.pallas_call(
        add_kernel,
        grid_spec=pltpu.PrefetchScalarGridSpec(
            num_scalar_prefetch=1,
            grid=(steps,),
            in_specs=[spec] * len(arrays),
            out_specs=pl.BlockSpec((step, cols), lambda t, tab: (t, 0)),
        ),
        out_shape=jax.ShapeDtypeStruct((steps * step, cols), dtype),
        compiler_params=pltpu.CompilerParams(vmem_limit_bytes=24 * 2**20),
        cost_estimate=pl.CostEstimate(
            flops=steps * step * cols,
            transcendentals=0,
            bytes_accessed=steps * step * cols * 4 * len(arrays),
        ),
    )(table, *arrays)


def plane_kernel(table_ref, *refs, groups, at):
    ins, outs, plane_ref = refs[: sum(groups)], refs[sum(groups) : -1], refs[-1]
    height = ins[0].shape[0]
    done = 0
    for i, count in enumerate(groups):
        total = ins[done][...].astype(jnp.float32)
        for got in ins[done + 1 : done + count]:
            total = total + got[...].astype(jnp.float32)
        plane_ref[i * height : (i + 1) * height, :] = total
        done += count
    for i, out in enumerate(outs):
        part = out.shape[0]
        rows = pl.ds(pl.multiple_of(table_ref[at + i] * part, part), part)
        out[...] = plane_ref[rows, :].astype(out.dtype)


def plane_parts(table, sums, height, at, outs):
    cols = sums[0][0][0].shape[1]

    def spec(place, block):
        if place is None:
            return pl.BlockSpec((height, cols), lambda t, tab: (block, 0))
        return pl.BlockSpec((height, cols), lambda t, tab: (tab[place], 0))

    return pl.pallas_call(
        functools.partial(plane_kernel, groups=[len(terms) for terms in sums], at=at),
        grid_spec=pltpu.PrefetchScalarGridSpec(
            num_scalar_prefetch=1,
            grid=(1,),
            in_specs=[spec(place, block) for terms in sums for _, place, block in terms],
            out_specs=[pl.BlockSpec(out.shape, lambda t, tab: (0, 0)) for out in outs],
            scratch_shapes=[pltpu.VMEM((height * len(sums), cols), jnp.float32)],
        ),
        out_shape=outs,
        compiler_params=pltpu.CompilerParams(vmem_limit_bytes=34 * 2**20),
        cost_estimate=pl.CostEstimate(
            flops=0, transcendentals=0, bytes_accessed=height * len(sums) * cols * 14
        ),
    )(table, *(array for terms in sums for array, _, _ in terms))


def swap_pairs():
    return [(0, 1), (1, 0)]


def join_kernel(table_ref, *refs, at):
    ins, outs = refs[:-2], refs[-2:]
    part = ins[0].shape[1]
    for d, block in enumerate(ins):
        rows = pl.ds(pl.multiple_of(table_ref[at + d] * part, part), part)
        for i, out in enumerate(outs):
            out[rows, :] = block[i]


def local(basis, classes, cond_table, ground_table, port_cells, port_load):
    sides = classes.shape
    cells_x, cells_y, cells_z = sides
    width_k = basis.shape[3]
    devices_x = lax.axis_size("gx")
    chips_y = lax.axis_size("gy")
    devices_z = lax.axis_size("gz")
    devices_y = 2 * chips_y
    spans = devices_x // 2
    split = spans // 2
    count = cells_x * cells_y * cells_z
    cols = PANELS * NB
    at_x, chip, core, at_z = (lax.axis_index(axis) for axis in ("gx", "gy", "core", "gz"))
    at_y = 2 * chip + core
    f32, bf16 = jnp.float32, jnp.bfloat16

    flat_basis = basis.reshape(count, width_k)
    wide = width_k // (devices_x * devices_z)
    narrow = wide // chips_y
    part = narrow // 2

    entries = []

    def put(values):
        entries.extend(values)
        return len(entries) - len(values), len(values)

    shift = core * spans * devices_z * chips_y

    def put_products(blocks):
        return [put([b + shift for b in blocks]), put(blocks)]

    lists_a, lists_b, next_a, next_b = [], [], [], []
    for d in range(devices_z):
        x = (at_z + d) % devices_z
        lists_a.append(
            put_products(
                [(zz * devices_z + x) * chips_y + y for zz in range(split) for y in range(chips_y)]
            )
        )
        next_b.append(put([zz * devices_z + x for zz in range(spans - split)]))
    for d in range(chips_y):
        y = (chip + d) % chips_y
        lists_b.append(
            put_products(
                [(zz * devices_z + x) * chips_y + y for zz in range(split, spans) for x in range(devices_z)]
            )
        )
        next_a.append(put([zz * chips_y + y for zz in range(split)]))
    leaving = [(at_x + step) % devices_x for step in range(devices_x)]
    leaving_at, _ = put(leaving + [at_x % spans * 2 + core, at_x % spans * 2 + 1 - core])
    given_at, _ = put([1 - core])
    last_at, _ = put([at_z == 1])
    places_at, _ = put([(at_y - d) % devices_y for d in range(devices_y)])
    order_at, _ = put([(at_y + d) % devices_y for d in range(devices_y)])
    home_at, _ = put([at_x // spans == core])
    first_at, _ = put([((at_x * devices_z + at_z) * devices_y + at_y) * part])
    table = jnp.stack([jnp.asarray(e, jnp.int32) for e in entries])

    def move(array, axis, d):
        size = lax.axis_size(axis)
        return lax.ppermute(array, axis, [(i, (i + d) % size) for i in range(size)])

    panel_spec = pl.BlockSpec((count, cols), lambda *_: (0, 0))
    port_rows, load_rows = port_cells[None, :], port_load[None, :]
    global_x = at_x * cells_x + jnp.arange(cells_x, dtype=jnp.int32)
    global_y = at_y * cells_y + jnp.arange(cells_y, dtype=jnp.int32)
    global_z = at_z * cells_z + jnp.arange(cells_z, dtype=jnp.int32)
    flat_ids = (
        (global_x[:, None, None] * (cells_y * devices_y) + global_y[None, :, None])
        * (cells_z * devices_z)
        + global_z[None, None, :]
    )
    info = jnp.stack([classes, flat_ids], -1).reshape(count, 2)
    face_rows = [cells_y * cells_z] * 2 + [cells_x * cells_z] * 2
    face_rows += [cells_x * cells_y] * (1 if devices_z == 2 else 2)
    outs = [jax.ShapeDtypeStruct((n, cols), bf16) for n in face_rows]
    outs += [jax.ShapeDtypeStruct((count, LEAF), f32)] * 2
    given = jax.ShapeDtypeStruct((count, width_k // 2), basis.dtype)
    *faces, conduct, grounds, given = pl.pallas_call(
        functools.partial(faces_kernel, sides=sides, at=given_at, last_at=last_at),
        out_shape=[*outs, given],
        grid_spec=pltpu.PrefetchScalarGridSpec(
            num_scalar_prefetch=1,
            grid=(1,),
            in_specs=[block_of(cond_table, pltpu.SMEM), block_of(ground_table, pltpu.SMEM)]
            + [block_of(info), block_of(port_rows), block_of(load_rows), panel_spec]
            + [pl.BlockSpec(memory_space=pl.ANY)],
            out_specs=[whole()] * len(outs) + [pl.BlockSpec(memory_space=pl.ANY)],
            scratch_shapes=[
                pltpu.VMEM((cols // LEAF, count, LEAF), f32),
                pltpu.VMEM((count, width_k // 2), basis.dtype),
                pltpu.SemaphoreType.DMA((4,)),
                pltpu.SemaphoreType.DMA((4,)),
            ],
        ),
        compiler_params=pltpu.CompilerParams(vmem_limit_bytes=56 * 2**20),
    )(table, cond_table, ground_table, info, port_rows, load_rows, flat_basis, flat_basis)
    halos = []
    for i, (axis, size) in enumerate(
        (("gx", devices_x), (("gy", "core"), devices_y), ("gz", devices_z))
    ):
        if i == 2 and size == 2:
            halos.append(lax.ppermute(faces[4], axis, swap_pairs()))
            continue
        low, high = faces[2 * i : 2 * i + 2]
        halos.append(lax.ppermute(high, axis, [(k, k + 1) for k in range(size - 1)]))
        halos.append(lax.ppermute(low, axis, [(k + 1, k) for k in range(size - 1)]))

    blocks = NB // LEAF
    lower_rows = blocks * (blocks + 1) // 2 * LEAF
    lead_rows = 2 * lower_rows + blocks * NB
    outs = [jax.ShapeDtypeStruct((n, width), bf16) for n, width in ((count, cols), (lead_rows, LEAF))]
    image, lead = pl.pallas_call(
        functools.partial(image_kernel, sides=sides, nb=NB, last_at=last_at),
        out_shape=outs,
        grid_spec=pltpu.PrefetchScalarGridSpec(
            num_scalar_prefetch=1,
            grid=(1,),
            in_specs=[panel_spec] + [whole()] * (2 + len(halos)),
            out_specs=[whole()] * 2,
            scratch_shapes=[pltpu.VMEM((count, LEAF), f32), pltpu.VMEM((NB, NB), f32)],
        ),
        compiler_params=pltpu.CompilerParams(vmem_limit_bytes=56 * 2**20),
    )(table, flat_basis, conduct, grounds, *halos)

    other_image = lax.ppermute(image, "core", swap_pairs())
    other_basis = lax.ppermute(given, "core", swap_pairs())

    plane_axes = ("gy", "gz")
    chips = chips_y * devices_z

    def exchanged(rows, axes):
        return lax.all_to_all(rows, axes, split_axis=0, concat_axis=0, tiled=True)

    def for_all(own, size):
        return jnp.broadcast_to(own, (size, *own.shape))

    lead_terms = exchanged(lead.reshape(chips, -1, LEAF), plane_axes)

    def chip_products(images, lists, dtype, weight=1):
        return products(table, [flat_basis, other_basis], images, lists, narrow, dtype, weight)

    images, _ = lax.optimization_barrier(([image, other_image], lead))
    sent_a = [chip_products(images, lists_a[d], bf16) for d in range(1, devices_z)]
    sent_b = [chip_products(images, lists_b[d], bf16) for d in range(1, chips_y)]
    got_a = [move(a, "gz", d) for d, a in enumerate(sent_a, 1)]
    got_b = [move(a, "gy", d) for d, a in enumerate(sent_b, 1)]
    images, _ = lax.optimization_barrier((images, (sent_a, sent_b)))
    own_a = chip_products(images, lists_a[0], f32, 4)
    lead_terms, _ = lax.optimization_barrier((lead_terms, (sent_a, sent_b)))
    own = jnp.sum(lead_terms.astype(f32), axis=0).reshape(2, -1, LEAF)
    kept = lax.dynamic_index_in_dim(own, core, 0, keepdims=False)
    sent = lax.dynamic_index_in_dim(own, 1 - core, 0, keepdims=False)
    own = kept + lax.ppermute(sent, "core", swap_pairs())
    own, _ = lax.optimization_barrier((own, own_a))
    images, _ = lax.optimization_barrier((images, own))
    own_b = chip_products(images, lists_b[0], f32)
    own = own.reshape(devices_x, -1, LEAF)
    terms, _ = lax.optimization_barrier((exchanged(own, "gx"), own_b))
    own = jnp.sum(terms, axis=0)
    own = exchanged(for_all(own, devices_x), "gx").reshape(-1, LEAF)
    own = for_all(own, chips)
    (got_a, got_b), _ = lax.optimization_barrier(((got_a, got_b), own))
    lead_half = exchanged(own, plane_axes)
    sums_a, sums_b = [own_a, *got_a], [own_b, *got_b]

    further_a = [add_blocks(table, sums_a, *next_a[d], narrow, bf16) for d in range(1, chips_y)]
    further_b = [add_blocks(table, sums_b, *next_b[d], narrow, bf16) for d in range(1, devices_z)]
    lead_half, _ = lax.optimization_barrier((lead_half, (further_a, further_b)))
    further_a = [move(a, "gy", d) for d, a in enumerate(further_a, 1)]
    further_b = [move(a, "gz", d) for d, a in enumerate(further_b, 1)]
    other = lax.ppermute(lead_half, "core", swap_pairs())
    halves = jnp.where(core == 0, lead_half, other), jnp.where(core == 0, other, lead_half)
    lead = jnp.stack(halves, 1).reshape(lead_rows, LEAF)
    first_rows, later_rows = lead[:lower_rows], lead[lower_rows:]
    inverse_0 = first_panel(first_rows, NB)
    (further_a, further_b), inverse_0 = lax.optimization_barrier(
        ((further_a, further_b), inverse_0)
    )

    terms = []
    for zz in range(split):
        at = next_a[0][0] + zz
        terms.append([(a, at, None) for a in sums_a] + [(a, None, zz) for a in further_a])
    for zz in range(spans - split):
        at = next_b[0][0] + zz
        terms.append([(a, at, None) for a in sums_b] + [(a, None, zz) for a in further_b])
    outs = [jax.ShapeDtypeStruct((part, cols), bf16)] * devices_x
    outs += [jax.ShapeDtypeStruct((part, cols), f32)] * 2
    *x_sent, own, swapped = plane_parts(table, terms, narrow, leaving_at, outs)
    x_got = []
    for step in range(devices_x):
        pairs = []
        for x in range(devices_x):
            for y in range(devices_y):
                to = (x + step) % devices_x
                dest_x = (y % 2) * spans + to // 2
                dest_y = (y // 2) * 2 + to % 2
                if dest_x != x:
                    pairs.append((x * devices_y + y, dest_x * devices_y + dest_y))
        x_got.append(lax.ppermute(x_sent[step], ("gx", "gy", "core"), pairs))
    swapped = lax.ppermute(swapped, "core", swap_pairs())
    later_rows, _ = lax.optimization_barrier((later_rows, x_sent))
    factor_10, inverse_1 = next_panel(later_rows, inverse_0)
    (x_got, swapped), inverse_1 = lax.optimization_barrier(((x_got, swapped), inverse_1))
    pair = jax.ShapeDtypeStruct((2, part, cols // devices_y), f32)
    ins = [own, swapped, *x_got, inverse_0, factor_10, inverse_1]
    pairs = list(pl.pallas_call(
        functools.partial(factor_kernel, at=(home_at, order_at, first_at)),
        out_shape=[pair] * devices_y,
        grid_spec=pltpu.PrefetchScalarGridSpec(
            num_scalar_prefetch=1,
            grid=(1,),
            in_specs=[block_of(a) for a in ins],
            out_specs=[block_of(pair)] * devices_y,
            scratch_shapes=[pltpu.VMEM((part, cols), f32)] * 2,
        ),
        compiler_params=pltpu.CompilerParams(vmem_limit_bytes=44 * 2**20),
    )(table, *ins))
    for d in range(1, devices_y):
        route = [(i, (i + d) % devices_y) for i in range(devices_y)]
        pairs[d] = lax.ppermute(pairs[d], ("gy", "core"), route)
    out = jax.ShapeDtypeStruct((devices_y * part, cols // devices_y), f32)
    return pl.pallas_call(
        functools.partial(join_kernel, at=places_at),
        out_shape=(out, out),
        grid_spec=pltpu.PrefetchScalarGridSpec(
            num_scalar_prefetch=1,
            grid=(1,),
            in_specs=[block_of(a) for a in pairs],
            out_specs=[block_of(out)] * 2,
        ),
        compiler_params=pltpu.CompilerParams(vmem_limit_bytes=44 * 2**20),
    )(table, *pairs)


def solution(mesh):
    sizes = mesh.shape
    fine = jax.sharding.Mesh(
        mesh.devices.reshape(sizes["gx"], sizes["gy"] // 2, 2, sizes["gz"]),
        ("gx", "gy", "core", "gz"),
    )
    grid = ("gx", ("gy", "core"), "gz")
    out = P(("gx", "gz"), ("gy", "core"))
    return jax.shard_map(
        local,
        mesh=fine,
        in_specs=(P(*grid, None), P(*grid), P(), P(), P(), P()),
        out_specs=(out, out),
        check_vma=False,
    )
```
